32 devices in a mesh: dp: 8 (over y, x, core), tensor: 4 (over z).
Axes of the slice: x: 2, y: 2, z: 4, core: 2. Of those that a mesh axis runs over, the one named last changes fastest.
Arguments:
- block_in: bfloat16 [10240, 1024], P(('dp', 'tensor')), may hold values from -6 to 6
- norm1_gain: bfloat16 [1024], P('dp'), may hold values from 0.099609375 to 1.8984375
- norm1_bias: bfloat16 [1024], P('dp'), may hold values from -1.75 to 1.75
- qkv_weight: bfloat16 [1024, 3072], P('dp', 'tensor'), may hold values from -0.1875 to 0.1875
- qv_bias: bfloat16 [16, 128], P('tensor', 'dp'), may hold values from -3 to 3
- dense_weight: bfloat16 [1024, 1024], P('tensor', 'dp'), may hold values from -0.75 to 0.75
- dense_bias: bfloat16 [1024], P('dp'), may hold values from -1.75 to 1.75
- norm2_gain: bfloat16 [1024], P('dp'), may hold values from 0.099609375 to 1.8984375
- norm2_bias: bfloat16 [1024], P('dp'), may hold values from -1.75 to 1.75
- up_weight: bfloat16 [1024, 4096], P('dp', 'tensor'), may hold values from -0.1875 to 0.1875
- up_bias: bfloat16 [32, 128], P('tensor', 'dp'), may hold values from -3 to 3
- down_weight: bfloat16 [4096, 1024], P('tensor', 'dp'), may hold values from -0.1875 to 0.1875
- down_bias: bfloat16 [1024], P('dp'), may hold values from -1.75 to 1.75
- cotangent: bfloat16 [10240, 1024], P(('dp', 'tensor')), may hold values from -12 to 12
- seg_parent: int32 [26], replicated, may hold values from 0 to 17, as said below
- seg_length: int32 [26], replicated, may hold values from 128 to 3072, as said below
Outputs:
- block_out: bfloat16 [10240, 1024], P(('dp', 'tensor'))
- input_grad: float32 [10240, 1024], P(('dp', 'tensor'))
- norm1_gain_grad: float32 [1024], P('dp')
- norm1_bias_grad: float32 [1024], P('dp')
- qkv_weight_grad: float32 [1024, 3072], P('dp', 'tensor')
- qv_bias_grad: float32 [16, 128], P('tensor', 'dp')
- dense_weight_grad: float32 [1024, 1024], P('tensor', 'dp')
- dense_bias_grad: float32 [1024], P('dp')
- norm2_gain_grad: float32 [1024], P('dp')
- norm2_bias_grad: float32 [1024], P('dp')
- up_weight_grad: float32 [1024, 4096], P('dp', 'tensor')
- up_bias_grad: float32 [32, 128], P('tensor', 'dp')
- down_weight_grad: float32 [4096, 1024], P('tensor', 'dp')
- down_bias_grad: float32 [1024], P('dp')
The draws below stay inside these ranges and needn't reach their ends.
Inputs may be any that keep to these rules, and one draw needn't show every extreme that they name: `seg_parent`: segments come in trees of 13, laid end to end: a tree's first segment is its trunk and names itself, the next four are branches naming the trunk, the last eight are leaves naming a branch of their own tree, two leaves on each branch. `seg_length`: branches have 256 tokens; the two leaves of one branch have 2 * 256 together; the trunks of trees 2m and 2m + 1 have 2 * 2048 together, so that every aligned pair of trees has 10240 tokens.
All inputs are finite; a program needn't handle non-finite values.
Results may differ from the reference program's by a relative error of at most 0.018.
Values may be sent and summed in bfloat16 or wider, within the bound.
A program may use at most 192 MiB of HBM per device.

```python
import jax
import jax.numpy as jnp
from jax import lax

D = 1024
HEADS = 16
HD = 64
FF = 4096
TRUNK = 2048
SEG = 256
TOK_DP = 1280
TOKENS = 10240
TREES = 2
SEGS = 26


def tree_layout(key):
    trunk_key, pick_key, leaf_key, mark_key, order_key = jax.random.split(key, 5)
    pair_count = TREES // 2
    trunk_shift = jax.random.randint(trunk_key, (pair_count,), -(TRUNK // 2), TRUNK // 2 + 1)
    chosen = jax.random.randint(pick_key, (), 0, pair_count)
    trunk_shift = jnp.where(jnp.arange(pair_count) == chosen, TRUNK // 2, trunk_shift)
    trunks = jnp.stack([TRUNK + trunk_shift, TRUNK - trunk_shift], axis=1).reshape(TREES, 1)
    offset = jax.random.randint(leaf_key, (TREES, 4), -(SEG // 2), SEG // 2 + 1)
    marked = jax.random.randint(mark_key, (), 0, TREES * 4)
    offset = jnp.where(jnp.arange(TREES * 4).reshape(TREES, 4) == marked, SEG // 2, offset)
    leaf_sizes = jnp.stack([SEG + offset, SEG - offset], axis=2).reshape(TREES, 8)
    leaf_branch = jnp.broadcast_to(jnp.repeat(jnp.arange(4), 2)[None, :], (TREES, 8))
    orders = jax.vmap(lambda subkey: jax.random.permutation(subkey, 8))(jax.random.split(order_key, TREES))
    leaf_sizes = jnp.take_along_axis(leaf_sizes, orders, axis=1)
    leaf_branch = jnp.take_along_axis(leaf_branch, orders, axis=1)
    root_ids = jnp.arange(TREES)[:, None] * 13
    lengths = jnp.concatenate([trunks, jnp.full((TREES, 4), SEG), leaf_sizes], axis=1).reshape(SEGS)
    parents = jnp.concatenate([root_ids, jnp.broadcast_to(root_ids, (TREES, 4)), root_ids + 1 + leaf_branch], axis=1).reshape(SEGS)
    return (parents.astype(jnp.int32), lengths.astype(jnp.int32))


def draw_seg_parent(key, part):
    return tree_layout(key)[0]


def draw_seg_length(key, part):
    return tree_layout(key)[1]


def with_spikes(drawn, rng, source, target, shards_of, factor):
    owner, partner = [(jnp.arange(drawn.shape[dim]) // (drawn.shape[dim] // shards_of)).reshape([-1 if axis == dim else 1 for axis in range(drawn.ndim)]) for dim in (source, target)]
    chosen = jax.random.permutation(rng, shards_of)[partner]
    strong = (owner == chosen) | (owner == (partner + shards_of // 2) % shards_of)
    return jnp.where(strong, factor * drawn, drawn)


def shard_levels(key, dims, pieces, low, high):
    gain, own = 1.0, jax.random.fold_in(key, 6)
    for position, blocks in pieces:
        draws = jnp.exp(jax.random.uniform(jax.random.fold_in(own, position), (blocks,), jnp.float32, low / len(pieces), high / len(pieces)))
        gain = gain * jnp.repeat(draws, dims[position] // blocks).reshape([-1 if axis == position else 1 for axis in range(len(dims))])
    return gain


def normal_values(key, extent, scale, most, shards=(), kind=jnp.bfloat16):
    values = scale * jax.random.normal(key, extent, jnp.float32)
    if shards:
        values = values * shard_levels(key, extent, shards, -0.22, 0.18)
    return jnp.clip(values, -most, most).astype(kind)


def noise_with(key, dims, deviation, bound, pieces, heavy, kind=jnp.bfloat16):
    drawn = deviation * jax.random.normal(key, dims, jnp.float32)
    if pieces:
        drawn = drawn * shard_levels(key, dims, pieces, -0.22, 0.18)
    return jnp.clip(with_spikes(drawn, jax.random.fold_in(key, 3), *heavy), -bound, bound).astype(kind)


def setup_inputs(seed: int = 0) -> dict:
    arg_keys = jax.random.split(jax.random.key(seed), 17)
    return {
        "block_in": normal_values(arg_keys[0], (TOKENS, D), 1.0, 6.0, ((0, 32),)),
        "norm1_gain": jnp.clip(1.0 + 0.18 * jax.random.normal(arg_keys[1], (D,), jnp.float32), 0.099609375, 1.8984375).astype(jnp.bfloat16),
        "norm1_bias": normal_values(arg_keys[2], (D,), 0.3, 1.75, ((0, 8),)),
        "qkv_weight": normal_values(arg_keys[3], (D, 3 * D), D ** -0.5, 0.1875, ((0, 8), (1, 4))),
        "qv_bias": normal_values(arg_keys[4], (HEADS, 2 * HD), 0.5, 3.0, ((0, 4), (1, 8))),
        "dense_weight": normal_values(arg_keys[5], (D, D), (D // 16) ** -0.5, 0.75, ((0, 4), (1, 8))),
        "dense_bias": normal_values(arg_keys[6], (D,), 0.3, 1.75, ((0, 8),)),
        "norm2_gain": jnp.clip(1.0 + 0.18 * jax.random.normal(arg_keys[7], (D,), jnp.float32), 0.099609375, 1.8984375).astype(jnp.bfloat16),
        "norm2_bias": normal_values(arg_keys[8], (D,), 0.3, 1.75, ((0, 8),)),
        "up_weight": normal_values(arg_keys[9], (D, FF), D ** -0.5, 0.1875, ((0, 8), (1, 4))),
        "up_bias": normal_values(arg_keys[10], (FF // 128, 128), 0.5, 3.0, ((0, 4), (1, 8))),
        "down_weight": normal_values(arg_keys[11], (FF, D), (FF // 4) ** -0.5, 0.1875, ((0, 4), (1, 8))),
        "down_bias": normal_values(arg_keys[12], (D,), 0.3, 1.75, ((0, 8),)),
        "cotangent": noise_with(arg_keys[13], (TOKENS, D), 1.0, 12.0, ((0, 32),), (0, 1, 32, 2.75)),
        "seg_parent": draw_seg_parent(jax.random.fold_in(arg_keys[16], 71), 0),
        "seg_length": draw_seg_length(jax.random.fold_in(arg_keys[16], 71), 0),
    }


epsilon = 1e-05
masked_score = -1e+30
highest = lax.Precision.HIGHEST

@jax.custom_vjp
def low(v):
    return lax.optimization_barrier(v.astype(jnp.bfloat16)).astype(jnp.float32)

@jax.custom_vjp
def low_back(v):
    return v

def low_keep(v):
    return (low(v), None)

def low_pass(kept, grad):
    return (grad,)

def back_keep(v):
    return (v, None)

def back_low(kept, grad):
    return (low(grad),)
low.defvjp(low_keep, low_pass)
low_back.defvjp(back_keep, back_low)

def normalize(values, gain_row, bias_row):
    average = lax.optimization_barrier(jnp.mean(values, axis=-1, keepdims=True))
    centred = values - average
    spread = lax.optimization_barrier(jnp.mean(centred * centred, axis=-1, keepdims=True))
    return centred * lax.rsqrt(spread + epsilon) * gain_row + bias_row

def token_meta(token_index, seg_parent, seg_length):
    total_segs = seg_length.shape[0]
    seg_ends = jnp.cumsum(seg_length).astype(jnp.int32)
    seg_starts = (seg_ends - seg_length).astype(jnp.int32)
    itself = jnp.arange(total_segs, dtype=jnp.int32)
    grandparent = seg_parent[seg_parent]
    path_start = jnp.where(seg_parent == itself, 0, seg_length[seg_parent] + jnp.where(grandparent == seg_parent, 0, seg_length[grandparent])).astype(jnp.int32)
    segment = jnp.minimum(jnp.searchsorted(seg_ends, token_index, side='right'), total_segs - 1).astype(jnp.int32)
    path_place = (token_index - seg_starts[segment] + path_start[segment]).astype(jnp.int32)
    return (segment, seg_parent[segment], grandparent[segment], path_place)

def attention_block(number, queries, key_rows, value_rows, slopes, meta, block_rows, window):
    segment, parent_of, grand_of, path_place = meta
    first_row = (number * block_rows).astype(jnp.int32)
    begin_row = jnp.maximum(first_row + block_rows - window, 0).astype(jnp.int32)
    query_block = lax.dynamic_slice_in_dim(queries, first_row, block_rows, 0)
    key_block = lax.dynamic_slice_in_dim(key_rows, begin_row, window, 0)
    value_block = lax.dynamic_slice_in_dim(value_rows, begin_row, window, 0)
    query_seg = lax.dynamic_slice_in_dim(segment, first_row, block_rows, 0)
    query_parent = lax.dynamic_slice_in_dim(parent_of, first_row, block_rows, 0)
    query_grand = lax.dynamic_slice_in_dim(grand_of, first_row, block_rows, 0)
    query_place = lax.dynamic_slice_in_dim(path_place, first_row, block_rows, 0)
    key_seg = lax.dynamic_slice_in_dim(segment, begin_row, window, 0)
    key_place = lax.dynamic_slice_in_dim(path_place, begin_row, window, 0)
    query_index = first_row + jnp.arange(block_rows, dtype=jnp.int32)
    key_index = begin_row + jnp.arange(window, dtype=jnp.int32)
    related = (key_seg[None, :] == query_seg[:, None]) | (key_seg[None, :] == query_parent[:, None]) | (key_seg[None, :] == query_grand[:, None])
    visible = related & (key_index[None, :] <= query_index[:, None])
    distance = (query_place[:, None] - key_place[None, :]).astype(jnp.float32)
    products = jnp.einsum('qhd,khd->hqk', query_block, key_block, precision=highest)
    scores = low_back(0.125 * products) - slopes[:, None, None] * distance[None]
    scores = jnp.where(visible[None], scores, masked_score)
    top_score = lax.optimization_barrier(jnp.max(scores, axis=2, keepdims=True))
    weights = jnp.exp(scores - top_score)
    probability = weights / lax.optimization_barrier(jnp.sum(weights, axis=2, keepdims=True))
    context_rows = jnp.einsum('hqk,khd->qhd', low(probability), value_block, precision=highest)
    return low(low_back(context_rows))

def attention(queries, key_rows, value_rows, slopes, meta):
    total_rows = queries.shape[0]
    block_rows = TOK_DP // max(1, TOK_DP // 512)
    longest = 3 * TRUNK // 2 + 12 * SEG
    window = min(total_rows, (longest - 1 + block_rows - 1) // block_rows * block_rows + block_rows)
    checked = jax.checkpoint(partial_block(block_rows, window))
    blocks = lax.map(lambda number: checked(number, queries, key_rows, value_rows, slopes, meta), jnp.arange(total_rows // block_rows, dtype=jnp.int32))
    return blocks.reshape(total_rows, HEADS, HD)

def partial_block(block_rows, window):

    def block_function(number, queries, key_rows, value_rows, slopes, meta):
        return attention_block(number, queries, key_rows, value_rows, slopes, meta, block_rows, window)
    return block_function

def layer(block_in, norm1_gain, norm1_bias, qkv_weight, qv_bias, dense_weight, dense_bias, norm2_gain, norm2_bias, up_weight, up_bias, down_weight, down_bias, meta, slopes):
    total_rows = block_in.shape[0]
    normed_one = low(normalize(block_in, norm1_gain, norm1_bias))
    key_zeros = jnp.zeros((HEADS, 1, HD), jnp.float32)
    qkv_shift = jnp.concatenate([qv_bias[:, None, :HD], key_zeros, qv_bias[:, None, HD:]], axis=1).reshape(3 * D)
    projected = jnp.dot(normed_one, qkv_weight, precision=highest) + qkv_shift
    projected = low(low_back(projected)).reshape(total_rows, HEADS, 3, HD)
    context = attention(projected[:, :, 0], projected[:, :, 1], projected[:, :, 2], slopes, meta)
    attended = low_back(jnp.dot(context.reshape(total_rows, D), dense_weight, precision=highest))
    middle = block_in + attended + dense_bias
    normed_two = low(normalize(middle, norm2_gain, norm2_bias))
    upper = low_back(jnp.dot(normed_two, up_weight, precision=highest) + up_bias.reshape(FF))
    active = low(jax.nn.gelu(upper, approximate=True))
    return middle + low_back(jnp.dot(active, down_weight, precision=highest)) + down_bias

def reference(block_in, norm1_gain, norm1_bias, qkv_weight, qv_bias, dense_weight, dense_bias, norm2_gain, norm2_bias, up_weight, up_bias, down_weight, down_bias, cotangent, seg_parent, seg_length):
    floats = tuple((operand.astype(jnp.float32) for operand in (block_in, norm1_gain, norm1_bias, qkv_weight, qv_bias, dense_weight, dense_bias, norm2_gain, norm2_bias, up_weight, up_bias, down_weight, down_bias)))
    token_index = jnp.arange(block_in.shape[0], dtype=jnp.int32)
    meta = token_meta(token_index, seg_parent, seg_length)
    slopes = jnp.exp2(-8.0 * (jnp.arange(HEADS, dtype=jnp.float32) + 1.0) / HEADS) / TRUNK

    def forward(*operands):
        return layer(*operands, meta, slopes)
    result, pullback = jax.vjp(forward, *floats)
    grads = pullback(cotangent.astype(jnp.float32))
    return (result.astype(jnp.bfloat16), grads[0], grads[1], grads[2], grads[3], grads[4], grads[5], grads[6], grads[7], grads[8], grads[9], grads[10], grads[11], grads[12])
```

```python
import functools

import jax
import jax.numpy as jnp
from jax import lax
from jax.experimental import pallas as pl
from jax.experimental.pallas import tpu as pltpu
from jax.sharding import PartitionSpec as P

HEADS = 16
HD = 64
TRUNK = 2048
SEG = 256
PAIR_TOKENS = 2 * (TRUNK + 12 * SEG)
PAIR_SEGS = 26
QUERY_BLOCK = 256
KEY_BLOCK = 512
BIG = 2.0**100
VALUE_ROWS = 80

epsilon = 1e-05
f32 = jnp.float32
bf16 = jnp.bfloat16


def normalize(values, gain_row, bias_row):
    average = jnp.mean(values, axis=-1, keepdims=True)
    centred = values - average
    spread = jnp.mean(centred * centred, axis=-1, keepdims=True)
    return centred * lax.rsqrt(spread + epsilon) * gain_row + bias_row


def norm_back(values, gain_row, bias_row, grad_rows):
    pullback = jax.vjp(normalize, values, gain_row.astype(f32), bias_row.astype(f32))[1]
    return pullback(grad_rows)


def gelu_tanh(values):
    return jax.nn.gelu(values, approximate=True)


def nn(left, right):
    return lax.dot_general(left, right, (((1,), (0,)), ((), ())), preferred_element_type=f32)


def nt(left, right):
    return lax.dot_general(left, right, (((1,), (1,)), ((), ())), preferred_element_type=f32)


def tn(left, right):
    return lax.dot_general(left, right, (((0,), (0,)), ((), ())), preferred_element_type=f32)


def pieces(value, count):
    parts = []
    for _ in range(count):
        part = lax.reduce_precision(value, 8, 7)
        parts.append(part)
        value = value - part
    return parts


def core_of(index):
    return (index ^ (index >> 1)) & 1


def token_tables(seg_parent, seg_length, group):
    first = group * PAIR_SEGS
    parent = lax.dynamic_slice_in_dim(seg_parent, first, PAIR_SEGS, 0) - first
    length = lax.dynamic_slice_in_dim(seg_length, first, PAIR_SEGS, 0)
    ids = jnp.arange(PAIR_SEGS, dtype=jnp.int32)
    begin = jnp.sum(jnp.where(ids[None, :] < ids[:, None], length[None, :], 0), axis=1)
    end = begin + length
    is_parent = parent[:, None] == ids[None, :]
    grand = jnp.sum(jnp.where(is_parent, parent[None, :], 0), axis=1)
    is_grand = grand[:, None] == ids[None, :]
    parent_length = jnp.sum(jnp.where(is_parent, length[None, :], 0), axis=1)
    grand_length = jnp.sum(jnp.where(is_grand, length[None, :], 0), axis=1)
    path_start = jnp.where(
        parent == ids, 0, parent_length + jnp.where(grand == parent, 0, grand_length)
    )
    related = is_parent | is_grand | (ids[:, None] == ids[None, :])
    token = jnp.arange(PAIR_TOKENS, dtype=jnp.int32)
    member = (token[:, None] >= begin[None, :]) & (token[:, None] < end[None, :])
    place = token + jnp.sum(jnp.where(member, (path_start - begin)[None, :], 0), axis=1)
    allowed = jnp.zeros(member.shape, bool)
    for other in range(PAIR_SEGS):
        allowed = allowed | (member[:, other : other + 1] & related[other][None, :])
    query_blocks, key_blocks = PAIR_TOKENS // QUERY_BLOCK, PAIR_TOKENS // KEY_BLOCK
    q_begin = jnp.arange(query_blocks, dtype=jnp.int32) * QUERY_BLOCK
    k_begin = jnp.arange(key_blocks, dtype=jnp.int32) * KEY_BLOCK
    q_has = (begin[None, :] < q_begin[:, None] + QUERY_BLOCK) & (end[None, :] > q_begin[:, None])
    k_has = (begin[None, :] < k_begin[:, None] + KEY_BLOCK) & (end[None, :] > k_begin[:, None])
    q_sees = jnp.any(q_has[:, :, None] & related[None], axis=1)
    seen = jnp.any(q_sees[:, None, :] & k_has[None, :, :], axis=2)
    seen = seen & (k_begin[None, :] + KEY_BLOCK <= q_begin[:, None])
    rank = jnp.sum(
        jnp.where(k_begin[None, None, :] < k_begin[None, :, None], seen[:, None, :], False),
        axis=2,
        dtype=jnp.int32,
    )
    slots = jnp.arange(key_blocks, dtype=jnp.int32)
    block_list = jnp.sum(
        jnp.where(
            seen[:, :, None] & (rank[:, :, None] == slots[None, None, :]), slots[None, :, None], 0
        ),
        axis=1,
    )
    block_count = jnp.sum(seen, axis=1, dtype=jnp.int32)
    return member, allowed, place, block_list, block_count


def causal_scores(scores, key_first, query_first):
    rows = key_first + lax.broadcasted_iota(jnp.int32, scores.shape, 0)
    columns = query_first + lax.broadcasted_iota(jnp.int32, scores.shape, 1)
    return jnp.where(rows <= columns, scores, -BIG)


def forward_kernel(block_of, count_of, list_of, q_ref, k_ref, v_ref, o_ref, log_ref):
    number = pl.program_id(0)
    query_first = block_of[number] * QUERY_BLOCK
    queries = q_ref[...]

    def attend(key_block, carry, masked):
        top, total = carry
        first = pl.multiple_of(key_block * KEY_BLOCK, KEY_BLOCK)
        scores = nt(k_ref[pl.ds(first, KEY_BLOCK), :], queries)
        if masked:
            scores = causal_scores(scores, first, query_first)
        new_top = jnp.maximum(top, jnp.max(scores, axis=0, keepdims=True))
        weights = jnp.exp(scores - new_top)
        total = total * jnp.exp(top - new_top) + nn(
            v_ref[:, pl.ds(first, KEY_BLOCK)], weights.astype(bf16)
        )
        return new_top, total

    carry = (jnp.full((1, QUERY_BLOCK), -BIG, f32), jnp.zeros((VALUE_ROWS, QUERY_BLOCK), f32))
    carry = attend(query_first // KEY_BLOCK, carry, True)
    top, total = lax.fori_loop(
        0, count_of[number], lambda step, kept: attend(list_of[number, step], kept, False), carry
    )
    row_sum = total[HD : HD + 1]
    o_ref[...] = (total[:HD] / row_sum).T
    log_ref[...] = jnp.broadcast_to(top + jnp.log(row_sum), log_ref.shape)


def attention_forward(blocks, counts, lists, queries, keys, values_t):
    steps = queries.shape[0] // QUERY_BLOCK
    whole = lambda shape: pl.BlockSpec(shape, lambda i, *_: (0, 0))
    return pl.pallas_call(
        forward_kernel,
        grid_spec=pltpu.PrefetchScalarGridSpec(
            num_scalar_prefetch=3,
            grid=(steps,),
            in_specs=[
                pl.BlockSpec((QUERY_BLOCK, 128), lambda i, *_: (i, 0)),
                whole(keys.shape),
                whole(values_t.shape),
            ],
            out_specs=[
                pl.BlockSpec((QUERY_BLOCK, HD), lambda i, *_: (i, 0)),
                pl.BlockSpec((8, QUERY_BLOCK), lambda i, *_: (0, i)),
            ],
        ),
        out_shape=[
            jax.ShapeDtypeStruct((queries.shape[0], HD), f32),
            jax.ShapeDtypeStruct((8, queries.shape[0]), f32),
        ],
        compiler_params=pltpu.CompilerParams(vmem_limit_bytes=40 * 2**20),
        cost_estimate=pl.CostEstimate(
            flops=2 * 256 * 2 * 12_000_000, bytes_accessed=10_000_000, transcendentals=12_000_000
        ),
        name="attention_forward",
    )(blocks, counts, lists, queries, keys, values_t)


def backward_kernel(
    block_of, count_of, list_of, q_ref, g_ref, k_ref, v_ref, kt_ref, dq_ref, dkv_ref, dk, dv
):
    number = pl.program_id(0)
    query_first = block_of[number] * QUERY_BLOCK

    @pl.when(number == 0)
    def _():
        dk[...] = jnp.zeros_like(dk)
        dv[...] = jnp.zeros_like(dv)

    queries = q_ref[...]
    grads = g_ref[...]

    def attend(key_block, dq, masked):
        first = pl.multiple_of(key_block * KEY_BLOCK, KEY_BLOCK)
        span = pl.ds(first, KEY_BLOCK)
        scores = nt(k_ref[span, :], queries)
        if masked:
            scores = causal_scores(scores, first, query_first)
        weights = jnp.exp(scores)
        score_grad = (weights * nt(v_ref[span, :], grads)).astype(bf16)
        dv[span, :] += nn(weights.astype(bf16), grads)
        dk[span, :] += nn(score_grad, queries)
        return dq + nn(kt_ref[:, span], score_grad)

    dq = attend(query_first // KEY_BLOCK, jnp.zeros((HD, QUERY_BLOCK), f32), True)
    dq = lax.fori_loop(
        0, count_of[number], lambda step, kept: attend(list_of[number, step], kept, False), dq
    )
    dq_ref[...] = (dq * 0.125).T

    @pl.when(number == pl.num_programs(0) - 1)
    def _():
        def write(step, _):
            span = pl.ds(pl.multiple_of(step * KEY_BLOCK, KEY_BLOCK), KEY_BLOCK)
            dkv_ref[span, :] = jnp.concatenate([dk[span, :HD], dv[span, :HD]], axis=1).astype(bf16)
            return 0

        lax.fori_loop(0, dk.shape[0] // KEY_BLOCK, write, 0)


def attention_backward(blocks, counts, lists, queries, grads, keys, values, keys_t):
    steps = queries.shape[0] // QUERY_BLOCK
    whole = lambda shape: pl.BlockSpec(shape, lambda i, *_: (0, 0))
    rows = pl.BlockSpec((QUERY_BLOCK, 128), lambda i, *_: (i, 0))
    return pl.pallas_call(
        backward_kernel,
        grid_spec=pltpu.PrefetchScalarGridSpec(
            num_scalar_prefetch=3,
            grid=(steps,),
            in_specs=[rows, rows, whole(keys.shape), whole(values.shape), whole(keys_t.shape)],
            out_specs=[
                pl.BlockSpec((QUERY_BLOCK, HD), lambda i, *_: (i, 0)),
                whole(keys.shape),
            ],
            scratch_shapes=[pltpu.VMEM(keys.shape, f32), pltpu.VMEM(keys.shape, f32)],
        ),
        out_shape=[
            jax.ShapeDtypeStruct((queries.shape[0], HD), f32),
            jax.ShapeDtypeStruct(keys.shape, bf16),
        ],
        compiler_params=pltpu.CompilerParams(vmem_limit_bytes=56 * 2**20),
        cost_estimate=pl.CostEstimate(
            flops=5 * 256 * 2 * 12_000_000, bytes_accessed=16_000_000, transcendentals=12_000_000
        ),
        name="attention_backward",
    )(blocks, counts, lists, queries, grads, keys, values, keys_t)


def per_device(
    block_in,
    norm1_gain,
    norm1_bias,
    qkv_weight,
    qv_bias,
    dense_weight,
    dense_bias,
    norm2_gain,
    norm2_bias,
    up_weight,
    up_bias,
    down_weight,
    down_bias,
    cotangent,
    seg_parent,
    seg_length,
):
    dp_count, tensor_count = lax.axis_size("dp"), lax.axis_size("tensor")
    dp_index, tensor_index = lax.axis_index("dp"), lax.axis_index("tensor")
    rows, width = block_in.shape
    dp_rows = rows * tensor_count
    span = PAIR_TOKENS // dp_rows
    heads_here = HEADS // tensor_count
    groups = [list(range(g * span, (g + 1) * span)) for g in range(dp_count // span)]
    local_index = lax.rem(dp_index, span)
    core = lax.rem(dp_index, 2)
    both = ("dp", "tensor")

    def gather_vector(value):
        return lax.all_gather(value, "dp", axis=0, tiled=True).astype(f32)

    gain_one, bias_one, gain_two, bias_two, dense_shift, down_shift = map(
        gather_vector, (norm1_gain, norm1_bias, norm2_gain, norm2_bias, dense_bias, down_bias)
    )

    def gather_matrix(value, dp_axis):
        value = lax.all_gather(value, "tensor", axis=1 - dp_axis, tiled=True)
        return lax.all_gather(value, "dp", axis=dp_axis, tiled=True)

    qkv_full = gather_matrix(qkv_weight, 0)
    dense_full = gather_matrix(dense_weight, 1)
    up_full = gather_matrix(up_weight, 0)
    down_full = gather_matrix(down_weight, 1)
    qv_full = gather_matrix(qv_bias, 1).astype(f32)
    up_shift = gather_matrix(up_bias, 1).astype(f32)

    member, allowed, place, block_list, block_count = token_tables(
        seg_parent, seg_length, dp_index // span
    )
    head = tensor_index * heads_here + local_index // 2
    slope = jnp.exp2(-8.0 * (head.astype(f32) + 1.0) / HEADS) / TRUNK
    key_shift = pieces(slope * place.astype(f32), 2)
    one = jnp.ones((PAIR_TOKENS, 1), f32)
    blank = jnp.zeros((PAIR_TOKENS, 64 - PAIR_SEGS - 5), f32)
    key_meta = jnp.concatenate(
        [member.astype(f32)] + [part[:, None] for part in key_shift] + [one] * 3 + [blank], axis=1
    ).astype(bf16)
    query_mask = jnp.where(allowed, 0.0, -BIG)
    mine = core_of(jnp.arange(span, dtype=jnp.int32)) == core
    half = span // 2
    taken = jnp.stack([2 * i + (core ^ (i & 1)) for i in range(half)])
    block_ids = (
        taken[:, None] * (dp_rows // QUERY_BLOCK)
        + jnp.arange(dp_rows // QUERY_BLOCK, dtype=jnp.int32)[None, :]
    ).reshape(-1)

    def take(whole):
        parts = whole.reshape((half, 2) + (dp_rows,) + whole.shape[1:])
        flip = jnp.stack([core ^ (i & 1) for i in range(half)])
        pick = flip.reshape((half,) + (1,) * (parts.ndim - 2))
        return jnp.where(pick == 0, parts[:, 0], parts[:, 1]).reshape(
            (half * dp_rows,) + whole.shape[1:]
        )

    def put(part):
        parts = part.reshape((half, dp_rows) + part.shape[1:])
        flip = jnp.stack([core ^ (i & 1) for i in range(half)])
        pick = flip.reshape((half,) + (1,) * (parts.ndim - 1))
        zero = jnp.zeros_like(parts)
        whole = jnp.stack(
            [jnp.where(pick == 0, parts, zero), jnp.where(pick == 0, zero, parts)], axis=1
        )
        return whole.reshape((span * dp_rows,) + part.shape[1:])

    def to_heads(values):
        n = values.shape[2]
        values = lax.all_to_all(values, "tensor", split_axis=1, concat_axis=0, tiled=True)
        values = jnp.repeat(values.transpose(1, 0, 2), 2, axis=0)
        values = lax.all_to_all(
            values, "dp", split_axis=0, concat_axis=0, tiled=True, axis_index_groups=groups
        )
        return values.reshape(PAIR_TOKENS, n)

    def to_tokens(values):
        n = values.shape[1]
        values = lax.all_to_all(
            values.reshape(span, dp_rows, n),
            "dp",
            split_axis=0,
            concat_axis=0,
            tiled=True,
            axis_index_groups=groups,
        )
        values = jnp.sum(values.reshape(heads_here, 2, dp_rows, n).astype(f32), axis=1)
        values = values.astype(bf16).transpose(1, 0, 2)
        return lax.all_to_all(values, "tensor", split_axis=0, concat_axis=1, tiled=True)

    inputs = block_in.astype(f32)
    normed_one = normalize(inputs, gain_one, bias_one).astype(bf16)
    key_zeros = jnp.zeros((HEADS, 1, HD), f32)
    qkv_shift = jnp.concatenate(
        [qv_full[:, None, :HD], key_zeros, qv_full[:, None, HD:]], axis=1
    ).reshape(-1)
    projected = (nn(normed_one, qkv_full) + qkv_shift).astype(bf16)
    mixed = to_heads(projected.reshape(rows, HEADS, 3 * HD))
    queries = take(mixed[:, :HD].astype(f32) * 0.125).astype(bf16)
    keys = jnp.concatenate([mixed[:, HD : 2 * HD], key_meta], axis=1)
    values = mixed[:, 2 * HD :]
    one_low = jnp.ones((PAIR_TOKENS, 1), bf16)
    values_t = jnp.concatenate(
        [values, one_low, jnp.zeros((PAIR_TOKENS, VALUE_ROWS - HD - 1), bf16)], axis=1
    ).T
    values_wide = jnp.concatenate(
        [values, one_low, one_low, one_low, jnp.zeros((PAIR_TOKENS, 64 - 3), bf16)], axis=1
    )
    my_mask = take(query_mask).astype(bf16)
    my_rows = my_mask.shape[0]
    ones_two = jnp.ones((my_rows, 2), bf16)
    queries_forward = jnp.concatenate(
        [queries, my_mask, ones_two, jnp.zeros((my_rows, 64 - PAIR_SEGS - 2), bf16)], axis=1
    )
    my_counts, my_lists = jnp.take(block_count, block_ids), jnp.take(block_list, block_ids, axis=0)
    out_float, log_total = attention_forward(
        block_ids, my_counts, my_lists, queries_forward, keys, values_t
    )
    context = to_tokens(put(out_float.astype(bf16))).reshape(rows, width)

    attended = nn(context, dense_full)
    middle = inputs + attended + dense_shift
    normed_two = normalize(middle, gain_two, bias_two).astype(bf16)
    upper = nn(normed_two, up_full) + up_shift.reshape(-1)
    active = gelu_tanh(upper).astype(bf16)
    block_out = (middle + nn(active, down_full) + down_shift).astype(bf16)

    out_grad = cotangent.astype(f32)
    down_grad = tn(active, cotangent)
    active_grad = nt(cotangent, down_full)
    upper_grad = jax.vjp(gelu_tanh, upper)[1](active_grad)[0].astype(bf16)
    up_shift_grad = jnp.sum(upper_grad, axis=0, dtype=f32).reshape(up_shift.shape)
    up_grad = tn(normed_two, upper_grad)
    middle_part, gain_two_grad, bias_two_grad = norm_back(
        middle, gain_two, bias_two, nt(upper_grad, up_full)
    )
    middle_grad = out_grad + middle_part
    middle_low = middle_grad.astype(bf16)
    dense_grad = tn(context, middle_low)
    context_grad = nt(middle_low, dense_full).astype(bf16)

    out_grads = take(to_heads(context_grad.reshape(rows, HEADS, HD)))
    inner = jnp.sum(out_grads.astype(f32) * out_float, axis=1, keepdims=True)
    log_parts = [part.astype(bf16) for part in pieces(-log_total[0][:, None], 3)]
    queries_backward = jnp.concatenate(
        [queries, my_mask, ones_two] + log_parts + [jnp.zeros((my_rows, 64 - PAIR_SEGS - 5), bf16)],
        axis=1,
    )
    inner_parts = [part.astype(bf16) for part in pieces(-inner, 3)]
    grads_wide = jnp.concatenate(
        [out_grads] + inner_parts + [jnp.zeros((my_rows, 64 - 3), bf16)], axis=1
    )
    dq, dkv = attention_backward(
        block_ids,
        my_counts,
        my_lists,
        queries_backward,
        grads_wide,
        keys,
        values_wide,
        mixed[:, HD : 2 * HD].T,
    )
    qkv_grad = to_tokens(jnp.concatenate([put(dq.astype(bf16)), dkv], axis=1))
    qkv_totals = jnp.sum(qkv_grad.reshape(rows, HEADS, 3, HD), axis=0, dtype=f32)
    qv_grad = jnp.concatenate([qkv_totals[:, 0], qkv_totals[:, 2]], axis=1)
    qkv_grad = qkv_grad.reshape(rows, HEADS * 3 * HD)
    qkv_weight_part = tn(normed_one, qkv_grad)
    input_part, gain_one_grad, bias_one_grad = norm_back(
        inputs, gain_one, bias_one, nt(qkv_grad, qkv_full)
    )
    input_grad = middle_grad + input_part

    def scatter_matrix(value, dp_axis, kind=bf16):
        value = lax.psum_scatter(
            value.astype(kind), "dp", scatter_dimension=dp_axis, tiled=True
        )
        return lax.psum_scatter(
            value, "tensor", scatter_dimension=1 - dp_axis, tiled=True
        ).astype(f32)

    def scatter_vector(value):
        return lax.psum(lax.psum_scatter(value, "dp", scatter_dimension=0, tiled=True), "tensor")

    return (
        block_out,
        input_grad,
        scatter_vector(gain_one_grad),
        scatter_vector(bias_one_grad),
        scatter_matrix(qkv_weight_part, 0),
        scatter_matrix(qv_grad, 1, f32),
        scatter_matrix(dense_grad, 1),
        scatter_vector(jnp.sum(middle_grad, axis=0)),
        scatter_vector(gain_two_grad),
        scatter_vector(bias_two_grad),
        scatter_matrix(up_grad, 0),
        scatter_matrix(up_shift_grad, 1, f32),
        scatter_matrix(down_grad, 1),
        scatter_vector(jnp.sum(out_grad, axis=0)),
    )


def solution(mesh):
    rows = P(("dp", "tensor"), None)
    in_specs = (
        rows,
        P("dp"),
        P("dp"),
        P("dp", "tensor"),
        P("tensor", "dp"),
        P("tensor", "dp"),
        P("dp"),
        P("dp"),
        P("dp"),
        P("dp", "tensor"),
        P("tensor", "dp"),
        P("tensor", "dp"),
        P("dp"),
        rows,
        P(),
        P(),
    )
    out_specs = (
        rows,
        rows,
        P("dp"),
        P("dp"),
        P("dp", "tensor"),
        P("tensor", "dp"),
        P("tensor", "dp"),
        P("dp"),
        P("dp"),
        P("dp"),
        P("dp", "tensor"),
        P("tensor", "dp"),
        P("tensor", "dp"),
        P("dp"),
    )
    return jax.shard_map(
        per_device, mesh=mesh, in_specs=in_specs, out_specs=out_specs, check_vma=False
    )
```

```python
import functools

import jax
import jax.numpy as jnp
from jax import lax
from jax.experimental import pallas as pl
from jax.experimental.pallas import tpu as pltpu
from jax.sharding import PartitionSpec as P

HEADS = 16
HD = 64
TRUNK = 2048
SEG = 256
PAIR_TOKENS = 2 * (TRUNK + 12 * SEG)
PAIR_SEGS = 26
QUERY_BLOCK = 256
KEY_BLOCK = 512
BIG = 2.0**100
VALUE_ROWS = 80

epsilon = 1e-05
f32 = jnp.float32
bf16 = jnp.bfloat16
MESH = pl.DeviceIdType.MESH


def normalize(values, gain_row, bias_row):
    average = jnp.mean(values, axis=-1, keepdims=True)
    centred = values - average
    spread = jnp.mean(centred * centred, axis=-1, keepdims=True)
    return centred * lax.rsqrt(spread + epsilon) * gain_row + bias_row


def norm_back(values, gain_row, bias_row, grad_rows):
    pullback = jax.vjp(normalize, values, gain_row.astype(f32), bias_row.astype(f32))[1]
    return pullback(grad_rows)


def gelu_tanh(values):
    return jax.nn.gelu(values, approximate=True)


def nn(left, right):
    return lax.dot_general(left, right, (((1,), (0,)), ((), ())), preferred_element_type=f32)


def nt(left, right):
    return lax.dot_general(left, right, (((1,), (1,)), ((), ())), preferred_element_type=f32)


def tn(left, right):
    return lax.dot_general(left, right, (((0,), (0,)), ((), ())), preferred_element_type=f32)


def pieces(value, count):
    parts = []
    for _ in range(count):
        part = lax.reduce_precision(value, 8, 7)
        parts.append(part)
        value = value - part
    return parts


def core_of(index):
    return (index ^ (index >> 1)) & 1


def pair_tables(seg_parent, seg_length, group, slope):
    first = group * PAIR_SEGS
    parent = lax.dynamic_slice_in_dim(seg_parent, first, PAIR_SEGS, 0) - first
    length = lax.dynamic_slice_in_dim(seg_length, first, PAIR_SEGS, 0)
    ids = jnp.arange(PAIR_SEGS, dtype=jnp.int32)
    begin = jnp.sum(jnp.where(ids[None, :] < ids[:, None], length[None, :], 0), axis=1)
    end = begin + length
    is_parent = parent[:, None] == ids[None, :]
    grand = jnp.sum(jnp.where(is_parent, parent[None, :], 0), axis=1)
    is_grand = grand[:, None] == ids[None, :]
    parent_length = jnp.sum(jnp.where(is_parent, length[None, :], 0), axis=1)
    grand_length = jnp.sum(jnp.where(is_grand, length[None, :], 0), axis=1)
    path_start = jnp.where(
        parent == ids, 0, parent_length + jnp.where(grand == parent, 0, grand_length)
    )
    related = is_parent | is_grand | (ids[:, None] == ids[None, :])
    high, low = pieces(slope * (path_start - begin).astype(f32), 2)
    slope_high, slope_low = pieces(slope, 2)
    by_segment = jnp.concatenate(
        [
            jnp.where(related, high[None, :], -BIG),
            jnp.where(related, low[None, :], 0.0),
            jnp.broadcast_to(
                jnp.stack([256.0 * slope_high, 256.0 * slope_low, slope_high, slope_low])[None, :],
                (PAIR_SEGS, 4),
            ),
        ],
        axis=1,
    )
    by_segment = jnp.pad(
        by_segment, ((0, 128 - PAIR_SEGS), (0, 128 - by_segment.shape[1]))
    ).astype(bf16)
    bounds = jnp.pad(jnp.stack([jnp.tile(begin, 2), jnp.tile(end, 2)]), ((0, 6), (0, 128 - 2 * PAIR_SEGS)))
    query_blocks, key_blocks = PAIR_TOKENS // QUERY_BLOCK, PAIR_TOKENS // KEY_BLOCK
    q_begin = jnp.arange(query_blocks, dtype=jnp.int32) * QUERY_BLOCK
    k_begin = jnp.arange(key_blocks, dtype=jnp.int32) * KEY_BLOCK
    q_has = (begin[None, :] < q_begin[:, None] + QUERY_BLOCK) & (end[None, :] > q_begin[:, None])
    k_has = (begin[None, :] < k_begin[:, None] + KEY_BLOCK) & (end[None, :] > k_begin[:, None])
    q_sees = jnp.any(q_has[:, :, None] & related[None], axis=1)
    seen = jnp.any(q_sees[:, None, :] & k_has[None, :, :], axis=2)
    seen = seen & (k_begin[None, :] + KEY_BLOCK <= q_begin[:, None])
    rank = jnp.sum(
        jnp.where(k_begin[None, None, :] < k_begin[None, :, None], seen[:, None, :], False),
        axis=2,
        dtype=jnp.int32,
    )
    slots = jnp.arange(key_blocks, dtype=jnp.int32)
    block_list = jnp.sum(
        jnp.where(
            seen[:, :, None] & (rank[:, :, None] == slots[None, None, :]), slots[None, :, None], 0
        ),
        axis=1,
    )
    block_count = jnp.sum(seen, axis=1, dtype=jnp.int32)
    return bounds, by_segment, block_list, block_count


def causal_scores(scores, key_first, query_first):
    rows = key_first + lax.broadcasted_iota(jnp.int32, scores.shape, 0)
    columns = query_first + lax.broadcasted_iota(jnp.int32, scores.shape, 1)
    return jnp.where(rows <= columns, scores, -BIG)


def token_lanes(bounds_ref, first, count):
    token = first + lax.broadcasted_iota(jnp.int32, (count, 128), 0)
    lane = lax.broadcasted_iota(jnp.int32, (count, 128), 1)
    member = (token >= bounds_ref[0:1, :]) & (token < bounds_ref[1:2, :])
    base = 2 * PAIR_SEGS
    number = jnp.where(lane < base + 2, token // 256, token % 256)
    number = jnp.where(lane < base + 4, number, 1)
    number = jnp.where(lane < base + 7, number, 0)
    return jnp.where(lane < base, member.astype(f32), number.astype(f32))


def pair_rows(packed):
    return jnp.concatenate([packed[:, :HD], packed[:, HD:]], axis=0)


def build_keys(bounds_ref, mixed_ref, keys, step):
    rows = mixed_ref.shape[1] * 2 // 3
    lane = lax.broadcasted_iota(jnp.int32, (rows, 128), 1)
    for part in range(2):
        first = (2 * step + part) * rows
        both = mixed_ref[2 * step + part, 0:rows, :].astype(f32)
        keys[pl.ds(pl.multiple_of(first, 64), rows), :] = jnp.where(
            lane < HD, token_lanes(bounds_ref, first, rows), both
        ).astype(bf16)


def query_lanes(bounds_ref, by_segment_ref, mixed_ref, number):
    rows = mixed_ref.shape[1] * 2 // 3
    meta = nn(token_lanes(bounds_ref, number * rows, rows).astype(bf16), by_segment_ref[...])
    queries = mixed_ref[number, 0:rows, 0:HD].astype(f32) * 0.125
    return jnp.concatenate([meta[:, :HD], queries], axis=1)


def forward_kernel(
    block_of,
    count_of,
    list_of,
    bounds_ref,
    by_segment_ref,
    mixed_ref,
    context_ref,
    out_ref,
    keys,
    values_t,
    queries_all,
):
    messages, message_rows, _ = mixed_ref.shape
    rows = message_rows * 2 // 3
    tensor_count = context_ref.shape[1]
    steps = queries_all.shape[0] // QUERY_BLOCK

    def prepare(step, _):
        build_keys(bounds_ref, mixed_ref, keys, step)
        values = jnp.concatenate(
            [pair_rows(mixed_ref[2 * step + part, rows:, :].astype(f32)) for part in range(2)], axis=0
        )
        lane = lax.broadcasted_iota(jnp.int32, (2 * rows, HD), 1)
        wide = jnp.concatenate([values, jnp.where(lane == 0, 1.0, 0.0)], axis=1)
        values_t[:, pl.ds(pl.multiple_of(step * 2 * rows, 128), 2 * rows)] = wide.T[
            :VALUE_ROWS
        ].astype(bf16)
        return 0

    lax.fori_loop(0, messages // 2, prepare, 0)
    half = messages // (2 * tensor_count)

    def prepare_queries(step, _):
        number = block_of[(step // tensor_count) * (steps // half)] * QUERY_BLOCK // rows
        number = number + step % tensor_count
        queries_all[pl.ds(pl.multiple_of(step * rows, 64), rows), :] = query_lanes(
            bounds_ref, by_segment_ref, mixed_ref, number
        ).astype(bf16)
        return 0

    lax.fori_loop(0, messages // 2, prepare_queries, 0)

    def one_block(number, _):
        query_first = block_of[number] * QUERY_BLOCK
        here = pl.ds(pl.multiple_of(number * QUERY_BLOCK, QUERY_BLOCK), QUERY_BLOCK)
        queries = queries_all[here, :]

        def attend(key_block, carry, masked):
            top, total = carry
            first = pl.multiple_of(key_block * KEY_BLOCK, KEY_BLOCK)
            scores = nt(keys[pl.ds(first, KEY_BLOCK), :], queries)
            if masked:
                scores = causal_scores(scores, first, query_first)
            new_top = jnp.maximum(top, jnp.max(scores, axis=0, keepdims=True))
            weights = jnp.exp(scores - new_top)
            total = total * jnp.exp(top - new_top) + nn(
                values_t[:, pl.ds(first, KEY_BLOCK)], weights.astype(bf16)
            )
            return new_top, total

        carry = (jnp.full((1, QUERY_BLOCK), -BIG, f32), jnp.zeros((VALUE_ROWS, QUERY_BLOCK), f32))
        carry = attend(query_first // KEY_BLOCK, carry, True)
        top, total = lax.fori_loop(
            0, count_of[number], lambda step, kept: attend(list_of[number, step], kept, False), carry
        )
        row_sum = total[HD : HD + 1]
        log_total = jnp.broadcast_to(top + jnp.log(row_sum), (HD, QUERY_BLOCK))
        out_ref[here, :] = jnp.concatenate([total[:HD] / row_sum, log_total], axis=0).T
        return 0

    lax.fori_loop(0, steps, one_block, 0)

    def pack(step, _):
        first = pl.multiple_of(step * rows, 64)
        half_rows = rows // 2
        context_ref[step // tensor_count, step % tensor_count] = jnp.concatenate(
            [
                out_ref[pl.ds(first, half_rows), 0:HD],
                out_ref[pl.ds(pl.multiple_of(first + half_rows, 32), half_rows), 0:HD],
            ],
            axis=1,
        ).astype(bf16)
        return 0

    lax.fori_loop(0, messages // 2, pack, 0)


def attention_forward(blocks, counts, lists, bounds, by_segment, mixed, tensor_count):
    messages, message_rows, _ = mixed.shape
    rows = message_rows * 2 // 3
    half = messages // 2 * rows
    smem = pl.BlockSpec(memory_space=pltpu.SMEM)
    vmem = pl.BlockSpec(memory_space=pltpu.VMEM)
    return pl.pallas_call(
        forward_kernel,
        in_specs=[smem] * 3 + [vmem] * 3,
        out_specs=[vmem, vmem],
        out_shape=[
            jax.ShapeDtypeStruct(
                (messages // 2 // tensor_count, tensor_count, rows // 2, 2 * HD), bf16
            ),
            jax.ShapeDtypeStruct((half, 128), f32),
        ],
        scratch_shapes=[
            pltpu.VMEM((PAIR_TOKENS, 128), bf16),
            pltpu.VMEM((VALUE_ROWS, PAIR_TOKENS), bf16),
            pltpu.VMEM((half, 128), bf16),
        ],
        compiler_params=pltpu.CompilerParams(vmem_limit_bytes=40 * 2**20),
        cost_estimate=pl.CostEstimate(
            flops=2 * 256 * 2 * 12_000_000, bytes_accessed=10_000_000, transcendentals=12_000_000
        ),
        name="attention_forward",
    )(blocks, counts, lists, bounds, by_segment, mixed)


def backward_kernel(
    block_of,
    count_of,
    list_of,
    bounds_ref,
    by_segment_ref,
    mixed_ref,
    grads_ref,
    out_ref,
    dq_ref,
    dkv_ref,
    keys,
    keys_t,
    values,
    queries_all,
    grads_all,
    dk,
    dv,
):
    messages, message_rows, _ = mixed_ref.shape
    rows = message_rows * 2 // 3
    tensor_count = grads_ref.shape[1]
    steps = queries_all.shape[0] // QUERY_BLOCK
    half = messages // (2 * tensor_count)

    def with_pieces(value, first_lane, wide):
        lane = lax.broadcasted_iota(jnp.int32, wide.shape, 1)
        for piece in range(3):
            part = value.astype(bf16).astype(f32)
            wide = jnp.where(lane == first_lane + piece, part, wide)
            value = value - part
        return wide

    def prepare(step, _):
        build_keys(bounds_ref, mixed_ref, keys, step)
        span = pl.ds(pl.multiple_of(step * 2 * rows, 128), 2 * rows)
        keys_t[:, span] = keys[span, :].astype(f32).T[HD:].astype(bf16)
        packed = jnp.concatenate(
            [pair_rows(mixed_ref[2 * step + part, rows:, :].astype(f32)) for part in range(2)], axis=0
        )
        lane = lax.broadcasted_iota(jnp.int32, (2 * rows, HD), 1)
        values[span, :] = jnp.concatenate([packed, jnp.where(lane < 3, 1.0, 0.0)], axis=1).astype(
            bf16
        )
        dk[span, :] = jnp.zeros((2 * rows, 128), f32)
        dv[span, :] = jnp.zeros((2 * rows, 128), f32)
        return 0

    lax.fori_loop(0, messages // 2, prepare, 0)

    def prepare_queries(step, _):
        number = block_of[(step // tensor_count) * (steps // half)] * QUERY_BLOCK // rows
        number = number + step % tensor_count
        span = pl.ds(pl.multiple_of(step * rows, 64), rows)
        wide = query_lanes(bounds_ref, by_segment_ref, mixed_ref, number)
        out = out_ref[span, :]
        queries_all[span, :] = with_pieces(-out[:, HD : HD + 1], 2 * PAIR_SEGS + 4, wide).astype(bf16)
        grads = pair_rows(grads_ref[step // tensor_count, step % tensor_count].astype(f32))
        inner = jnp.sum(grads * out[:, :HD], axis=1, keepdims=True)
        wide = jnp.concatenate([grads, jnp.zeros((rows, HD), f32)], axis=1)
        grads_all[span, :] = with_pieces(-inner, HD, wide).astype(bf16)
        return 0

    lax.fori_loop(0, messages // 2, prepare_queries, 0)

    def one_block(number, _):
        query_first = block_of[number] * QUERY_BLOCK
        here = pl.ds(pl.multiple_of(number * QUERY_BLOCK, QUERY_BLOCK), QUERY_BLOCK)
        queries = queries_all[here, :]
        grads = grads_all[here, :]

        def attend(key_block, dq, masked):
            first = pl.multiple_of(key_block * KEY_BLOCK, KEY_BLOCK)
            span = pl.ds(first, KEY_BLOCK)
            scores = nt(keys[span, :], queries)
            if masked:
                scores = causal_scores(scores, first, query_first)
            weights = jnp.exp(scores)
            score_grad = (weights * nt(values[span, :], grads)).astype(bf16)
            dv[span, :] += nn(weights.astype(bf16), grads)
            dk[span, :] += nn(score_grad, queries)
            return dq + nn(keys_t[:, span], score_grad)

        dq = attend(query_first // KEY_BLOCK, jnp.zeros((HD, QUERY_BLOCK), f32), True)
        dq = lax.fori_loop(
            0, count_of[number], lambda step, kept: attend(list_of[number, step], kept, False), dq
        )
        dq_ref[here, :] = (dq * 0.125).T.astype(bf16)
        return 0

    lax.fori_loop(0, steps, one_block, 0)

    def write(step, _):
        span = pl.ds(pl.multiple_of(step * KEY_BLOCK, KEY_BLOCK), KEY_BLOCK)
        dkv_ref[span, :] = jnp.concatenate([dk[span, HD:], dv[span, :HD]], axis=1).astype(bf16)
        return 0

    lax.fori_loop(0, PAIR_TOKENS // KEY_BLOCK, write, 0)


def attention_backward(blocks, counts, lists, bounds, by_segment, mixed, grads, out):
    smem = pl.BlockSpec(memory_space=pltpu.SMEM)
    vmem = pl.BlockSpec(memory_space=pltpu.VMEM)
    half = out.shape[0]
    return pl.pallas_call(
        backward_kernel,
        in_specs=[smem] * 3 + [vmem] * 5,
        out_specs=[vmem, vmem],
        out_shape=[
            jax.ShapeDtypeStruct((half, HD), bf16),
            jax.ShapeDtypeStruct((PAIR_TOKENS, 128), bf16),
        ],
        scratch_shapes=[
            pltpu.VMEM((PAIR_TOKENS, 128), bf16),
            pltpu.VMEM((HD, PAIR_TOKENS), bf16),
            pltpu.VMEM((PAIR_TOKENS, 128), bf16),
            pltpu.VMEM((half, 128), bf16),
            pltpu.VMEM((half, 128), bf16),
            pltpu.VMEM((PAIR_TOKENS, 128), f32),
            pltpu.VMEM((PAIR_TOKENS, 128), f32),
        ],
        compiler_params=pltpu.CompilerParams(vmem_limit_bytes=56 * 2**20),
        cost_estimate=pl.CostEstimate(
            flops=5 * 256 * 2 * 12_000_000, bytes_accessed=16_000_000, transcendentals=12_000_000
        ),
        name="attention_backward",
    )(blocks, counts, lists, bounds, by_segment, mixed, grads, out)


def greet_all(dp_count, tensor_count, dp_index, tensor_index):
    barrier = pltpu.get_barrier_semaphore()
    total = dp_count * tensor_count
    me = dp_index * tensor_count + tensor_index

    def greet(step, _):
        other = (me + step) % total
        pl.semaphore_signal(
            barrier,
            inc=1,
            device_id=(other // tensor_count, other % tensor_count),
            device_id_type=MESH,
        )
        return 0

    lax.fori_loop(1, total, greet, 0)
    pl.semaphore_wait(barrier, total - 1)


def project_kernel(
    dp_count,
    tensor_count,
    span,
    x_ref,
    gain_ref,
    bias_ref,
    shift_ref,
    weight_ref,
    normed_ref,
    mixed_ref,
    normed,
    weight,
    outbox,
    weight_sem,
    swap_sem,
    send_sem,
    recv_sem,
    local_sem,
    pass_send,
    pass_recv,
):
    dp_index, tensor_index = lax.axis_index("dp"), lax.axis_index("tensor")
    rows = x_ref.shape[0]
    core = dp_index % 2
    base = dp_index // span * span
    chip = dp_index % span // 2
    chips = span // 2
    partner = (dp_index + 1 - 2 * core, tensor_index)
    columns = weight.shape[2]

    def weight_copy(owner):
        return pltpu.make_async_copy(
            weight_ref.at[:, pl.ds(pl.multiple_of((2 * owner + core) * columns, 128), columns)],
            weight.at[owner],
            weight_sem.at[owner],
        )

    lax.fori_loop(0, tensor_count, lambda i, _: (weight_copy(i).start(), 0)[1], 0)
    greet_all(dp_count, tensor_count, dp_index, tensor_index)

    normed[core] = normalize(x_ref[...].astype(f32), gain_ref[...], bias_ref[...]).astype(bf16)
    swap = pltpu.make_async_remote_copy(
        src_ref=normed.at[core],
        dst_ref=normed.at[core],
        send_sem=swap_sem.at[0],
        recv_sem=swap_sem.at[1],
        device_id=partner,
        device_id_type=MESH,
    )
    swap.start()
    swap.wait_recv()

    def slot(place_dp, place_tensor):
        return mixed_ref.at[place_dp * tensor_count + place_tensor]

    def send(owner, part, pair):
        head_chip = 2 * core + pair
        target = (base + 2 * head_chip + (part + chip) % 2, owner)
        here = (target[0] == dp_index) & (owner == tensor_index)
        return here, pltpu.make_async_remote_copy(
            src_ref=outbox.at[owner, part, pair],
            dst_ref=slot(2 * chip + part, tensor_index),
            send_sem=send_sem.at[owner, part, pair],
            recv_sem=recv_sem.at[chip, tensor_index],
            device_id=target,
            device_id_type=MESH,
        ), pltpu.make_async_copy(
            outbox.at[owner, part, pair], slot(2 * chip + part, tensor_index), local_sem.at[0]
        )

    def one_part(step, _):
        owner = (tensor_index + 1 + step // 2) % tensor_count
        part = step % 2

        @pl.when(part == 0)
        def _():
            weight_copy(owner).wait()

        result = nn(normed[part], weight[owner]) + shift_ref[owner]
        first = [result[:, 0:128], result[:, 192:320]]
        last = [result[:, 128:192], result[:, 320:384]]
        for pair in range(2):
            outbox[owner, part, pair, 0:rows, :] = first[pair].astype(bf16)
            outbox[owner, part, pair, rows:, :] = jnp.concatenate(
                [last[pair][: rows // 2], last[pair][rows // 2 :]], axis=1
            ).astype(bf16)
            here, far, near = send(owner, part, pair)

            @pl.when(here)
            def _():
                near.start()

            @pl.when(jnp.logical_not(here))
            def _():
                far.start()

        return 0

    lax.fori_loop(0, 2 * tensor_count, one_part, 0)
    normed_ref[...] = normed[...]

    def arrival(step):
        from_chip, from_tensor = step // tensor_count, step % tensor_count
        mine = slot(2 * from_chip + (core + from_chip) % 2, from_tensor)
        theirs = slot(2 * from_chip + (core + from_chip + 1) % 2, from_tensor)
        here = (from_chip == chip) & (from_tensor == tensor_index) & (chip // 2 == core)

        def passing(place):
            return pltpu.make_async_remote_copy(
                src_ref=place,
                dst_ref=place,
                send_sem=pass_send.at[from_chip, from_tensor],
                recv_sem=pass_recv.at[from_chip, from_tensor],
                device_id=partner,
                device_id_type=MESH,
            )

        return mine, theirs, here, passing, from_chip, from_tensor

    def hand_on(step, _):
        mine, _theirs, here, passing, from_chip, from_tensor = arrival(step)

        @pl.when(here)
        def _():
            pltpu.make_async_copy(mine, mine, local_sem.at[0]).wait()

        @pl.when(jnp.logical_not(here))
        def _():
            pltpu.make_async_remote_copy(
                src_ref=mine,
                dst_ref=mine,
                send_sem=pass_send.at[from_chip, from_tensor],
                recv_sem=recv_sem.at[from_chip, from_tensor],
                device_id=partner,
                device_id_type=MESH,
            ).wait_recv()

        passing(mine).start()
        return 0

    lax.fori_loop(0, chips * tensor_count, hand_on, 0)

    def finish(step, _):
        mine, theirs, _here, passing, _a, _b = arrival(step)
        passing(mine).wait_send()
        passing(theirs).wait_recv()
        return 0

    lax.fori_loop(0, chips * tensor_count, finish, 0)

    def sent(step, _):
        here, far, _near = send(step // 4, step // 2 % 2, step % 2)

        @pl.when(jnp.logical_not(here))
        def _():
            far.wait_send()

        return 0

    lax.fori_loop(0, 4 * tensor_count, sent, 0)
    swap.wait_send()


def project(inputs, gain, bias, shift, weight, dp_count, tensor_count, span):
    rows, width = inputs.shape
    columns = weight.shape[1] // (2 * tensor_count)
    messages = span * tensor_count
    chips = span // 2
    dma = pltpu.SemaphoreType.DMA
    vmem = pl.BlockSpec(memory_space=pltpu.VMEM)
    anywhere = pl.BlockSpec(memory_space=pl.ANY)
    return pl.pallas_call(
        functools.partial(project_kernel, dp_count, tensor_count, span),
        in_specs=[vmem] * 4 + [anywhere],
        out_specs=[vmem, anywhere],
        out_shape=[
            jax.ShapeDtypeStruct((2, rows, width), bf16),
            jax.ShapeDtypeStruct((messages, rows * 3 // 2, 128), bf16),
        ],
        scratch_shapes=[
            pltpu.VMEM((2, rows, width), bf16),
            pltpu.VMEM((tensor_count, width, columns), bf16),
            pltpu.VMEM((tensor_count, 2, 2, rows * 3 // 2, 128), bf16),
            dma((tensor_count,)),
            dma((2,)),
            dma((tensor_count, 2, 2)),
            dma((chips, tensor_count)),
            dma((1,)),
            dma((chips, tensor_count)),
            dma((chips, tensor_count)),
        ],
        compiler_params=pltpu.CompilerParams(
            collective_id=0, has_side_effects=True, vmem_limit_bytes=40 * 2**20
        ),
        cost_estimate=pl.CostEstimate(
            flops=2 * 2 * rows * width * weight.shape[1] // 2,
            bytes_accessed=20_000_000,
            transcendentals=0,
        ),
        name="project",
    )(inputs, gain, bias, shift, weight)


def per_device(
    block_in,
    norm1_gain,
    norm1_bias,
    qkv_weight,
    qv_bias,
    dense_weight,
    dense_bias,
    norm2_gain,
    norm2_bias,
    up_weight,
    up_bias,
    down_weight,
    down_bias,
    cotangent,
    seg_parent,
    seg_length,
):
    dp_count, tensor_count = lax.axis_size("dp"), lax.axis_size("tensor")
    dp_index, tensor_index = lax.axis_index("dp"), lax.axis_index("tensor")
    rows, width = block_in.shape
    dp_rows = rows * tensor_count
    span = PAIR_TOKENS // dp_rows
    heads_here = HEADS // tensor_count
    groups = [list(range(g * span, (g + 1) * span)) for g in range(dp_count // span)]
    local_index = lax.rem(dp_index, span)
    core = lax.rem(dp_index, 2)
    both = ("dp", "tensor")

    vectors = (norm1_gain, norm1_bias, norm2_gain, norm2_bias, dense_bias, down_bias)
    small = jnp.concatenate([value.reshape(-1) for value in vectors + (qv_bias, up_bias)])
    small = lax.all_gather(small, both, axis=0, tiled=False).astype(f32)
    small = small.reshape(dp_count, tensor_count, -1)
    piece = norm1_gain.shape[0]
    gain_one, bias_one, gain_two, bias_two, dense_shift, down_shift = (
        small[:, 0, i * piece : (i + 1) * piece].reshape(-1) for i in range(6)
    )

    def unpack(first, shape):
        value = small[:, :, first : first + shape[0] * shape[1]]
        value = value.reshape(dp_count, tensor_count, *shape).transpose(1, 2, 0, 3)
        return value.reshape(tensor_count * shape[0], dp_count * shape[1])

    qv_full = unpack(6 * piece, qv_bias.shape)
    up_shift = unpack(6 * piece + qv_bias.size, up_bias.shape)

    def gather_matrix(value, dp_axis):
        value = lax.all_gather(value, "tensor", axis=1 - dp_axis, tiled=True)
        return lax.all_gather(value, "dp", axis=dp_axis, tiled=True)

    qkv_full = gather_matrix(qkv_weight, 0)
    dense_full = gather_matrix(dense_weight, 1)
    up_full = gather_matrix(up_weight, 0)
    down_full = gather_matrix(down_weight, 1)

    head = tensor_index * heads_here + local_index // 2
    slope = jnp.exp2(-8.0 * (head.astype(f32) + 1.0) / HEADS) / TRUNK
    bounds, by_segment, block_list, block_count = pair_tables(
        seg_parent, seg_length, dp_index // span, slope
    )
    mine = core_of(jnp.arange(span, dtype=jnp.int32)) == core
    half = span // 2
    taken = jnp.stack([2 * i + (core ^ (i & 1)) for i in range(half)])
    block_ids = (
        taken[:, None] * (dp_rows // QUERY_BLOCK)
        + jnp.arange(dp_rows // QUERY_BLOCK, dtype=jnp.int32)[None, :]
    ).reshape(-1)

    def take(whole):
        parts = whole.reshape((half, 2) + (dp_rows,) + whole.shape[1:])
        flip = jnp.stack([core ^ (i & 1) for i in range(half)])
        pick = flip.reshape((half,) + (1,) * (parts.ndim - 2))
        return jnp.where(pick == 0, parts[:, 0], parts[:, 1]).reshape(
            (half * dp_rows,) + whole.shape[1:]
        )

    def put(part):
        parts = part.reshape((half, dp_rows) + part.shape[1:])
        flip = jnp.stack([core ^ (i & 1) for i in range(half)])
        pick = flip.reshape((half,) + (1,) * (parts.ndim - 1))
        zero = jnp.zeros_like(parts)
        whole = jnp.stack(
            [jnp.where(pick == 0, parts, zero), jnp.where(pick == 0, zero, parts)], axis=1
        )
        return whole.reshape((span * dp_rows,) + part.shape[1:])

    def to_heads(values):
        n = values.shape[2]
        values = lax.all_to_all(values, "tensor", split_axis=1, concat_axis=0, tiled=True)
        values = jnp.repeat(values.transpose(1, 0, 2), 2, axis=0)
        values = lax.all_to_all(
            values, "dp", split_axis=0, concat_axis=0, tiled=True, axis_index_groups=groups
        )
        return values.reshape(PAIR_TOKENS, n)

    def to_tokens(values):
        n = values.shape[1]
        values = lax.all_to_all(
            values.reshape(span, dp_rows, n),
            "dp",
            split_axis=0,
            concat_axis=0,
            tiled=True,
            axis_index_groups=groups,
        )
        values = jnp.sum(values.reshape(heads_here, 2, dp_rows, n).astype(f32), axis=1)
        values = values.astype(bf16).transpose(1, 0, 2)
        return lax.all_to_all(values, "tensor", split_axis=0, concat_axis=1, tiled=True)

    inputs = block_in.astype(f32)
    key_zeros = jnp.zeros((HEADS, 1, HD), f32)
    qkv_shift = jnp.concatenate(
        [qv_full[:, None, :HD], key_zeros, qv_full[:, None, HD:]], axis=1
    ).reshape(tensor_count, 2, 1, -1)
    qkv_shift = lax.dynamic_index_in_dim(qkv_shift, core, 1, keepdims=False)
    normed_both, mixed = project(
        block_in, gain_one[None], bias_one[None], qkv_shift, qkv_full, dp_count, tensor_count, span
    )
    normed_one = lax.dynamic_index_in_dim(normed_both, core, 0, keepdims=False)
    my_counts, my_lists = jnp.take(block_count, block_ids), jnp.take(block_list, block_ids, axis=0)
    tables = (block_ids, my_counts, my_lists, bounds, by_segment)
    packed_context, out_float = attention_forward(*tables, mixed, tensor_count)
    my_rows = half * dp_rows
    context_part = (
        packed_context.reshape(-1, rows // 2, 2, HD).transpose(0, 2, 1, 3).reshape(my_rows, HD)
    )
    context = to_tokens(put(context_part)).reshape(rows, width)

    attended = nn(context, dense_full)
    middle = inputs + attended + dense_shift
    normed_two = normalize(middle, gain_two, bias_two).astype(bf16)
    upper = nn(normed_two, up_full) + up_shift.reshape(-1)
    active = gelu_tanh(upper).astype(bf16)
    block_out = (middle + nn(active, down_full) + down_shift).astype(bf16)

    out_grad = cotangent.astype(f32)
    down_grad = tn(active, cotangent)
    active_grad = nt(cotangent, down_full)
    upper_grad = jax.vjp(gelu_tanh, upper)[1](active_grad)[0].astype(bf16)
    up_shift_grad = jnp.sum(upper_grad, axis=0, dtype=f32).reshape(up_shift.shape)
    up_grad = tn(normed_two, upper_grad)
    middle_part, gain_two_grad, bias_two_grad = norm_back(
        middle, gain_two, bias_two, nt(upper_grad, up_full)
    )
    middle_grad = out_grad + middle_part
    middle_low = middle_grad.astype(bf16)
    dense_grad = tn(context, middle_low)
    context_grad = nt(middle_low, dense_full).astype(bf16)

    out_grads = take(to_heads(context_grad.reshape(rows, HEADS, HD)))
    packed_grads = (
        out_grads.reshape(half, tensor_count, 2, rows // 2, HD)
        .transpose(0, 1, 3, 2, 4)
        .reshape(half, tensor_count, rows // 2, 2 * HD)
    )
    dq, dkv = attention_backward(*tables, mixed, packed_grads, out_float)
    qkv_grad = to_tokens(jnp.concatenate([put(dq), dkv], axis=1))
    qkv_totals = jnp.sum(qkv_grad.reshape(rows, HEADS, 3, HD), axis=0, dtype=f32)
    qv_grad = jnp.concatenate([qkv_totals[:, 0], qkv_totals[:, 2]], axis=1)
    qkv_grad = qkv_grad.reshape(rows, HEADS * 3 * HD)
    qkv_weight_part = tn(normed_one, qkv_grad)
    input_part, gain_one_grad, bias_one_grad = norm_back(
        inputs, gain_one, bias_one, nt(qkv_grad, qkv_full)
    )
    input_grad = middle_grad + input_part

    def scatter_matrix(value, dp_axis):
        value = lax.psum_scatter(
            value.astype(bf16), "dp", scatter_dimension=dp_axis, tiled=True
        )
        return lax.psum_scatter(
            value, "tensor", scatter_dimension=1 - dp_axis, tiled=True
        ).astype(f32)

    small_grads = (
        gain_one_grad,
        bias_one_grad,
        jnp.sum(middle_grad, axis=0),
        gain_two_grad,
        bias_two_grad,
        jnp.sum(out_grad, axis=0),
        qv_grad,
        up_shift_grad,
    )
    summed = lax.psum(jnp.concatenate([value.reshape(-1) for value in small_grads]), both)

    def own_vector(number):
        return lax.dynamic_slice_in_dim(summed, number * width + dp_index * piece, piece, 0)

    def own_matrix(first, shape):
        whole = summed[first : first + shape[0] * shape[1] * dp_count * tensor_count]
        whole = whole.reshape(tensor_count, shape[0], dp_count, shape[1])
        whole = lax.dynamic_index_in_dim(whole, tensor_index, 0, keepdims=False)
        return lax.dynamic_index_in_dim(whole, dp_index, 1, keepdims=False)

    return (
        block_out,
        input_grad,
        own_vector(0),
        own_vector(1),
        scatter_matrix(qkv_weight_part, 0),
        own_matrix(6 * width, qv_bias.shape),
        scatter_matrix(dense_grad, 1),
        own_vector(2),
        own_vector(3),
        own_vector(4),
        scatter_matrix(up_grad, 0),
        own_matrix(6 * width + qv_grad.size, up_bias.shape),
        scatter_matrix(down_grad, 1),
        own_vector(5),
    )


def solution(mesh):
    rows = P(("dp", "tensor"), None)
    in_specs = (
        rows,
        P("dp"),
        P("dp"),
        P("dp", "tensor"),
        P("tensor", "dp"),
        P("tensor", "dp"),
        P("dp"),
        P("dp"),
        P("dp"),
        P("dp", "tensor"),
        P("tensor", "dp"),
        P("tensor", "dp"),
        P("dp"),
        rows,
        P(),
        P(),
    )
    out_specs = (
        rows,
        rows,
        P("dp"),
        P("dp"),
        P("dp", "tensor"),
        P("tensor", "dp"),
        P("tensor", "dp"),
        P("dp"),
        P("dp"),
        P("dp"),
        P("dp", "tensor"),
        P("tensor", "dp"),
        P("tensor", "dp"),
        P("dp"),
    )
    return jax.shard_map(
        per_device, mesh=mesh, in_specs=in_specs, out_specs=out_specs, check_vma=False
    )
```

```python
import functools

import jax
import jax.numpy as jnp
from jax import lax
from jax.experimental import pallas as pl
from jax.experimental.pallas import tpu as pltpu
from jax.sharding import PartitionSpec as P

HEADS = 16
HD = 64
TRUNK = 2048
SEG = 256
PAIR_TOKENS = 2 * (TRUNK + 12 * SEG)
PAIR_SEGS = 26
QUERY_BLOCK = 256
KEY_BLOCK = 512
BIG = 2.0**100
VALUE_ROWS = 80

epsilon = 1e-05
f32 = jnp.float32
bf16 = jnp.bfloat16
MESH = pl.DeviceIdType.MESH


def normalize(values, gain_row, bias_row):
    average = jnp.mean(values, axis=-1, keepdims=True)
    centred = values - average
    spread = jnp.mean(centred * centred, axis=-1, keepdims=True)
    return centred * lax.rsqrt(spread + epsilon) * gain_row + bias_row


def nn(left, right):
    return lax.dot_general(left, right, (((1,), (0,)), ((), ())), preferred_element_type=f32)


def nt(left, right):
    return lax.dot_general(left, right, (((1,), (1,)), ((), ())), preferred_element_type=f32)


def tn(left, right):
    return lax.dot_general(left, right, (((0,), (0,)), ((), ())), preferred_element_type=f32)


def pieces(value, count):
    parts = []
    for _ in range(count):
        part = lax.reduce_precision(value, 8, 7)
        parts.append(part)
        value = value - part
    return parts


def pair_tables(seg_parent, seg_length, group, slope):
    first = group * PAIR_SEGS
    parent = lax.dynamic_slice_in_dim(seg_parent, first, PAIR_SEGS, 0) - first
    length = lax.dynamic_slice_in_dim(seg_length, first, PAIR_SEGS, 0)
    ids = jnp.arange(PAIR_SEGS, dtype=jnp.int32)
    begin = jnp.sum(jnp.where(ids[None, :] < ids[:, None], length[None, :], 0), axis=1)
    end = begin + length
    is_parent = parent[:, None] == ids[None, :]
    grand = jnp.sum(jnp.where(is_parent, parent[None, :], 0), axis=1)
    is_grand = grand[:, None] == ids[None, :]
    parent_length = jnp.sum(jnp.where(is_parent, length[None, :], 0), axis=1)
    grand_length = jnp.sum(jnp.where(is_grand, length[None, :], 0), axis=1)
    path_start = jnp.where(
        parent == ids, 0, parent_length + jnp.where(grand == parent, 0, grand_length)
    )
    related = is_parent | is_grand | (ids[:, None] == ids[None, :])
    high, low = pieces(slope * (path_start - begin).astype(f32), 2)
    slope_high, slope_low = pieces(slope, 2)
    by_segment = jnp.concatenate(
        [
            jnp.where(related, high[None, :], -BIG),
            jnp.where(related, low[None, :], 0.0),
            jnp.broadcast_to(
                jnp.stack([256.0 * slope_high, 256.0 * slope_low, slope_high, slope_low])[None, :],
                (PAIR_SEGS, 4),
            ),
        ],
        axis=1,
    )
    by_segment = jnp.pad(
        by_segment, ((0, 128 - PAIR_SEGS), (0, 128 - by_segment.shape[1]))
    ).astype(bf16)
    bounds = jnp.pad(jnp.stack([jnp.tile(begin, 2), jnp.tile(end, 2)]), ((0, 6), (0, 128 - 2 * PAIR_SEGS)))
    query_blocks, key_blocks = PAIR_TOKENS // QUERY_BLOCK, PAIR_TOKENS // KEY_BLOCK
    q_begin = jnp.arange(query_blocks, dtype=jnp.int32) * QUERY_BLOCK
    k_begin = jnp.arange(key_blocks, dtype=jnp.int32) * KEY_BLOCK
    q_has = (begin[None, :] < q_begin[:, None] + QUERY_BLOCK) & (end[None, :] > q_begin[:, None])
    k_has = (begin[None, :] < k_begin[:, None] + KEY_BLOCK) & (end[None, :] > k_begin[:, None])
    q_sees = jnp.any(q_has[:, :, None] & related[None], axis=1)
    seen = jnp.any(q_sees[:, None, :] & k_has[None, :, :], axis=2)
    seen = seen & (k_begin[None, :] + KEY_BLOCK <= q_begin[:, None])
    rank = jnp.sum(
        jnp.where(k_begin[None, None, :] < k_begin[None, :, None], seen[:, None, :], False),
        axis=2,
        dtype=jnp.int32,
    )
    slots = jnp.arange(key_blocks, dtype=jnp.int32)
    block_list = jnp.sum(
        jnp.where(
            seen[:, :, None] & (rank[:, :, None] == slots[None, None, :]), slots[None, :, None], 0
        ),
        axis=1,
    )
    block_count = jnp.sum(seen, axis=1, dtype=jnp.int32)
    return bounds, by_segment, block_list, block_count


def causal_scores(scores, key_first, query_first):
    rows = key_first + lax.broadcasted_iota(jnp.int32, scores.shape, 0)
    columns = query_first + lax.broadcasted_iota(jnp.int32, scores.shape, 1)
    return jnp.where(rows <= columns, scores, -BIG)


def token_lanes(bounds_ref, first, count):
    token = first + lax.broadcasted_iota(jnp.int32, (count, 128), 0)
    lane = lax.broadcasted_iota(jnp.int32, (count, 128), 1)
    member = (token >= bounds_ref[0:1, :]) & (token < bounds_ref[1:2, :])
    base = 2 * PAIR_SEGS
    number = jnp.where(lane < base + 2, token // 256, token % 256)
    number = jnp.where(lane < base + 4, number, 1)
    number = jnp.where(lane < base + 7, number, 0)
    return jnp.where(lane < base, member.astype(f32), number.astype(f32))


def pair_rows(packed):
    return jnp.concatenate([packed[:, :HD], packed[:, HD:]], axis=0)


def build_keys(bounds_ref, mixed_ref, keys, step):
    rows = mixed_ref.shape[1] * 2 // 3
    lane = lax.broadcasted_iota(jnp.int32, (rows, 128), 1)
    for part in range(2):
        first = (2 * step + part) * rows
        both = mixed_ref[2 * step + part, 0:rows, :].astype(f32)
        keys[pl.ds(pl.multiple_of(first, 64), rows), :] = jnp.where(
            lane < HD, token_lanes(bounds_ref, first, rows), both
        ).astype(bf16)


def query_lanes(bounds_ref, by_segment_ref, mixed_ref, number):
    rows = mixed_ref.shape[1] * 2 // 3
    meta = nn(token_lanes(bounds_ref, number * rows, rows).astype(bf16), by_segment_ref[...])
    queries = mixed_ref[number, 0:rows, 0:HD].astype(f32) * 0.125
    return jnp.concatenate([meta[:, :HD], queries], axis=1)


def forward_kernel(
    block_of,
    count_of,
    list_of,
    bounds_ref,
    by_segment_ref,
    mixed_ref,
    context_ref,
    out_ref,
    keys,
    values_t,
    queries_all,
):
    messages, message_rows, _ = mixed_ref.shape
    rows = message_rows * 2 // 3
    tensor_count = context_ref.shape[1]
    steps = queries_all.shape[0] // QUERY_BLOCK

    def prepare(step, _):
        build_keys(bounds_ref, mixed_ref, keys, step)
        values = jnp.concatenate(
            [pair_rows(mixed_ref[2 * step + part, rows:, :].astype(f32)) for part in range(2)], axis=0
        )
        lane = lax.broadcasted_iota(jnp.int32, (2 * rows, HD), 1)
        wide = jnp.concatenate([values, jnp.where(lane == 0, 1.0, 0.0)], axis=1)
        values_t[:, pl.ds(pl.multiple_of(step * 2 * rows, 128), 2 * rows)] = wide.T[
            :VALUE_ROWS
        ].astype(bf16)
        return 0

    lax.fori_loop(0, messages // 2, prepare, 0)
    half = messages // (2 * tensor_count)

    def prepare_queries(step, _):
        number = block_of[(step // tensor_count) * (steps // half)] * QUERY_BLOCK // rows
        number = number + step % tensor_count
        queries_all[pl.ds(pl.multiple_of(step * rows, 64), rows), :] = query_lanes(
            bounds_ref, by_segment_ref, mixed_ref, number
        ).astype(bf16)
        return 0

    lax.fori_loop(0, messages // 2, prepare_queries, 0)

    def one_block(number, _):
        query_first = block_of[number] * QUERY_BLOCK
        here = pl.ds(pl.multiple_of(number * QUERY_BLOCK, QUERY_BLOCK), QUERY_BLOCK)
        queries = queries_all[here, :]

        def attend(key_block, carry, masked):
            top, total = carry
            first = pl.multiple_of(key_block * KEY_BLOCK, KEY_BLOCK)
            scores = nt(keys[pl.ds(first, KEY_BLOCK), :], queries)
            if masked:
                scores = causal_scores(scores, first, query_first)
            new_top = jnp.maximum(top, jnp.max(scores, axis=0, keepdims=True))
            weights = jnp.exp(scores - new_top)
            total = total * jnp.exp(top - new_top) + nn(
                values_t[:, pl.ds(first, KEY_BLOCK)], weights.astype(bf16)
            )
            return new_top, total

        carry = (jnp.full((1, QUERY_BLOCK), -BIG, f32), jnp.zeros((VALUE_ROWS, QUERY_BLOCK), f32))
        carry = attend(query_first // KEY_BLOCK, carry, True)
        top, total = lax.fori_loop(
            0, count_of[number], lambda step, kept: attend(list_of[number, step], kept, False), carry
        )
        row_sum = total[HD : HD + 1]
        log_total = jnp.broadcast_to(top + jnp.log(row_sum), (HD, QUERY_BLOCK))
        out_ref[here, :] = jnp.concatenate([total[:HD] / row_sum, log_total], axis=0).T
        return 0

    lax.fori_loop(0, steps, one_block, 0)

    def pack(step, _):
        first = pl.multiple_of(step * rows, 64)
        half_rows = rows // 2
        context_ref[step // tensor_count, step % tensor_count] = jnp.concatenate(
            [
                out_ref[pl.ds(first, half_rows), 0:HD],
                out_ref[pl.ds(pl.multiple_of(first + half_rows, 32), half_rows), 0:HD],
            ],
            axis=1,
        ).astype(bf16)
        return 0

    lax.fori_loop(0, messages // 2, pack, 0)


def attention_forward(blocks, counts, lists, bounds, by_segment, mixed, tensor_count):
    messages, message_rows, _ = mixed.shape
    rows = message_rows * 2 // 3
    half = messages // 2 * rows
    smem = pl.BlockSpec(memory_space=pltpu.SMEM)
    vmem = pl.BlockSpec(memory_space=pltpu.VMEM)
    return pl.pallas_call(
        forward_kernel,
        in_specs=[smem] * 3 + [vmem] * 3,
        out_specs=[vmem, vmem],
        out_shape=[
            jax.ShapeDtypeStruct(
                (messages // 2 // tensor_count, tensor_count, rows // 2, 2 * HD), bf16
            ),
            jax.ShapeDtypeStruct((half, 128), f32),
        ],
        scratch_shapes=[
            pltpu.VMEM((PAIR_TOKENS, 128), bf16),
            pltpu.VMEM((VALUE_ROWS, PAIR_TOKENS), bf16),
            pltpu.VMEM((half, 128), bf16),
        ],
        compiler_params=pltpu.CompilerParams(vmem_limit_bytes=40 * 2**20),
        cost_estimate=pl.CostEstimate(
            flops=2 * 256 * 2 * 12_000_000, bytes_accessed=10_000_000, transcendentals=12_000_000
        ),
        name="attention_forward",
    )(blocks, counts, lists, bounds, by_segment, mixed)


def backward_kernel(
    block_of,
    count_of,
    list_of,
    bounds_ref,
    by_segment_ref,
    mixed_ref,
    grads_ref,
    out_ref,
    dq_ref,
    dkv_ref,
    keys,
    keys_t,
    values,
    queries_all,
    grads_all,
    dk,
    dv,
):
    messages, message_rows, _ = mixed_ref.shape
    rows = message_rows * 2 // 3
    tensor_count = grads_ref.shape[1]
    steps = queries_all.shape[0] // QUERY_BLOCK
    half = messages // (2 * tensor_count)

    def with_pieces(value, first_lane, wide):
        lane = lax.broadcasted_iota(jnp.int32, wide.shape, 1)
        for piece in range(3):
            part = value.astype(bf16).astype(f32)
            wide = jnp.where(lane == first_lane + piece, part, wide)
            value = value - part
        return wide

    def prepare(step, _):
        build_keys(bounds_ref, mixed_ref, keys, step)
        span = pl.ds(pl.multiple_of(step * 2 * rows, 128), 2 * rows)
        keys_t[:, span] = keys[span, :].astype(f32).T[HD:].astype(bf16)
        packed = jnp.concatenate(
            [pair_rows(mixed_ref[2 * step + part, rows:, :].astype(f32)) for part in range(2)], axis=0
        )
        lane = lax.broadcasted_iota(jnp.int32, (2 * rows, HD), 1)
        values[span, :] = jnp.concatenate([packed, jnp.where(lane < 3, 1.0, 0.0)], axis=1).astype(
            bf16
        )
        dk[span, :] = jnp.zeros((2 * rows, 128), f32)
        dv[span, :] = jnp.zeros((2 * rows, 128), f32)
        return 0

    lax.fori_loop(0, messages // 2, prepare, 0)

    def prepare_queries(step, _):
        number = block_of[(step // tensor_count) * (steps // half)] * QUERY_BLOCK // rows
        number = number + step % tensor_count
        span = pl.ds(pl.multiple_of(step * rows, 64), rows)
        wide = query_lanes(bounds_ref, by_segment_ref, mixed_ref, number)
        out = out_ref[span, :]
        queries_all[span, :] = with_pieces(-out[:, HD : HD + 1], 2 * PAIR_SEGS + 4, wide).astype(bf16)
        grads = pair_rows(grads_ref[step // tensor_count, step % tensor_count].astype(f32))
        inner = jnp.sum(grads * out[:, :HD], axis=1, keepdims=True)
        wide = jnp.concatenate([grads, jnp.zeros((rows, HD), f32)], axis=1)
        grads_all[span, :] = with_pieces(-inner, HD, wide).astype(bf16)
        return 0

    lax.fori_loop(0, messages // 2, prepare_queries, 0)

    def one_block(number, _):
        query_first = block_of[number] * QUERY_BLOCK
        here = pl.ds(pl.multiple_of(number * QUERY_BLOCK, QUERY_BLOCK), QUERY_BLOCK)
        queries = queries_all[here, :]
        grads = grads_all[here, :]

        def attend(key_block, dq, masked):
            first = pl.multiple_of(key_block * KEY_BLOCK, KEY_BLOCK)
            span = pl.ds(first, KEY_BLOCK)
            scores = nt(keys[span, :], queries)
            if masked:
                scores = causal_scores(scores, first, query_first)
            weights = jnp.exp(scores)
            score_grad = (weights * nt(values[span, :], grads)).astype(bf16)
            dv[span, :] += nn(weights.astype(bf16), grads)
            dk[span, :] += nn(score_grad, queries)
            return dq + nn(keys_t[:, span], score_grad)

        dq = attend(query_first // KEY_BLOCK, jnp.zeros((HD, QUERY_BLOCK), f32), True)
        dq = lax.fori_loop(
            0, count_of[number], lambda step, kept: attend(list_of[number, step], kept, False), dq
        )
        dq_ref[here, :] = (dq * 0.125).T.astype(bf16)
        return 0

    lax.fori_loop(0, steps, one_block, 0)

    def write(step, _):
        span = pl.ds(pl.multiple_of(step * KEY_BLOCK, KEY_BLOCK), KEY_BLOCK)
        dkv_ref[span, :] = jnp.concatenate([dk[span, HD:], dv[span, :HD]], axis=1).astype(bf16)
        return 0

    lax.fori_loop(0, PAIR_TOKENS // KEY_BLOCK, write, 0)


def attention_backward(blocks, counts, lists, bounds, by_segment, mixed, grads, out):
    smem = pl.BlockSpec(memory_space=pltpu.SMEM)
    vmem = pl.BlockSpec(memory_space=pltpu.VMEM)
    half = out.shape[0]
    return pl.pallas_call(
        backward_kernel,
        in_specs=[smem] * 3 + [vmem] * 5,
        out_specs=[vmem, vmem],
        out_shape=[
            jax.ShapeDtypeStruct((half, HD), bf16),
            jax.ShapeDtypeStruct((PAIR_TOKENS, 128), bf16),
        ],
        scratch_shapes=[
            pltpu.VMEM((PAIR_TOKENS, 128), bf16),
            pltpu.VMEM((HD, PAIR_TOKENS), bf16),
            pltpu.VMEM((PAIR_TOKENS, 128), bf16),
            pltpu.VMEM((half, 128), bf16),
            pltpu.VMEM((half, 128), bf16),
            pltpu.VMEM((PAIR_TOKENS, 128), f32),
            pltpu.VMEM((PAIR_TOKENS, 128), f32),
        ],
        compiler_params=pltpu.CompilerParams(vmem_limit_bytes=56 * 2**20),
        cost_estimate=pl.CostEstimate(
            flops=5 * 256 * 2 * 12_000_000, bytes_accessed=16_000_000, transcendentals=12_000_000
        ),
        name="attention_backward",
    )(blocks, counts, lists, bounds, by_segment, mixed, grads, out)


def greet_all(dp_count, tensor_count, dp_index, tensor_index):
    barrier = pltpu.get_barrier_semaphore()
    total = dp_count * tensor_count
    me = dp_index * tensor_count + tensor_index

    def greet(step, _):
        other = (me + step) % total
        pl.semaphore_signal(
            barrier,
            inc=1,
            device_id=(other // tensor_count, other % tensor_count),
            device_id_type=MESH,
        )
        return 0

    lax.fori_loop(1, total, greet, 0)
    pl.semaphore_wait(barrier, total - 1)


def project_kernel(
    dp_count,
    tensor_count,
    span,
    x_ref,
    gain_ref,
    bias_ref,
    shift_ref,
    weight_ref,
    normed_ref,
    mixed_ref,
    normed,
    weight,
    outbox,
    weight_sem,
    swap_sem,
    send_sem,
    recv_sem,
    local_sem,
    pass_send,
    pass_recv,
):
    dp_index, tensor_index = lax.axis_index("dp"), lax.axis_index("tensor")
    rows = x_ref.shape[0]
    core = dp_index % 2
    base = dp_index // span * span
    chip = dp_index % span // 2
    chips = span // 2
    partner = (dp_index + 1 - 2 * core, tensor_index)
    columns = weight.shape[2]

    def weight_copy(owner):
        return pltpu.make_async_copy(
            weight_ref.at[:, pl.ds(pl.multiple_of((2 * owner + core) * columns, 128), columns)],
            weight.at[owner],
            weight_sem.at[owner],
        )

    lax.fori_loop(0, tensor_count, lambda i, _: (weight_copy(i).start(), 0)[1], 0)
    greet_all(dp_count, tensor_count, dp_index, tensor_index)

    normed[core] = normalize(x_ref[...].astype(f32), gain_ref[...], bias_ref[...]).astype(bf16)
    swap = pltpu.make_async_remote_copy(
        src_ref=normed.at[core],
        dst_ref=normed.at[core],
        send_sem=swap_sem.at[0],
        recv_sem=swap_sem.at[1],
        device_id=partner,
        device_id_type=MESH,
    )
    swap.start()
    swap.wait_recv()

    def slot(place_dp, place_tensor):
        return mixed_ref.at[place_dp * tensor_count + place_tensor]

    def send(owner, part, pair):
        head_chip = 2 * core + pair
        target = (base + 2 * head_chip + (part + chip) % 2, owner)
        here = (target[0] == dp_index) & (owner == tensor_index)
        return here, pltpu.make_async_remote_copy(
            src_ref=outbox.at[owner, part, pair],
            dst_ref=slot(2 * chip + part, tensor_index),
            send_sem=send_sem.at[owner, part, pair],
            recv_sem=recv_sem.at[chip, tensor_index],
            device_id=target,
            device_id_type=MESH,
        ), pltpu.make_async_copy(
            outbox.at[owner, part, pair], slot(2 * chip + part, tensor_index), local_sem.at[0]
        )

    def one_part(step, _):
        owner = (tensor_index + 1 + step // 2) % tensor_count
        part = step % 2

        @pl.when(part == 0)
        def _():
            weight_copy(owner).wait()

        result = nn(normed[part], weight[owner]) + shift_ref[owner]
        first = [result[:, 0:128], result[:, 192:320]]
        last = [result[:, 128:192], result[:, 320:384]]
        for pair in range(2):
            outbox[owner, part, pair, 0:rows, :] = first[pair].astype(bf16)
            outbox[owner, part, pair, rows:, :] = jnp.concatenate(
                [last[pair][: rows // 2], last[pair][rows // 2 :]], axis=1
            ).astype(bf16)
            here, far, near = send(owner, part, pair)

            @pl.when(here)
            def _():
                near.start()

            @pl.when(jnp.logical_not(here))
            def _():
                far.start()

        return 0

    lax.fori_loop(0, 2 * tensor_count, one_part, 0)
    normed_ref[...] = normed[...]

    def arrival(step):
        from_chip, from_tensor = step // tensor_count, step % tensor_count
        mine = slot(2 * from_chip + (core + from_chip) % 2, from_tensor)
        theirs = slot(2 * from_chip + (core + from_chip + 1) % 2, from_tensor)
        here = (from_chip == chip) & (from_tensor == tensor_index) & (chip // 2 == core)

        def passing(place):
            return pltpu.make_async_remote_copy(
                src_ref=place,
                dst_ref=place,
                send_sem=pass_send.at[from_chip, from_tensor],
                recv_sem=pass_recv.at[from_chip, from_tensor],
                device_id=partner,
                device_id_type=MESH,
            )

        return mine, theirs, here, passing, from_chip, from_tensor

    def hand_on(step, _):
        mine, _theirs, here, passing, from_chip, from_tensor = arrival(step)

        @pl.when(here)
        def _():
            pltpu.make_async_copy(mine, mine, local_sem.at[0]).wait()

        @pl.when(jnp.logical_not(here))
        def _():
            pltpu.make_async_remote_copy(
                src_ref=mine,
                dst_ref=mine,
                send_sem=pass_send.at[from_chip, from_tensor],
                recv_sem=recv_sem.at[from_chip, from_tensor],
                device_id=partner,
                device_id_type=MESH,
            ).wait_recv()

        passing(mine).start()
        return 0

    lax.fori_loop(0, chips * tensor_count, hand_on, 0)

    def finish(step, _):
        mine, theirs, _here, passing, _a, _b = arrival(step)
        passing(mine).wait_send()
        passing(theirs).wait_recv()
        return 0

    lax.fori_loop(0, chips * tensor_count, finish, 0)

    def sent(step, _):
        here, far, _near = send(step // 4, step // 2 % 2, step % 2)

        @pl.when(jnp.logical_not(here))
        def _():
            far.wait_send()

        return 0

    lax.fori_loop(0, 4 * tensor_count, sent, 0)
    swap.wait_send()


def project(inputs, gain, bias, shift, weight, dp_count, tensor_count, span):
    rows, width = inputs.shape
    columns = weight.shape[1] // (2 * tensor_count)
    messages = span * tensor_count
    chips = span // 2
    dma = pltpu.SemaphoreType.DMA
    vmem = pl.BlockSpec(memory_space=pltpu.VMEM)
    anywhere = pl.BlockSpec(memory_space=pl.ANY)
    return pl.pallas_call(
        functools.partial(project_kernel, dp_count, tensor_count, span),
        in_specs=[vmem] * 4 + [anywhere],
        out_specs=[vmem, anywhere],
        out_shape=[
            jax.ShapeDtypeStruct((2, rows, width), bf16),
            jax.ShapeDtypeStruct((messages, rows * 3 // 2, 128), bf16),
        ],
        scratch_shapes=[
            pltpu.VMEM((2, rows, width), bf16),
            pltpu.VMEM((tensor_count, width, columns), bf16),
            pltpu.VMEM((tensor_count, 2, 2, rows * 3 // 2, 128), bf16),
            dma((tensor_count,)),
            dma((2,)),
            dma((tensor_count, 2, 2)),
            dma((chips, tensor_count)),
            dma((1,)),
            dma((chips, tensor_count)),
            dma((chips, tensor_count)),
        ],
        compiler_params=pltpu.CompilerParams(
            collective_id=0, has_side_effects=True, vmem_limit_bytes=40 * 2**20
        ),
        cost_estimate=pl.CostEstimate(
            flops=2 * 2 * rows * width * weight.shape[1] // 2,
            bytes_accessed=20_000_000,
            transcendentals=0,
        ),
        name="project",
    )(inputs, gain, bias, shift, weight)


def halving_scatter(parts, inbox, send_sem, recv_sem, chip, chips, core, layer):
    def stages():
        return chips.bit_length() - 1

    def places(order, stage, step):
        size = jnp.where(order == 0, 2**stage, chips // 2 ** (stage + 1))
        bit = chip // size % 2
        low, high = chip % size, chip // (2 * size) * (2 * size)
        rest = jnp.where(order == 0, low + step * 2 * size, high + step)
        theirs = rest + (1 - bit) * size
        return theirs, rest + bit * size, chip + (1 - 2 * bit) * size

    def copy(item, order, stage, step):
        theirs, _, partner = places(order, stage, step)
        where = chips - chips // 2**stage + step
        return pltpu.make_async_remote_copy(
            src_ref=parts.at[item, theirs],
            dst_ref=inbox.at[item, where],
            send_sem=send_sem.at[item, where],
            recv_sem=recv_sem.at[item, where],
            device_id=(2 * partner + core, layer),
            device_id_type=MESH,
        )

    def start(item, order, stage):
        def one(step, _):
            copy(item, order, stage, step).start()
            return 0

        lax.fori_loop(0, chips // 2 ** (stage + 1), one, 0)

    def finish(item, order, stage):
        def one(step, _):
            copy(item, order, stage, step).wait_recv()
            _, keep, _ = places(order, stage, step)
            where = chips - chips // 2**stage + step
            parts[item, keep] = (
                parts[item, keep].astype(f32) + inbox[item, where].astype(f32)
            ).astype(bf16)
            return 0

        lax.fori_loop(0, chips // 2 ** (stage + 1), one, 0)

    def sent(item, order, stage):
        def one(step, _):
            copy(item, order, stage, step).wait_send()
            return 0

        lax.fori_loop(0, chips // 2 ** (stage + 1), one, 0)

    return stages(), start, finish, sent


def repeat(count, body):
    def one(step, _):
        body(step)
        return 0

    lax.fori_loop(0, count, one, 0)


def swap_copy(source, target, sems, number, partner):
    return pltpu.make_async_remote_copy(
        src_ref=source,
        dst_ref=target,
        send_sem=sems.at[0, number],
        recv_sem=sems.at[1, number],
        device_id=partner,
        device_id_type=MESH,
    )


def layer_norm_back(values, gain, grads):
    average = jnp.mean(values, axis=-1, keepdims=True)
    centred = values - average
    scale = lax.rsqrt(jnp.mean(centred * centred, axis=-1, keepdims=True) + epsilon)
    normed = centred * scale
    scaled = grads * gain
    first = jnp.mean(scaled, axis=-1, keepdims=True)
    second = jnp.mean(scaled * normed, axis=-1, keepdims=True)
    return (scaled - first - normed * second) * scale, grads * normed


def column_sum(values):
    return jnp.sum(values, axis=0, keepdims=True)


def transpose_rows(source, target):
    size = min(256, target.shape[0])

    def one(step):
        span = pl.ds(pl.multiple_of(step * size, size), size)
        target[span, :] = source[:, span].T

    repeat(target.shape[0] // size, one)


def middle_kernel(
    dp_count,
    tensor_count,
    span,
    context_ref,
    x_ref,
    cot_ref,
    gain_ref,
    bias_ref,
    dense_shift_ref,
    down_shift_ref,
    up_shift_ref,
    dense_ref,
    up_ref,
    down_ref,
    block_ref,
    middle_grad_ref,
    up_grad_ref,
    down_grad_ref,
    dense_grad_ref,
    vectors_ref,
    up_shift_grad_ref,
    grads_ref,
    context_in,
    context,
    dense,
    up,
    down,
    middle,
    normed,
    cot,
    turned_normed,
    turned_cot,
    active,
    upper_grad,
    out_total,
    normed_total,
    swap_out,
    swap_in,
    low_grad,
    outbox,
    parts,
    inbox,
    layer_inbox,
    dense_inbox,
    last_out,
    last_in,
    last_dense_out,
    last_dense_in,
    weight_sem,
    swap_sem,
    context_send,
    context_recv,
    parts_send,
    parts_recv,
    layer_send,
    layer_recv,
    dense_send,
    dense_recv,
    outbox_send,
    outbox_recv,
    local_sem,
):
    dp_index, tensor_index = lax.axis_index("dp"), lax.axis_index("tensor")
    rows, width = x_ref.shape
    hidden = up.shape[2]
    core = dp_index % 2
    base = dp_index // span * span
    chip = dp_index % span // 2
    chips = span // 2
    layer_chip, layer_chips = dp_index // 2, dp_count // 2
    pair_rows_count = parts.shape[2]
    piece = pair_rows_count // 2
    partner = (dp_index + 1 - 2 * core, tensor_index)
    part_span = lambda part: pl.ds(pl.multiple_of(part * rows, 64), rows)
    mine, theirs = part_span(core), part_span(1 - core)

    def dense_copy(owner):
        return pltpu.make_async_copy(
            dense_ref.at[pl.ds(pl.multiple_of((2 * owner + core) * 128, 128), 128)],
            dense.at[pl.ds(pl.multiple_of(owner * 128, 128), 128)],
            weight_sem.at[0, owner],
        )

    def up_copy(owner):
        return pltpu.make_async_copy(
            up_ref.at[:, pl.ds(pl.multiple_of((2 * owner + core) * hidden, 128), hidden)],
            up.at[owner],
            weight_sem.at[1, owner],
        )

    def down_copy(owner):
        return pltpu.make_async_copy(
            down_ref.at[pl.ds(pl.multiple_of((2 * owner + core) * hidden, 128), hidden)],
            down.at[owner],
            weight_sem.at[2, owner],
        )

    for copy in (dense_copy, up_copy, down_copy):
        repeat(tensor_count, lambda owner, copy=copy: copy(owner).start())
    cot[mine, :] = cot_ref[...]
    greet_all(dp_count, tensor_count, dp_index, tensor_index)

    def context_out(step):
        place, owner = step // tensor_count, step % tensor_count
        owner = (tensor_index + 1 + owner) % tensor_count
        part = (core + place) % 2
        target = (base + 2 * place + chip // 2, owner)
        here = (target[0] == dp_index) & (owner == tensor_index)
        source = context_ref.at[place, owner]
        destination = context_in.at[tensor_index, chip % 2, part]
        far = pltpu.make_async_remote_copy(
            src_ref=source,
            dst_ref=destination,
            send_sem=context_send.at[place, owner],
            recv_sem=context_recv.at[tensor_index, chip % 2, part],
            device_id=target,
            device_id_type=MESH,
        )
        near = pltpu.make_async_copy(source, destination, local_sem.at[0])
        return here, far, near

    def send_context(step):
        here, far, near = context_out(step)

        @pl.when(here)
        def _():
            near.start()

        @pl.when(jnp.logical_not(here))
        def _():
            far.start()

    repeat(chips * tensor_count, send_context)
    cot_swap = swap_copy(cot.at[mine], cot.at[mine], swap_sem, 0, partner)
    cot_swap.start()
    swap_copy(cot.at[theirs], cot.at[theirs], swap_sem, 0, partner).wait_recv()
    transpose_rows(cot, turned_cot)
    repeat(2, lambda part: out_total.__setitem__(part, jnp.zeros((rows, width), f32)))
    repeat(2, lambda part: normed_total.__setitem__(part, jnp.zeros((rows, width), f32)))

    def take_context(step):
        owner, part = (tensor_index + step // 2) % tensor_count, step % 2
        for pair in range(2):
            destination = context_in.at[owner, pair, part]
            here = (
                (owner == tensor_index)
                & (chip == 2 * core + pair)
                & ((part + chip) % 2 == core)
            )

            @pl.when(here)
            def _():
                pltpu.make_async_copy(destination, destination, local_sem.at[0]).wait()

            @pl.when(jnp.logical_not(here))
            def _():
                pltpu.make_async_remote_copy(
                    src_ref=destination,
                    dst_ref=destination,
                    send_sem=context_send.at[0, 0],
                    recv_sem=context_recv.at[owner, pair, part],
                    device_id=partner,
                    device_id_type=MESH,
                ).wait_recv()

        first, second = context_in[owner, 0, part], context_in[owner, 1, part]
        lanes = pl.ds(pl.multiple_of(owner * 128, 128), 128)
        half = rows // 2
        for number in range(2):
            cut = slice(number * HD, (number + 1) * HD)
            where = pl.ds(pl.multiple_of(part * rows + number * half, 32), half)
            context[where, lanes] = jnp.concatenate([first[:, cut], second[:, cut]], axis=1)

    repeat(2 * tensor_count, take_context)
    repeat(tensor_count, lambda owner: dense_copy(owner).wait())

    swap_out[0] = nn(context[theirs, :], dense[...]).astype(bf16)
    first_swap = swap_copy(swap_out.at[0], swap_in.at[0], swap_sem, 1, partner)
    first_swap.start()
    own = x_ref[...].astype(f32) + dense_shift_ref[...] + nn(context[mine, :], dense[...])
    first_swap.wait_recv()
    middle[...] = own + swap_in[0].astype(f32)
    normed[mine, :] = normalize(middle[...], gain_ref[...], bias_ref[...]).astype(bf16)
    normed_swap = swap_copy(normed.at[mine], normed.at[mine], swap_sem, 2, partner)
    normed_swap.start()
    swap_copy(normed.at[theirs], normed.at[theirs], swap_sem, 2, partner).wait_recv()
    transpose_rows(normed, turned_normed)

    stages, start, finish, sent = halving_scatter(
        parts, inbox, parts_send, parts_recv, layer_chip, layer_chips, core, tensor_index
    )

    def layer_copy(step, kind):
        return pltpu.make_async_remote_copy(
            src_ref=parts.at[2 * step + kind, layer_chip],
            dst_ref=layer_inbox.at[kind, step - 1],
            send_sem=layer_send.at[kind, step - 1],
            recv_sem=layer_recv.at[kind, step - 1],
            device_id=(dp_index, (tensor_index + step) % tensor_count),
            device_id_type=MESH,
        )

    def advance(step):
        for stage in range(stages):
            tile = step - 1 - stage

            @pl.when((tile >= 0) & (tile < tensor_count))
            def _():
                for kind in range(2):
                    finish(2 * tile + kind, kind, stage)
                    if stage + 1 < stages:
                        start(2 * tile + kind, kind, stage + 1)
                if stage + 1 == stages:

                    @pl.when(tile > 0)
                    def _():
                        for kind in range(2):
                            layer_copy(tile, kind).start()

    def one_tile(step):
        owner = (tensor_index + step) % tensor_count
        up_copy(owner).wait()
        down_copy(owner).wait()
        up_shift_grad_ref[owner] = jnp.zeros((8, hidden), f32)

        def one_part(part):
            here = part_span(part)
            upper = nn(normed[here, :], up[owner]) + up_shift_ref[owner]
            active_grad = nt(cot[here, :], down[owner])
            square = upper * upper
            bent = jnp.tanh(0.7978845608 * upper * (1.0 + 0.044715 * square))
            rising = 0.5 * (1.0 + bent)
            slope = rising + 0.5 * upper * (1.0 - bent * bent) * 0.7978845608 * (
                1.0 + 3.0 * 0.044715 * square
            )
            low = (active_grad * slope).astype(bf16)
            active_low = (upper * rising).astype(bf16)
            active[here, :] = active_low
            upper_grad[here, :] = low
            up_shift_grad_ref[owner, 0:1] += column_sum(low.astype(f32))
            out_total[part] += nn(active_low, down[owner])
            normed_total[part] += nt(low, up[owner])

        repeat(2, one_part)

        def one_chip(place):
            here = pl.ds(pl.multiple_of(place * pair_rows_count, pair_rows_count), pair_rows_count)
            parts[2 * step, place] = nn(turned_normed[here, :], upper_grad[...]).astype(bf16)
            parts[2 * step + 1, place] = nn(turned_cot[here, :], active[...]).astype(bf16)

        repeat(layer_chips, one_chip)
        for kind in range(2):
            start(2 * step + kind, kind, 0)
        advance(step)

    repeat(tensor_count, one_tile)

    swap_out[1] = normed_total[1 - core].astype(bf16)
    second_swap = swap_copy(swap_out.at[1], swap_in.at[1], swap_sem, 3, partner)
    second_swap.start()
    swap_out[2] = out_total[1 - core].astype(bf16)
    third_swap = swap_copy(swap_out.at[2], swap_in.at[2], swap_sem, 4, partner)
    third_swap.start()
    second_swap.wait_recv()
    grads = normed_total[core] + swap_in[1].astype(f32)
    vectors_ref[...] = jnp.zeros_like(vectors_ref)
    vectors_ref[2:3] = column_sum(grads)
    part_grad, gain_part = layer_norm_back(middle[...], gain_ref[...], grads)
    vectors_ref[1:2] = column_sum(gain_part)
    own_cot = cot_ref[...].astype(f32)
    vectors_ref[3:4] = column_sum(own_cot)
    middle_grad = own_cot + part_grad
    middle_grad_ref[...] = middle_grad
    vectors_ref[0:1] = column_sum(middle_grad)
    low_grad[mine, :] = middle_grad.astype(bf16)
    low_swap = swap_copy(low_grad.at[mine], low_grad.at[mine], swap_sem, 5, partner)
    low_swap.start()
    third_swap.wait_recv()
    block_ref[...] = (
        middle[...] + out_total[core] + swap_in[2].astype(f32) + down_shift_ref[...]
    ).astype(bf16)
    swap_copy(low_grad.at[theirs], low_grad.at[theirs], swap_sem, 5, partner).wait_recv()

    def grads_out(owner, part, pair):
        target = (base + 2 * (2 * core + pair) + (part + chip) % 2, owner)
        here = (target[0] == dp_index) & (owner == tensor_index)
        source = outbox.at[owner, part, pair]
        destination = grads_ref.at[chip, tensor_index]
        far = pltpu.make_async_remote_copy(
            src_ref=source,
            dst_ref=destination,
            send_sem=outbox_send.at[owner, part, pair],
            recv_sem=outbox_recv.at[chip, tensor_index],
            device_id=target,
            device_id_type=MESH,
        )
        return here, far, pltpu.make_async_copy(source, destination, local_sem.at[1])

    def send_grads(step):
        owner, part = (tensor_index + 1 + step // 2) % tensor_count, step % 2
        lanes = pl.ds(pl.multiple_of(owner * 128, 128), 128)
        result = nt(low_grad[part_span(part), :], dense[lanes, :]).astype(bf16)
        half = rows // 2
        for pair in range(2):
            cut = slice(pair * HD, (pair + 1) * HD)
            outbox[owner, part, pair] = jnp.concatenate(
                [result[:half, cut], result[half:, cut]], axis=1
            )
            here, far, near = grads_out(owner, part, pair)

            @pl.when(here)
            def _():
                near.start()

            @pl.when(jnp.logical_not(here))
            def _():
                far.start()

    repeat(2 * tensor_count, send_grads)

    dense_item = 2 * tensor_count
    transpose_rows(low_grad, turned_cot)

    def dense_chip(place):
        here = pl.ds(pl.multiple_of(place * pair_rows_count, pair_rows_count), pair_rows_count)
        parts[dense_item, place] = nn(turned_cot[here, :], context[...]).astype(bf16)

    repeat(layer_chips, dense_chip)
    start(dense_item, 0, 0)
    for step in range(tensor_count, tensor_count + stages):
        advance(step)
        stage = step - tensor_count
        finish(dense_item, 0, stage)
        if stage + 1 < stages:
            start(dense_item, 0, stage + 1)

    def dense_layer_copy(step):
        owner = (tensor_index + step) % tensor_count
        return pltpu.make_async_remote_copy(
            src_ref=parts.at[
                dense_item, layer_chip, :, pl.ds(pl.multiple_of(owner * 128, 128), 128)
            ],
            dst_ref=dense_inbox.at[step - 1],
            send_sem=dense_send.at[step - 1],
            recv_sem=dense_recv.at[step - 1],
            device_id=(dp_index, owner),
            device_id_type=MESH,
        )

    for step in range(1, tensor_count):
        dense_layer_copy(step).start()

    my_half = pl.ds(pl.multiple_of(core * hidden, 128), hidden)
    their_half = pl.ds(pl.multiple_of((1 - core) * hidden, 128), hidden)
    kept = pl.ds(pl.multiple_of(core * piece, piece), piece)
    given = pl.ds(pl.multiple_of((1 - core) * piece, piece), piece)
    results = (up_grad_ref, down_grad_ref)
    for kind in range(2):
        for step in range(1, tensor_count):
            layer_copy(step, kind).wait_recv()

        def total(where):
            value = parts[kind, layer_chip, where, :].astype(f32)
            for step in range(1, tensor_count):
                value = value + layer_inbox[kind, step - 1, where, :].astype(f32)
            return value

        last_out[kind] = total(given)
        swap_copy(last_out.at[kind], last_in.at[kind], swap_sem, 6 + kind, partner).start()
        results[kind][:, my_half] = total(kept)
    for step in range(1, tensor_count):
        dense_layer_copy(step).wait_recv()

    def dense_total(where):
        value = parts[
            dense_item, layer_chip, where, pl.ds(pl.multiple_of(tensor_index * 128, 128), 128)
        ].astype(f32)
        for step in range(1, tensor_count):
            value = value + dense_inbox[step - 1, where, :].astype(f32)
        return value

    last_dense_out[...] = dense_total(given)
    swap_copy(last_dense_out, last_dense_in, swap_sem, 8, partner).start()
    dense_grad_ref[:, pl.ds(pl.multiple_of(core * 128, 128), 128)] = dense_total(kept)
    for kind in range(2):
        swap_copy(last_out.at[kind], last_in.at[kind], swap_sem, 6 + kind, partner).wait()
        results[kind][:, their_half] = last_in[kind]
    swap_copy(last_dense_out, last_dense_in, swap_sem, 8, partner).wait()
    dense_grad_ref[:, pl.ds(pl.multiple_of((1 - core) * 128, 128), 128)] = last_dense_in[...]

    def arrived(step):
        place, owner = step // tensor_count, step % tensor_count
        destination = grads_ref.at[place, owner]
        here = (place == chip) & (owner == tensor_index) & (chip // 2 == core)

        @pl.when(here)
        def _():
            pltpu.make_async_copy(destination, destination, local_sem.at[1]).wait()

        @pl.when(jnp.logical_not(here))
        def _():
            pltpu.make_async_remote_copy(
                src_ref=destination,
                dst_ref=destination,
                send_sem=context_send.at[0, 0],
                recv_sem=outbox_recv.at[place, owner],
                device_id=partner,
                device_id_type=MESH,
            ).wait_recv()

    repeat(chips * tensor_count, arrived)

    def context_sent(step):
        here, far, _near = context_out(step)

        @pl.when(jnp.logical_not(here))
        def _():
            far.wait_send()

    repeat(chips * tensor_count, context_sent)

    def grads_sent(step):
        here, far, _near = grads_out(step // 4, step // 2 % 2, step % 2)

        @pl.when(jnp.logical_not(here))
        def _():
            far.wait_send()

    repeat(4 * tensor_count, grads_sent)

    def parts_sent(step):
        for kind in range(2):
            for stage in range(stages):
                sent(2 * step + kind, kind, stage)

    repeat(tensor_count, parts_sent)
    for stage in range(stages):
        sent(dense_item, 0, stage)
    for step in range(1, tensor_count):
        dense_layer_copy(step).wait_send()
        for kind in range(2):
            layer_copy(step, kind).wait_send()
    for copy in (cot_swap, first_swap, normed_swap, second_swap, third_swap, low_swap):
        copy.wait_send()


def middle_part(
    context,
    inputs,
    cotangent,
    vectors,
    up_shift,
    dense_full,
    up_full,
    down_full,
    dp_count,
    tensor_count,
    span,
):
    rows, width = inputs.shape
    hidden = up_full.shape[1] // (2 * tensor_count)
    columns = dense_full.shape[0] // tensor_count
    piece = width // dp_count
    chips, layer_chips = span // 2, dp_count // 2
    dma = pltpu.SemaphoreType.DMA
    vmem = pl.BlockSpec(memory_space=pltpu.VMEM)
    anywhere = pl.BlockSpec(memory_space=pl.ANY)
    items = 2 * tensor_count + 1
    both_rows = (2 * rows, width)
    part = (2 * piece, hidden)
    return pl.pallas_call(
        functools.partial(middle_kernel, dp_count, tensor_count, span),
        in_specs=[vmem] * 8 + [anywhere] * 3,
        out_specs=[vmem] * 7 + [anywhere],
        out_shape=[
            jax.ShapeDtypeStruct((rows, width), bf16),
            jax.ShapeDtypeStruct((rows, width), f32),
            jax.ShapeDtypeStruct((piece, 2 * hidden), f32),
            jax.ShapeDtypeStruct((piece, 2 * hidden), f32),
            jax.ShapeDtypeStruct((piece, columns), f32),
            jax.ShapeDtypeStruct((8, width), f32),
            jax.ShapeDtypeStruct((tensor_count, 8, hidden), f32),
            jax.ShapeDtypeStruct((chips, tensor_count, rows // 2, 128), bf16),
        ],
        scratch_shapes=[
            pltpu.VMEM((tensor_count, 2, 2, rows // 2, 128), bf16),
            pltpu.VMEM((2 * rows, 128 * tensor_count), bf16),
            pltpu.VMEM((128 * tensor_count, width), bf16),
            pltpu.VMEM((tensor_count, width, hidden), bf16),
            pltpu.VMEM((tensor_count, hidden, width), bf16),
            pltpu.VMEM((rows, width), f32),
            pltpu.VMEM(both_rows, bf16),
            pltpu.VMEM(both_rows, bf16),
            pltpu.VMEM((width, 2 * rows), bf16),
            pltpu.VMEM((width, 2 * rows), bf16),
            pltpu.VMEM((2 * rows, hidden), bf16),
            pltpu.VMEM((2 * rows, hidden), bf16),
            pltpu.VMEM((2, rows, width), f32),
            pltpu.VMEM((2, rows, width), f32),
            pltpu.VMEM((3, rows, width), bf16),
            pltpu.VMEM((3, rows, width), bf16),
            pltpu.VMEM(both_rows, bf16),
            pltpu.VMEM((tensor_count, 2, 2, rows // 2, 128), bf16),
            pltpu.VMEM((items, layer_chips, *part), bf16),
            pltpu.VMEM((items, layer_chips - 1, *part), bf16),
            pltpu.VMEM((2, tensor_count - 1, *part), bf16),
            pltpu.VMEM((tensor_count - 1, 2 * piece, 128), bf16),
            pltpu.VMEM((2, piece, hidden), f32),
            pltpu.VMEM((2, piece, hidden), f32),
            pltpu.VMEM((piece, 128), f32),
            pltpu.VMEM((piece, 128), f32),
            dma((3, tensor_count)),
            dma((2, 9)),
            dma((chips, tensor_count)),
            dma((tensor_count, 2, 2)),
            dma((items, layer_chips - 1)),
            dma((items, layer_chips - 1)),
            dma((2, tensor_count - 1)),
            dma((2, tensor_count - 1)),
            dma((tensor_count - 1,)),
            dma((tensor_count - 1,)),
            dma((tensor_count, 2, 2)),
            dma((chips, tensor_count)),
            dma((2,)),
        ],
        compiler_params=pltpu.CompilerParams(
            collective_id=1, has_side_effects=True, vmem_limit_bytes=60 * 2**20
        ),
        cost_estimate=pl.CostEstimate(
            flops=6 * 2 * 2 * rows * width * hidden * tensor_count,
            bytes_accessed=40_000_000,
            transcendentals=0,
        ),
        name="middle_part",
    )(context, inputs, cotangent, *vectors, up_shift, dense_full, up_full, down_full)


def finish_kernel(
    dp_count,
    tensor_count,
    span,
    dq_ref,
    dkv_ref,
    normed_ref,
    x_ref,
    gain_ref,
    middle_grad_ref,
    early_ref,
    weight_ref,
    input_grad_ref,
    weight_grad_ref,
    early_out_ref,
    late_out_ref,
    weight,
    turned_normed,
    dkv_in,
    outbox,
    mixed_in,
    gathered,
    normed_total,
    swap_out,
    swap_in,
    parts,
    inbox,
    layer_inbox,
    last_out,
    last_in,
    sums,
    sums_in,
    weight_sem,
    swap_sem,
    dkv_send,
    dkv_recv,
    outbox_send,
    mixed_recv,
    parts_send,
    parts_recv,
    layer_send,
    layer_recv,
    sums_send,
    sums_recv,
    local_sem,
):
    dp_index, tensor_index = lax.axis_index("dp"), lax.axis_index("tensor")
    rows, width = x_ref.shape
    columns = weight.shape[2]
    core = dp_index % 2
    base = dp_index // span * span
    chip = dp_index % span // 2
    chips = span // 2
    layer_chip, layer_chips = dp_index // 2, dp_count // 2
    pair_rows_count = parts.shape[2]
    piece = pair_rows_count // 2
    partner = (dp_index + 1 - 2 * core, tensor_index)
    part_span = lambda part: pl.ds(pl.multiple_of(part * rows, 64), rows)
    dp_rows = rows * tensor_count

    def weight_copy(owner):
        return pltpu.make_async_copy(
            weight_ref.at[:, pl.ds(pl.multiple_of((2 * owner + core) * columns, 128), columns)],
            weight.at[owner],
            weight_sem.at[owner],
        )

    repeat(tensor_count, lambda owner: weight_copy(owner).start())
    greet_all(dp_count, tensor_count, dp_index, tensor_index)

    def dkv_copy(place, whose):
        taken = 2 * place + (whose + place) % 2
        return pltpu.make_async_remote_copy(
            src_ref=dkv_ref.at[pl.ds(pl.multiple_of(taken * dp_rows, 128), dp_rows)],
            dst_ref=dkv_in.at[place],
            send_sem=dkv_send.at[place],
            recv_sem=dkv_recv.at[place],
            device_id=partner,
            device_id_type=MESH,
        )

    repeat(chips, lambda place: dkv_copy(place, 1 - core).start())
    transpose_rows(normed_ref, turned_normed)
    repeat(2, lambda part: normed_total.__setitem__(part, jnp.zeros((rows, width), f32)))
    repeat(chips, lambda place: dkv_copy(place, 1 - core).wait_recv())

    def message(place, owner):
        part = (core + place) % 2
        target = (base + 2 * place + chip // 2, owner)
        here = (target[0] == dp_index) & (owner == tensor_index)
        source = outbox.at[place, owner]
        destination = mixed_in.at[tensor_index, chip % 2, part]
        far = pltpu.make_async_remote_copy(
            src_ref=source,
            dst_ref=destination,
            send_sem=outbox_send.at[place, owner],
            recv_sem=mixed_recv.at[tensor_index, chip % 2, part],
            device_id=target,
            device_id_type=MESH,
        )
        return here, far, pltpu.make_async_copy(source, destination, local_sem.at[0])

    def send_message(step):
        owner, place = (tensor_index + 1 + step // chips) % tensor_count, step % chips
        taken = 2 * place + (core + place) % 2
        own = pl.ds(pl.multiple_of(taken * dp_rows + owner * rows, 64), rows)
        total = dkv_ref[own, :].astype(f32) + dkv_in[
            place, pl.ds(pl.multiple_of(owner * rows, 64), rows), :
        ].astype(f32)
        queries = dq_ref[
            pl.ds(pl.multiple_of(place * dp_rows + owner * rows, 64), rows), :
        ].astype(f32)
        outbox[place, owner, 0:rows, :] = jnp.concatenate([queries, total[:, :HD]], axis=1).astype(
            bf16
        )
        half = rows // 2
        outbox[place, owner, rows:, :] = jnp.concatenate(
            [total[:half, HD:], total[half:, HD:]], axis=1
        ).astype(bf16)
        here, far, near = message(place, owner)

        @pl.when(here)
        def _():
            near.start()

        @pl.when(jnp.logical_not(here))
        def _():
            far.start()

    repeat(chips * tensor_count, send_message)

    dp_steps = dp_count.bit_length() - 1
    tensor_steps = tensor_count.bit_length() - 1

    def add_up(which):
        for step in range(dp_steps + tensor_steps):
            if step < dp_steps:
                size = 2**step
                peer = (dp_index + size * (1 - 2 * (dp_index // size % 2)), tensor_index)
            else:
                size = 2 ** (step - dp_steps)
                peer = (dp_index, tensor_index + size * (1 - 2 * (tensor_index // size % 2)))
            copy = pltpu.make_async_remote_copy(
                src_ref=sums.at[which, step],
                dst_ref=sums_in.at[which, step],
                send_sem=sums_send.at[which, step],
                recv_sem=sums_recv.at[which, step],
                device_id=peer,
                device_id_type=MESH,
            )
            copy.start()
            copy.wait()
            sums[which, step + 1] = sums[which, step] + sums_in[which, step]
        return sums[which, dp_steps + tensor_steps]

    sums[0, 0] = early_ref[...]
    sums[1, 0] = jnp.zeros(sums.shape[2:], f32)
    early_out_ref[...] = add_up(0)

    stages, start, finish, sent = halving_scatter(
        parts, inbox, parts_send, parts_recv, layer_chip, layer_chips, core, tensor_index
    )

    def layer_copy(step):
        return pltpu.make_async_remote_copy(
            src_ref=parts.at[step, layer_chip],
            dst_ref=layer_inbox.at[step - 1],
            send_sem=layer_send.at[step - 1],
            recv_sem=layer_recv.at[step - 1],
            device_id=(dp_index, (tensor_index + step) % tensor_count),
            device_id_type=MESH,
        )

    def advance(step):
        for stage in range(stages):
            tile = step - 1 - stage

            @pl.when((tile >= 0) & (tile < tensor_count))
            def _():
                finish(tile, tile % 2, stage)
                if stage + 1 < stages:
                    start(tile, tile % 2, stage + 1)
                else:

                    @pl.when(tile > 0)
                    def _():
                        layer_copy(tile).start()

    def one_owner(step):
        owner = (tensor_index + step) % tensor_count
        weight_copy(owner).wait()

        def one_part(part):
            for pair in range(2):
                destination = mixed_in.at[owner, pair, part]
                here = (
                    (owner == tensor_index)
                    & (chip == 2 * core + pair)
                    & ((part + chip) % 2 == core)
                )

                @pl.when(here)
                def _():
                    pltpu.make_async_copy(destination, destination, local_sem.at[0]).wait()

                @pl.when(jnp.logical_not(here))
                def _():
                    pltpu.make_async_remote_copy(
                        src_ref=destination,
                        dst_ref=destination,
                        send_sem=outbox_send.at[0, 0],
                        recv_sem=mixed_recv.at[owner, pair, part],
                        device_id=partner,
                        device_id_type=MESH,
                    ).wait_recv()

            pieces_here = []
            for pair in range(2):
                value = mixed_in[owner, pair, part]
                pieces_here += [value[:rows], pair_rows(value[rows:])]
            grads = jnp.concatenate(pieces_here, axis=1)
            gathered[part_span(part), :] = grads
            place = pl.ds(2 * owner + core, 1)
            sums[1, 0, place, 0:columns] += column_sum(grads.astype(f32))
            normed_total[part] += nt(grads, weight[owner])

        repeat(2, one_part)

        def one_chip(place):
            here = pl.ds(pl.multiple_of(place * pair_rows_count, pair_rows_count), pair_rows_count)
            parts[step, place] = nn(turned_normed[here, :], gathered[...]).astype(bf16)

        repeat(layer_chips, one_chip)
        start(step, step % 2, 0)
        advance(step)

    repeat(tensor_count, one_owner)

    swap_out[...] = normed_total[1 - core].astype(bf16)
    swap = swap_copy(swap_out, swap_in, swap_sem, 0, partner)
    swap.start()
    swap.wait_recv()
    grads = normed_total[core] + swap_in[...].astype(f32)
    part_grad, gain_part = layer_norm_back(x_ref[...].astype(f32), gain_ref[...], grads)
    input_grad_ref[...] = middle_grad_ref[...] + part_grad
    first = sums.shape[3] - width
    sums[1, 0, 0:1, first:] = column_sum(gain_part)
    sums[1, 0, 1:2, first:] = column_sum(grads)
    late_out_ref[...] = add_up(1)

    for step in range(tensor_count, tensor_count + stages):
        advance(step)
    for step in range(1, tensor_count):
        layer_copy(step).wait_recv()

    def total(where):
        value = parts[0, layer_chip, where, :].astype(f32)
        for step in range(1, tensor_count):
            value = value + layer_inbox[step - 1, where, :].astype(f32)
        return value

    last_out[...] = total(pl.ds(pl.multiple_of((1 - core) * piece, piece), piece))
    last = swap_copy(last_out, last_in, swap_sem, 1, partner)
    last.start()
    weight_grad_ref[:, pl.ds(pl.multiple_of(core * columns, 128), columns)] = total(
        pl.ds(pl.multiple_of(core * piece, piece), piece)
    )
    last.wait()
    weight_grad_ref[:, pl.ds(pl.multiple_of((1 - core) * columns, 128), columns)] = last_in[...]

    repeat(chips, lambda place: dkv_copy(place, 1 - core).wait_send())

    def message_sent(step):
        here, far, _near = message(step // tensor_count, step % tensor_count)

        @pl.when(jnp.logical_not(here))
        def _():
            far.wait_send()

    repeat(chips * tensor_count, message_sent)
    for step in range(tensor_count):
        for stage in range(stages):
            sent(step, step % 2, stage)
    for step in range(1, tensor_count):
        layer_copy(step).wait_send()
    swap.wait_send()


def finish_part(
    dq, dkv, normed, inputs, gain, middle_grad, early, weight, dp_count, tensor_count, span
):
    rows, width = inputs.shape
    columns = weight.shape[1] // (2 * tensor_count)
    piece = width // dp_count
    chips, layer_chips = span // 2, dp_count // 2
    dma = pltpu.SemaphoreType.DMA
    vmem = pl.BlockSpec(memory_space=pltpu.VMEM)
    anywhere = pl.BlockSpec(memory_space=pl.ANY)
    message = (rows * 3 // 2, 128)
    steps = dp_count.bit_length() + tensor_count.bit_length() - 2
    part = (2 * piece, columns)
    return pl.pallas_call(
        functools.partial(finish_kernel, dp_count, tensor_count, span),
        in_specs=[vmem] * 7 + [anywhere],
        out_specs=[vmem] * 4,
        out_shape=[
            jax.ShapeDtypeStruct((rows, width), f32),
            jax.ShapeDtypeStruct((piece, 2 * columns), f32),
            jax.ShapeDtypeStruct(early.shape, f32),
            jax.ShapeDtypeStruct(early.shape, f32),
        ],
        scratch_shapes=[
            pltpu.VMEM((tensor_count, width, columns), bf16),
            pltpu.VMEM((width, 2 * rows), bf16),
            pltpu.VMEM((chips, rows * tensor_count, 128), bf16),
            pltpu.VMEM((chips, tensor_count, *message), bf16),
            pltpu.VMEM((tensor_count, 2, 2, *message), bf16),
            pltpu.VMEM((2 * rows, columns), bf16),
            pltpu.VMEM((2, rows, width), f32),
            pltpu.VMEM((rows, width), bf16),
            pltpu.VMEM((rows, width), bf16),
            pltpu.VMEM((tensor_count, layer_chips, *part), bf16),
            pltpu.VMEM((tensor_count, layer_chips - 1, *part), bf16),
            pltpu.VMEM((tensor_count - 1, *part), bf16),
            pltpu.VMEM((piece, columns), f32),
            pltpu.VMEM((piece, columns), f32),
            pltpu.VMEM((2, steps + 1, *early.shape), f32),
            pltpu.VMEM((2, steps, *early.shape), f32),
            dma((tensor_count,)),
            dma((2, 2)),
            dma((chips,)),
            dma((chips,)),
            dma((chips, tensor_count)),
            dma((tensor_count, 2, 2)),
            dma((tensor_count, layer_chips - 1)),
            dma((tensor_count, layer_chips - 1)),
            dma((tensor_count - 1,)),
            dma((tensor_count - 1,)),
            dma((2, steps)),
            dma((2, steps)),
            dma((1,)),
        ],
        compiler_params=pltpu.CompilerParams(
            collective_id=2, has_side_effects=True, vmem_limit_bytes=56 * 2**20
        ),
        cost_estimate=pl.CostEstimate(
            flops=2 * 2 * 2 * rows * width * columns * tensor_count,
            bytes_accessed=30_000_000,
            transcendentals=0,
        ),
        name="finish_part",
    )(dq, dkv, normed, inputs, gain, middle_grad, early, weight)


def per_device(
    block_in,
    norm1_gain,
    norm1_bias,
    qkv_weight,
    qv_bias,
    dense_weight,
    dense_bias,
    norm2_gain,
    norm2_bias,
    up_weight,
    up_bias,
    down_weight,
    down_bias,
    cotangent,
    seg_parent,
    seg_length,
):
    dp_count, tensor_count = lax.axis_size("dp"), lax.axis_size("tensor")
    dp_index, tensor_index = lax.axis_index("dp"), lax.axis_index("tensor")
    rows, width = block_in.shape
    dp_rows = rows * tensor_count
    span = PAIR_TOKENS // dp_rows
    heads_here = HEADS // tensor_count
    local_index = lax.rem(dp_index, span)
    core = lax.rem(dp_index, 2)
    both = ("dp", "tensor")

    vectors = (norm1_gain, norm1_bias, norm2_gain, norm2_bias, dense_bias, down_bias)
    small = jnp.concatenate([value.reshape(-1) for value in vectors + (qv_bias, up_bias)])
    small = lax.all_gather(small, both, axis=0, tiled=False).astype(f32)
    small = small.reshape(dp_count, tensor_count, -1)
    piece = norm1_gain.shape[0]
    gain_one, bias_one, gain_two, bias_two, dense_shift, down_shift = (
        small[:, 0, i * piece : (i + 1) * piece].reshape(-1) for i in range(6)
    )

    def unpack(first, shape):
        value = small[:, :, first : first + shape[0] * shape[1]]
        value = value.reshape(dp_count, tensor_count, *shape).transpose(1, 2, 0, 3)
        return value.reshape(tensor_count * shape[0], dp_count * shape[1])

    qv_full = unpack(6 * piece, qv_bias.shape)
    up_shift = unpack(6 * piece + qv_bias.size, up_bias.shape)

    def gather_matrix(value, dp_axis):
        value = lax.all_gather(value, "tensor", axis=1 - dp_axis, tiled=True)
        return lax.all_gather(value, "dp", axis=dp_axis, tiled=True)

    qkv_full = gather_matrix(qkv_weight, 0)
    dense_full = gather_matrix(dense_weight, 1)
    up_full = gather_matrix(up_weight, 0)
    down_full = gather_matrix(down_weight, 1)

    head = tensor_index * heads_here + local_index // 2
    slope = jnp.exp2(-8.0 * (head.astype(f32) + 1.0) / HEADS) / TRUNK
    bounds, by_segment, block_list, block_count = pair_tables(
        seg_parent, seg_length, dp_index // span, slope
    )
    half = span // 2
    taken = jnp.stack([2 * i + (core ^ (i & 1)) for i in range(half)])
    block_ids = (
        taken[:, None] * (dp_rows // QUERY_BLOCK)
        + jnp.arange(dp_rows // QUERY_BLOCK, dtype=jnp.int32)[None, :]
    ).reshape(-1)

    key_zeros = jnp.zeros((HEADS, 1, HD), f32)
    qkv_shift = jnp.concatenate(
        [qv_full[:, None, :HD], key_zeros, qv_full[:, None, HD:]], axis=1
    ).reshape(tensor_count, 2, 1, -1)
    qkv_shift = lax.dynamic_index_in_dim(qkv_shift, core, 1, keepdims=False)
    normed_both, mixed = project(
        block_in, gain_one[None], bias_one[None], qkv_shift, qkv_full, dp_count, tensor_count, span
    )
    normed_one = lax.dynamic_index_in_dim(normed_both, core, 0, keepdims=False)
    my_counts, my_lists = jnp.take(block_count, block_ids), jnp.take(block_list, block_ids, axis=0)
    tables = (block_ids, my_counts, my_lists, bounds, by_segment)
    packed_context, out_float = attention_forward(*tables, mixed, tensor_count)
    up_rows = up_shift.reshape(tensor_count, 2, 1, -1)
    up_rows = lax.dynamic_index_in_dim(up_rows, core, 1, keepdims=False)
    vectors = tuple(value[None] for value in (gain_two, bias_two, dense_shift, down_shift))
    (
        block_out,
        middle_grad,
        up_grad,
        down_grad,
        dense_grad,
        vector_grads,
        up_shift_part,
        packed_grads,
    ) = middle_part(
        packed_context,
        block_in,
        cotangent,
        vectors,
        up_rows,
        dense_full,
        up_full,
        down_full,
        dp_count,
        tensor_count,
        span,
    )
    dq, dkv = attention_backward(*tables, mixed, packed_grads, out_float)
    hidden = up_shift_part.shape[2]
    up_part = jnp.zeros((tensor_count, 2, hidden), f32)
    up_part = lax.dynamic_update_slice_in_dim(up_part, up_shift_part[:, :1], core, 1)
    early = jnp.concatenate([up_part.reshape(2 * tensor_count, hidden), vector_grads], axis=1)
    input_grad, qkv_weight_grad, early_sums, late_sums = finish_part(
        dq,
        dkv,
        normed_both.reshape(2 * rows, width),
        block_in,
        gain_one[None],
        middle_grad,
        early,
        qkv_full,
        dp_count,
        tensor_count,
        span,
    )

    def own_vector(value):
        return lax.dynamic_slice_in_dim(value, dp_index * piece, piece, 0)

    def own_matrix(whole, shape):
        whole = whole.reshape(tensor_count, shape[0], dp_count, shape[1])
        whole = lax.dynamic_index_in_dim(whole, tensor_index, 0, keepdims=False)
        return lax.dynamic_index_in_dim(whole, dp_index, 1, keepdims=False)

    early_vectors, late_vectors = early_sums[:, hidden:], late_sums[:, hidden:]
    qkv_totals = late_sums[:, : qkv_full.shape[1] // (2 * tensor_count)].reshape(HEADS, 3, HD)
    qv_grad = jnp.concatenate([qkv_totals[:, 0], qkv_totals[:, 2]], axis=1)
    return (
        block_out,
        input_grad,
        own_vector(late_vectors[0]),
        own_vector(late_vectors[1]),
        qkv_weight_grad,
        own_matrix(qv_grad, qv_bias.shape),
        dense_grad.T,
        own_vector(early_vectors[0]),
        own_vector(early_vectors[1]),
        own_vector(early_vectors[2]),
        up_grad,
        own_matrix(early_sums[:, :hidden], up_bias.shape),
        down_grad.T,
        own_vector(early_vectors[3]),
    )


def solution(mesh):
    rows = P(("dp", "tensor"), None)
    in_specs = (
        rows,
        P("dp"),
        P("dp"),
        P("dp", "tensor"),
        P("tensor", "dp"),
        P("tensor", "dp"),
        P("dp"),
        P("dp"),
        P("dp"),
        P("dp", "tensor"),
        P("tensor", "dp"),
        P("tensor", "dp"),
        P("dp"),
        rows,
        P(),
        P(),
    )
    out_specs = (
        rows,
        rows,
        P("dp"),
        P("dp"),
        P("dp", "tensor"),
        P("tensor", "dp"),
        P("tensor", "dp"),
        P("dp"),
        P("dp"),
        P("dp"),
        P("dp", "tensor"),
        P("tensor", "dp"),
        P("tensor", "dp"),
        P("dp"),
    )
    return jax.shard_map(
        per_device, mesh=mesh, in_specs=in_specs, out_specs=out_specs, check_vma=False
    )
```

```python
import functools

import jax
import jax.numpy as jnp
from jax import lax
from jax.experimental import pallas as pl
from jax.experimental.pallas import tpu as pltpu
from jax.sharding import PartitionSpec as P

HEADS = 16
HD = 64
TRUNK = 2048
SEG = 256
PAIR_TOKENS = 2 * (TRUNK + 12 * SEG)
PAIR_SEGS = 26
QUERY_BLOCK = 256
KEY_BLOCK = 512
BIG = 2.0**100
VALUE_ROWS = 80

epsilon = 1e-05
f32 = jnp.float32
bf16 = jnp.bfloat16
MESH = pl.DeviceIdType.MESH


def normalize(values, gain_row, bias_row):
    average = jnp.mean(values, axis=-1, keepdims=True)
    centred = values - average
    spread = jnp.mean(centred * centred, axis=-1, keepdims=True)
    return centred * lax.rsqrt(spread + epsilon) * gain_row + bias_row


def nn(left, right):
    return lax.dot_general(left, right, (((1,), (0,)), ((), ())), preferred_element_type=f32)


def nt(left, right):
    return lax.dot_general(left, right, (((1,), (1,)), ((), ())), preferred_element_type=f32)


def tn(left, right):
    return lax.dot_general(left, right, (((0,), (0,)), ((), ())), preferred_element_type=f32)


def pieces(value, count):
    parts = []
    for _ in range(count):
        part = lax.reduce_precision(value, 8, 7)
        parts.append(part)
        value = value - part
    return parts


def pair_tables(seg_parent, seg_length, group, slope):
    first = group * PAIR_SEGS
    parent = lax.dynamic_slice_in_dim(seg_parent, first, PAIR_SEGS, 0) - first
    length = lax.dynamic_slice_in_dim(seg_length, first, PAIR_SEGS, 0)
    ids = jnp.arange(PAIR_SEGS, dtype=jnp.int32)
    begin = jnp.sum(jnp.where(ids[None, :] < ids[:, None], length[None, :], 0), axis=1)
    end = begin + length
    is_parent = parent[:, None] == ids[None, :]
    grand = jnp.sum(jnp.where(is_parent, parent[None, :], 0), axis=1)
    is_grand = grand[:, None] == ids[None, :]
    parent_length = jnp.sum(jnp.where(is_parent, length[None, :], 0), axis=1)
    grand_length = jnp.sum(jnp.where(is_grand, length[None, :], 0), axis=1)
    path_start = jnp.where(
        parent == ids, 0, parent_length + jnp.where(grand == parent, 0, grand_length)
    )
    related = is_parent | is_grand | (ids[:, None] == ids[None, :])
    high, low = pieces(slope * (path_start - begin).astype(f32), 2)
    slope_high, slope_low = pieces(slope, 2)
    by_segment = jnp.concatenate(
        [
            jnp.where(related, high[None, :], -BIG),
            jnp.where(related, low[None, :], 0.0),
            jnp.broadcast_to(
                jnp.stack([256.0 * slope_high, 256.0 * slope_low, slope_high, slope_low])[None, :],
                (PAIR_SEGS, 4),
            ),
        ],
        axis=1,
    )
    by_segment = jnp.pad(
        by_segment, ((0, 128 - PAIR_SEGS), (0, 128 - by_segment.shape[1]))
    ).astype(bf16)
    bounds = jnp.pad(jnp.stack([jnp.tile(begin, 2), jnp.tile(end, 2)]), ((0, 6), (0, 128 - 2 * PAIR_SEGS)))
    query_blocks, key_blocks = PAIR_TOKENS // QUERY_BLOCK, PAIR_TOKENS // KEY_BLOCK
    q_begin = jnp.arange(query_blocks, dtype=jnp.int32) * QUERY_BLOCK
    k_begin = jnp.arange(key_blocks, dtype=jnp.int32) * KEY_BLOCK
    q_has = (begin[None, :] < q_begin[:, None] + QUERY_BLOCK) & (end[None, :] > q_begin[:, None])
    k_has = (begin[None, :] < k_begin[:, None] + KEY_BLOCK) & (end[None, :] > k_begin[:, None])
    q_sees = jnp.any(q_has[:, :, None] & related[None], axis=1)
    seen = jnp.any(q_sees[:, None, :] & k_has[None, :, :], axis=2)
    seen = seen & (k_begin[None, :] + KEY_BLOCK <= q_begin[:, None])
    rank = jnp.sum(
        jnp.where(k_begin[None, None, :] < k_begin[None, :, None], seen[:, None, :], False),
        axis=2,
        dtype=jnp.int32,
    )
    slots = jnp.arange(key_blocks + 2, dtype=jnp.int32)
    numbers = jnp.arange(key_blocks, dtype=jnp.int32)
    block_list = jnp.sum(
        jnp.where(
            seen[:, :, None] & (rank[:, :, None] == slots[None, None, :]), numbers[None, :, None], 0
        ),
        axis=1,
    )
    block_count = jnp.sum(seen, axis=1, dtype=jnp.int32)
    return bounds, by_segment, block_list, block_count


def causal_scores(scores, key_first, query_first):
    rows = key_first + lax.broadcasted_iota(jnp.int32, scores.shape, 0)
    columns = query_first + lax.broadcasted_iota(jnp.int32, scores.shape, 1)
    return jnp.where(rows <= columns, scores, -BIG)


def token_lanes(bounds_ref, first, count):
    token = first + lax.broadcasted_iota(jnp.int32, (count, 128), 0)
    lane = lax.broadcasted_iota(jnp.int32, (count, 128), 1)
    member = (token >= bounds_ref[0:1, :]) & (token < bounds_ref[1:2, :])
    base = 2 * PAIR_SEGS
    number = jnp.where(lane < base + 2, lax.shift_right_logical(token, 8), token & 255)
    fixed = jnp.where(lane < base + 7, 1, 0)
    number = jnp.where(lane < base + 4, number, fixed)
    return jnp.where(lane < base, jnp.where(member, 1, 0), number).astype(f32)


def pair_rows(packed):
    return jnp.concatenate([packed[:, :HD], packed[:, HD:]], axis=0)


def build_keys(bounds_ref, mixed_ref, keys, step):
    rows = mixed_ref.shape[1] * 2 // 3
    lane = lax.broadcasted_iota(jnp.int32, (rows, 128), 1)
    for part in range(2):
        first = (2 * step + part) * rows
        both = mixed_ref[2 * step + part, 0:rows, :].astype(f32)
        keys[pl.ds(pl.multiple_of(first, 64), rows), :] = jnp.where(
            lane < HD, token_lanes(bounds_ref, first, rows), both
        ).astype(bf16)


def query_lanes(bounds_ref, by_segment_ref, mixed_ref, number):
    rows = mixed_ref.shape[1] * 2 // 3
    meta = nn(token_lanes(bounds_ref, number * rows, rows).astype(bf16), by_segment_ref[...])
    queries = mixed_ref[number, 0:rows, 0:HD].astype(f32) * 0.125
    return jnp.concatenate([meta[:, :HD], queries], axis=1)


def forward_kernel(
    block_of,
    count_of,
    list_of,
    bounds_ref,
    by_segment_ref,
    mixed_ref,
    context_ref,
    out_ref,
    keys,
    values_t,
    queries_all,
    scores_a,
    scores_b,
):
    messages, message_rows, _ = mixed_ref.shape
    rows = message_rows * 2 // 3
    tensor_count = context_ref.shape[1]
    steps = queries_all.shape[0] // QUERY_BLOCK

    def prepare(step, _):
        build_keys(bounds_ref, mixed_ref, keys, step)
        values = jnp.concatenate(
            [pair_rows(mixed_ref[2 * step + part, rows:, :].astype(f32)) for part in range(2)], axis=0
        )
        lane = lax.broadcasted_iota(jnp.int32, (2 * rows, HD), 1)
        wide = jnp.concatenate([values, jnp.where(lane == 0, 1.0, 0.0)], axis=1)
        values_t[:, pl.ds(pl.multiple_of(step * 2 * rows, 128), 2 * rows)] = wide.T[
            :VALUE_ROWS
        ].astype(bf16)
        return 0

    lax.fori_loop(0, messages // 2, prepare, 0)
    half = messages // (2 * tensor_count)

    def prepare_queries(step, _):
        number = block_of[(step // tensor_count) * (steps // half)] * QUERY_BLOCK // rows
        number = number + step % tensor_count
        queries_all[pl.ds(pl.multiple_of(step * rows, 64), rows), :] = query_lanes(
            bounds_ref, by_segment_ref, mixed_ref, number
        ).astype(bf16)
        return 0

    lax.fori_loop(0, messages // 2, prepare_queries, 0)

    def one_block(number, _):
        query_first = block_of[number] * QUERY_BLOCK
        here = pl.ds(pl.multiple_of(number * QUERY_BLOCK, QUERY_BLOCK), QUERY_BLOCK)
        queries = queries_all[here, :]

        count = count_of[number]

        def scores_of(step):
            first = pl.multiple_of(list_of[number, step] * KEY_BLOCK, KEY_BLOCK)
            return nt(keys[pl.ds(first, KEY_BLOCK), :], queries)

        def absorb(scores, first, carry):
            top, total = carry
            new_top = jnp.maximum(top, jnp.max(scores, axis=0, keepdims=True))
            weights = jnp.exp(scores - new_top).astype(bf16)
            total = total * jnp.exp(top - new_top) + nn(
                values_t[:, pl.ds(first, KEY_BLOCK)], weights
            )
            return new_top, total

        def absorb_listed(buffer, step, carry):
            first = pl.multiple_of(list_of[number, step] * KEY_BLOCK, KEY_BLOCK)
            return absorb(buffer[...], first, carry)

        first = pl.multiple_of(query_first // KEY_BLOCK * KEY_BLOCK, KEY_BLOCK)
        scores_a[...] = scores_of(0)
        scores = causal_scores(nt(keys[pl.ds(first, KEY_BLOCK), :], queries), first, query_first)
        carry = (jnp.full((1, QUERY_BLOCK), -BIG, f32), jnp.zeros((VALUE_ROWS, QUERY_BLOCK), f32))
        carry = absorb(scores, first, carry)

        def two_blocks(step, carry):
            scores_b[...] = scores_of(2 * step + 1)
            carry = absorb_listed(scores_a, 2 * step, carry)
            scores_a[...] = scores_of(2 * step + 2)
            return absorb_listed(scores_b, 2 * step + 1, carry)

        carry = lax.fori_loop(0, count // 2, two_blocks, carry)
        top, total = lax.fori_loop(
            0, count % 2, lambda _, kept: absorb_listed(scores_a, count - 1, kept), carry
        )
        row_sum = total[HD : HD + 1]
        log_total = jnp.broadcast_to(top + jnp.log(row_sum), (HD, QUERY_BLOCK))
        out_ref[here, :] = jnp.concatenate([total[:HD] / row_sum, log_total], axis=0).T
        return 0

    lax.fori_loop(0, steps, one_block, 0)

    def pack(step, _):
        first = pl.multiple_of(step * rows, 64)
        half_rows = rows // 2
        context_ref[step // tensor_count, step % tensor_count] = jnp.concatenate(
            [
                out_ref[pl.ds(first, half_rows), 0:HD],
                out_ref[pl.ds(pl.multiple_of(first + half_rows, 32), half_rows), 0:HD],
            ],
            axis=1,
        ).astype(bf16)
        return 0

    lax.fori_loop(0, messages // 2, pack, 0)


def attention_forward(blocks, counts, lists, bounds, by_segment, mixed, tensor_count):
    messages, message_rows, _ = mixed.shape
    rows = message_rows * 2 // 3
    half = messages // 2 * rows
    smem = pl.BlockSpec(memory_space=pltpu.SMEM)
    vmem = pl.BlockSpec(memory_space=pltpu.VMEM)
    return pl.pallas_call(
        forward_kernel,
        in_specs=[smem] * 3 + [vmem] * 3,
        out_specs=[vmem, vmem],
        out_shape=[
            jax.ShapeDtypeStruct(
                (messages // 2 // tensor_count, tensor_count, rows // 2, 2 * HD), bf16
            ),
            jax.ShapeDtypeStruct((half, 128), f32),
        ],
        scratch_shapes=[
            pltpu.VMEM((PAIR_TOKENS, 128), bf16),
            pltpu.VMEM((VALUE_ROWS, PAIR_TOKENS), bf16),
            pltpu.VMEM((half, 128), bf16),
            pltpu.VMEM((KEY_BLOCK, QUERY_BLOCK), f32),
            pltpu.VMEM((KEY_BLOCK, QUERY_BLOCK), f32),
        ],
        compiler_params=pltpu.CompilerParams(vmem_limit_bytes=40 * 2**20),
        cost_estimate=pl.CostEstimate(
            flops=2 * 256 * 2 * 12_000_000, bytes_accessed=10_000_000, transcendentals=12_000_000
        ),
        name="attention_forward",
    )(blocks, counts, lists, bounds, by_segment, mixed)


def backward_kernel(
    block_of,
    count_of,
    list_of,
    bounds_ref,
    by_segment_ref,
    mixed_ref,
    grads_ref,
    out_ref,
    dq_ref,
    dkv_ref,
    keys,
    keys_t,
    values,
    queries_all,
    grads_all,
    dk,
    dv,
):
    messages, message_rows, _ = mixed_ref.shape
    rows = message_rows * 2 // 3
    tensor_count = grads_ref.shape[1]
    steps = queries_all.shape[0] // QUERY_BLOCK
    half = messages // (2 * tensor_count)

    def with_pieces(value, first_lane, wide):
        lane = lax.broadcasted_iota(jnp.int32, wide.shape, 1)
        for piece in range(3):
            part = value.astype(bf16).astype(f32)
            wide = jnp.where(lane == first_lane + piece, part, wide)
            value = value - part
        return wide

    def prepare(step, _):
        build_keys(bounds_ref, mixed_ref, keys, step)
        span = pl.ds(pl.multiple_of(step * 2 * rows, 128), 2 * rows)
        keys_t[:, span] = keys[span, :].astype(f32).T[HD:].astype(bf16)
        packed = jnp.concatenate(
            [pair_rows(mixed_ref[2 * step + part, rows:, :].astype(f32)) for part in range(2)], axis=0
        )
        lane = lax.broadcasted_iota(jnp.int32, (2 * rows, HD), 1)
        values[span, :] = jnp.concatenate([packed, jnp.where(lane < 3, 1.0, 0.0)], axis=1).astype(
            bf16
        )
        dk[span, :] = jnp.zeros((2 * rows, 128), f32)
        dv[span, :] = jnp.zeros((2 * rows, 128), f32)
        return 0

    lax.fori_loop(0, messages // 2, prepare, 0)

    def prepare_queries(step, _):
        number = block_of[(step // tensor_count) * (steps // half)] * QUERY_BLOCK // rows
        number = number + step % tensor_count
        span = pl.ds(pl.multiple_of(step * rows, 64), rows)
        wide = query_lanes(bounds_ref, by_segment_ref, mixed_ref, number)
        out = out_ref[span, :]
        queries_all[span, :] = with_pieces(-out[:, HD : HD + 1], 2 * PAIR_SEGS + 4, wide).astype(bf16)
        grads = pair_rows(grads_ref[step // tensor_count, step % tensor_count].astype(f32))
        inner = jnp.sum(grads * out[:, :HD], axis=1, keepdims=True)
        wide = jnp.concatenate([grads, jnp.zeros((rows, HD), f32)], axis=1)
        grads_all[span, :] = with_pieces(-inner, HD, wide).astype(bf16)
        return 0

    lax.fori_loop(0, messages // 2, prepare_queries, 0)

    def one_block(number, _):
        query_first = block_of[number] * QUERY_BLOCK
        here = pl.ds(pl.multiple_of(number * QUERY_BLOCK, QUERY_BLOCK), QUERY_BLOCK)
        queries = queries_all[here, :]
        grads = grads_all[here, :]

        count = count_of[number]

        def attend(blocks, dq, masked):
            spans = [pl.ds(pl.multiple_of(block * KEY_BLOCK, KEY_BLOCK), KEY_BLOCK) for block in blocks]
            scores = [nt(keys[span, :], queries) for span in spans]
            if masked:
                scores = [causal_scores(scores[0], blocks[0] * KEY_BLOCK, query_first)]
            grads_of = [nt(values[span, :], grads) for span in spans]
            for span, score, grad in zip(spans, scores, grads_of):
                weights = jnp.exp(score)
                score_grad = (weights * grad).astype(bf16)
                dv[span, :] += nn(weights.astype(bf16), grads)
                dk[span, :] += nn(score_grad, queries)
                dq = dq + nn(keys_t[:, span], score_grad)
            return dq

        dq = attend([query_first // KEY_BLOCK], jnp.zeros((HD, QUERY_BLOCK), f32), True)
        dq = lax.fori_loop(
            0,
            count // 2,
            lambda step, kept: attend(
                [list_of[number, 2 * step], list_of[number, 2 * step + 1]], kept, False
            ),
            dq,
        )
        dq = lax.fori_loop(
            0, count % 2, lambda _, kept: attend([list_of[number, count - 1]], kept, False), dq
        )
        dq_ref[here, :] = (dq * 0.125).T.astype(bf16)
        return 0

    lax.fori_loop(0, steps, one_block, 0)

    def write(step, _):
        span = pl.ds(pl.multiple_of(step * KEY_BLOCK, KEY_BLOCK), KEY_BLOCK)
        dkv_ref[span, :] = jnp.concatenate([dk[span, HD:], dv[span, :HD]], axis=1).astype(bf16)
        return 0

    lax.fori_loop(0, PAIR_TOKENS // KEY_BLOCK, write, 0)


def attention_backward(blocks, counts, lists, bounds, by_segment, mixed, grads, out):
    smem = pl.BlockSpec(memory_space=pltpu.SMEM)
    vmem = pl.BlockSpec(memory_space=pltpu.VMEM)
    half = out.shape[0]
    return pl.pallas_call(
        backward_kernel,
        in_specs=[smem] * 3 + [vmem] * 5,
        out_specs=[vmem, vmem],
        out_shape=[
            jax.ShapeDtypeStruct((half, HD), bf16),
            jax.ShapeDtypeStruct((PAIR_TOKENS, 128), bf16),
        ],
        scratch_shapes=[
            pltpu.VMEM((PAIR_TOKENS, 128), bf16),
            pltpu.VMEM((HD, PAIR_TOKENS), bf16),
            pltpu.VMEM((PAIR_TOKENS, 128), bf16),
            pltpu.VMEM((half, 128), bf16),
            pltpu.VMEM((half, 128), bf16),
            pltpu.VMEM((PAIR_TOKENS, 128), f32),
            pltpu.VMEM((PAIR_TOKENS, 128), f32),
        ],
        compiler_params=pltpu.CompilerParams(vmem_limit_bytes=56 * 2**20),
        cost_estimate=pl.CostEstimate(
            flops=5 * 256 * 2 * 12_000_000, bytes_accessed=16_000_000, transcendentals=12_000_000
        ),
        name="attention_backward",
    )(blocks, counts, lists, bounds, by_segment, mixed, grads, out)


def flipped(chip, chips):
    return (chip + chips - 1) // chips


def greet_all(dp_count, tensor_count, dp_index, tensor_index):
    barrier = pltpu.get_barrier_semaphore()
    total = dp_count * tensor_count
    me = dp_index * tensor_count + tensor_index

    def greet(step, _):
        other = (me + step) % total
        pl.semaphore_signal(
            barrier,
            inc=1,
            device_id=(other // tensor_count, other % tensor_count),
            device_id_type=MESH,
        )
        return 0

    lax.fori_loop(1, total, greet, 0)
    pl.semaphore_wait(barrier, total - 1)


def repeat(count, body):
    def one(step, _):
        body(step)
        return 0

    lax.fori_loop(0, count, one, 0)


def swap_copy(source, target, sems, number, partner):
    return pltpu.make_async_remote_copy(
        src_ref=source,
        dst_ref=target,
        send_sem=sems.at[0, number],
        recv_sem=sems.at[1, number],
        device_id=partner,
        device_id_type=MESH,
    )


def layer_norm_back(values, gain, grads):
    average = jnp.mean(values, axis=-1, keepdims=True)
    centred = values - average
    scale = lax.rsqrt(jnp.mean(centred * centred, axis=-1, keepdims=True) + epsilon)
    normed = centred * scale
    scaled = grads * gain
    first = jnp.mean(scaled, axis=-1, keepdims=True)
    second = jnp.mean(scaled * normed, axis=-1, keepdims=True)
    return (scaled - first - normed * second) * scale, grads * normed


def column_sum(values):
    return jnp.sum(values, axis=0, keepdims=True)


def transpose_rows(source, target):
    size = min(256, target.shape[0])

    def one(step):
        span = pl.ds(pl.multiple_of(step * size, size), size)
        target[span, :] = source[:, span].T

    repeat(target.shape[0] // size, one)


def doubling_gather(
    weight, recv_sem, send_sem, layer_recv, layer_send, chip, chips, core, layer, layers, dp_index
):
    stages = chips.bit_length() - 1
    steps = weight.shape[0]

    def layer_copy(step):
        return pltpu.make_async_remote_copy(
            src_ref=weight.at[0, chip],
            dst_ref=weight.at[steps - step, chip],
            send_sem=layer_send.at[step - 1],
            recv_sem=layer_recv.at[steps - step],
            device_id=(dp_index, (layer + step * (layers // steps)) % layers),
            device_id_type=MESH,
        )

    def spread():
        for step in range(1, steps):
            layer_copy(step).start()

    rows = weight.shape[2] // 2

    def half(order):
        return pl.ds(pl.multiple_of(order * rows, rows), rows)

    def place(order, stage, step):
        size = jnp.where(order == 0, 2**stage, chips // 2 ** (stage + 1))
        bit = chip // size % 2
        across = size * (1 - 2 * bit)
        held = jnp.where(
            order == 0,
            chip // 2**stage * 2**stage + step,
            chip % (chips // 2**stage) + step * (chips // 2**stage),
        )
        return held, held + across, chip + across

    def copy(step, stage, order, number):
        held, _, partner = place(order, stage, number)
        block = weight.at[step, held, half(order), :]
        return pltpu.make_async_remote_copy(
            src_ref=block,
            dst_ref=block,
            send_sem=send_sem.at[step, 2**stage - 1 + number, order],
            recv_sem=recv_sem.at[step, held, order],
            device_id=(2 * partner + core, layer),
            device_id_type=MESH,
        )

    def wait_block(block, sem):
        pltpu.make_async_remote_copy(
            src_ref=block,
            dst_ref=block,
            send_sem=send_sem.at[0, 0, 0],
            recv_sem=sem,
            device_id=(2 * chip + 1 - core, layer),
            device_id_type=MESH,
        ).wait_recv()

    def each(stage, body):
        repeat(2 * 2**stage, lambda number: body(number % 2, number // 2))

    def arrived(step, stage):
        def one(order, number):
            _, got, _ = place(order, stage, number)
            wait_block(weight.at[step, got, half(order), :], recv_sem.at[step, got, order])

        each(stage, one)

    def advance(number):
        for stage in range(stages):
            step = number - stage

            @pl.when((step >= 0) & (step < steps))
            def _():
                if stage > 0:
                    arrived(step, stage - 1)
                else:

                    if layer_recv is not None:

                        @pl.when(step > 0)
                        def _():
                            wait_block(weight.at[step, chip], layer_recv.at[step])

                each(stage, lambda order, each_number: copy(step, stage, order, each_number).start())

    def ready(step):
        arrived(step, stages - 1)

    def sent():
        if layer_send is not None:
            for step in range(1, steps):
                layer_copy(step).wait_send()

        def one(step):
            for stage in range(stages):
                each(
                    stage,
                    lambda order, number: copy(step, stage, order, number).wait_send(),
                )

        repeat(steps, one)

    return spread, advance, ready, sent


def picked(rows, lanes, owner_of, lane_of, keep):
    lane = lax.broadcasted_iota(jnp.int32, (128, lanes), 1)
    source = lax.broadcasted_iota(jnp.int32, (128, lanes), 0)
    spread = nn(rows.astype(bf16), jnp.where(source == lane_of(lane), 1.0, 0.0).astype(bf16))
    lane = lax.broadcasted_iota(jnp.int32, (rows.shape[0], lanes), 1)
    owner = lax.broadcasted_iota(jnp.int32, (rows.shape[0], lanes), 0)
    return column_sum(jnp.where((owner == owner_of(lane)) & keep(lane), spread, 0.0))


def project_kernel(
    dp_count,
    tensor_count,
    span,
    x_ref,
    small_ref,
    shard_ref,
    feed_ref,
    normed_ref,
    mixed_ref,
    weight_out_ref,
    vectors_ref,
    up_shift_ref,
    block_ref,
    normed,
    weight,
    smalls,
    outbox,
    swap_sem,
    small_send,
    small_recv,
    half_sem,
    gather_recv,
    gather_send,
    layer_recv,
    layer_send,
    out_sem,
    send_sem,
    recv_sem,
    local_sem,
    pass_send,
    pass_recv,
):
    dp_index, tensor_index = lax.axis_index("dp"), lax.axis_index("tensor")
    rows, width = x_ref.shape
    hidden = weight.shape[3]
    columns = hidden - 128
    piece = shard_ref.shape[1]
    core = dp_index % 2
    base = dp_index // span * span
    chip = dp_index % span // 2
    chips = span // 2
    layer_chip, layer_chips = dp_index // 2, dp_count // 2
    partner = (dp_index + 1 - 2 * core, tensor_index)
    total = dp_count * tensor_count
    me = dp_index * tensor_count + tensor_index

    def small_copy(step):
        other = (me + step) % total
        place = smalls.at[dp_index, tensor_index]
        return pltpu.make_async_remote_copy(
            src_ref=place,
            dst_ref=place,
            send_sem=small_send.at[other // tensor_count, other % tensor_count],
            recv_sem=small_recv.at[dp_index, tensor_index],
            device_id=(other // tensor_count, other % tensor_count),
            device_id_type=MESH,
        )

    def small_wait(step):
        other = (me + step) % total
        there = other // tensor_count, other % tensor_count
        place = smalls.at[there[0], there[1]]
        pltpu.make_async_remote_copy(
            src_ref=place,
            dst_ref=place,
            send_sem=small_send.at[there[0], there[1]],
            recv_sem=small_recv.at[there[0], there[1]],
            device_id=partner,
            device_id_type=MESH,
        ).wait_recv()

    own_rows = pl.ds(pl.multiple_of(core * piece, piece), piece)
    smalls[dp_index, tensor_index] = small_ref[...]
    weight[0, layer_chip, own_rows, :] = shard_ref[core]
    greet_all(dp_count, tensor_count, dp_index, tensor_index)
    half = pltpu.make_async_remote_copy(
        src_ref=shard_ref.at[1 - core],
        dst_ref=weight.at[0, layer_chip, own_rows, :],
        send_sem=half_sem.at[0],
        recv_sem=half_sem.at[1],
        device_id=partner,
        device_id_type=MESH,
    )
    half.start()
    block_ref[own_rows, :] = feed_ref[core]
    feed_half = pltpu.make_async_remote_copy(
        src_ref=feed_ref.at[1 - core],
        dst_ref=block_ref.at[own_rows, :],
        send_sem=half_sem.at[2],
        recv_sem=half_sem.at[3],
        device_id=partner,
        device_id_type=MESH,
    )
    feed_half.start()
    repeat(total - 1, lambda step: small_copy(step + 1).start())
    spread, advance, ready, gather_sent = doubling_gather(
        weight,
        gather_recv,
        gather_send,
        layer_recv,
        layer_send,
        layer_chip,
        layer_chips,
        core,
        tensor_index,
        tensor_count,
        dp_index,
    )
    half.wait_recv()
    spread()
    advance(0)
    repeat(total - 1, lambda step: small_wait(step + 1))

    def vector(number):
        here = smalls[:, tensor_index].astype(f32)[:, number, :]
        return picked(
            here, width, lambda lane: lane // piece, lambda lane: lane % piece, lambda lane: lane >= 0
        )

    normed[core] = normalize(x_ref[...].astype(f32), vector(0), vector(1)).astype(bf16)
    swap = pltpu.make_async_remote_copy(
        src_ref=normed.at[core],
        dst_ref=normed.at[core],
        send_sem=swap_sem.at[0],
        recv_sem=swap_sem.at[1],
        device_id=partner,
        device_id_type=MESH,
    )
    swap.start()
    stages = layer_chips.bit_length() - 1
    for number in range(1, stages):
        advance(number)
    vectors_ref[...] = jnp.zeros_like(vectors_ref)
    for number in (0, 2, 3, 4, 5):
        vectors_ref[number : number + 1, :] = vector(number)

    bias_width = 2 * HD // dp_count

    def qkv_shift(owner):
        here = smalls[:, owner].astype(f32)[:, 6, :]

        def column(lane):
            return lane % HD + jnp.where(lane % (3 * HD) < HD, 0, HD)

        return picked(
            here,
            columns,
            lambda lane: column(lane) // bias_width,
            lambda lane: (2 * core + lane // (3 * HD)) * bias_width + column(lane) % bias_width,
            lambda lane: (lane % (3 * HD) < HD) | (lane % (3 * HD) >= 2 * HD),
        )

    def up_shift(owner):
        here = smalls[:, owner].astype(f32)[:, 7, :]
        return picked(
            here,
            hidden,
            lambda lane: lane % 128 // bias_width,
            lambda lane: (core * (hidden // 128) + lane // 128) * bias_width
            + lane % 128 % bias_width,
            lambda lane: lane >= 0,
        )

    swap.wait_recv()

    def out_copy(step):
        return pltpu.make_async_copy(
            weight.at[step], weight_out_ref.at[(tensor_index + step) % tensor_count], out_sem.at[step]
        )

    def slot(place_dp, place_tensor):
        return mixed_ref.at[place_dp * tensor_count + place_tensor]

    def send(owner, part, pair):
        head_chip = 2 * core + pair
        target = (base + 2 * head_chip + (part + flipped(chip, chips)) % 2, owner)
        here = (target[0] == dp_index) & (owner == tensor_index)
        return here, pltpu.make_async_remote_copy(
            src_ref=outbox.at[owner, part, pair],
            dst_ref=slot(2 * chip + part, tensor_index),
            send_sem=send_sem.at[owner, part, pair],
            recv_sem=recv_sem.at[chip, tensor_index],
            device_id=target,
            device_id_type=MESH,
        ), pltpu.make_async_copy(
            outbox.at[owner, part, pair], slot(2 * chip + part, tensor_index), local_sem.at[0]
        )

    def one_tile(step):
        owner = (tensor_index + step) % tensor_count
        advance(step + stages)
        ready(step)
        out_copy(step).start()
        shift = qkv_shift(owner)
        up_shift_ref[owner] = jnp.broadcast_to(up_shift(owner), up_shift_ref.shape[1:])

        def one_part(part):
            matrix = weight[step, :, :, 0:columns].reshape(width, columns)
            result = nn(normed[part], matrix) + shift
            first = [result[:, 0:128], result[:, 192:320]]
            last = [result[:, 128:192], result[:, 320:384]]
            for pair in range(2):
                outbox[owner, part, pair, 0:rows, :] = first[pair].astype(bf16)
                outbox[owner, part, pair, rows:, :] = jnp.concatenate(
                    [last[pair][: rows // 2], last[pair][rows // 2 :]], axis=1
                ).astype(bf16)
                here, far, near = send(owner, part, pair)

                @pl.when(here)
                def _():
                    near.start()

                @pl.when(jnp.logical_not(here))
                def _():
                    far.start()

        repeat(2, one_part)

    repeat(tensor_count, one_tile)
    normed_ref[...] = normed[...]

    def arrival(step):
        from_chip, from_tensor = step % chips, (tensor_index + step // chips) % tensor_count
        mine = slot(2 * from_chip + (core + flipped(from_chip, chips)) % 2, from_tensor)
        theirs = slot(2 * from_chip + (core + flipped(from_chip, chips) + 1) % 2, from_tensor)
        here = (from_chip == chip) & (from_tensor == tensor_index) & (chip // 2 == core)

        def passing(place):
            return pltpu.make_async_remote_copy(
                src_ref=place,
                dst_ref=place,
                send_sem=pass_send.at[from_chip, from_tensor],
                recv_sem=pass_recv.at[from_chip, from_tensor],
                device_id=partner,
                device_id_type=MESH,
            )

        return mine, theirs, here, passing, from_chip, from_tensor

    def hand_on(step):
        mine, _theirs, here, passing, from_chip, from_tensor = arrival(step)

        @pl.when(here)
        def _():
            pltpu.make_async_copy(mine, mine, local_sem.at[0]).wait()

        @pl.when(jnp.logical_not(here))
        def _():
            pltpu.make_async_remote_copy(
                src_ref=mine,
                dst_ref=mine,
                send_sem=pass_send.at[from_chip, from_tensor],
                recv_sem=recv_sem.at[from_chip, from_tensor],
                device_id=partner,
                device_id_type=MESH,
            ).wait_recv()

        passing(mine).start()

    repeat(chips * tensor_count, hand_on)

    def finish(step):
        mine, theirs, _here, passing, _a, _b = arrival(step)
        passing(mine).wait_send()
        passing(theirs).wait_recv()

    repeat(chips * tensor_count, finish)

    def sent(step):
        here, far, _near = send(step // 4, step // 2 % 2, step % 2)

        @pl.when(jnp.logical_not(here))
        def _():
            far.wait_send()

    repeat(4 * tensor_count, sent)
    repeat(total - 1, lambda step: small_copy(step + 1).wait_send())
    repeat(tensor_count, lambda step: out_copy(step).wait())
    half.wait_send()
    feed_half.wait()
    swap.wait_send()
    gather_sent()


def project(inputs, small, shard, feed, dp_count, tensor_count, span):
    rows, width = inputs.shape
    _, piece, hidden = shard.shape
    messages = span * tensor_count
    chips, layer_chips = span // 2, dp_count // 2
    dma = pltpu.SemaphoreType.DMA
    vmem = pl.BlockSpec(memory_space=pltpu.VMEM)
    anywhere = pl.BlockSpec(memory_space=pl.ANY)
    weight = (tensor_count, layer_chips, 2 * piece, hidden)
    return pl.pallas_call(
        functools.partial(project_kernel, dp_count, tensor_count, span),
        in_specs=[vmem] * 4,
        out_specs=[vmem, anywhere, anywhere, vmem, vmem, vmem],
        out_shape=[
            jax.ShapeDtypeStruct((2, rows, width), bf16),
            jax.ShapeDtypeStruct((messages, rows * 3 // 2, 128), bf16),
            jax.ShapeDtypeStruct(weight, bf16),
            jax.ShapeDtypeStruct((8, width), f32),
            jax.ShapeDtypeStruct((tensor_count, 8, hidden), f32),
            jax.ShapeDtypeStruct((2 * piece, feed.shape[2]), bf16),
        ],
        scratch_shapes=[
            pltpu.VMEM((2, rows, width), bf16),
            pltpu.VMEM(weight, bf16),
            pltpu.VMEM((dp_count, tensor_count, 16, 128), bf16),
            pltpu.VMEM((tensor_count, 2, 2, rows * 3 // 2, 128), bf16),
            dma((2,)),
            dma((dp_count, tensor_count)),
            dma((dp_count, tensor_count)),
            dma((4,)),
            dma((tensor_count, layer_chips, 2)),
            dma((tensor_count, layer_chips - 1, 2)),
            dma((tensor_count,)),
            dma((tensor_count - 1,)),
            dma((tensor_count,)),
            dma((tensor_count, 2, 2)),
            dma((chips, tensor_count)),
            dma((1,)),
            dma((chips, tensor_count)),
            dma((chips, tensor_count)),
        ],
        compiler_params=pltpu.CompilerParams(
            collective_id=0, has_side_effects=True, vmem_limit_bytes=40 * 2**20
        ),
        cost_estimate=pl.CostEstimate(
            flops=2 * 2 * rows * width * hidden * tensor_count,
            bytes_accessed=20_000_000,
            transcendentals=0,
        ),
        name="project",
    )(inputs, small, shard, feed)


def halving_scatter(parts, inbox, send_sem, recv_sem, chip, chips, core, layer):
    stages = chips.bit_length() - 1
    rows = parts.shape[2] // 2

    def places(order, stage, step):
        size = jnp.where(order == 0, 2**stage, chips // 2 ** (stage + 1))
        bit = chip // size % 2
        low, high = chip % size, chip // (2 * size) * (2 * size)
        rest = jnp.where(order == 0, low + step * 2 * size, high + step)
        theirs = rest + (1 - bit) * size
        return theirs, rest + bit * size, chip + (1 - 2 * bit) * size

    def half(order):
        return pl.ds(pl.multiple_of(order * rows, rows), rows)

    def copy(item, stage, order, step):
        theirs, _, partner = places(order, stage, step)
        where = chips - chips // 2**stage + step
        return pltpu.make_async_remote_copy(
            src_ref=parts.at[item, theirs, half(order), :],
            dst_ref=inbox.at[item, where, half(order), :],
            send_sem=send_sem.at[item, where, order],
            recv_sem=recv_sem.at[item, where, order],
            device_id=(2 * partner + core, layer),
            device_id_type=MESH,
        )

    def each(stage, body):
        count = chips // 2 ** (stage + 1)
        repeat(2 * count, lambda number: body(number % 2, number // 2))

    def start(item, stage):
        each(stage, lambda order, step: copy(item, stage, order, step).start())

    def finish(item, stage):
        def one(order, step):
            copy(item, stage, order, step).wait_recv()
            _, keep, _ = places(order, stage, step)
            where = chips - chips // 2**stage + step
            parts[item, keep, half(order), :] = (
                parts[item, keep, half(order), :].astype(f32)
                + inbox[item, where, half(order), :].astype(f32)
            ).astype(bf16)

        each(stage, one)

    def sent(item, stage):
        each(stage, lambda order, step: copy(item, stage, order, step).wait_send())

    return stages, start, finish, sent


def middle_kernel(
    dp_count,
    tensor_count,
    span,
    context_ref,
    x_ref,
    cot_ref,
    cot_across_ref,
    vectors_in_ref,
    up_shift_ref,
    feed_ref,
    weight_ref,
    block_ref,
    middle_grad_ref,
    parts_ref,
    dense_parts_ref,
    vectors_ref,
    up_shift_grad_ref,
    grads_ref,
    context_in,
    context,
    dense,
    feed,
    middle,
    normed,
    cot,
    turned_normed,
    turned_cot,
    active,
    upper_grad,
    out_total,
    normed_total,
    swap_in,
    core_in,
    pair_in,
    low_grad,
    outbox,
    parts,
    weight_sem,
    swap_sem,
    share_send,
    share_recv,
    context_send,
    context_recv,
    outbox_send,
    outbox_recv,
    local_sem,
    gather_recv,
    gather_send,
    parts_sem,
):
    dp_index, tensor_index = lax.axis_index("dp"), lax.axis_index("tensor")
    rows, width = x_ref.shape
    hidden = active.shape[1]
    steps = feed.shape[0]
    core = dp_index % 2
    base = dp_index // span * span
    chip = dp_index % span // 2
    chips = span // 2
    layer_chip, layer_chips = dp_index // 2, dp_count // 2
    pair_rows_count = parts.shape[2]
    side = tensor_index % 2
    partner = (dp_index + 1 - 2 * core, tensor_index)
    across = (dp_index, tensor_index + 1 - 2 * side)
    own_part = 2 * side + core
    part_span = lambda part: pl.ds(pl.multiple_of(part * rows, 64), rows)
    mine, theirs = part_span(core), part_span(1 - core)

    def dense_copy(owner):
        return pltpu.make_async_copy(
            weight_ref.at[owner, :, pl.ds(weight_ref.shape[2] - 128, 128)],
            dense.at[:, pl.ds(pl.multiple_of(owner * 128, 128), 128)],
            weight_sem.at[owner],
        )

    repeat(tensor_count, lambda owner: dense_copy(owner).start())
    gain_ref, bias_ref, dense_shift_ref, down_shift_ref = (
        vectors_in_ref.at[number : number + 1] for number in range(2, 6)
    )
    across_part = own_part + 2 - 4 * side
    cot[part_span(own_part), :] = cot_ref[...]
    cot[part_span(across_part), :] = cot_across_ref[...]
    feed[:, layer_chip] = feed_ref[...]
    greet_all(dp_count, tensor_count, dp_index, tensor_index)
    _, gather, ready, gather_sent = doubling_gather(
        feed,
        gather_recv,
        gather_send,
        None,
        None,
        layer_chip,
        layer_chips,
        core,
        tensor_index,
        tensor_count,
        dp_index,
    )
    gather_steps = steps + layer_chips.bit_length() - 2

    def context_out(step):
        place, owner = step // tensor_count, step % tensor_count
        owner = (tensor_index + 1 + owner) % tensor_count
        part = (core + flipped(place, chips)) % 2
        target = (base + 2 * place + chip // 2, owner)
        here = (target[0] == dp_index) & (owner == tensor_index)
        source = context_ref.at[place, owner]
        destination = context_in.at[tensor_index, chip % 2, part]
        far = pltpu.make_async_remote_copy(
            src_ref=source,
            dst_ref=destination,
            send_sem=context_send.at[place, owner],
            recv_sem=context_recv.at[tensor_index, chip % 2, part],
            device_id=target,
            device_id_type=MESH,
        )
        near = pltpu.make_async_copy(source, destination, local_sem.at[0])
        return here, far, near

    def send_context(step):
        here, far, near = context_out(step)

        @pl.when(here)
        def _():
            near.start()

        @pl.when(jnp.logical_not(here))
        def _():
            far.start()

    repeat(chips * tensor_count, send_context)

    def share_copy(array, which, number):
        source = own_part if number < 2 else own_part + 2 - 4 * side
        block = array.at[part_span(source)]
        return pltpu.make_async_remote_copy(
            src_ref=block,
            dst_ref=block,
            send_sem=share_send.at[which, number],
            recv_sem=share_recv.at[which, number],
            device_id=across if number == 1 else partner,
            device_id_type=MESH,
        )

    def share_arrival(array, which, number):
        source = (
            own_part + 1 - 2 * core,
            own_part + 2 - 4 * side,
            own_part + 2 - 4 * side + 1 - 2 * core,
        )[number]
        block = array.at[part_span(source)]
        return pltpu.make_async_remote_copy(
            src_ref=block,
            dst_ref=block,
            send_sem=share_send.at[which, number],
            recv_sem=share_recv.at[which, number],
            device_id=partner,
            device_id_type=MESH,
        )

    gather(0)
    share_copy(cot, 0, 0).start()
    share_copy(cot, 0, 2).start()
    repeat(4, lambda part: out_total.__setitem__(part, jnp.zeros((rows, width), f32)))
    repeat(4, lambda part: normed_total.__setitem__(part, jnp.zeros((rows, width), f32)))

    def take_context(step):
        owner, part = (tensor_index + step // 2) % tensor_count, step % 2
        for pair in range(2):
            destination = context_in.at[owner, pair, part]
            here = (
                (owner == tensor_index)
                & (chip == 2 * core + pair)
                & ((part + flipped(chip, chips)) % 2 == core)
            )

            @pl.when(here)
            def _():
                pltpu.make_async_copy(destination, destination, local_sem.at[0]).wait()

            @pl.when(jnp.logical_not(here))
            def _():
                pltpu.make_async_remote_copy(
                    src_ref=destination,
                    dst_ref=destination,
                    send_sem=context_send.at[0, 0],
                    recv_sem=context_recv.at[owner, pair, part],
                    device_id=partner,
                    device_id_type=MESH,
                ).wait_recv()

        first, second = context_in[owner, 0, part], context_in[owner, 1, part]
        lanes = pl.ds(pl.multiple_of(owner * 128, 128), 128)
        half = rows // 2
        for number in range(2):
            cut = slice(number * HD, (number + 1) * HD)
            where = pl.ds(pl.multiple_of(part * rows + number * half, 32), half)
            context[where, lanes] = jnp.concatenate([first[:, cut], second[:, cut]], axis=1)

    repeat(2 * tensor_count, take_context)
    repeat(tensor_count, lambda owner: dense_copy(owner).wait())

    low_grad[theirs, :] = nt(context[theirs, :], dense[...]).astype(bf16)
    first_swap = swap_copy(low_grad.at[theirs], swap_in, swap_sem, 0, partner)
    first_swap.start()
    own = x_ref[...].astype(f32) + dense_shift_ref[...] + nt(context[mine, :], dense[...])
    first_swap.wait()
    middle[...] = own + swap_in[...].astype(f32)
    normed[part_span(own_part), :] = normalize(middle[...], gain_ref[...], bias_ref[...]).astype(bf16)
    share_copy(normed, 1, 1).start()
    share_copy(normed, 1, 0).start()
    for number in range(1, gather_steps):
        gather(number)
    share_arrival(cot, 0, 0).wait_recv()
    share_arrival(cot, 0, 2).wait_recv()
    transpose_rows(cot, turned_cot)
    share_arrival(normed, 1, 0).wait_recv()

    def parts_copy(step):
        return pltpu.make_async_copy(parts.at[step], parts_ref.at[step], parts_sem.at[step])

    def one_tile(step):
        owner = (tensor_index + step * (tensor_count // steps)) % tensor_count
        ready(step)
        up_shift_grad_ref[step] = jnp.zeros((8, hidden), f32)

        def one_part(turn):
            part = 2 * ((side + turn // 2) % 2) + (core + turn) % 2

            @pl.when((step == 0) & (turn == 2))
            def _():
                share_arrival(normed, 1, 1).wait_recv()
                share_copy(normed, 1, 2).start()

            @pl.when((step == 0) & (turn == 3))
            def _():
                share_arrival(normed, 1, 2).wait_recv()

            here = part_span(part)
            up_matrix = feed[step, :, :, 0:hidden].reshape(width, hidden)
            down_matrix = feed[step, :, :, hidden:].reshape(width, hidden)
            upper = nn(normed[here, :], up_matrix) + up_shift_ref[owner, 0:1]
            active_grad = nn(cot[here, :], down_matrix)
            square = upper * upper
            bent = jnp.tanh(0.7978845608 * upper * (1.0 + 0.044715 * square))
            rising = 0.5 * (1.0 + bent)
            slope = rising + 0.5 * upper * (1.0 - bent * bent) * 0.7978845608 * (
                1.0 + 3.0 * 0.044715 * square
            )
            low = (active_grad * slope).astype(bf16)
            active_low = (upper * rising).astype(bf16)
            active[here, :] = active_low
            upper_grad[here, :] = low
            up_shift_grad_ref[step, 0:1] += column_sum(low.astype(f32))
            out_total[part] += nt(active_low, down_matrix)
            normed_total[part] += nt(low, up_matrix)

        repeat(4, one_part)

        @pl.when(step == 0)
        def _():
            transpose_rows(normed, turned_normed)

        def one_chip(place):
            here = pl.ds(pl.multiple_of(place * pair_rows_count, pair_rows_count), pair_rows_count)
            parts[step, place, :, 0:hidden] = nn(turned_normed[here, :], upper_grad[...]).astype(bf16)
            parts[step, place, :, hidden:] = nn(turned_cot[here, :], active[...]).astype(bf16)

        repeat(layer_chips, one_chip)
        parts_copy(step).start()

    repeat(steps, one_tile)

    def core_copy(which):
        return swap_copy(
            normed.at[pl.ds(2 * which * rows, 2 * rows)], core_in.at[which], swap_sem, 1 + which, partner
        )

    def pair_copy(which):
        return swap_copy(cot.at[part_span(which)], pair_in.at[which], swap_sem, 3 + which, across)

    totals = (normed_total, out_total)
    for number in range(3):
        share_copy(normed, 1, number).wait_send()
    for number in (0, 2):
        share_copy(cot, 0, number).wait_send()
    for which in range(2):
        for number in range(2):
            normed[pl.ds((2 * which + number) * rows, rows), :] = totals[which][
                2 * number + 1 - core
            ].astype(bf16)
        core_copy(which).start()
    def add_cores(which):
        core_copy(which).wait_recv()
        cot[part_span(which), :] = (
            totals[which][2 * (1 - side) + core] + core_in[which, part_span(1 - side), :].astype(f32)
        ).astype(bf16)
        pair_copy(which).start()

    def whole(which):
        pair_copy(which).wait_recv()
        return (
            totals[which][own_part]
            + core_in[which, part_span(side), :].astype(f32)
            + pair_in[which].astype(f32)
        )

    add_cores(0)
    grads = whole(0)
    vectors_ref[...] = jnp.zeros_like(vectors_ref)
    vectors_ref[2:3] = column_sum(grads)
    part_grad, gain_part = layer_norm_back(middle[...], gain_ref[...], grads)
    vectors_ref[1:2] = column_sum(gain_part)
    own_cot = cot_ref[...].astype(f32)
    vectors_ref[3:4] = column_sum(own_cot)
    middle_grad = own_cot + part_grad
    middle_grad_ref[...] = middle_grad
    vectors_ref[0:1] = column_sum(middle_grad)
    low_grad[mine, :] = middle_grad.astype(bf16)
    low_swap = swap_copy(low_grad.at[mine], low_grad.at[mine], swap_sem, 5, partner)
    low_swap.start()
    swap_copy(low_grad.at[theirs], low_grad.at[theirs], swap_sem, 5, partner).wait_recv()

    def grads_out(owner, part, pair):
        target = (base + 2 * (2 * core + pair) + (part + flipped(chip, chips)) % 2, owner)
        here = (target[0] == dp_index) & (owner == tensor_index)
        source = outbox.at[owner, part, pair]
        destination = grads_ref.at[chip, tensor_index]
        far = pltpu.make_async_remote_copy(
            src_ref=source,
            dst_ref=destination,
            send_sem=outbox_send.at[owner, part, pair],
            recv_sem=outbox_recv.at[chip, tensor_index],
            device_id=target,
            device_id_type=MESH,
        )
        return here, far, pltpu.make_async_copy(source, destination, local_sem.at[1])

    def send_grads(step):
        owner, part = (tensor_index + 1 + step // 2) % tensor_count, step % 2
        lanes = pl.ds(pl.multiple_of(owner * 128, 128), 128)
        result = nn(low_grad[part_span(part), :], dense[:, lanes]).astype(bf16)
        half = rows // 2
        for pair in range(2):
            cut = slice(pair * HD, (pair + 1) * HD)
            outbox[owner, part, pair] = jnp.concatenate(
                [result[:half, cut], result[half:, cut]], axis=1
            )
            here, far, near = grads_out(owner, part, pair)

            @pl.when(here)
            def _():
                near.start()

            @pl.when(jnp.logical_not(here))
            def _():
                far.start()

    repeat(2 * tensor_count, send_grads)

    add_cores(1)
    turned_low = turned_cot.at[:, 0 : 2 * rows]
    transpose_rows(low_grad, turned_low)

    def dense_chip(place):
        here = pl.ds(pl.multiple_of(place * pair_rows_count, pair_rows_count), pair_rows_count)
        dense_parts_ref[place] = nn(turned_low[here, :], context[...]).astype(bf16)

    repeat(layer_chips, dense_chip)
    block_ref[...] = (middle[...] + whole(1) + down_shift_ref[...]).astype(bf16)
    repeat(steps, lambda step: parts_copy(step).wait())

    def arrived(step):
        place, owner = step // tensor_count, step % tensor_count
        destination = grads_ref.at[place, owner]
        here = (place == chip) & (owner == tensor_index) & (chip // 2 == core)

        @pl.when(here)
        def _():
            pltpu.make_async_copy(destination, destination, local_sem.at[1]).wait()

        @pl.when(jnp.logical_not(here))
        def _():
            pltpu.make_async_remote_copy(
                src_ref=destination,
                dst_ref=destination,
                send_sem=context_send.at[0, 0],
                recv_sem=outbox_recv.at[place, owner],
                device_id=partner,
                device_id_type=MESH,
            ).wait_recv()

    repeat(chips * tensor_count, arrived)

    def context_sent(step):
        here, far, _near = context_out(step)

        @pl.when(jnp.logical_not(here))
        def _():
            far.wait_send()

    repeat(chips * tensor_count, context_sent)

    def grads_sent(step):
        here, far, _near = grads_out(step // 4, step // 2 % 2, step % 2)

        @pl.when(jnp.logical_not(here))
        def _():
            far.wait_send()

    repeat(4 * tensor_count, grads_sent)

    for which in range(2):
        core_copy(which).wait_send()
        pair_copy(which).wait_send()
    gather_sent()
    low_swap.wait_send()


def middle_part(
    context, inputs, cotangent, across, vectors, up_shift, feed, weight, dp_count, tensor_count, span
):
    rows, width = inputs.shape
    hidden = feed.shape[2] // 2
    piece = width // dp_count
    steps = tensor_count // 2
    chips, layer_chips = span // 2, dp_count // 2
    dma = pltpu.SemaphoreType.DMA
    vmem = pl.BlockSpec(memory_space=pltpu.VMEM)
    anywhere = pl.BlockSpec(memory_space=pl.ANY)
    part = (2 * piece, 2 * hidden)
    dense_part = (2 * piece, 128 * tensor_count)
    return pl.pallas_call(
        functools.partial(middle_kernel, dp_count, tensor_count, span),
        in_specs=[vmem] * 7 + [anywhere],
        out_specs=[vmem] * 2 + [anywhere] + [vmem] * 3 + [anywhere],
        out_shape=[
            jax.ShapeDtypeStruct((rows, width), bf16),
            jax.ShapeDtypeStruct((rows, width), f32),
            jax.ShapeDtypeStruct((steps, layer_chips, *part), bf16),
            jax.ShapeDtypeStruct((layer_chips, *dense_part), bf16),
            jax.ShapeDtypeStruct((8, width), f32),
            jax.ShapeDtypeStruct((steps, 8, hidden), f32),
            jax.ShapeDtypeStruct((chips, tensor_count, rows // 2, 128), bf16),
        ],
        scratch_shapes=[
            pltpu.VMEM((tensor_count, 2, 2, rows // 2, 128), bf16),
            pltpu.VMEM((2 * rows, 128 * tensor_count), bf16),
            pltpu.VMEM((width, 128 * tensor_count), bf16),
            pltpu.VMEM((steps, layer_chips, *part), bf16),
            pltpu.VMEM((rows, width), f32),
            pltpu.VMEM((4 * rows, width), bf16),
            pltpu.VMEM((4 * rows, width), bf16),
            pltpu.VMEM((width, 4 * rows), bf16),
            pltpu.VMEM((width, 4 * rows), bf16),
            pltpu.VMEM((4 * rows, hidden), bf16),
            pltpu.VMEM((4 * rows, hidden), bf16),
            pltpu.VMEM((4, rows, width), f32),
            pltpu.VMEM((4, rows, width), f32),
            pltpu.VMEM((rows, width), bf16),
            pltpu.VMEM((2, 2 * rows, width), bf16),
            pltpu.VMEM((2, rows, width), bf16),
            pltpu.VMEM((2 * rows, width), bf16),
            pltpu.VMEM((tensor_count, 2, 2, rows // 2, 128), bf16),
            pltpu.VMEM((steps, layer_chips, *part), bf16),
            dma((tensor_count,)),
            dma((2, 8)),
            dma((2, 3)),
            dma((2, 3)),
            dma((chips, tensor_count)),
            dma((tensor_count, 2, 2)),
            dma((tensor_count, 2, 2)),
            dma((chips, tensor_count)),
            dma((2,)),
            dma((steps, layer_chips, 2)),
            dma((steps, layer_chips - 1, 2)),
            dma((steps,)),
        ],
        compiler_params=pltpu.CompilerParams(
            collective_id=1, has_side_effects=True, vmem_limit_bytes=62 * 2**20
        ),
        cost_estimate=pl.CostEstimate(
            flops=6 * 2 * 2 * rows * width * hidden * tensor_count,
            bytes_accessed=40_000_000,
            transcendentals=0,
        ),
        name="middle_part",
    )(context, inputs, cotangent, across, vectors, up_shift, feed, weight)


def finish_kernel(
    dp_count,
    tensor_count,
    span,
    dq_ref,
    dkv_ref,
    normed_ref,
    x_ref,
    vectors_in_ref,
    middle_grad_ref,
    vector_grads_ref,
    up_rows_ref,
    feed_parts_ref,
    dense_parts_ref,
    weight_ref,
    input_grad_ref,
    weight_grad_ref,
    feed_grad_ref,
    dense_grad_ref,
    sums_ref,
    weight,
    turned_normed,
    dkv_in,
    outbox,
    mixed_in,
    gathered,
    normed_total,
    swap_out,
    swap_in,
    parts,
    inbox,
    layer_inbox,
    feed_parts,
    feed_inbox,
    feed_layer_inbox,
    dense_parts,
    dense_inbox,
    dense_layer_inbox,
    last_out,
    last_in,
    last_feed_out,
    last_feed_in,
    last_dense_out,
    last_dense_in,
    late,
    column_sums,
    sums_out,
    sums_in,
    weight_sem,
    load_sem,
    swap_sem,
    dkv_send,
    dkv_recv,
    outbox_send,
    mixed_recv,
    parts_send,
    parts_recv,
    layer_send,
    layer_recv,
    feed_send,
    feed_recv,
    feed_layer_send,
    feed_layer_recv,
    dense_send,
    dense_recv,
    dense_layer_send,
    dense_layer_recv,
    sums_send,
    sums_recv,
    local_sem,
):
    dp_index, tensor_index = lax.axis_index("dp"), lax.axis_index("tensor")
    rows, width = x_ref.shape
    columns = weight.shape[2]
    hidden = up_rows_ref.shape[1]
    steps = feed_parts.shape[0]
    core = dp_index % 2
    base = dp_index // span * span
    chip = dp_index % span // 2
    chips = span // 2
    layer_chip, layer_chips = dp_index // 2, dp_count // 2
    pair_rows_count = parts.shape[2]
    piece = pair_rows_count // 2
    partner = (dp_index + 1 - 2 * core, tensor_index)
    part_span = lambda part: pl.ds(pl.multiple_of(part * rows, 64), rows)
    dp_rows = rows * tensor_count
    devices = dp_count * tensor_count
    me = dp_index * tensor_count + tensor_index

    def weight_copy(owner):
        return pltpu.make_async_copy(
            weight_ref.at[owner, :, pl.ds(0, columns)], weight.at[owner], weight_sem.at[owner]
        )

    feed_load = pltpu.make_async_copy(feed_parts_ref, feed_parts, load_sem.at[0])
    dense_load = pltpu.make_async_copy(dense_parts_ref, dense_parts, load_sem.at[1])
    feed_load.start()
    dense_load.start()
    repeat(tensor_count, lambda owner: weight_copy(owner).start())
    greet_all(dp_count, tensor_count, dp_index, tensor_index)

    def dkv_copy(place, whose):
        taken = 2 * place + (whose + flipped(place, chips)) % 2
        return pltpu.make_async_remote_copy(
            src_ref=dkv_ref.at[pl.ds(pl.multiple_of(taken * dp_rows, 128), dp_rows)],
            dst_ref=dkv_in.at[place],
            send_sem=dkv_send.at[place],
            recv_sem=dkv_recv.at[place],
            device_id=partner,
            device_id_type=MESH,
        )

    repeat(chips, lambda place: dkv_copy(place, 1 - core).start())
    place_here = (layer_chip, layer_chips, core, tensor_index)
    stages, start, finish, sent = halving_scatter(parts, inbox, parts_send, parts_recv, *place_here)
    _, feed_start, feed_finish, feed_sent = halving_scatter(
        feed_parts, feed_inbox, feed_send, feed_recv, *place_here
    )
    _, dense_start, dense_finish, dense_sent = halving_scatter(
        dense_parts, dense_inbox, dense_send, dense_recv, *place_here
    )
    repeat(2, lambda part: normed_total.__setitem__(part, jnp.zeros((rows, width), f32)))
    repeat(chips, lambda place: dkv_copy(place, 1 - core).wait_recv())

    def message(place, owner):
        part = (core + flipped(place, chips)) % 2
        target = (base + 2 * place + chip // 2, owner)
        here = (target[0] == dp_index) & (owner == tensor_index)
        source = outbox.at[place, owner]
        destination = mixed_in.at[tensor_index, chip % 2, part]
        far = pltpu.make_async_remote_copy(
            src_ref=source,
            dst_ref=destination,
            send_sem=outbox_send.at[place, owner],
            recv_sem=mixed_recv.at[tensor_index, chip % 2, part],
            device_id=target,
            device_id_type=MESH,
        )
        return here, far, pltpu.make_async_copy(source, destination, local_sem.at[0])

    def send_message(step):
        owner, place = (tensor_index + 1 + step // chips) % tensor_count, step % chips
        taken = 2 * place + (core + flipped(place, chips)) % 2
        own = pl.ds(pl.multiple_of(taken * dp_rows + owner * rows, 64), rows)
        total = dkv_ref[own, :].astype(f32) + dkv_in[
            place, pl.ds(pl.multiple_of(owner * rows, 64), rows), :
        ].astype(f32)
        queries = dq_ref[
            pl.ds(pl.multiple_of(place * dp_rows + owner * rows, 64), rows), :
        ].astype(f32)
        outbox[place, owner, 0:rows, :] = jnp.concatenate([queries, total[:, :HD]], axis=1).astype(
            bf16
        )
        half = rows // 2
        outbox[place, owner, rows:, :] = jnp.concatenate(
            [total[:half, HD:], total[half:, HD:]], axis=1
        ).astype(bf16)
        here, far, near = message(place, owner)

        @pl.when(here)
        def _():
            near.start()

        @pl.when(jnp.logical_not(here))
        def _():
            far.start()

    repeat(chips * tensor_count, send_message)

    def feed_layer_copy(step):
        return pltpu.make_async_remote_copy(
            src_ref=feed_parts.at[step, layer_chip],
            dst_ref=feed_layer_inbox.at[step - 1],
            send_sem=feed_layer_send.at[step - 1],
            recv_sem=feed_layer_recv.at[step - 1],
            device_id=(dp_index, (tensor_index + step * (tensor_count // steps)) % tensor_count),
            device_id_type=MESH,
        )

    def dense_layer_copy(step):
        owner = (tensor_index + step) % tensor_count
        return pltpu.make_async_remote_copy(
            src_ref=dense_parts.at[
                0, layer_chip, :, pl.ds(pl.multiple_of(owner * 128, 128), 128)
            ],
            dst_ref=dense_layer_inbox.at[step - 1],
            send_sem=dense_layer_send.at[step - 1],
            recv_sem=dense_layer_recv.at[step - 1],
            device_id=(dp_index, owner),
            device_id_type=MESH,
        )

    feed_load.wait()
    dense_load.wait()
    repeat(steps, lambda step: feed_start(step, 0))
    dense_start(0, 0)
    transpose_rows(normed_ref, turned_normed)

    def sum_copy(which, step):
        other = (me + step) % devices
        there = (other // tensor_count, other % tensor_count)
        return pltpu.make_async_remote_copy(
            src_ref=sums_out.at[which, there[0], there[1]],
            dst_ref=sums_in.at[which, dp_index, tensor_index],
            send_sem=sums_send.at[which, there[0], there[1]],
            recv_sem=sums_recv.at[which, dp_index, tensor_index],
            device_id=there,
            device_id_type=MESH,
        )

    def sum_message(which, owner_dp, owner, vector_rows, row, count, vectors):
        block = pl.ds(pl.multiple_of(owner_dp * piece // 128 * 128, 128), 128)
        sums_out[which, owner_dp, owner] = jnp.zeros((8, 128), f32)
        sums_out[which, owner_dp, owner, 0:vector_rows, :] = vectors[0:vector_rows, block]
        for number in range(count):
            sums_out[which, owner_dp, owner, vector_rows + number : vector_rows + number + 1, :] = row[
                :, number * 128 : (number + 1) * 128
            ]

    def send_sums(which, vector_rows, row_of, count, vectors):
        def one(step):
            other = (me + step) % devices
            owner_dp, owner = other // tensor_count, other % tensor_count
            sum_message(which, owner_dp, owner, vector_rows, row_of(owner), count, vectors)

            @pl.when(step > 0)
            def _():
                sum_copy(which, step).start()

        repeat(devices, one)
        sums_in[which, dp_index, tensor_index] = sums_out[which, dp_index, tensor_index]

    send_sums(
        0, 4, lambda owner: up_rows_ref[pl.ds(2 * owner + core, 1), :], hidden // 128, vector_grads_ref
    )

    def layer_copy(step):
        return pltpu.make_async_remote_copy(
            src_ref=parts.at[step, layer_chip],
            dst_ref=layer_inbox.at[step - 1],
            send_sem=layer_send.at[step - 1],
            recv_sem=layer_recv.at[step - 1],
            device_id=(dp_index, (tensor_index + step) % tensor_count),
            device_id_type=MESH,
        )

    def advance(step):
        for stage in range(stages):
            tile = step - 1 - stage

            @pl.when((tile >= 0) & (tile < tensor_count))
            def _():
                finish(tile, stage)
                if stage + 1 < stages:
                    start(tile, stage + 1)
                else:

                    @pl.when(tile > 0)
                    def _():
                        layer_copy(tile).start()

    def feed_advance(stage):
        for step in range(steps):
            feed_finish(step, stage)
            if stage + 1 < stages:
                feed_start(step, stage + 1)
        dense_finish(0, stage)
        if stage + 1 < stages:
            dense_start(0, stage + 1)
        else:
            for step in range(1, steps):
                feed_layer_copy(step).start()
            for step in range(1, tensor_count):
                dense_layer_copy(step).start()

    def one_owner(step):
        owner = (tensor_index + step) % tensor_count
        weight_copy(owner).wait()
        column_sums[owner] = jnp.zeros(column_sums.shape[1:], f32)

        def one_part(part):
            for pair in range(2):
                destination = mixed_in.at[owner, pair, part]
                here = (
                    (owner == tensor_index)
                    & (chip == 2 * core + pair)
                    & ((part + flipped(chip, chips)) % 2 == core)
                )

                @pl.when(here)
                def _():
                    pltpu.make_async_copy(destination, destination, local_sem.at[0]).wait()

                @pl.when(jnp.logical_not(here))
                def _():
                    pltpu.make_async_remote_copy(
                        src_ref=destination,
                        dst_ref=destination,
                        send_sem=outbox_send.at[0, 0],
                        recv_sem=mixed_recv.at[owner, pair, part],
                        device_id=partner,
                        device_id_type=MESH,
                    ).wait_recv()

            pieces_here = []
            for pair in range(2):
                value = mixed_in[owner, pair, part]
                pieces_here += [value[:rows], pair_rows(value[rows:])]
            grads = jnp.concatenate(pieces_here, axis=1)
            gathered[part_span(part), :] = grads
            column_sums[owner, 0:1] += column_sum(grads.astype(f32))
            normed_total[part] += nt(grads, weight[owner])

        repeat(2, one_part)

        def one_chip(place):
            here = pl.ds(pl.multiple_of(place * pair_rows_count, pair_rows_count), pair_rows_count)
            parts[step, place] = nn(turned_normed[here, :], gathered[...]).astype(bf16)

        repeat(layer_chips, one_chip)
        start(step, 0)
        advance(step)
        for stage in range(stages):

            @pl.when(step == min(stage + 1, tensor_count - 1))
            def _():
                feed_advance(stage)

    repeat(tensor_count, one_owner)

    swap_out[...] = normed_total[1 - core].astype(bf16)
    swap = swap_copy(swap_out, swap_in, swap_sem, 0, partner)
    swap.start()
    advance(tensor_count)
    swap.wait_recv()
    grads = normed_total[core] + swap_in[...].astype(f32)
    part_grad, gain_part = layer_norm_back(x_ref[...].astype(f32), vectors_in_ref[0:1, :], grads)
    input_grad_ref[...] = middle_grad_ref[...] + part_grad
    late[...] = jnp.zeros_like(late)
    late[0:1] = column_sum(gain_part)
    late[1:2] = column_sum(grads)
    send_sums(1, 2, lambda owner: column_sums[owner, 0:1, :], columns // 128, late)

    for step in range(tensor_count + 1, tensor_count + stages):
        advance(step)

    kept = pl.ds(pl.multiple_of(core * piece, piece), piece)
    given = pl.ds(pl.multiple_of((1 - core) * piece, piece), piece)

    def total(array, arrived, where):
        value = array[0, layer_chip, where, :].astype(f32)
        for step in range(arrived.shape[0]):
            value = value + arrived[step, where, :].astype(f32)
        return value

    def dense_total(where):
        lanes = pl.ds(pl.multiple_of(tensor_index * 128, 128), 128)
        value = dense_parts[0, layer_chip, where, lanes].astype(f32)
        for step in range(1, tensor_count):
            value = value + dense_layer_inbox[step - 1, where, :].astype(f32)
        return value

    for step in range(1, steps):
        feed_layer_copy(step).wait_recv()
    last_feed_out[...] = total(feed_parts, feed_layer_inbox, given)
    last_feed = swap_copy(last_feed_out, last_feed_in, swap_sem, 2, partner)
    last_feed.start()
    own_total = total(feed_parts, feed_layer_inbox, kept)
    for kind in range(2):
        feed_grad_ref[kind, :, pl.ds(pl.multiple_of(core * hidden, 128), hidden)] = own_total[
            :, kind * hidden : (kind + 1) * hidden
        ]
    for step in range(1, tensor_count):
        dense_layer_copy(step).wait_recv()
    last_dense_out[...] = dense_total(given)
    last_dense = swap_copy(last_dense_out, last_dense_in, swap_sem, 3, partner)
    last_dense.start()
    dense_grad_ref[:, pl.ds(pl.multiple_of(core * 128, 128), 128)] = dense_total(kept)

    for step in range(1, tensor_count):
        layer_copy(step).wait_recv()
    last_out[...] = total(parts, layer_inbox, given)
    last = swap_copy(last_out, last_in, swap_sem, 1, partner)
    last.start()
    weight_grad_ref[:, pl.ds(pl.multiple_of(core * columns, 128), columns)] = total(
        parts, layer_inbox, kept
    )
    last_feed.wait()
    for kind in range(2):
        feed_grad_ref[kind, :, pl.ds(pl.multiple_of((1 - core) * hidden, 128), hidden)] = last_feed_in[
            :, kind * hidden : (kind + 1) * hidden
        ]
    last_dense.wait()
    dense_grad_ref[:, pl.ds(pl.multiple_of((1 - core) * 128, 128), 128)] = last_dense_in[...]
    last.wait()
    weight_grad_ref[:, pl.ds(pl.multiple_of((1 - core) * columns, 128), columns)] = last_in[...]

    for which in range(2):

        def sum_wait(step):
            other = (me + step + 1) % devices
            there = (other // tensor_count, other % tensor_count)
            place = sums_in.at[which, there[0], there[1]]
            pltpu.make_async_remote_copy(
                src_ref=place,
                dst_ref=place,
                send_sem=sums_send.at[which, there[0], there[1]],
                recv_sem=sums_recv.at[which, there[0], there[1]],
                device_id=partner,
                device_id_type=MESH,
            ).wait_recv()

        repeat(devices - 1, sum_wait)
        sums_ref[which] = jnp.zeros(sums_ref.shape[1:], f32)

        def add_one(step):
            owner_dp, owner = step // tensor_count, step % tensor_count
            sums_ref[which, owner_dp % 2] += sums_in[which, owner_dp, owner]

        repeat(devices, add_one)

    repeat(chips, lambda place: dkv_copy(place, 1 - core).wait_send())

    def message_sent(step):
        here, far, _near = message(step // tensor_count, step % tensor_count)

        @pl.when(jnp.logical_not(here))
        def _():
            far.wait_send()

    repeat(chips * tensor_count, message_sent)
    for stage in range(stages):
        repeat(tensor_count, lambda step: sent(step, stage))
        repeat(steps, lambda step: feed_sent(step, stage))
        dense_sent(0, stage)
    for step in range(1, tensor_count):
        layer_copy(step).wait_send()
        dense_layer_copy(step).wait_send()
    for step in range(1, steps):
        feed_layer_copy(step).wait_send()
    for which in range(2):
        repeat(devices - 1, lambda step: sum_copy(which, step + 1).wait_send())
    swap.wait_send()


def finish_part(
    dq,
    dkv,
    normed,
    inputs,
    vectors,
    middle_grad,
    vector_grads,
    up_rows,
    feed_parts,
    dense_parts,
    weight,
    dp_count,
    tensor_count,
    span,
):
    rows, width = inputs.shape
    columns = weight.shape[2] - 128
    hidden = up_rows.shape[1]
    piece = width // dp_count
    chips, layer_chips = span // 2, dp_count // 2
    steps = feed_parts.shape[0]
    dma = pltpu.SemaphoreType.DMA
    vmem = pl.BlockSpec(memory_space=pltpu.VMEM)
    anywhere = pl.BlockSpec(memory_space=pl.ANY)
    message = (rows * 3 // 2, 128)
    part = (2 * piece, columns)
    feed_part, dense_part = feed_parts.shape[2:], dense_parts.shape[2:]
    halving = (layer_chips - 1, 2)
    return pl.pallas_call(
        functools.partial(finish_kernel, dp_count, tensor_count, span),
        in_specs=[vmem] * 8 + [anywhere] * 3,
        out_specs=[vmem] * 5,
        out_shape=[
            jax.ShapeDtypeStruct((rows, width), f32),
            jax.ShapeDtypeStruct((piece, 2 * columns), f32),
            jax.ShapeDtypeStruct((2, piece, 2 * hidden), f32),
            jax.ShapeDtypeStruct((piece, 2 * 128), f32),
            jax.ShapeDtypeStruct((2, 2, 8, 128), f32),
        ],
        scratch_shapes=[
            pltpu.VMEM((tensor_count, width, columns), bf16),
            pltpu.VMEM((width, 2 * rows), bf16),
            pltpu.VMEM((chips, rows * tensor_count, 128), bf16),
            pltpu.VMEM((chips, tensor_count, *message), bf16),
            pltpu.VMEM((tensor_count, 2, 2, *message), bf16),
            pltpu.VMEM((2 * rows, columns), bf16),
            pltpu.VMEM((2, rows, width), f32),
            pltpu.VMEM((rows, width), bf16),
            pltpu.VMEM((rows, width), bf16),
            pltpu.VMEM((tensor_count, layer_chips, *part), bf16),
            pltpu.VMEM((tensor_count, layer_chips - 1, *part), bf16),
            pltpu.VMEM((tensor_count - 1, *part), bf16),
            pltpu.VMEM((steps, layer_chips, *feed_part), bf16),
            pltpu.VMEM((steps, layer_chips - 1, *feed_part), bf16),
            pltpu.VMEM((steps - 1, *feed_part), bf16),
            pltpu.VMEM((1, layer_chips, *dense_part), bf16),
            pltpu.VMEM((1, layer_chips - 1, *dense_part), bf16),
            pltpu.VMEM((tensor_count - 1, 2 * piece, 128), bf16),
            pltpu.VMEM((piece, columns), f32),
            pltpu.VMEM((piece, columns), f32),
            pltpu.VMEM((piece, 2 * hidden), f32),
            pltpu.VMEM((piece, 2 * hidden), f32),
            pltpu.VMEM((piece, 128), f32),
            pltpu.VMEM((piece, 128), f32),
            pltpu.VMEM((8, width), f32),
            pltpu.VMEM((tensor_count, 8, columns), f32),
            pltpu.VMEM((2, dp_count, tensor_count, 8, 128), f32),
            pltpu.VMEM((2, dp_count, tensor_count, 8, 128), f32),
            dma((tensor_count,)),
            dma((2,)),
            dma((2, 4)),
            dma((chips,)),
            dma((chips,)),
            dma((chips, tensor_count)),
            dma((tensor_count, 2, 2)),
            dma((tensor_count, *halving)),
            dma((tensor_count, *halving)),
            dma((tensor_count - 1,)),
            dma((tensor_count - 1,)),
            dma((steps, *halving)),
            dma((steps, *halving)),
            dma((steps - 1,)),
            dma((steps - 1,)),
            dma((1, *halving)),
            dma((1, *halving)),
            dma((tensor_count - 1,)),
            dma((tensor_count - 1,)),
            dma((2, dp_count, tensor_count)),
            dma((2, dp_count, tensor_count)),
            dma((1,)),
        ],
        compiler_params=pltpu.CompilerParams(
            collective_id=2, has_side_effects=True, vmem_limit_bytes=60 * 2**20
        ),
        cost_estimate=pl.CostEstimate(
            flops=2 * 2 * 2 * rows * width * columns * tensor_count,
            bytes_accessed=30_000_000,
            transcendentals=0,
        ),
        name="finish_part",
    )(
        dq,
        dkv,
        normed,
        inputs,
        vectors,
        middle_grad,
        vector_grads,
        up_rows,
        feed_parts,
        dense_parts,
        weight,
    )


def per_device(
    block_in,
    norm1_gain,
    norm1_bias,
    qkv_weight,
    qv_bias,
    dense_weight,
    dense_bias,
    norm2_gain,
    norm2_bias,
    up_weight,
    up_bias,
    down_weight,
    down_bias,
    cotangent,
    seg_parent,
    seg_length,
):
    dp_count, tensor_count = lax.axis_size("dp"), lax.axis_size("tensor")
    dp_index, tensor_index = lax.axis_index("dp"), lax.axis_index("tensor")
    rows, width = block_in.shape
    dp_rows = rows * tensor_count
    span = PAIR_TOKENS // dp_rows
    heads_here = HEADS // tensor_count
    local_index = lax.rem(dp_index, span)
    core = lax.rem(dp_index, 2)

    piece = norm1_gain.shape[0]

    def small_row(value):
        return jnp.pad(value.reshape(1, -1), ((0, 0), (0, 128 - value.size)))

    small = [norm1_gain, norm1_bias, norm2_gain, norm2_bias, dense_bias, down_bias, qv_bias, up_bias]
    small = jnp.pad(jnp.concatenate([small_row(value) for value in small]), ((0, 8), (0, 0)))

    def by_core(value):
        return value.reshape(value.shape[0], 2, -1).transpose(1, 0, 2)

    shard = jnp.concatenate([by_core(qkv_weight), by_core(dense_weight.T)], axis=2)
    feed_shard = jnp.concatenate([by_core(up_weight), by_core(down_weight.T)], axis=2)
    head = tensor_index * heads_here + local_index // 2
    slope = jnp.exp2(-8.0 * (head.astype(f32) + 1.0) / HEADS) / TRUNK
    bounds, by_segment, block_list, block_count = pair_tables(
        seg_parent, seg_length, dp_index // span, slope
    )
    half = span // 2
    taken = jnp.stack([2 * i + (core + flipped(i, half)) % 2 for i in range(half)])
    block_ids = (
        taken[:, None] * (dp_rows // QUERY_BLOCK)
        + jnp.arange(dp_rows // QUERY_BLOCK, dtype=jnp.int32)[None, :]
    ).reshape(-1)

    across = [(layer, layer + 1 - 2 * (layer % 2)) for layer in range(tensor_count)]
    cot_across = lax.ppermute(cotangent, "tensor", across)
    normed_both, mixed, weight, vectors, up_shift, feed_block = project(
        block_in, small, shard, feed_shard, dp_count, tensor_count, span
    )
    feed_far = [
        lax.ppermute(
            feed_block, "tensor", [(layer, (layer + hop) % tensor_count) for layer in range(tensor_count)]
        )
        for hop in range(2, tensor_count, 2)
    ]
    feed = jnp.stack([feed_block] + feed_far[::-1])
    weight = weight.reshape(tensor_count, width, -1)
    my_counts, my_lists = jnp.take(block_count, block_ids), jnp.take(block_list, block_ids, axis=0)
    tables = (block_ids, my_counts, my_lists, bounds, by_segment)
    packed_context, out_float = attention_forward(*tables, mixed, tensor_count)
    (
        block_out,
        middle_grad,
        feed_parts,
        dense_parts,
        vector_grads,
        up_shift_part,
        packed_grads,
    ) = middle_part(
        packed_context,
        block_in,
        cotangent,
        cot_across,
        vectors,
        up_shift,
        feed,
        weight,
        dp_count,
        tensor_count,
        span,
    )
    dq, dkv = attention_backward(*tables, mixed, packed_grads, out_float)
    hidden = up_shift_part.shape[2]
    up_part = jnp.zeros((tensor_count, 2, hidden), f32)
    for step in range(up_shift_part.shape[0]):
        owner = lax.rem(tensor_index + step * (tensor_count // up_shift_part.shape[0]), tensor_count)
        up_part = lax.dynamic_update_slice(up_part, up_shift_part[step, :1][None], (owner, core, 0))
    up_rows = up_part.reshape(2 * tensor_count, hidden)
    input_grad, qkv_weight_grad, feed_grad, dense_grad, sums = finish_part(
        dq,
        dkv,
        normed_both.reshape(2 * rows, width),
        block_in,
        vectors,
        middle_grad,
        vector_grads,
        up_rows,
        feed_parts,
        dense_parts[None],
        weight,
        dp_count,
        tensor_count,
        span,
    )
    offset = lax.rem(dp_index * piece, 128)

    def own_vector(which, number):
        value = sums[which, 0, number] + sums[which, 1, number]
        return lax.dynamic_slice_in_dim(value, offset, piece, 0)

    def own_matrix(whole, shape):
        return lax.dynamic_slice_in_dim(whole, dp_index * shape[1], shape[1], 1)

    qkv_totals = sums[1, :, 2:5].reshape(heads_here, 3, HD)
    qv_grad = jnp.concatenate([qkv_totals[:, 0], qkv_totals[:, 2]], axis=1)
    up_totals = sums[0, :, 4:].reshape(up_bias.shape[0], 128)
    return (
        block_out,
        input_grad,
        own_vector(1, 0),
        own_vector(1, 1),
        qkv_weight_grad,
        own_matrix(qv_grad, qv_bias.shape),
        dense_grad.T,
        own_vector(0, 0),
        own_vector(0, 1),
        own_vector(0, 2),
        feed_grad[0],
        own_matrix(up_totals, up_bias.shape),
        feed_grad[1].T,
        own_vector(0, 3),
    )


def solution(mesh):
    rows = P(("dp", "tensor"), None)
    in_specs = (
        rows,
        P("dp"),
        P("dp"),
        P("dp", "tensor"),
        P("tensor", "dp"),
        P("tensor", "dp"),
        P("dp"),
        P("dp"),
        P("dp"),
        P("dp", "tensor"),
        P("tensor", "dp"),
        P("tensor", "dp"),
        P("dp"),
        rows,
        P(),
        P(),
    )
    out_specs = (
        rows,
        rows,
        P("dp"),
        P("dp"),
        P("dp", "tensor"),
        P("tensor", "dp"),
        P("tensor", "dp"),
        P("dp"),
        P("dp"),
        P("dp"),
        P("dp", "tensor"),
        P("tensor", "dp"),
        P("tensor", "dp"),
        P("dp"),
    )
    return jax.shard_map(
        per_device, mesh=mesh, in_specs=in_specs, out_specs=out_specs, check_vma=False
    )
```

```python
import functools

import jax
import jax.numpy as jnp
from jax import lax
from jax.experimental import pallas as pl
from jax.experimental.pallas import tpu as pltpu
from jax.sharding import PartitionSpec as P

HEADS = 16
HD = 64
TRUNK = 2048
SEG = 256
PAIR_TOKENS = 2 * (TRUNK + 12 * SEG)
PAIR_SEGS = 26
QUERY_BLOCK = 256
KEY_BLOCK = 256
BIG = 2.0**100
VALUE_ROWS = 80

epsilon = 1e-05
f32 = jnp.float32
bf16 = jnp.bfloat16
MESH = pl.DeviceIdType.MESH


def normalize(values, gain_row, bias_row):
    average = jnp.mean(values, axis=-1, keepdims=True)
    centred = values - average
    spread = jnp.mean(centred * centred, axis=-1, keepdims=True)
    return centred * lax.rsqrt(spread + epsilon) * gain_row + bias_row


def nn(left, right):
    return lax.dot_general(left, right, (((1,), (0,)), ((), ())), preferred_element_type=f32)


def nt(left, right):
    return lax.dot_general(left, right, (((1,), (1,)), ((), ())), preferred_element_type=f32)


def tn(left, right):
    return lax.dot_general(left, right, (((0,), (0,)), ((), ())), preferred_element_type=f32)


def pieces(value, count):
    parts = []
    for _ in range(count):
        part = lax.reduce_precision(value, 8, 7)
        parts.append(part)
        value = value - part
    return parts


def pair_tables(seg_parent, seg_length, group, slope):
    first = group * PAIR_SEGS
    parent = lax.dynamic_slice_in_dim(seg_parent, first, PAIR_SEGS, 0) - first
    length = lax.dynamic_slice_in_dim(seg_length, first, PAIR_SEGS, 0)
    ids = jnp.arange(PAIR_SEGS, dtype=jnp.int32)
    begin = jnp.sum(jnp.where(ids[None, :] < ids[:, None], length[None, :], 0), axis=1)
    end = begin + length
    is_parent = parent[:, None] == ids[None, :]
    grand = jnp.sum(jnp.where(is_parent, parent[None, :], 0), axis=1)
    is_grand = grand[:, None] == ids[None, :]
    parent_length = jnp.sum(jnp.where(is_parent, length[None, :], 0), axis=1)
    grand_length = jnp.sum(jnp.where(is_grand, length[None, :], 0), axis=1)
    path_start = jnp.where(
        parent == ids, 0, parent_length + jnp.where(grand == parent, 0, grand_length)
    )
    related = is_parent | is_grand | (ids[:, None] == ids[None, :])
    high, low = pieces(slope * (path_start - begin).astype(f32), 2)
    slope_high, slope_low = pieces(slope, 2)
    by_segment = jnp.concatenate(
        [
            jnp.where(related, high[None, :], -BIG),
            jnp.where(related, low[None, :], 0.0),
            jnp.broadcast_to(
                jnp.stack([256.0 * slope_high, 256.0 * slope_low, slope_high, slope_low])[None, :],
                (PAIR_SEGS, 4),
            ),
        ],
        axis=1,
    )
    by_segment = jnp.pad(
        by_segment, ((0, 128 - PAIR_SEGS), (0, 128 - by_segment.shape[1]))
    ).astype(bf16)
    bounds = jnp.pad(jnp.stack([jnp.tile(begin, 2), jnp.tile(end, 2)]), ((0, 6), (0, 128 - 2 * PAIR_SEGS)))
    query_blocks, key_blocks = PAIR_TOKENS // QUERY_BLOCK, PAIR_TOKENS // KEY_BLOCK
    q_begin = jnp.arange(query_blocks, dtype=jnp.int32) * QUERY_BLOCK
    k_begin = jnp.arange(key_blocks, dtype=jnp.int32) * KEY_BLOCK
    q_has = (begin[None, :] < q_begin[:, None] + QUERY_BLOCK) & (end[None, :] > q_begin[:, None])
    k_has = (begin[None, :] < k_begin[:, None] + KEY_BLOCK) & (end[None, :] > k_begin[:, None])
    q_sees = jnp.any(q_has[:, :, None] & related[None], axis=1)
    seen = jnp.any(q_sees[:, None, :] & k_has[None, :, :], axis=2)
    seen = seen & (k_begin[None, :] + KEY_BLOCK <= q_begin[:, None])
    rank = jnp.sum(
        jnp.where(k_begin[None, None, :] < k_begin[None, :, None], seen[:, None, :], False),
        axis=2,
        dtype=jnp.int32,
    )
    slots = jnp.arange(key_blocks + 8, dtype=jnp.int32)
    numbers = jnp.arange(key_blocks, dtype=jnp.int32)
    block_list = jnp.sum(
        jnp.where(
            seen[:, :, None] & (rank[:, :, None] == slots[None, None, :]), numbers[None, :, None], 0
        ),
        axis=1,
    )
    block_count = jnp.sum(seen, axis=1, dtype=jnp.int32)
    return bounds, by_segment, block_list, block_count


def causal_scores(scores, key_first, query_first):
    rows = key_first + lax.broadcasted_iota(jnp.int32, scores.shape, 0)
    columns = query_first + lax.broadcasted_iota(jnp.int32, scores.shape, 1)
    return jnp.where(rows <= columns, scores, -BIG)


def token_lanes(bounds_ref, first, count):
    token = first + lax.broadcasted_iota(jnp.int32, (count, 128), 0)
    lane = lax.broadcasted_iota(jnp.int32, (count, 128), 1)
    member = (token >= bounds_ref[0:1, :]) & (token < bounds_ref[1:2, :])
    base = 2 * PAIR_SEGS
    number = jnp.where(lane < base + 2, lax.shift_right_logical(token, 8), token & 255)
    fixed = jnp.where(lane < base + 7, 1, 0)
    number = jnp.where(lane < base + 4, number, fixed)
    return jnp.where(lane < base, jnp.where(member, 1, 0), number).astype(f32)


def pair_rows(packed):
    return jnp.concatenate([packed[:, :HD], packed[:, HD:]], axis=0)


def build_keys(bounds_ref, mixed_ref, keys, step):
    rows = mixed_ref.shape[1] * 2 // 3
    lane = lax.broadcasted_iota(jnp.int32, (rows, 128), 1)
    for part in range(2):
        first = (2 * step + part) * rows
        both = mixed_ref[2 * step + part, 0:rows, :].astype(f32)
        keys[pl.ds(pl.multiple_of(first, 64), rows), :] = jnp.where(
            lane < HD, token_lanes(bounds_ref, first, rows), both
        ).astype(bf16)


def query_lanes(bounds_ref, by_segment_ref, mixed_ref, number):
    rows = mixed_ref.shape[1] * 2 // 3
    meta = nn(token_lanes(bounds_ref, number * rows, rows).astype(bf16), by_segment_ref[...])
    queries = mixed_ref[number, 0:rows, 0:HD].astype(f32) * 0.125
    return jnp.concatenate([meta[:, :HD], queries], axis=1)


def forward_kernel(
    block_of,
    count_of,
    list_of,
    bounds_ref,
    by_segment_ref,
    mixed_ref,
    context_ref,
    out_ref,
    keys,
    values_t,
    queries_all,
    scores_a,
    scores_b,
):
    messages, message_rows, _ = mixed_ref.shape
    rows = message_rows * 2 // 3
    tensor_count = context_ref.shape[1]
    steps = queries_all.shape[0] // QUERY_BLOCK

    def prepare(step, _):
        build_keys(bounds_ref, mixed_ref, keys, step)
        values = jnp.concatenate(
            [pair_rows(mixed_ref[2 * step + part, rows:, :]) for part in range(2)], axis=0
        )
        lane = lax.broadcasted_iota(jnp.int32, (2 * rows, HD), 1)
        ones = jnp.where(lane == 0, 1.0, 0.0).astype(bf16)
        wide = jnp.concatenate([values, ones], axis=1)
        values_t[:, pl.ds(pl.multiple_of(step * 2 * rows, 128), 2 * rows)] = wide.T[:VALUE_ROWS]
        return 0

    lax.fori_loop(0, messages // 2, prepare, 0)
    half = messages // (2 * tensor_count)

    def prepare_queries(step, _):
        number = block_of[(step // tensor_count) * (steps // half)] * QUERY_BLOCK // rows
        number = number + step % tensor_count
        queries_all[pl.ds(pl.multiple_of(step * rows, 64), rows), :] = query_lanes(
            bounds_ref, by_segment_ref, mixed_ref, number
        ).astype(bf16)
        return 0

    lax.fori_loop(0, messages // 2, prepare_queries, 0)

    def one_block(number, _):
        query_first = block_of[number] * QUERY_BLOCK
        here = pl.ds(pl.multiple_of(number * QUERY_BLOCK, QUERY_BLOCK), QUERY_BLOCK)
        queries = queries_all[here, :]

        count = count_of[number]

        def block_span(step):
            first = pl.multiple_of(list_of[number, step] * KEY_BLOCK, KEY_BLOCK)
            return pl.ds(first, KEY_BLOCK)

        def score_four(buffer, step):
            for part in range(4):
                buffer[part * KEY_BLOCK : (part + 1) * KEY_BLOCK, :] = nt(
                    keys[block_span(4 * step + part), :], queries
                )

        def absorb(scores, spans, carry):
            top, total = carry
            new_top = jnp.maximum(top, jnp.max(scores, axis=0, keepdims=True))
            weights = jnp.exp(scores - new_top).astype(bf16)
            total = total * jnp.exp(top - new_top)
            for part, span in enumerate(spans):
                total = total + nn(
                    values_t[:, span], weights[part * KEY_BLOCK : (part + 1) * KEY_BLOCK]
                )
            return new_top, total

        def absorb_four(buffer, step, carry):
            return absorb(buffer[...], [block_span(4 * step + part) for part in range(4)], carry)

        score_four(scores_a, 0)
        span = pl.ds(pl.multiple_of(query_first, KEY_BLOCK), KEY_BLOCK)
        scores = causal_scores(nt(keys[span, :], queries), query_first, query_first)
        carry = (jnp.full((1, QUERY_BLOCK), -BIG, f32), jnp.zeros((VALUE_ROWS, QUERY_BLOCK), f32))
        carry = absorb(scores, [span], carry)

        def eight_blocks(step, carry):
            score_four(scores_b, 2 * step + 1)
            carry = absorb_four(scores_a, 2 * step, carry)
            score_four(scores_a, 2 * step + 2)
            return absorb_four(scores_b, 2 * step + 1, carry)

        fours = count // 4
        carry = lax.fori_loop(0, fours // 2, eight_blocks, carry)
        carry = lax.fori_loop(
            0, fours % 2, lambda _, kept: absorb_four(scores_a, fours - 1, kept), carry
        )

        def last_blocks(blocks):
            def one(_, kept):
                spans = [block_span(count - count % (2 * blocks) + part) for part in range(blocks)]
                scores = [nt(keys[span, :], queries) for span in spans]
                return absorb(jnp.concatenate(scores, axis=0), spans, kept)

            return one

        carry = lax.fori_loop(0, count % 4 // 2, last_blocks(2), carry)
        top, total = lax.fori_loop(0, count % 2, last_blocks(1), carry)
        row_sum = total[HD : HD + 1]
        log_total = jnp.broadcast_to(top + jnp.log(row_sum), (HD, QUERY_BLOCK))
        out_ref[here, :] = jnp.concatenate([total[:HD] / row_sum, log_total], axis=0).T
        return 0

    lax.fori_loop(0, steps, one_block, 0)

    def pack(step, _):
        first = pl.multiple_of(step * rows, 64)
        half_rows = rows // 2
        context_ref[step // tensor_count, step % tensor_count] = jnp.concatenate(
            [
                out_ref[pl.ds(first, half_rows), 0:HD],
                out_ref[pl.ds(pl.multiple_of(first + half_rows, 32), half_rows), 0:HD],
            ],
            axis=1,
        ).astype(bf16)
        return 0

    lax.fori_loop(0, messages // 2, pack, 0)


def attention_forward(blocks, counts, lists, bounds, by_segment, mixed, tensor_count):
    messages, message_rows, _ = mixed.shape
    rows = message_rows * 2 // 3
    half = messages // 2 * rows
    smem = pl.BlockSpec(memory_space=pltpu.SMEM)
    vmem = pl.BlockSpec(memory_space=pltpu.VMEM)
    return pl.pallas_call(
        forward_kernel,
        in_specs=[smem] * 3 + [vmem] * 3,
        out_specs=[vmem, vmem],
        out_shape=[
            jax.ShapeDtypeStruct(
                (messages // 2 // tensor_count, tensor_count, rows // 2, 2 * HD), bf16
            ),
            jax.ShapeDtypeStruct((half, 128), f32),
        ],
        scratch_shapes=[
            pltpu.VMEM((PAIR_TOKENS, 128), bf16),
            pltpu.VMEM((VALUE_ROWS, PAIR_TOKENS), bf16),
            pltpu.VMEM((half, 128), bf16),
            pltpu.VMEM((4 * KEY_BLOCK, QUERY_BLOCK), f32),
            pltpu.VMEM((4 * KEY_BLOCK, QUERY_BLOCK), f32),
        ],
        compiler_params=pltpu.CompilerParams(vmem_limit_bytes=40 * 2**20),
        cost_estimate=pl.CostEstimate(
            flops=2 * 256 * 2 * 12_000_000, bytes_accessed=10_000_000, transcendentals=12_000_000
        ),
        name="attention_forward",
    )(blocks, counts, lists, bounds, by_segment, mixed)


def backward_kernel(
    block_of,
    count_of,
    list_of,
    bounds_ref,
    by_segment_ref,
    mixed_ref,
    grads_ref,
    out_ref,
    dq_ref,
    dkv_ref,
    keys,
    keys_t,
    values,
    queries_all,
    grads_all,
    queries_only,
    grads_only,
    dkv,
):
    messages, message_rows, _ = mixed_ref.shape
    rows = message_rows * 2 // 3
    tensor_count = grads_ref.shape[1]
    steps = queries_all.shape[0] // QUERY_BLOCK
    half = messages // (2 * tensor_count)

    def with_pieces(value, first_lane, wide):
        lane = lax.broadcasted_iota(jnp.int32, wide.shape, 1)
        for piece in range(3):
            part = value.astype(bf16).astype(f32)
            wide = jnp.where(lane == first_lane + piece, part, wide)
            value = value - part
        return wide

    def prepare(step, _):
        build_keys(bounds_ref, mixed_ref, keys, step)
        span = pl.ds(pl.multiple_of(step * 2 * rows, 128), 2 * rows)
        keys_t[:, span] = keys[span, :].T[HD:]
        packed = jnp.concatenate(
            [pair_rows(mixed_ref[2 * step + part, rows:, :]) for part in range(2)], axis=0
        )
        lane = lax.broadcasted_iota(jnp.int32, (2 * rows, HD), 1)
        ones = jnp.where(lane < 3, 1.0, 0.0).astype(bf16)
        values[span, :] = jnp.concatenate([ones, packed], axis=1)
        dkv[span, :] = jnp.zeros((2 * rows, 128), f32)
        return 0

    lax.fori_loop(0, messages // 2, prepare, 0)

    def prepare_queries(step, _):
        number = block_of[(step // tensor_count) * (steps // half)] * QUERY_BLOCK // rows
        number = number + step % tensor_count
        span = pl.ds(pl.multiple_of(step * rows, 64), rows)
        wide = query_lanes(bounds_ref, by_segment_ref, mixed_ref, number)
        out = out_ref[span, :]
        queries_all[span, :] = with_pieces(-out[:, HD : HD + 1], 2 * PAIR_SEGS + 4, wide).astype(bf16)
        lane = lax.broadcasted_iota(jnp.int32, (rows, 128), 1)
        queries = mixed_ref[number, 0:rows, :].astype(f32) * 0.125
        queries_only[span, :] = jnp.where(lane < HD, queries, 0.0).astype(bf16)
        grads = pair_rows(grads_ref[step // tensor_count, step % tensor_count].astype(f32))
        inner = jnp.sum(grads * out[:, :HD], axis=1, keepdims=True)
        wide = jnp.concatenate([jnp.zeros((rows, HD), f32), grads], axis=1)
        grads_only[span, :] = wide.astype(bf16)
        grads_all[span, :] = with_pieces(-inner, 0, wide).astype(bf16)
        return 0

    lax.fori_loop(0, messages // 2, prepare_queries, 0)

    def one_block(number, _):
        query_first = block_of[number] * QUERY_BLOCK
        here = pl.ds(pl.multiple_of(number * QUERY_BLOCK, QUERY_BLOCK), QUERY_BLOCK)
        queries = queries_all[here, :]
        grads = grads_all[here, :]
        both = jnp.concatenate([queries_only[here, :], grads_only[here, :]], axis=0)

        count = count_of[number]

        def attend(blocks, dq, masked):
            spans = [pl.ds(pl.multiple_of(block * KEY_BLOCK, KEY_BLOCK), KEY_BLOCK) for block in blocks]
            scores = [nt(keys[span, :], queries) for span in spans]
            if masked:
                scores = [causal_scores(scores[0], blocks[0] * KEY_BLOCK, query_first)]
            grads_of = [nt(values[span, :], grads) for span in spans]
            for span, score, grad in zip(spans, scores, grads_of):
                weights = jnp.exp(score)
                score_grad = (weights * grad).astype(bf16)
                dkv[span, :] += nn(
                    jnp.concatenate([score_grad, weights.astype(bf16)], axis=1), both
                )
                dq = dq + nn(keys_t[:, span], score_grad)
            return dq

        def listed(first, blocks):
            return lambda step, kept: attend(
                [list_of[number, first + blocks * step + part] for part in range(blocks)], kept, False
            )

        dq = attend([query_first // KEY_BLOCK], jnp.zeros((HD, QUERY_BLOCK), f32), True)
        eights, rest = count // 8, count % 8
        dq = lax.fori_loop(0, eights, listed(0, 8), dq)
        dq = lax.fori_loop(0, rest // 4, listed(8 * eights, 4), dq)
        dq = lax.fori_loop(0, rest % 4 // 2, listed(count - rest % 4, 2), dq)
        dq = lax.fori_loop(0, rest % 2, listed(count - 1, 1), dq)
        dq_ref[here, :] = (dq * 0.125).T.astype(bf16)
        return 0

    lax.fori_loop(0, steps, one_block, 0)

    def write(step, _):
        span = pl.ds(pl.multiple_of(step * KEY_BLOCK, KEY_BLOCK), KEY_BLOCK)
        dkv_ref[span, :] = dkv[span, :].astype(bf16)
        return 0

    lax.fori_loop(0, PAIR_TOKENS // KEY_BLOCK, write, 0)


def attention_backward(blocks, counts, lists, bounds, by_segment, mixed, grads, out):
    smem = pl.BlockSpec(memory_space=pltpu.SMEM)
    vmem = pl.BlockSpec(memory_space=pltpu.VMEM)
    half = out.shape[0]
    return pl.pallas_call(
        backward_kernel,
        in_specs=[smem] * 3 + [vmem] * 5,
        out_specs=[vmem, vmem],
        out_shape=[
            jax.ShapeDtypeStruct((half, HD), bf16),
            jax.ShapeDtypeStruct((PAIR_TOKENS, 128), bf16),
        ],
        scratch_shapes=[
            pltpu.VMEM((PAIR_TOKENS, 128), bf16),
            pltpu.VMEM((HD, PAIR_TOKENS), bf16),
            pltpu.VMEM((PAIR_TOKENS, 128), bf16),
            pltpu.VMEM((half, 128), bf16),
            pltpu.VMEM((half, 128), bf16),
            pltpu.VMEM((half, 128), bf16),
            pltpu.VMEM((half, 128), bf16),
            pltpu.VMEM((PAIR_TOKENS, 128), f32),
        ],
        compiler_params=pltpu.CompilerParams(vmem_limit_bytes=56 * 2**20),
        cost_estimate=pl.CostEstimate(
            flops=5 * 256 * 2 * 12_000_000, bytes_accessed=16_000_000, transcendentals=12_000_000
        ),
        name="attention_backward",
    )(blocks, counts, lists, bounds, by_segment, mixed, grads, out)


def flipped(chip, chips):
    return (chip + chips - 1) // chips


def greet_all(dp_count, tensor_count, dp_index, tensor_index):
    barrier = pltpu.get_barrier_semaphore()
    total = dp_count * tensor_count
    me = dp_index * tensor_count + tensor_index

    def greet(step, _):
        other = (me + step) % total
        pl.semaphore_signal(
            barrier,
            inc=1,
            device_id=(other // tensor_count, other % tensor_count),
            device_id_type=MESH,
        )
        return 0

    lax.fori_loop(1, total, greet, 0)
    pl.semaphore_wait(barrier, total - 1)


def repeat(count, body):
    def one(step, _):
        body(step)
        return 0

    lax.fori_loop(0, count, one, 0)


def swap_copy(source, target, sems, number, partner):
    return pltpu.make_async_remote_copy(
        src_ref=source,
        dst_ref=target,
        send_sem=sems.at[0, number],
        recv_sem=sems.at[1, number],
        device_id=partner,
        device_id_type=MESH,
    )


def layer_norm_back(values, gain, grads):
    average = jnp.mean(values, axis=-1, keepdims=True)
    centred = values - average
    scale = lax.rsqrt(jnp.mean(centred * centred, axis=-1, keepdims=True) + epsilon)
    normed = centred * scale
    scaled = grads * gain
    first = jnp.mean(scaled, axis=-1, keepdims=True)
    second = jnp.mean(scaled * normed, axis=-1, keepdims=True)
    return (scaled - first - normed * second) * scale, grads * normed


def column_sum(values):
    return jnp.sum(values, axis=0, keepdims=True)


def transpose_rows(source, target):
    size = min(256, target.shape[0])

    def one(step):
        span = pl.ds(pl.multiple_of(step * size, size), size)
        target[span, :] = source[:, span].T

    repeat(target.shape[0] // size, one)


def nearest(layer, layers, step):
    tile = 0 * layer
    for here in range(layers):
        order = sorted(range(layers), key=lambda there: (abs(there - here), there))
        for number, there in enumerate(order):
            tile = jnp.where((layer == here) & (step == number), there, tile)
    return tile


def doubling_gather(
    weight, recv_sem, send_sem, layer_recv, layer_send, chip, chips, core, layer, layers, dp_index
):
    stages = chips.bit_length() - 1
    steps = weight.shape[0]
    slot_of = (lambda step: step) if layer_recv is None else (lambda step: nearest(layer, layers, step))

    def layer_copy(tile, way):
        block = weight.at[tile, chip]
        return pltpu.make_async_remote_copy(
            src_ref=block,
            dst_ref=block,
            send_sem=layer_send.at[tile, way],
            recv_sem=layer_recv.at[tile],
            device_id=(dp_index, layer + 2 * way - 1),
            device_id_type=MESH,
        )

    def ways(tile, body):
        for way in range(2):
            inside = (layer + 1 < layers) & (tile <= layer) if way else (layer > 0) & (tile >= layer)

            @pl.when(inside)
            def _():
                body(layer_copy(tile, way))

    def spread():
        ways(layer, lambda copy: copy.start())

    rows = weight.shape[2] // 2

    def half(order):
        return pl.ds(pl.multiple_of(order * rows, rows), rows)

    def place(order, stage, step):
        size = jnp.where(order == 0, 2**stage, chips // 2 ** (stage + 1))
        bit = chip // size % 2
        across = size * (1 - 2 * bit)
        held = jnp.where(
            order == 0,
            chip // 2**stage * 2**stage + step,
            chip % (chips // 2**stage) + step * (chips // 2**stage),
        )
        return held, held + across, chip + across

    def copy(step, stage, order, number):
        slot = slot_of(step)
        held, _, partner = place(order, stage, number)
        block = weight.at[slot, held, half(order), :]
        return pltpu.make_async_remote_copy(
            src_ref=block,
            dst_ref=block,
            send_sem=send_sem.at[slot, 2**stage - 1 + number, order],
            recv_sem=recv_sem.at[slot, held, order],
            device_id=(2 * partner + core, layer),
            device_id_type=MESH,
        )

    def wait_block(block, sem):
        pltpu.make_async_remote_copy(
            src_ref=block,
            dst_ref=block,
            send_sem=send_sem.at[0, 0, 0],
            recv_sem=sem,
            device_id=(2 * chip + 1 - core, layer),
            device_id_type=MESH,
        ).wait_recv()

    def each(stage, body):
        repeat(2 * 2**stage, lambda number: body(number % 2, number // 2))

    def arrived(step, stage):
        slot = slot_of(step)

        def one(order, number):
            _, got, _ = place(order, stage, number)
            wait_block(weight.at[slot, got, half(order), :], recv_sem.at[slot, got, order])

        each(stage, one)

    def advance(number):
        for stage in range(stages):
            step = number - stage

            @pl.when((step >= 0) & (step < steps))
            def _():
                if stage > 0:
                    arrived(step, stage - 1)
                else:

                    if layer_recv is not None:

                        @pl.when(step > 0)
                        def _():
                            tile = slot_of(step)
                            wait_block(weight.at[tile, chip], layer_recv.at[tile])
                            ways(tile, lambda copy: copy.start())

                each(stage, lambda order, each_number: copy(step, stage, order, each_number).start())

    def ready(step):
        arrived(step, stages - 1)

    def sent():
        if layer_send is not None:
            repeat(steps, lambda tile: ways(tile, lambda copy: copy.wait_send()))

        def one(step):
            for stage in range(stages):
                each(
                    stage,
                    lambda order, number: copy(step, stage, order, number).wait_send(),
                )

        repeat(steps, one)

    return spread, advance, ready, sent


def picked(rows, lanes, owner_of, lane_of, keep):
    lane = lax.broadcasted_iota(jnp.int32, (128, lanes), 1)
    source = lax.broadcasted_iota(jnp.int32, (128, lanes), 0)
    spread = nn(rows.astype(bf16), jnp.where(source == lane_of(lane), 1.0, 0.0).astype(bf16))
    lane = lax.broadcasted_iota(jnp.int32, (rows.shape[0], lanes), 1)
    owner = lax.broadcasted_iota(jnp.int32, (rows.shape[0], lanes), 0)
    return column_sum(jnp.where((owner == owner_of(lane)) & keep(lane), spread, 0.0))


def project_kernel(
    dp_count,
    tensor_count,
    span,
    x_ref,
    small_ref,
    shard_ref,
    feed_ref,
    normed_ref,
    mixed_ref,
    weight_out_ref,
    vectors_ref,
    up_shift_ref,
    block_ref,
    normed,
    weight,
    smalls,
    outbox,
    swap_sem,
    small_send,
    small_recv,
    half_sem,
    gather_recv,
    gather_send,
    layer_recv,
    layer_send,
    out_sem,
    send_sem,
    recv_sem,
    local_sem,
    pass_send,
    pass_recv,
):
    dp_index, tensor_index = lax.axis_index("dp"), lax.axis_index("tensor")
    rows, width = x_ref.shape
    hidden = weight.shape[3]
    columns = hidden - 128
    piece = shard_ref.shape[1]
    core = dp_index % 2
    base = dp_index // span * span
    chip = dp_index % span // 2
    chips = span // 2
    layer_chip, layer_chips = dp_index // 2, dp_count // 2
    partner = (dp_index + 1 - 2 * core, tensor_index)
    total = dp_count * tensor_count
    me = dp_index * tensor_count + tensor_index

    def small_copy(step):
        other = (me + step) % total
        place = smalls.at[dp_index, tensor_index]
        return pltpu.make_async_remote_copy(
            src_ref=place,
            dst_ref=place,
            send_sem=small_send.at[other // tensor_count, other % tensor_count],
            recv_sem=small_recv.at[dp_index, tensor_index],
            device_id=(other // tensor_count, other % tensor_count),
            device_id_type=MESH,
        )

    def small_wait(step):
        other = (me + step) % total
        there = other // tensor_count, other % tensor_count
        place = smalls.at[there[0], there[1]]
        pltpu.make_async_remote_copy(
            src_ref=place,
            dst_ref=place,
            send_sem=small_send.at[there[0], there[1]],
            recv_sem=small_recv.at[there[0], there[1]],
            device_id=partner,
            device_id_type=MESH,
        ).wait_recv()

    own_rows = pl.ds(pl.multiple_of(core * piece, piece), piece)
    smalls[dp_index, tensor_index] = small_ref[...]
    weight[tensor_index, layer_chip, own_rows, :] = shard_ref[core]
    greet_all(dp_count, tensor_count, dp_index, tensor_index)
    half = pltpu.make_async_remote_copy(
        src_ref=shard_ref.at[1 - core],
        dst_ref=weight.at[tensor_index, layer_chip, own_rows, :],
        send_sem=half_sem.at[0],
        recv_sem=half_sem.at[1],
        device_id=partner,
        device_id_type=MESH,
    )
    half.start()
    block_ref[own_rows, :] = feed_ref[core]
    feed_half = pltpu.make_async_remote_copy(
        src_ref=feed_ref.at[1 - core],
        dst_ref=block_ref.at[own_rows, :],
        send_sem=half_sem.at[2],
        recv_sem=half_sem.at[3],
        device_id=partner,
        device_id_type=MESH,
    )
    feed_half.start()
    repeat(total - 1, lambda step: small_copy(step + 1).start())
    spread, advance, ready, gather_sent = doubling_gather(
        weight,
        gather_recv,
        gather_send,
        layer_recv,
        layer_send,
        layer_chip,
        layer_chips,
        core,
        tensor_index,
        tensor_count,
        dp_index,
    )
    half.wait_recv()
    spread()
    advance(0)
    repeat(total - 1, lambda step: small_wait(step + 1))

    def vector(number):
        here = smalls[:, tensor_index].astype(f32)[:, number, :]
        return picked(
            here, width, lambda lane: lane // piece, lambda lane: lane % piece, lambda lane: lane >= 0
        )

    normed[core] = normalize(x_ref[...].astype(f32), vector(0), vector(1)).astype(bf16)
    swap = pltpu.make_async_remote_copy(
        src_ref=normed.at[core],
        dst_ref=normed.at[core],
        send_sem=swap_sem.at[0],
        recv_sem=swap_sem.at[1],
        device_id=partner,
        device_id_type=MESH,
    )
    swap.start()
    stages = layer_chips.bit_length() - 1
    for number in range(1, stages):
        advance(number)
    vectors_ref[...] = jnp.zeros_like(vectors_ref)
    for number in (0, 2, 3, 4, 5):
        vectors_ref[number : number + 1, :] = vector(number)

    bias_width = 2 * HD // dp_count

    def qkv_shift(owner):
        here = smalls[:, owner].astype(f32)[:, 6, :]

        def column(lane):
            return lane % HD + jnp.where(lane % (3 * HD) < HD, 0, HD)

        return picked(
            here,
            columns,
            lambda lane: column(lane) // bias_width,
            lambda lane: (2 * core + lane // (3 * HD)) * bias_width + column(lane) % bias_width,
            lambda lane: (lane % (3 * HD) < HD) | (lane % (3 * HD) >= 2 * HD),
        )

    def up_shift(owner):
        here = smalls[:, owner].astype(f32)[:, 7, :]
        return picked(
            here,
            hidden,
            lambda lane: lane % 128 // bias_width,
            lambda lane: (core * (hidden // 128) + lane // 128) * bias_width
            + lane % 128 % bias_width,
            lambda lane: lane >= 0,
        )

    swap.wait_recv()

    def out_copy(owner):
        return pltpu.make_async_copy(weight.at[owner], weight_out_ref.at[owner], out_sem.at[owner])

    def slot(place_dp, place_tensor):
        return mixed_ref.at[place_dp * tensor_count + place_tensor]

    def send(owner, part, pair):
        head_chip = 2 * core + pair
        target = (base + 2 * head_chip + (part + flipped(chip, chips)) % 2, owner)
        here = (target[0] == dp_index) & (owner == tensor_index)
        return here, pltpu.make_async_remote_copy(
            src_ref=outbox.at[owner, part, pair],
            dst_ref=slot(2 * chip + part, tensor_index),
            send_sem=send_sem.at[owner, part, pair],
            recv_sem=recv_sem.at[chip, tensor_index],
            device_id=target,
            device_id_type=MESH,
        ), pltpu.make_async_copy(
            outbox.at[owner, part, pair], slot(2 * chip + part, tensor_index), local_sem.at[0]
        )

    def one_tile(step):
        owner = nearest(tensor_index, tensor_count, step)
        advance(step + stages)
        ready(step)
        out_copy(owner).start()
        shift = qkv_shift(owner)
        up_shift_ref[owner] = jnp.broadcast_to(up_shift(owner), up_shift_ref.shape[1:])

        def one_part(part):
            matrix = weight[owner, :, :, 0:columns].reshape(width, columns)
            result = nn(normed[part], matrix) + shift
            first = [result[:, 0:128], result[:, 192:320]]
            last = [result[:, 128:192], result[:, 320:384]]
            for pair in range(2):
                outbox[owner, part, pair, 0:rows, :] = first[pair].astype(bf16)
                outbox[owner, part, pair, rows:, :] = jnp.concatenate(
                    [last[pair][: rows // 2], last[pair][rows // 2 :]], axis=1
                ).astype(bf16)
                here, far, near = send(owner, part, pair)

                @pl.when(here)
                def _():
                    near.start()

                @pl.when(jnp.logical_not(here))
                def _():
                    far.start()

        repeat(2, one_part)

    repeat(tensor_count, one_tile)
    normed_ref[...] = normed[...]

    def arrival(step):
        from_chip, from_tensor = step % chips, (tensor_index + step // chips) % tensor_count
        mine = slot(2 * from_chip + (core + flipped(from_chip, chips)) % 2, from_tensor)
        theirs = slot(2 * from_chip + (core + flipped(from_chip, chips) + 1) % 2, from_tensor)
        here = (from_chip == chip) & (from_tensor == tensor_index) & (chip // 2 == core)

        def passing(place):
            return pltpu.make_async_remote_copy(
                src_ref=place,
                dst_ref=place,
                send_sem=pass_send.at[from_chip, from_tensor],
                recv_sem=pass_recv.at[from_chip, from_tensor],
                device_id=partner,
                device_id_type=MESH,
            )

        return mine, theirs, here, passing, from_chip, from_tensor

    def hand_on(step):
        mine, _theirs, here, passing, from_chip, from_tensor = arrival(step)

        @pl.when(here)
        def _():
            pltpu.make_async_copy(mine, mine, local_sem.at[0]).wait()

        @pl.when(jnp.logical_not(here))
        def _():
            pltpu.make_async_remote_copy(
                src_ref=mine,
                dst_ref=mine,
                send_sem=pass_send.at[from_chip, from_tensor],
                recv_sem=recv_sem.at[from_chip, from_tensor],
                device_id=partner,
                device_id_type=MESH,
            ).wait_recv()

        passing(mine).start()

    repeat(chips * tensor_count, hand_on)

    def finish(step):
        mine, theirs, _here, passing, _a, _b = arrival(step)
        passing(mine).wait_send()
        passing(theirs).wait_recv()

    repeat(chips * tensor_count, finish)

    def sent(step):
        here, far, _near = send(step // 4, step // 2 % 2, step % 2)

        @pl.when(jnp.logical_not(here))
        def _():
            far.wait_send()

    repeat(4 * tensor_count, sent)
    repeat(total - 1, lambda step: small_copy(step + 1).wait_send())
    repeat(tensor_count, lambda owner: out_copy(owner).wait())
    half.wait_send()
    feed_half.wait()
    swap.wait_send()
    gather_sent()


def project(inputs, small, shard, feed, dp_count, tensor_count, span):
    rows, width = inputs.shape
    _, piece, hidden = shard.shape
    messages = span * tensor_count
    chips, layer_chips = span // 2, dp_count // 2
    dma = pltpu.SemaphoreType.DMA
    vmem = pl.BlockSpec(memory_space=pltpu.VMEM)
    anywhere = pl.BlockSpec(memory_space=pl.ANY)
    weight = (tensor_count, layer_chips, 2 * piece, hidden)
    return pl.pallas_call(
        functools.partial(project_kernel, dp_count, tensor_count, span),
        in_specs=[vmem] * 4,
        out_specs=[vmem, anywhere, anywhere, vmem, vmem, vmem],
        out_shape=[
            jax.ShapeDtypeStruct((2, rows, width), bf16),
            jax.ShapeDtypeStruct((messages, rows * 3 // 2, 128), bf16),
            jax.ShapeDtypeStruct(weight, bf16),
            jax.ShapeDtypeStruct((8, width), f32),
            jax.ShapeDtypeStruct((tensor_count, 8, hidden), f32),
            jax.ShapeDtypeStruct((2 * piece, feed.shape[2]), bf16),
        ],
        scratch_shapes=[
            pltpu.VMEM((2, rows, width), bf16),
            pltpu.VMEM(weight, bf16),
            pltpu.VMEM((dp_count, tensor_count, 16, 128), bf16),
            pltpu.VMEM((tensor_count, 2, 2, rows * 3 // 2, 128), bf16),
            dma((2,)),
            dma((dp_count, tensor_count)),
            dma((dp_count, tensor_count)),
            dma((4,)),
            dma((tensor_count, layer_chips, 2)),
            dma((tensor_count, layer_chips - 1, 2)),
            dma((tensor_count,)),
            dma((tensor_count, 2)),
            dma((tensor_count,)),
            dma((tensor_count, 2, 2)),
            dma((chips, tensor_count)),
            dma((1,)),
            dma((chips, tensor_count)),
            dma((chips, tensor_count)),
        ],
        compiler_params=pltpu.CompilerParams(
            collective_id=0, has_side_effects=True, vmem_limit_bytes=40 * 2**20
        ),
        cost_estimate=pl.CostEstimate(
            flops=2 * 2 * rows * width * hidden * tensor_count,
            bytes_accessed=20_000_000,
            transcendentals=0,
        ),
        name="project",
    )(inputs, small, shard, feed)


def halving_scatter(parts, inbox, send_sem, recv_sem, chip, chips, core, layer):
    stages = chips.bit_length() - 1
    rows = parts.shape[2] // 2

    def places(order, stage, step):
        size = jnp.where(order == 0, 2**stage, chips // 2 ** (stage + 1))
        bit = chip // size % 2
        low, high = chip % size, chip // (2 * size) * (2 * size)
        rest = jnp.where(order == 0, low + step * 2 * size, high + step)
        theirs = rest + (1 - bit) * size
        return theirs, rest + bit * size, chip + (1 - 2 * bit) * size

    def half(order):
        return pl.ds(pl.multiple_of(order * rows, rows), rows)

    def copy(item, stage, order, step):
        theirs, _, partner = places(order, stage, step)
        where = chips - chips // 2**stage + step
        return pltpu.make_async_remote_copy(
            src_ref=parts.at[item, theirs, half(order), :],
            dst_ref=inbox.at[item, where, half(order), :],
            send_sem=send_sem.at[item, where, order],
            recv_sem=recv_sem.at[item, where, order],
            device_id=(2 * partner + core, layer),
            device_id_type=MESH,
        )

    def each(stage, body):
        count = chips // 2 ** (stage + 1)
        repeat(2 * count, lambda number: body(number % 2, number // 2))

    def start(item, stage):
        each(stage, lambda order, step: copy(item, stage, order, step).start())

    def finish(item, stage):
        def one(order, step):
            copy(item, stage, order, step).wait_recv()
            _, keep, _ = places(order, stage, step)
            where = chips - chips // 2**stage + step
            parts[item, keep, half(order), :] = (
                parts[item, keep, half(order), :].astype(f32)
                + inbox[item, where, half(order), :].astype(f32)
            ).astype(bf16)

        each(stage, one)

    def add(item, stage):
        def one(order, step):
            _, keep, _ = places(order, stage, step)
            where = chips - chips // 2**stage + step
            parts[item, keep, half(order), :] = (
                parts[item, keep, half(order), :].astype(f32)
                + inbox[item, where, half(order), :].astype(f32)
            ).astype(bf16)

        each(stage, one)

    def sent(item, stage):
        each(stage, lambda order, step: copy(item, stage, order, step).wait_send())

    return stages, start, finish, sent, add


def middle_kernel(
    dp_count,
    tensor_count,
    span,
    context_ref,
    x_ref,
    cot_ref,
    cot_across_ref,
    vectors_in_ref,
    up_shift_ref,
    feed_ref,
    weight_ref,
    block_ref,
    middle_grad_ref,
    feed_sum_ref,
    dense_send0_ref,
    dense_send1_ref,
    dense_keep_ref,
    vectors_ref,
    up_shift_grad_ref,
    grads_ref,
    context_in,
    context,
    dense,
    feed,
    middle,
    normed,
    cot,
    turned_normed,
    turned_cot,
    active,
    upper_grad,
    out_total,
    normed_total,
    swap_in,
    core_in,
    pair_in,
    low_grad,
    outbox,
    parts,
    inbox,
    dense_parts,
    weight_sem,
    swap_sem,
    share_send,
    share_recv,
    context_send,
    context_recv,
    outbox_send,
    outbox_recv,
    local_sem,
    gather_recv,
    gather_send,
    parts_send,
    parts_recv,
    dense_sem,
):
    dp_index, tensor_index = lax.axis_index("dp"), lax.axis_index("tensor")
    rows, width = x_ref.shape
    hidden = active.shape[2]
    steps = feed.shape[0]
    core = dp_index % 2
    base = dp_index // span * span
    chip = dp_index % span // 2
    chips = span // 2
    layer_chip, layer_chips = dp_index // 2, dp_count // 2
    pair_rows_count = parts.shape[2]
    piece = pair_rows_count // 2
    side = tensor_index % 2
    partner = (dp_index + 1 - 2 * core, tensor_index)
    across = (dp_index, tensor_index + 1 - 2 * side)
    own_part = 2 * side + core
    part_span = lambda part: pl.ds(pl.multiple_of(part * rows, 64), rows)
    mine, theirs = part_span(core), part_span(1 - core)

    def dense_copy(owner):
        return pltpu.make_async_copy(
            weight_ref.at[owner, :, pl.ds(weight_ref.shape[2] - 128, 128)],
            dense.at[:, pl.ds(pl.multiple_of(owner * 128, 128), 128)],
            weight_sem.at[owner],
        )

    repeat(tensor_count, lambda owner: dense_copy(owner).start())
    gain_ref, bias_ref, dense_shift_ref, down_shift_ref = (
        vectors_in_ref.at[number : number + 1] for number in range(2, 6)
    )
    across_part = own_part + 2 - 4 * side
    cot[part_span(own_part), :] = cot_ref[...]
    cot[part_span(across_part), :] = cot_across_ref[...]
    feed[:, layer_chip] = feed_ref[...]
    greet_all(dp_count, tensor_count, dp_index, tensor_index)
    _, gather, ready, gather_sent = doubling_gather(
        feed,
        gather_recv,
        gather_send,
        None,
        None,
        layer_chip,
        layer_chips,
        core,
        tensor_index,
        tensor_count,
        dp_index,
    )
    gather_steps = steps + layer_chips.bit_length() - 2

    def context_out(step):
        place, owner = step // tensor_count, step % tensor_count
        owner = (tensor_index + 1 + owner) % tensor_count
        part = (core + flipped(place, chips)) % 2
        target = (base + 2 * place + chip // 2, owner)
        here = (target[0] == dp_index) & (owner == tensor_index)
        source = context_ref.at[place, owner]
        destination = context_in.at[tensor_index, chip % 2, part]
        far = pltpu.make_async_remote_copy(
            src_ref=source,
            dst_ref=destination,
            send_sem=context_send.at[place, owner],
            recv_sem=context_recv.at[tensor_index, chip % 2, part],
            device_id=target,
            device_id_type=MESH,
        )
        near = pltpu.make_async_copy(source, destination, local_sem.at[0])
        return here, far, near

    def send_context(step):
        here, far, near = context_out(step)

        @pl.when(here)
        def _():
            near.start()

        @pl.when(jnp.logical_not(here))
        def _():
            far.start()

    repeat(chips * tensor_count, send_context)

    def share_copy(array, which, number):
        source = own_part if number < 2 else own_part + 2 - 4 * side
        block = array.at[part_span(source)]
        return pltpu.make_async_remote_copy(
            src_ref=block,
            dst_ref=block,
            send_sem=share_send.at[which, number],
            recv_sem=share_recv.at[which, number],
            device_id=across if number == 1 else partner,
            device_id_type=MESH,
        )

    def share_arrival(array, which, number):
        source = (
            own_part + 1 - 2 * core,
            own_part + 2 - 4 * side,
            own_part + 2 - 4 * side + 1 - 2 * core,
        )[number]
        block = array.at[part_span(source)]
        return pltpu.make_async_remote_copy(
            src_ref=block,
            dst_ref=block,
            send_sem=share_send.at[which, number],
            recv_sem=share_recv.at[which, number],
            device_id=partner,
            device_id_type=MESH,
        )

    gather(0)
    share_copy(cot, 0, 0).start()
    share_copy(cot, 0, 2).start()
    repeat(4, lambda part: out_total.__setitem__(part, jnp.zeros((rows, width), f32)))
    repeat(4, lambda part: normed_total.__setitem__(part, jnp.zeros((rows, width), f32)))

    def take_context(step):
        owner, part = (tensor_index + step // 2) % tensor_count, step % 2
        for pair in range(2):
            destination = context_in.at[owner, pair, part]
            here = (
                (owner == tensor_index)
                & (chip == 2 * core + pair)
                & ((part + flipped(chip, chips)) % 2 == core)
            )

            @pl.when(here)
            def _():
                pltpu.make_async_copy(destination, destination, local_sem.at[0]).wait()

            @pl.when(jnp.logical_not(here))
            def _():
                pltpu.make_async_remote_copy(
                    src_ref=destination,
                    dst_ref=destination,
                    send_sem=context_send.at[0, 0],
                    recv_sem=context_recv.at[owner, pair, part],
                    device_id=partner,
                    device_id_type=MESH,
                ).wait_recv()

        first, second = context_in[owner, 0, part], context_in[owner, 1, part]
        lanes = pl.ds(pl.multiple_of(owner * 128, 128), 128)
        half = rows // 2
        for number in range(2):
            cut = slice(number * HD, (number + 1) * HD)
            where = pl.ds(pl.multiple_of(part * rows + number * half, 32), half)
            context[where, lanes] = jnp.concatenate([first[:, cut], second[:, cut]], axis=1)

    for number in range(1, gather_steps):
        gather(number)
    repeat(2 * tensor_count, take_context)
    repeat(tensor_count, lambda owner: dense_copy(owner).wait())

    low_grad[theirs, :] = nt(context[theirs, :], dense[...]).astype(bf16)
    first_swap = swap_copy(low_grad.at[theirs], swap_in, swap_sem, 0, partner)
    first_swap.start()
    own = x_ref[...].astype(f32) + dense_shift_ref[...] + nt(context[mine, :], dense[...])
    first_swap.wait()
    middle[...] = own + swap_in[...].astype(f32)
    normed[part_span(own_part), :] = normalize(middle[...], gain_ref[...], bias_ref[...]).astype(bf16)
    share_copy(normed, 1, 1).start()
    share_copy(normed, 1, 0).start()
    share_arrival(cot, 0, 0).wait_recv()
    share_arrival(cot, 0, 2).wait_recv()
    transpose_rows(cot, turned_cot)
    share_arrival(normed, 1, 0).wait_recv()

    def one_part(index):
        step, turn = index % (2 * steps) // 2, index // (2 * steps) * 2 + index % 2
        owner = (tensor_index + step * (tensor_count // steps)) % tensor_count
        part = 2 * ((side + turn // 2) % 2) + (core + turn) % 2

        @pl.when(turn == 0)
        def _():
            ready(step)
            up_shift_grad_ref[step] = jnp.zeros((8, hidden), f32)

        @pl.when((step == 0) & (turn == 2))
        def _():
            share_arrival(normed, 1, 1).wait_recv()
            share_copy(normed, 1, 2).start()

        @pl.when((step == 0) & (turn == 3))
        def _():
            share_arrival(normed, 1, 2).wait_recv()

        here = part_span(part)
        up_matrix = feed[step, :, :, 0:hidden].reshape(width, hidden)
        down_matrix = feed[step, :, :, hidden:].reshape(width, hidden)
        upper = nn(normed[here, :], up_matrix) + up_shift_ref[owner, 0:1]
        active_grad = nn(cot[here, :], down_matrix)
        square = upper * upper
        bent = jnp.tanh(0.7978845608 * upper * (1.0 + 0.044715 * square))
        rising = 0.5 * (1.0 + bent)
        slope = rising + 0.5 * upper * (1.0 - bent * bent) * 0.7978845608 * (
            1.0 + 3.0 * 0.044715 * square
        )
        low = (active_grad * slope).astype(bf16)
        active_low = (upper * rising).astype(bf16)
        active[step, here, :] = active_low
        upper_grad[step, here, :] = low
        up_shift_grad_ref[step, 0:1] += column_sum(low.astype(f32))
        normed_total[part] += nt(low, up_matrix)
        out_total[part] += nt(active_low, down_matrix)

    repeat(4 * steps, one_part)

    def core_copy(which):
        return swap_copy(
            cot.at[pl.ds(2 * which * rows, 2 * rows)], core_in.at[which], swap_sem, 1 + which, partner
        )

    def pair_copy(which):
        source = normed.at[pl.ds(0, rows)] if which else swap_in
        return swap_copy(source, pair_in.at[which], swap_sem, 3 + which, across)

    totals = (normed_total, out_total)
    for number in (0, 2):
        share_copy(cot, 0, number).wait_send()
    for which in range(2):
        for number in range(2):
            cot[pl.ds((2 * which + number) * rows, rows), :] = totals[which][
                2 * number + 1 - core
            ].astype(bf16)
        core_copy(which).start()
    def add_cores(which):
        core_copy(which).wait_recv()
        value = (
            totals[which][2 * (1 - side) + core] + core_in[which, part_span(1 - side), :].astype(f32)
        ).astype(bf16)
        if which:
            normed[pl.ds(0, rows), :] = value
        else:
            swap_in[...] = value
        pair_copy(which).start()

    def whole(which):
        pair_copy(which).wait_recv()
        return (
            totals[which][own_part]
            + core_in[which, part_span(side), :].astype(f32)
            + pair_in[which].astype(f32)
        )

    add_cores(0)

    transpose_rows(normed, turned_normed)
    half_chips = layer_chips // 2

    def set_out(array, refs, item, place, sems):
        for order in range(2):
            bit = place % 2 if order == 0 else place // half_chips
            own_bit = layer_chip % 2 if order == 0 else layer_chip // half_chips
            slot = place // 2 if order == 0 else place % half_chips
            block = array.at[pl.ds(order * piece, piece), :]
            goes = pltpu.make_async_copy(block, refs[order].at[item, slot], sems.at[order])
            stays = pltpu.make_async_copy(block, refs[2].at[order, item, slot], sems.at[order])

            @pl.when(bit == own_bit)
            def _():
                stays.start()

            @pl.when(bit != own_bit)
            def _():
                goes.start()

    def set_out_wait(array, refs, sems):
        for order in range(2):
            block = array.at[pl.ds(order * piece, piece), :]
            pltpu.make_async_copy(block, refs[2].at[order, 0, 0], sems.at[order]).wait()

    stages, start, finish, sent, _ = halving_scatter(
        parts, inbox, parts_send, parts_recv, layer_chip, layer_chips, core, tensor_index
    )
    dense_refs = (dense_send0_ref, dense_send1_ref, dense_keep_ref)

    def one_chip(index):
        step, place = index // layer_chips, index % layer_chips
        here = pl.ds(pl.multiple_of(place * pair_rows_count, pair_rows_count), pair_rows_count)
        parts[step, place, :, 0:hidden] = nn(turned_normed[here, :], upper_grad[step]).astype(bf16)
        parts[step, place, :, hidden:] = nn(turned_cot[here, :], active[step]).astype(bf16)

        @pl.when(place == layer_chips - 1)
        def _():
            start(step, 0)

    repeat(steps * layer_chips, one_chip)
    grads = whole(0)
    for number in range(3):
        share_copy(normed, 1, number).wait_send()
    add_cores(1)
    vectors_ref[...] = jnp.zeros_like(vectors_ref)
    vectors_ref[2:3] = column_sum(grads)
    part_grad, gain_part = layer_norm_back(middle[...], gain_ref[...], grads)
    vectors_ref[1:2] = column_sum(gain_part)
    own_cot = cot_ref[...].astype(f32)
    vectors_ref[3:4] = column_sum(own_cot)
    middle_grad = own_cot + part_grad
    middle_grad_ref[...] = middle_grad
    vectors_ref[0:1] = column_sum(middle_grad)
    low_grad[mine, :] = middle_grad.astype(bf16)
    low_swap = swap_copy(low_grad.at[mine], low_grad.at[mine], swap_sem, 5, partner)
    low_swap.start()
    swap_copy(low_grad.at[theirs], low_grad.at[theirs], swap_sem, 5, partner).wait_recv()

    def grads_out(owner, part, pair):
        target = (base + 2 * (2 * core + pair) + (part + flipped(chip, chips)) % 2, owner)
        here = (target[0] == dp_index) & (owner == tensor_index)
        source = outbox.at[owner, part, pair]
        destination = grads_ref.at[chip, tensor_index]
        far = pltpu.make_async_remote_copy(
            src_ref=source,
            dst_ref=destination,
            send_sem=outbox_send.at[owner, part, pair],
            recv_sem=outbox_recv.at[chip, tensor_index],
            device_id=target,
            device_id_type=MESH,
        )
        return here, far, pltpu.make_async_copy(source, destination, local_sem.at[1])

    def send_grads(step):
        owner, part = (tensor_index + 1 + step // 2) % tensor_count, step % 2
        lanes = pl.ds(pl.multiple_of(owner * 128, 128), 128)
        result = nn(low_grad[part_span(part), :], dense[:, lanes]).astype(bf16)
        half = rows // 2
        for pair in range(2):
            cut = slice(pair * HD, (pair + 1) * HD)
            outbox[owner, part, pair] = jnp.concatenate(
                [result[:half, cut], result[half:, cut]], axis=1
            )
            here, far, near = grads_out(owner, part, pair)

            @pl.when(here)
            def _():
                near.start()

            @pl.when(jnp.logical_not(here))
            def _():
                far.start()

    repeat(2 * tensor_count, send_grads)

    def advance(stage):
        for step in range(steps):
            finish(step, stage)
            if stage + 1 < stages:
                start(step, stage + 1)

    advance(0)
    turned_low = turned_cot.at[:, 0 : 2 * rows]
    transpose_rows(low_grad, turned_low)

    def dense_chip(place):
        here = pl.ds(pl.multiple_of(place * pair_rows_count, pair_rows_count), pair_rows_count)
        dense_parts[place] = nn(turned_low[here, :], context[...]).astype(bf16)
        set_out(dense_parts.at[place], dense_refs, 0, place, dense_sem.at[place])

    repeat(layer_chips, dense_chip)
    block_ref[...] = (middle[...] + whole(1) + down_shift_ref[...]).astype(bf16)

    for stage in range(1, stages):
        advance(stage)
    for step in range(steps):
        feed_sum_ref[step] = parts[step, layer_chip]
    repeat(
        layer_chips,
        lambda place: set_out_wait(dense_parts.at[place], dense_refs, dense_sem.at[place]),
    )

    def arrived(step):
        place, owner = step // tensor_count, step % tensor_count
        destination = grads_ref.at[place, owner]
        here = (place == chip) & (owner == tensor_index) & (chip // 2 == core)

        @pl.when(here)
        def _():
            pltpu.make_async_copy(destination, destination, local_sem.at[1]).wait()

        @pl.when(jnp.logical_not(here))
        def _():
            pltpu.make_async_remote_copy(
                src_ref=destination,
                dst_ref=destination,
                send_sem=context_send.at[0, 0],
                recv_sem=outbox_recv.at[place, owner],
                device_id=partner,
                device_id_type=MESH,
            ).wait_recv()

    repeat(chips * tensor_count, arrived)

    def context_sent(step):
        here, far, _near = context_out(step)

        @pl.when(jnp.logical_not(here))
        def _():
            far.wait_send()

    repeat(chips * tensor_count, context_sent)

    def grads_sent(step):
        here, far, _near = grads_out(step // 4, step // 2 % 2, step % 2)

        @pl.when(jnp.logical_not(here))
        def _():
            far.wait_send()

    repeat(4 * tensor_count, grads_sent)

    for step in range(steps):
        for stage in range(stages):
            sent(step, stage)
    for which in range(2):
        core_copy(which).wait_send()
        pair_copy(which).wait_send()
    gather_sent()
    low_swap.wait_send()


def middle_part(
    context, inputs, cotangent, across, vectors, up_shift, feed, weight, dp_count, tensor_count, span
):
    rows, width = inputs.shape
    hidden = feed.shape[2] // 2
    piece = width // dp_count
    steps = tensor_count // 2
    chips, layer_chips = span // 2, dp_count // 2
    dma = pltpu.SemaphoreType.DMA
    vmem = pl.BlockSpec(memory_space=pltpu.VMEM)
    anywhere = pl.BlockSpec(memory_space=pl.ANY)
    dense_part = (piece, 128 * tensor_count)
    return pl.pallas_call(
        functools.partial(middle_kernel, dp_count, tensor_count, span),
        in_specs=[vmem] * 7 + [anywhere],
        out_specs=[vmem] * 3 + [anywhere] * 3 + [vmem] * 2 + [anywhere],
        out_shape=[
            jax.ShapeDtypeStruct((rows, width), bf16),
            jax.ShapeDtypeStruct((rows, width), f32),
            jax.ShapeDtypeStruct((steps, 2 * piece, 2 * hidden), bf16),
            jax.ShapeDtypeStruct((1, layer_chips // 2, *dense_part), bf16),
            jax.ShapeDtypeStruct((1, layer_chips // 2, *dense_part), bf16),
            jax.ShapeDtypeStruct((2, 1, layer_chips // 2, *dense_part), bf16),
            jax.ShapeDtypeStruct((8, width), f32),
            jax.ShapeDtypeStruct((steps, 8, hidden), f32),
            jax.ShapeDtypeStruct((chips, tensor_count, rows // 2, 128), bf16),
        ],
        scratch_shapes=[
            pltpu.VMEM((tensor_count, 2, 2, rows // 2, 128), bf16),
            pltpu.VMEM((2 * rows, 128 * tensor_count), bf16),
            pltpu.VMEM((width, 128 * tensor_count), bf16),
            pltpu.VMEM((steps, layer_chips, 2 * piece, 2 * hidden), bf16),
            pltpu.VMEM((rows, width), f32),
            pltpu.VMEM((4 * rows, width), bf16),
            pltpu.VMEM((4 * rows, width), bf16),
            pltpu.VMEM((width, 4 * rows), bf16),
            pltpu.VMEM((width, 4 * rows), bf16),
            pltpu.VMEM((steps, 4 * rows, hidden), bf16),
            pltpu.VMEM((steps, 4 * rows, hidden), bf16),
            pltpu.VMEM((4, rows, width), f32),
            pltpu.VMEM((4, rows, width), f32),
            pltpu.VMEM((rows, width), bf16),
            pltpu.VMEM((2, 2 * rows, width), bf16),
            pltpu.VMEM((2, rows, width), bf16),
            pltpu.VMEM((2 * rows, width), bf16),
            pltpu.VMEM((tensor_count, 2, 2, rows // 2, 128), bf16),
            pltpu.VMEM((steps, layer_chips, 2 * piece, 2 * hidden), bf16),
            pltpu.VMEM((steps, layer_chips - 1, 2 * piece, 2 * hidden), bf16),
            pltpu.VMEM((layer_chips, 2 * piece, 128 * tensor_count), bf16),
            dma((tensor_count,)),
            dma((2, 8)),
            dma((2, 3)),
            dma((2, 3)),
            dma((chips, tensor_count)),
            dma((tensor_count, 2, 2)),
            dma((tensor_count, 2, 2)),
            dma((chips, tensor_count)),
            dma((2,)),
            dma((steps, layer_chips, 2)),
            dma((steps, layer_chips - 1, 2)),
            dma((steps, layer_chips - 1, 2)),
            dma((steps, layer_chips - 1, 2)),
            dma((layer_chips, 2)),
        ],
        compiler_params=pltpu.CompilerParams(
            collective_id=1, has_side_effects=True, vmem_limit_bytes=62 * 2**20
        ),
        cost_estimate=pl.CostEstimate(
            flops=6 * 2 * 2 * rows * width * hidden * tensor_count,
            bytes_accessed=40_000_000,
            transcendentals=0,
        ),
        name="middle_part",
    )(context, inputs, cotangent, across, vectors, up_shift, feed, weight)


def finish_kernel(
    dp_count,
    tensor_count,
    span,
    dq_ref,
    dkv_ref,
    normed_ref,
    x_ref,
    vectors_in_ref,
    middle_grad_ref,
    vector_grads_ref,
    up_rows_ref,
    feed_sum_ref,
    feed_got_ref,
    dense_keep_ref,
    dense_got0_ref,
    dense_got1_ref,
    weight_ref,
    input_grad_ref,
    weight_grad_ref,
    feed_grad_ref,
    dense_grad_ref,
    sums_ref,
    weight,
    turned_normed,
    dkv_in,
    outbox,
    mixed_in,
    gathered,
    normed_total,
    swap_out,
    swap_in,
    parts,
    inbox,
    layer_inbox,
    dense_parts,
    dense_inbox,
    dense_layer_inbox,
    last_out,
    last_in,
    last_feed_out,
    last_feed_in,
    last_dense_out,
    last_dense_in,
    late,
    column_sums,
    sums_out,
    sums_in,
    weight_sem,
    dense_load_sem,
    swap_sem,
    dkv_send,
    dkv_recv,
    outbox_send,
    mixed_recv,
    parts_send,
    parts_recv,
    layer_send,
    layer_recv,
    dense_send,
    dense_recv,
    dense_layer_send,
    dense_layer_recv,
    sums_send,
    sums_recv,
    local_sem,
):
    dp_index, tensor_index = lax.axis_index("dp"), lax.axis_index("tensor")
    rows, width = x_ref.shape
    columns = weight.shape[2]
    hidden = up_rows_ref.shape[1]
    core = dp_index % 2
    base = dp_index // span * span
    chip = dp_index % span // 2
    chips = span // 2
    layer_chip, layer_chips = dp_index // 2, dp_count // 2
    pair_rows_count = parts.shape[2]
    piece = pair_rows_count // 2
    partner = (dp_index + 1 - 2 * core, tensor_index)
    part_span = lambda part: pl.ds(pl.multiple_of(part * rows, 64), rows)
    dp_rows = rows * tensor_count
    devices = dp_count * tensor_count
    me = dp_index * tensor_count + tensor_index

    def weight_copy(owner):
        return pltpu.make_async_copy(
            weight_ref.at[owner, :, pl.ds(0, columns)], weight.at[owner], weight_sem.at[owner]
        )

    def loads(parts, inbox, keep_ref, got_refs, sems, item, slot):
        copies = []
        for order in range(2):
            rows_here = pl.ds(order * piece, piece)
            if order == 0:
                place = 2 * slot + layer_chip % 2
            else:
                place = slot + layer_chip // (layer_chips // 2) * (layer_chips // 2)
            copies += [
                pltpu.make_async_copy(
                    keep_ref.at[order, item, slot],
                    parts.at[item, place, rows_here, :],
                    sems.at[item, slot, order],
                ),
                pltpu.make_async_copy(
                    got_refs[order].at[item, slot],
                    inbox.at[item, slot, rows_here, :],
                    sems.at[item, slot, 2 + order],
                ),
            ]
        return copies

    def dense_loads(index):
        return loads(
            dense_parts,
            dense_inbox,
            dense_keep_ref,
            (dense_got0_ref, dense_got1_ref),
            dense_load_sem,
            0,
            index,
        )

    repeat(layer_chips // 2, lambda index: [copy.start() for copy in dense_loads(index)])
    repeat(tensor_count, lambda owner: weight_copy(owner).start())
    greet_all(dp_count, tensor_count, dp_index, tensor_index)

    def dkv_copy(place, whose):
        taken = 2 * place + (whose + flipped(place, chips)) % 2
        return pltpu.make_async_remote_copy(
            src_ref=dkv_ref.at[pl.ds(pl.multiple_of(taken * dp_rows, 128), dp_rows)],
            dst_ref=dkv_in.at[place],
            send_sem=dkv_send.at[place],
            recv_sem=dkv_recv.at[place],
            device_id=partner,
            device_id_type=MESH,
        )

    repeat(chips, lambda place: dkv_copy(place, 1 - core).start())
    place_here = (layer_chip, layer_chips, core, tensor_index)
    stages = layer_chips.bit_length() - 1
    _, dense_start, dense_finish, dense_sent, dense_add = halving_scatter(
        dense_parts, dense_inbox, dense_send, dense_recv, *place_here
    )
    repeat(2, lambda part: normed_total.__setitem__(part, jnp.zeros((rows, width), f32)))
    repeat(chips, lambda place: dkv_copy(place, 1 - core).wait_recv())

    def message(place, owner):
        part = (core + flipped(place, chips)) % 2
        target = (base + 2 * place + chip // 2, owner)
        here = (target[0] == dp_index) & (owner == tensor_index)
        source = outbox.at[place, owner]
        destination = mixed_in.at[tensor_index, chip % 2, part]
        far = pltpu.make_async_remote_copy(
            src_ref=source,
            dst_ref=destination,
            send_sem=outbox_send.at[place, owner],
            recv_sem=mixed_recv.at[tensor_index, chip % 2, part],
            device_id=target,
            device_id_type=MESH,
        )
        return here, far, pltpu.make_async_copy(source, destination, local_sem.at[0])

    def send_message(step):
        owner, place = (tensor_index + 1 + step // chips) % tensor_count, step % chips
        taken = 2 * place + (core + flipped(place, chips)) % 2
        own = pl.ds(pl.multiple_of(taken * dp_rows + owner * rows, 64), rows)
        total = dkv_ref[own, :].astype(f32) + dkv_in[
            place, pl.ds(pl.multiple_of(owner * rows, 64), rows), :
        ].astype(f32)
        queries = dq_ref[
            pl.ds(pl.multiple_of(place * dp_rows + owner * rows, 64), rows), :
        ].astype(f32)
        outbox[place, owner, 0:rows, :] = jnp.concatenate([queries, total[:, :HD]], axis=1).astype(
            bf16
        )
        half = rows // 2
        outbox[place, owner, rows:, :] = jnp.concatenate(
            [total[:half, HD:], total[half:, HD:]], axis=1
        ).astype(bf16)
        here, far, near = message(place, owner)

        @pl.when(here)
        def _():
            near.start()

        @pl.when(jnp.logical_not(here))
        def _():
            far.start()

    repeat(chips * tensor_count, send_message)

    def dense_layer_copy(step):
        owner = (tensor_index + step) % tensor_count
        return pltpu.make_async_remote_copy(
            src_ref=dense_parts.at[
                0, layer_chip, :, pl.ds(pl.multiple_of(owner * 128, 128), 128)
            ],
            dst_ref=dense_layer_inbox.at[step - 1],
            send_sem=dense_layer_send.at[step - 1],
            recv_sem=dense_layer_recv.at[step - 1],
            device_id=(dp_index, owner),
            device_id_type=MESH,
        )

    repeat(layer_chips // 2, lambda index: [copy.wait() for copy in dense_loads(index)])
    dense_add(0, 0)
    if stages > 1:
        dense_start(0, 1)
    transpose_rows(normed_ref, turned_normed)

    def sum_copy(which, step):
        other = (me + step) % devices
        there = (other // tensor_count, other % tensor_count)
        return pltpu.make_async_remote_copy(
            src_ref=sums_out.at[which, there[0], there[1]],
            dst_ref=sums_in.at[which, dp_index, tensor_index],
            send_sem=sums_send.at[which, there[0], there[1]],
            recv_sem=sums_recv.at[which, dp_index, tensor_index],
            device_id=there,
            device_id_type=MESH,
        )

    def sum_message(which, owner_dp, owner, vector_rows, row, count, vectors):
        block = pl.ds(pl.multiple_of(owner_dp * piece // 128 * 128, 128), 128)
        sums_out[which, owner_dp, owner] = jnp.zeros((8, 128), f32)
        sums_out[which, owner_dp, owner, 0:vector_rows, :] = vectors[0:vector_rows, block]
        for number in range(count):
            sums_out[which, owner_dp, owner, vector_rows + number : vector_rows + number + 1, :] = row[
                :, number * 128 : (number + 1) * 128
            ]

    def send_sums(which, vector_rows, row_of, count, vectors):
        def one(step):
            other = (me + step) % devices
            owner_dp, owner = other // tensor_count, other % tensor_count
            sum_message(which, owner_dp, owner, vector_rows, row_of(owner), count, vectors)

            @pl.when(step > 0)
            def _():
                sum_copy(which, step).start()

        repeat(devices, one)
        sums_in[which, dp_index, tensor_index] = sums_out[which, dp_index, tensor_index]

    send_sums(
        0, 4, lambda owner: up_rows_ref[pl.ds(2 * owner + core, 1), :], hidden // 128, vector_grads_ref
    )

    def layer_copy(step):
        return pltpu.make_async_remote_copy(
            src_ref=parts.at[step, layer_chip],
            dst_ref=layer_inbox.at[step - 1],
            send_sem=layer_send.at[step - 1],
            recv_sem=layer_recv.at[step - 1],
            device_id=(dp_index, (tensor_index + step) % tensor_count),
            device_id_type=MESH,
        )

    def chip_copy(step, hop):
        target = (layer_chip + hop) % layer_chips
        return pltpu.make_async_remote_copy(
            src_ref=parts.at[step, target],
            dst_ref=inbox.at[step, hop - 1],
            send_sem=parts_send.at[step, hop - 1],
            recv_sem=parts_recv.at[step, hop - 1],
            device_id=(2 * target + core, tensor_index),
            device_id_type=MESH,
        )

    def hops(body):
        repeat(layer_chips - 1, lambda number: body(number + 1))

    def advance(step):
        tile = step - 1

        @pl.when(tile >= 0)
        def _():
            hops(lambda hop: chip_copy(tile, hop).wait_recv())
            value = parts[tile, layer_chip].astype(f32)
            for number in range(layer_chips - 1):
                value = value + inbox[tile, number].astype(f32)
            parts[tile, layer_chip] = value.astype(bf16)

            @pl.when(tile > 0)
            def _():
                layer_copy(tile).start()

    def dense_advance(stage):
        dense_finish(0, stage)
        if stage + 1 < stages:
            dense_start(0, stage + 1)
        else:
            for step in range(1, tensor_count):
                dense_layer_copy(step).start()

    def one_owner(step):
        owner = (tensor_index + step) % tensor_count
        weight_copy(owner).wait()
        column_sums[owner] = jnp.zeros(column_sums.shape[1:], f32)

        def one_part(part):
            for pair in range(2):
                destination = mixed_in.at[owner, pair, part]
                here = (
                    (owner == tensor_index)
                    & (chip == 2 * core + pair)
                    & ((part + flipped(chip, chips)) % 2 == core)
                )

                @pl.when(here)
                def _():
                    pltpu.make_async_copy(destination, destination, local_sem.at[0]).wait()

                @pl.when(jnp.logical_not(here))
                def _():
                    pltpu.make_async_remote_copy(
                        src_ref=destination,
                        dst_ref=destination,
                        send_sem=outbox_send.at[0, 0],
                        recv_sem=mixed_recv.at[owner, pair, part],
                        device_id=partner,
                        device_id_type=MESH,
                    ).wait_recv()

            pieces_here = []
            for pair in range(2):
                value = mixed_in[owner, pair, part]
                pieces_here += [value[:rows], pair_rows(value[rows:])]
            grads = jnp.concatenate(pieces_here, axis=1)
            gathered[part_span(part), :] = grads
            column_sums[owner, 0:1] += column_sum(grads.astype(f32))
            normed_total[part] += nt(grads, weight[owner])

        repeat(2, one_part)

        def one_chip(place):
            here = pl.ds(pl.multiple_of(place * pair_rows_count, pair_rows_count), pair_rows_count)
            parts[step, place] = nn(turned_normed[here, :], gathered[...]).astype(bf16)

        repeat(layer_chips, one_chip)
        hops(lambda hop: chip_copy(step, hop).start())
        advance(step)
        for stage in range(1, stages):

            @pl.when(step == min(stage, tensor_count - 1))
            def _():
                dense_advance(stage)

    repeat(tensor_count, one_owner)

    swap_out[...] = normed_total[1 - core].astype(bf16)
    swap = swap_copy(swap_out, swap_in, swap_sem, 0, partner)
    swap.start()
    advance(tensor_count)
    swap.wait_recv()
    grads = normed_total[core] + swap_in[...].astype(f32)
    part_grad, gain_part = layer_norm_back(x_ref[...].astype(f32), vectors_in_ref[0:1, :], grads)
    input_grad_ref[...] = middle_grad_ref[...] + part_grad
    late[...] = jnp.zeros_like(late)
    late[0:1] = column_sum(gain_part)
    late[1:2] = column_sum(grads)
    send_sums(1, 2, lambda owner: column_sums[owner, 0:1, :], columns // 128, late)

    kept = pl.ds(pl.multiple_of(core * piece, piece), piece)
    given = pl.ds(pl.multiple_of((1 - core) * piece, piece), piece)

    def total(array, arrived, where):
        value = array[0, layer_chip, where, :].astype(f32)
        for step in range(arrived.shape[0]):
            value = value + arrived[step, where, :].astype(f32)
        return value

    def dense_total(where):
        lanes = pl.ds(pl.multiple_of(tensor_index * 128, 128), 128)
        value = dense_parts[0, layer_chip, where, lanes].astype(f32)
        for step in range(1, tensor_count):
            value = value + dense_layer_inbox[step - 1, where, :].astype(f32)
        return value

    def feed_total(where):
        value = feed_sum_ref[0, where, :].astype(f32)
        for number in range(feed_got_ref.shape[0]):
            value = value + feed_got_ref[number, where, :].astype(f32)
        return value

    last_feed_out[...] = feed_total(given)
    last_feed = swap_copy(last_feed_out, last_feed_in, swap_sem, 2, partner)
    last_feed.start()
    own_total = feed_total(kept)
    for kind in range(2):
        feed_grad_ref[kind, :, pl.ds(pl.multiple_of(core * hidden, 128), hidden)] = own_total[
            :, kind * hidden : (kind + 1) * hidden
        ]
    for step in range(1, tensor_count):
        dense_layer_copy(step).wait_recv()
    last_dense_out[...] = dense_total(given)
    last_dense = swap_copy(last_dense_out, last_dense_in, swap_sem, 3, partner)
    last_dense.start()
    dense_grad_ref[:, pl.ds(pl.multiple_of(core * 128, 128), 128)] = dense_total(kept)

    for step in range(1, tensor_count):
        layer_copy(step).wait_recv()
    last_out[...] = total(parts, layer_inbox, given)
    last = swap_copy(last_out, last_in, swap_sem, 1, partner)
    last.start()
    weight_grad_ref[:, pl.ds(pl.multiple_of(core * columns, 128), columns)] = total(
        parts, layer_inbox, kept
    )
    last_feed.wait()
    for kind in range(2):
        feed_grad_ref[kind, :, pl.ds(pl.multiple_of((1 - core) * hidden, 128), hidden)] = last_feed_in[
            :, kind * hidden : (kind + 1) * hidden
        ]
    last_dense.wait()
    dense_grad_ref[:, pl.ds(pl.multiple_of((1 - core) * 128, 128), 128)] = last_dense_in[...]
    last.wait()
    weight_grad_ref[:, pl.ds(pl.multiple_of((1 - core) * columns, 128), columns)] = last_in[...]

    for which in range(2):

        def sum_wait(step):
            other = (me + step + 1) % devices
            there = (other // tensor_count, other % tensor_count)
            place = sums_in.at[which, there[0], there[1]]
            pltpu.make_async_remote_copy(
                src_ref=place,
                dst_ref=place,
                send_sem=sums_send.at[which, there[0], there[1]],
                recv_sem=sums_recv.at[which, there[0], there[1]],
                device_id=partner,
                device_id_type=MESH,
            ).wait_recv()

        repeat(devices - 1, sum_wait)
        sums_ref[which] = jnp.zeros(sums_ref.shape[1:], f32)

        def add_one(step):
            owner_dp, owner = step // tensor_count, step % tensor_count
            sums_ref[which, owner_dp % 2] += sums_in[which, owner_dp, owner]

        repeat(devices, add_one)

    repeat(chips, lambda place: dkv_copy(place, 1 - core).wait_send())

    def message_sent(step):
        here, far, _near = message(step // tensor_count, step % tensor_count)

        @pl.when(jnp.logical_not(here))
        def _():
            far.wait_send()

    repeat(chips * tensor_count, message_sent)
    for stage in range(stages):
        if stage > 0:
            dense_sent(0, stage)
    repeat(tensor_count, lambda step: hops(lambda hop: chip_copy(step, hop).wait_send()))
    for step in range(1, tensor_count):
        layer_copy(step).wait_send()
        dense_layer_copy(step).wait_send()
    for which in range(2):
        repeat(devices - 1, lambda step: sum_copy(which, step + 1).wait_send())
    swap.wait_send()


def finish_part(
    dq,
    dkv,
    normed,
    inputs,
    vectors,
    middle_grad,
    vector_grads,
    up_rows,
    feed_sum,
    feed_got,
    dense_keep,
    dense_got,
    weight,
    dp_count,
    tensor_count,
    span,
):
    rows, width = inputs.shape
    columns = weight.shape[2] - 128
    hidden = up_rows.shape[1]
    piece = width // dp_count
    chips, layer_chips = span // 2, dp_count // 2
    dma = pltpu.SemaphoreType.DMA
    vmem = pl.BlockSpec(memory_space=pltpu.VMEM)
    anywhere = pl.BlockSpec(memory_space=pl.ANY)
    message = (rows * 3 // 2, 128)
    part = (2 * piece, columns)
    dense_part = (2 * piece, dense_keep.shape[4])
    halving = (layer_chips - 1, 2)
    return pl.pallas_call(
        functools.partial(finish_kernel, dp_count, tensor_count, span),
        in_specs=[vmem] * 10 + [anywhere] * 4,
        out_specs=[vmem] * 5,
        out_shape=[
            jax.ShapeDtypeStruct((rows, width), f32),
            jax.ShapeDtypeStruct((piece, 2 * columns), f32),
            jax.ShapeDtypeStruct((2, piece, 2 * hidden), f32),
            jax.ShapeDtypeStruct((piece, 2 * 128), f32),
            jax.ShapeDtypeStruct((2, 2, 8, 128), f32),
        ],
        scratch_shapes=[
            pltpu.VMEM((tensor_count, width, columns), bf16),
            pltpu.VMEM((width, 2 * rows), bf16),
            pltpu.VMEM((chips, rows * tensor_count, 128), bf16),
            pltpu.VMEM((chips, tensor_count, *message), bf16),
            pltpu.VMEM((tensor_count, 2, 2, *message), bf16),
            pltpu.VMEM((2 * rows, columns), bf16),
            pltpu.VMEM((2, rows, width), f32),
            pltpu.VMEM((rows, width), bf16),
            pltpu.VMEM((rows, width), bf16),
            pltpu.VMEM((tensor_count, layer_chips, *part), bf16),
            pltpu.VMEM((tensor_count, layer_chips - 1, *part), bf16),
            pltpu.VMEM((tensor_count - 1, *part), bf16),
            pltpu.VMEM((1, layer_chips, *dense_part), bf16),
            pltpu.VMEM((1, layer_chips - 1, *dense_part), bf16),
            pltpu.VMEM((tensor_count - 1, 2 * piece, 128), bf16),
            pltpu.VMEM((piece, columns), f32),
            pltpu.VMEM((piece, columns), f32),
            pltpu.VMEM((piece, 2 * hidden), f32),
            pltpu.VMEM((piece, 2 * hidden), f32),
            pltpu.VMEM((piece, 128), f32),
            pltpu.VMEM((piece, 128), f32),
            pltpu.VMEM((8, width), f32),
            pltpu.VMEM((tensor_count, 8, columns), f32),
            pltpu.VMEM((2, dp_count, tensor_count, 8, 128), f32),
            pltpu.VMEM((2, dp_count, tensor_count, 8, 128), f32),
            dma((tensor_count,)),
            dma((1, layer_chips // 2, 4)),
            dma((2, 4)),
            dma((chips,)),
            dma((chips,)),
            dma((chips, tensor_count)),
            dma((tensor_count, 2, 2)),
            dma((tensor_count, layer_chips - 1)),
            dma((tensor_count, layer_chips - 1)),
            dma((tensor_count - 1,)),
            dma((tensor_count - 1,)),
            dma((1, *halving)),
            dma((1, *halving)),
            dma((tensor_count - 1,)),
            dma((tensor_count - 1,)),
            dma((2, dp_count, tensor_count)),
            dma((2, dp_count, tensor_count)),
            dma((1,)),
        ],
        compiler_params=pltpu.CompilerParams(
            collective_id=2, has_side_effects=True, vmem_limit_bytes=60 * 2**20
        ),
        cost_estimate=pl.CostEstimate(
            flops=2 * 2 * 2 * rows * width * columns * tensor_count,
            bytes_accessed=30_000_000,
            transcendentals=0,
        ),
        name="finish_part",
    )(
        dq,
        dkv,
        normed,
        inputs,
        vectors,
        middle_grad,
        vector_grads,
        up_rows,
        feed_sum,
        feed_got,
        dense_keep,
        *dense_got,
        weight,
    )


def per_device(
    block_in,
    norm1_gain,
    norm1_bias,
    qkv_weight,
    qv_bias,
    dense_weight,
    dense_bias,
    norm2_gain,
    norm2_bias,
    up_weight,
    up_bias,
    down_weight,
    down_bias,
    cotangent,
    seg_parent,
    seg_length,
):
    dp_count, tensor_count = lax.axis_size("dp"), lax.axis_size("tensor")
    dp_index, tensor_index = lax.axis_index("dp"), lax.axis_index("tensor")
    rows, width = block_in.shape
    dp_rows = rows * tensor_count
    span = PAIR_TOKENS // dp_rows
    heads_here = HEADS // tensor_count
    local_index = lax.rem(dp_index, span)
    core = lax.rem(dp_index, 2)

    piece = norm1_gain.shape[0]

    def small_row(value):
        return jnp.pad(value.reshape(1, -1), ((0, 0), (0, 128 - value.size)))

    small = [norm1_gain, norm1_bias, norm2_gain, norm2_bias, dense_bias, down_bias, qv_bias, up_bias]
    small = jnp.pad(jnp.concatenate([small_row(value) for value in small]), ((0, 8), (0, 0)))

    def by_core(value):
        return value.reshape(value.shape[0], 2, -1).transpose(1, 0, 2)

    shard = jnp.concatenate([by_core(qkv_weight), by_core(dense_weight.T)], axis=2)
    feed_shard = jnp.concatenate([by_core(up_weight), by_core(down_weight.T)], axis=2)
    head = tensor_index * heads_here + local_index // 2
    slope = jnp.exp2(-8.0 * (head.astype(f32) + 1.0) / HEADS) / TRUNK
    bounds, by_segment, block_list, block_count = pair_tables(
        seg_parent, seg_length, dp_index // span, slope
    )
    half = span // 2
    taken = jnp.stack([2 * i + (core + flipped(i, half)) % 2 for i in range(half)])
    block_ids = (
        taken[:, None] * (dp_rows // QUERY_BLOCK)
        + jnp.arange(dp_rows // QUERY_BLOCK, dtype=jnp.int32)[None, :]
    ).reshape(-1)

    across = [(layer, layer + 1 - 2 * (layer % 2)) for layer in range(tensor_count)]
    normed_both, mixed, weight, vectors, up_shift, feed_block = project(
        block_in, small, shard, feed_shard, dp_count, tensor_count, span
    )
    weight = weight.reshape(tensor_count, width, -1)
    feed_block, cotangent = lax.optimization_barrier((feed_block, cotangent))
    cot_across = lax.ppermute(cotangent, "tensor", across)
    feed_far = [
        lax.ppermute(
            feed_block, "tensor", [(layer, (layer + hop) % tensor_count) for layer in range(tensor_count)]
        )
        for hop in range(tensor_count - 2, 0, -2)
    ]
    feed = jnp.stack([feed_block] + feed_far)
    my_counts, my_lists = jnp.take(block_count, block_ids), jnp.take(block_list, block_ids, axis=0)
    tables = (block_ids, my_counts, my_lists, bounds, by_segment)
    packed_context, out_float = attention_forward(*tables, mixed, tensor_count)
    (
        block_out,
        middle_grad,
        feed_sum,
        dense_send0,
        dense_send1,
        dense_keep,
        vector_grads,
        up_shift_part,
        packed_grads,
    ) = middle_part(
        packed_context,
        block_in,
        cotangent,
        cot_across,
        vectors,
        up_shift,
        feed,
        weight,
        dp_count,
        tensor_count,
        span,
    )
    low_bit = [(device, device + 2 - 4 * (device // 2 % 2)) for device in range(dp_count)]
    half_dp = dp_count // 2
    high_bit = [(device, (device + half_dp) % dp_count) for device in range(dp_count)]
    feed_got = jnp.stack(
        [
            lax.ppermute(
                feed_sum[step],
                "tensor",
                [(layer, (layer + 2 * step) % tensor_count) for layer in range(tensor_count)],
            )
            for step in range(1, feed_sum.shape[0])
        ]
    )
    dense_got = (lax.ppermute(dense_send0, "dp", low_bit), lax.ppermute(dense_send1, "dp", high_bit))
    dq, dkv = attention_backward(*tables, mixed, packed_grads, out_float)
    hidden = up_shift_part.shape[2]
    up_part = jnp.zeros((tensor_count, 2, hidden), f32)
    for step in range(up_shift_part.shape[0]):
        owner = lax.rem(tensor_index + step * (tensor_count // up_shift_part.shape[0]), tensor_count)
        up_part = lax.dynamic_update_slice(up_part, up_shift_part[step, :1][None], (owner, core, 0))
    up_rows = up_part.reshape(2 * tensor_count, hidden)
    input_grad, qkv_weight_grad, feed_grad, dense_grad, sums = finish_part(
        dq,
        dkv,
        normed_both.reshape(2 * rows, width),
        block_in,
        vectors,
        middle_grad,
        vector_grads,
        up_rows,
        feed_sum,
        feed_got,
        dense_keep,
        dense_got,
        weight,
        dp_count,
        tensor_count,
        span,
    )
    offset = lax.rem(dp_index * piece, 128)

    def own_vector(which, number):
        value = sums[which, 0, number] + sums[which, 1, number]
        return lax.dynamic_slice_in_dim(value, offset, piece, 0)

    def own_matrix(whole, shape):
        return lax.dynamic_slice_in_dim(whole, dp_index * shape[1], shape[1], 1)

    qkv_totals = sums[1, :, 2:5].reshape(heads_here, 3, HD)
    qv_grad = jnp.concatenate([qkv_totals[:, 0], qkv_totals[:, 2]], axis=1)
    up_totals = sums[0, :, 4:].reshape(up_bias.shape[0], 128)
    return (
        block_out,
        input_grad,
        own_vector(1, 0),
        own_vector(1, 1),
        qkv_weight_grad,
        own_matrix(qv_grad, qv_bias.shape),
        dense_grad.T,
        own_vector(0, 0),
        own_vector(0, 1),
        own_vector(0, 2),
        feed_grad[0],
        own_matrix(up_totals, up_bias.shape),
        feed_grad[1].T,
        own_vector(0, 3),
    )


def solution(mesh):
    rows = P(("dp", "tensor"), None)
    in_specs = (
        rows,
        P("dp"),
        P("dp"),
        P("dp", "tensor"),
        P("tensor", "dp"),
        P("tensor", "dp"),
        P("dp"),
        P("dp"),
        P("dp"),
        P("dp", "tensor"),
        P("tensor", "dp"),
        P("tensor", "dp"),
        P("dp"),
        rows,
        P(),
        P(),
    )
    out_specs = (
        rows,
        rows,
        P("dp"),
        P("dp"),
        P("dp", "tensor"),
        P("tensor", "dp"),
        P("tensor", "dp"),
        P("dp"),
        P("dp"),
        P("dp"),
        P("dp", "tensor"),
        P("tensor", "dp"),
        P("tensor", "dp"),
        P("dp"),
    )
    return jax.shard_map(
        per_device, mesh=mesh, in_specs=in_specs, out_specs=out_specs, check_vma=False
    )
```

```python
import functools

import jax
import jax.numpy as jnp
from jax import lax
from jax.experimental import pallas as pl
from jax.experimental.pallas import tpu as pltpu
from jax.sharding import PartitionSpec as P

HEADS = 16
HD = 64
TRUNK = 2048
SEG = 256
PAIR_TOKENS = 2 * (TRUNK + 12 * SEG)
PAIR_SEGS = 26
QUERY_BLOCK = 256
KEY_BLOCK = 256
BIG = 2.0**100
VALUE_ROWS = 80

epsilon = 1e-05
f32 = jnp.float32
bf16 = jnp.bfloat16
MESH = pl.DeviceIdType.MESH


def normalize(values, gain_row, bias_row):
    average = jnp.mean(values, axis=-1, keepdims=True)
    centred = values - average
    spread = jnp.mean(centred * centred, axis=-1, keepdims=True)
    return centred * lax.rsqrt(spread + epsilon) * gain_row + bias_row


def nn(left, right):
    return lax.dot_general(left, right, (((1,), (0,)), ((), ())), preferred_element_type=f32)


def nt(left, right):
    return lax.dot_general(left, right, (((1,), (1,)), ((), ())), preferred_element_type=f32)


def tn(left, right):
    return lax.dot_general(left, right, (((0,), (0,)), ((), ())), preferred_element_type=f32)


def pieces(value, count):
    parts = []
    for _ in range(count):
        part = lax.reduce_precision(value, 8, 7)
        parts.append(part)
        value = value - part
    return parts


def pair_tables(seg_parent, seg_length, group, slope, block_ids):
    first = group * PAIR_SEGS
    parent = lax.dynamic_slice_in_dim(seg_parent, first, PAIR_SEGS, 0) - first
    length = lax.dynamic_slice_in_dim(seg_length, first, PAIR_SEGS, 0)
    ids = jnp.arange(PAIR_SEGS, dtype=jnp.int32)
    begin = jnp.sum(jnp.where(ids[None, :] < ids[:, None], length[None, :], 0), axis=1)
    end = begin + length
    is_parent = parent[:, None] == ids[None, :]
    grand = jnp.sum(jnp.where(is_parent, parent[None, :], 0), axis=1)
    is_grand = grand[:, None] == ids[None, :]
    parent_length = jnp.sum(jnp.where(is_parent, length[None, :], 0), axis=1)
    grand_length = jnp.sum(jnp.where(is_grand, length[None, :], 0), axis=1)
    path_start = jnp.where(
        parent == ids, 0, parent_length + jnp.where(grand == parent, 0, grand_length)
    )
    related = is_parent | is_grand | (ids[:, None] == ids[None, :])
    high, low = pieces(slope * (path_start - begin).astype(f32), 2)
    slope_high, slope_low = pieces(slope, 2)
    by_segment = jnp.concatenate(
        [
            jnp.where(related, high[None, :], -BIG),
            jnp.where(related, low[None, :], 0.0),
            jnp.broadcast_to(
                jnp.stack([256.0 * slope_high, 256.0 * slope_low, slope_high, slope_low])[None, :],
                (PAIR_SEGS, 4),
            ),
        ],
        axis=1,
    )
    by_segment = jnp.pad(
        by_segment, ((0, 128 - PAIR_SEGS), (0, 128 - by_segment.shape[1]))
    ).astype(bf16)
    bounds = jnp.pad(jnp.stack([jnp.tile(begin, 2), jnp.tile(end, 2)]), ((0, 6), (0, 128 - 2 * PAIR_SEGS)))
    key_blocks = PAIR_TOKENS // KEY_BLOCK
    q_begin = block_ids * QUERY_BLOCK
    k_begin = jnp.arange(key_blocks, dtype=jnp.int32) * KEY_BLOCK
    q_has = (begin[None, :] < q_begin[:, None] + QUERY_BLOCK) & (end[None, :] > q_begin[:, None])
    k_has = (begin[None, :] < k_begin[:, None] + KEY_BLOCK) & (end[None, :] > k_begin[:, None])
    q_sees = jnp.any(q_has[:, :, None] & related[None], axis=1)
    seen = jnp.any(q_sees[:, None, :] & k_has[None, :, :], axis=2)
    seen = seen & (k_begin[None, :] + KEY_BLOCK <= q_begin[:, None])
    rank = jnp.sum(
        jnp.where(k_begin[None, None, :] < k_begin[None, :, None], seen[:, None, :], False),
        axis=2,
        dtype=jnp.int32,
    )
    slots = jnp.arange(key_blocks + 8, dtype=jnp.int32)
    numbers = jnp.arange(key_blocks, dtype=jnp.int32)
    block_list = jnp.sum(
        jnp.where(
            seen[:, :, None] & (rank[:, :, None] == slots[None, None, :]), numbers[None, :, None], 0
        ),
        axis=1,
    )
    block_count = jnp.sum(seen, axis=1, dtype=jnp.int32)
    return bounds, by_segment, block_list, block_count


def causal_scores(scores, key_first, query_first):
    rows = key_first + lax.broadcasted_iota(jnp.int32, scores.shape, 0)
    columns = query_first + lax.broadcasted_iota(jnp.int32, scores.shape, 1)
    return jnp.where(rows <= columns, scores, -BIG)


def token_lanes(bounds_ref, first, count):
    token = first + lax.broadcasted_iota(jnp.int32, (count, 128), 0)
    lane = lax.broadcasted_iota(jnp.int32, (count, 128), 1)
    member = (token >= bounds_ref[0:1, :]) & (token < bounds_ref[1:2, :])
    base = 2 * PAIR_SEGS
    number = jnp.where(lane < base + 2, lax.shift_right_logical(token, 8), token & 255)
    fixed = jnp.where(lane < base + 7, 1, 0)
    number = jnp.where(lane < base + 4, number, fixed)
    return jnp.where(lane < base, jnp.where(member, 1, 0), number).astype(f32)


def pair_rows(packed):
    return jnp.concatenate([packed[:, :HD], packed[:, HD:]], axis=0)


def build_keys(bounds_ref, mixed_ref, keys, step):
    rows = mixed_ref.shape[1] * 2 // 3
    lane = lax.broadcasted_iota(jnp.int32, (rows, 128), 1)
    for part in range(2):
        first = (2 * step + part) * rows
        both = mixed_ref[2 * step + part, 0:rows, :].astype(f32)
        keys[pl.ds(pl.multiple_of(first, 64), rows), :] = jnp.where(
            lane < HD, token_lanes(bounds_ref, first, rows), both
        ).astype(bf16)


def query_lanes(bounds_ref, by_segment_ref, mixed_ref, number):
    rows = mixed_ref.shape[1] * 2 // 3
    meta = nn(token_lanes(bounds_ref, number * rows, rows).astype(bf16), by_segment_ref[...])
    queries = mixed_ref[number, 0:rows, 0:HD].astype(f32) * 0.125
    return jnp.concatenate([meta[:, :HD], queries], axis=1)


def forward_kernel(
    block_of,
    count_of,
    list_of,
    bounds_ref,
    by_segment_ref,
    mixed_ref,
    context_ref,
    out_ref,
    keys,
    values_t,
    queries_all,
    scores_a,
    scores_b,
):
    messages, message_rows, _ = mixed_ref.shape
    rows = message_rows * 2 // 3
    tensor_count = context_ref.shape[1]
    steps = queries_all.shape[0] // QUERY_BLOCK

    def prepare(step, _):
        build_keys(bounds_ref, mixed_ref, keys, step)
        values = jnp.concatenate(
            [pair_rows(mixed_ref[2 * step + part, rows:, :]) for part in range(2)], axis=0
        )
        lane = lax.broadcasted_iota(jnp.int32, (2 * rows, HD), 1)
        ones = jnp.where(lane == 0, 1.0, 0.0).astype(bf16)
        wide = jnp.concatenate([values, ones], axis=1)
        values_t[:, pl.ds(pl.multiple_of(step * 2 * rows, 128), 2 * rows)] = wide.T[:VALUE_ROWS]
        return 0

    lax.fori_loop(0, messages // 2, prepare, 0)
    half = messages // (2 * tensor_count)

    def prepare_queries(step, _):
        number = block_of[(step // tensor_count) * (steps // half)] * QUERY_BLOCK // rows
        number = number + step % tensor_count
        queries_all[pl.ds(pl.multiple_of(step * rows, 64), rows), :] = query_lanes(
            bounds_ref, by_segment_ref, mixed_ref, number
        ).astype(bf16)
        return 0

    lax.fori_loop(0, messages // 2, prepare_queries, 0)

    def one_block(number, _):
        query_first = block_of[number] * QUERY_BLOCK
        here = pl.ds(pl.multiple_of(number * QUERY_BLOCK, QUERY_BLOCK), QUERY_BLOCK)
        queries = queries_all[here, :]

        count = count_of[number]

        def block_span(step):
            first = pl.multiple_of(list_of[number, step] * KEY_BLOCK, KEY_BLOCK)
            return pl.ds(first, KEY_BLOCK)

        def score_four(buffer, step):
            for part in range(4):
                buffer[part * KEY_BLOCK : (part + 1) * KEY_BLOCK, :] = nt(
                    keys[block_span(4 * step + part), :], queries
                )

        def absorb(scores, spans, carry):
            top, total = carry
            new_top = jnp.maximum(top, jnp.max(scores, axis=0, keepdims=True))
            weights = jnp.exp(scores - new_top).astype(bf16)
            total = total * jnp.exp(top - new_top)
            for part, span in enumerate(spans):
                total = total + nn(
                    values_t[:, span], weights[part * KEY_BLOCK : (part + 1) * KEY_BLOCK]
                )
            return new_top, total

        def absorb_four(buffer, step, carry):
            return absorb(buffer[...], [block_span(4 * step + part) for part in range(4)], carry)

        score_four(scores_a, 0)
        span = pl.ds(pl.multiple_of(query_first, KEY_BLOCK), KEY_BLOCK)
        scores = causal_scores(nt(keys[span, :], queries), query_first, query_first)
        carry = (jnp.full((1, QUERY_BLOCK), -BIG, f32), jnp.zeros((VALUE_ROWS, QUERY_BLOCK), f32))
        carry = absorb(scores, [span], carry)

        def eight_blocks(step, carry):
            score_four(scores_b, 2 * step + 1)
            carry = absorb_four(scores_a, 2 * step, carry)
            score_four(scores_a, 2 * step + 2)
            return absorb_four(scores_b, 2 * step + 1, carry)

        fours = count // 4
        carry = lax.fori_loop(0, fours // 2, eight_blocks, carry)
        carry = lax.fori_loop(
            0, fours % 2, lambda _, kept: absorb_four(scores_a, fours - 1, kept), carry
        )

        def last_blocks(blocks):
            def one(_, kept):
                spans = [block_span(count - count % (2 * blocks) + part) for part in range(blocks)]
                scores = [nt(keys[span, :], queries) for span in spans]
                return absorb(jnp.concatenate(scores, axis=0), spans, kept)

            return one

        carry = lax.fori_loop(0, count % 4 // 2, last_blocks(2), carry)
        top, total = lax.fori_loop(0, count % 2, last_blocks(1), carry)
        row_sum = total[HD : HD + 1]
        log_total = jnp.broadcast_to(top + jnp.log(row_sum), (HD, QUERY_BLOCK))
        out_ref[here, :] = jnp.concatenate([total[:HD] / row_sum, log_total], axis=0).T
        return 0

    lax.fori_loop(0, steps, one_block, 0)

    def pack(step, _):
        first = pl.multiple_of(step * rows, 64)
        half_rows = rows // 2
        context_ref[step // tensor_count, step % tensor_count] = jnp.concatenate(
            [
                out_ref[pl.ds(first, half_rows), 0:HD],
                out_ref[pl.ds(pl.multiple_of(first + half_rows, 32), half_rows), 0:HD],
            ],
            axis=1,
        ).astype(bf16)
        return 0

    lax.fori_loop(0, messages // 2, pack, 0)


def attention_forward(blocks, counts, lists, bounds, by_segment, mixed, tensor_count):
    messages, message_rows, _ = mixed.shape
    rows = message_rows * 2 // 3
    half = messages // 2 * rows
    smem = pl.BlockSpec(memory_space=pltpu.SMEM)
    vmem = pl.BlockSpec(memory_space=pltpu.VMEM)
    return pl.pallas_call(
        forward_kernel,
        in_specs=[smem] * 3 + [vmem] * 3,
        out_specs=[vmem, vmem],
        out_shape=[
            jax.ShapeDtypeStruct(
                (messages // 2 // tensor_count, tensor_count, rows // 2, 2 * HD), bf16
            ),
            jax.ShapeDtypeStruct((half, 128), f32),
        ],
        scratch_shapes=[
            pltpu.VMEM((PAIR_TOKENS, 128), bf16),
            pltpu.VMEM((VALUE_ROWS, PAIR_TOKENS), bf16),
            pltpu.VMEM((half, 128), bf16),
            pltpu.VMEM((4 * KEY_BLOCK, QUERY_BLOCK), f32),
            pltpu.VMEM((4 * KEY_BLOCK, QUERY_BLOCK), f32),
        ],
        compiler_params=pltpu.CompilerParams(vmem_limit_bytes=40 * 2**20),
        cost_estimate=pl.CostEstimate(
            flops=2 * 256 * 2 * 12_000_000, bytes_accessed=10_000_000, transcendentals=12_000_000
        ),
        name="attention_forward",
    )(blocks, counts, lists, bounds, by_segment, mixed)


def backward_kernel(
    block_of,
    count_of,
    list_of,
    bounds_ref,
    by_segment_ref,
    mixed_ref,
    grads_ref,
    out_ref,
    dq_ref,
    dkv_ref,
    keys,
    keys_t,
    values,
    queries_all,
    grads_all,
    queries_only,
    grads_only,
    dkv,
):
    messages, message_rows, _ = mixed_ref.shape
    rows = message_rows * 2 // 3
    tensor_count = grads_ref.shape[1]
    steps = queries_all.shape[0] // QUERY_BLOCK
    half = messages // (2 * tensor_count)

    def with_pieces(value, first_lane, wide):
        lane = lax.broadcasted_iota(jnp.int32, wide.shape, 1)
        for piece in range(3):
            part = value.astype(bf16).astype(f32)
            wide = jnp.where(lane == first_lane + piece, part, wide)
            value = value - part
        return wide

    def prepare(step, _):
        build_keys(bounds_ref, mixed_ref, keys, step)
        span = pl.ds(pl.multiple_of(step * 2 * rows, 128), 2 * rows)
        keys_t[:, span] = keys[span, :].T[HD:]
        packed = jnp.concatenate(
            [pair_rows(mixed_ref[2 * step + part, rows:, :]) for part in range(2)], axis=0
        )
        lane = lax.broadcasted_iota(jnp.int32, (2 * rows, HD), 1)
        ones = jnp.where(lane < 3, 1.0, 0.0).astype(bf16)
        values[span, :] = jnp.concatenate([ones, packed], axis=1)
        dkv[span, :] = jnp.zeros((2 * rows, 128), f32)
        return 0

    lax.fori_loop(0, messages // 2, prepare, 0)

    def prepare_queries(step, _):
        number = block_of[(step // tensor_count) * (steps // half)] * QUERY_BLOCK // rows
        number = number + step % tensor_count
        span = pl.ds(pl.multiple_of(step * rows, 64), rows)
        wide = query_lanes(bounds_ref, by_segment_ref, mixed_ref, number)
        out = out_ref[span, :]
        queries_all[span, :] = with_pieces(-out[:, HD : HD + 1], 2 * PAIR_SEGS + 4, wide).astype(bf16)
        lane = lax.broadcasted_iota(jnp.int32, (rows, 128), 1)
        queries = mixed_ref[number, 0:rows, :].astype(f32) * 0.125
        queries_only[span, :] = jnp.where(lane < HD, queries, 0.0).astype(bf16)
        grads = pair_rows(grads_ref[step // tensor_count, step % tensor_count].astype(f32))
        inner = jnp.sum(grads * out[:, :HD], axis=1, keepdims=True)
        wide = jnp.concatenate([jnp.zeros((rows, HD), f32), grads], axis=1)
        grads_only[span, :] = wide.astype(bf16)
        grads_all[span, :] = with_pieces(-inner, 0, wide).astype(bf16)
        return 0

    lax.fori_loop(0, messages // 2, prepare_queries, 0)

    def one_block(number, _):
        query_first = block_of[number] * QUERY_BLOCK
        here = pl.ds(pl.multiple_of(number * QUERY_BLOCK, QUERY_BLOCK), QUERY_BLOCK)
        queries = queries_all[here, :]
        grads = grads_all[here, :]
        both = jnp.concatenate([queries_only[here, :], grads_only[here, :]], axis=0)

        count = count_of[number]

        def attend(blocks, dq, masked):
            spans = [pl.ds(pl.multiple_of(block * KEY_BLOCK, KEY_BLOCK), KEY_BLOCK) for block in blocks]
            scores = [nt(keys[span, :], queries) for span in spans]
            if masked:
                scores = [causal_scores(scores[0], blocks[0] * KEY_BLOCK, query_first)]
            grads_of = [nt(values[span, :], grads) for span in spans]
            for span, score, grad in zip(spans, scores, grads_of):
                weights = jnp.exp(score)
                score_grad = (weights * grad).astype(bf16)
                dkv[span, :] += nn(
                    jnp.concatenate([score_grad, weights.astype(bf16)], axis=1), both
                )
                dq = dq + nn(keys_t[:, span], score_grad)
            return dq

        def listed(first, blocks):
            return lambda step, kept: attend(
                [list_of[number, first + blocks * step + part] for part in range(blocks)], kept, False
            )

        dq = attend([query_first // KEY_BLOCK], jnp.zeros((HD, QUERY_BLOCK), f32), True)
        eights, rest = count // 8, count % 8
        dq = lax.fori_loop(0, eights, listed(0, 8), dq)
        dq = lax.fori_loop(0, rest // 4, listed(8 * eights, 4), dq)
        dq = lax.fori_loop(0, rest % 4 // 2, listed(count - rest % 4, 2), dq)
        dq = lax.fori_loop(0, rest % 2, listed(count - 1, 1), dq)
        dq_ref[here, :] = (dq * 0.125).T.astype(bf16)
        return 0

    lax.fori_loop(0, steps, one_block, 0)

    def write(step, _):
        span = pl.ds(pl.multiple_of(step * KEY_BLOCK, KEY_BLOCK), KEY_BLOCK)
        dkv_ref[span, :] = dkv[span, :].astype(bf16)
        return 0

    lax.fori_loop(0, PAIR_TOKENS // KEY_BLOCK, write, 0)


def attention_backward(blocks, counts, lists, bounds, by_segment, mixed, grads, out):
    smem = pl.BlockSpec(memory_space=pltpu.SMEM)
    vmem = pl.BlockSpec(memory_space=pltpu.VMEM)
    half = out.shape[0]
    return pl.pallas_call(
        backward_kernel,
        in_specs=[smem] * 3 + [vmem] * 5,
        out_specs=[vmem, vmem],
        out_shape=[
            jax.ShapeDtypeStruct((half, HD), bf16),
            jax.ShapeDtypeStruct((PAIR_TOKENS, 128), bf16),
        ],
        scratch_shapes=[
            pltpu.VMEM((PAIR_TOKENS, 128), bf16),
            pltpu.VMEM((HD, PAIR_TOKENS), bf16),
            pltpu.VMEM((PAIR_TOKENS, 128), bf16),
            pltpu.VMEM((half, 128), bf16),
            pltpu.VMEM((half, 128), bf16),
            pltpu.VMEM((half, 128), bf16),
            pltpu.VMEM((half, 128), bf16),
            pltpu.VMEM((PAIR_TOKENS, 128), f32),
        ],
        compiler_params=pltpu.CompilerParams(vmem_limit_bytes=56 * 2**20),
        cost_estimate=pl.CostEstimate(
            flops=5 * 256 * 2 * 12_000_000, bytes_accessed=16_000_000, transcendentals=12_000_000
        ),
        name="attention_backward",
    )(blocks, counts, lists, bounds, by_segment, mixed, grads, out)


def flipped(chip, chips):
    return (chip + chips - 1) // chips


def greet_all(dp_count, tensor_count, dp_index, tensor_index):
    barrier = pltpu.get_barrier_semaphore()
    total = dp_count * tensor_count
    me = dp_index * tensor_count + tensor_index

    def greet(step, _):
        other = (me + step) % total
        pl.semaphore_signal(
            barrier,
            inc=1,
            device_id=(other // tensor_count, other % tensor_count),
            device_id_type=MESH,
        )
        return 0

    lax.fori_loop(1, total, greet, 0)
    pl.semaphore_wait(barrier, total - 1)


def repeat(count, body):
    def one(step, _):
        body(step)
        return 0

    lax.fori_loop(0, count, one, 0)


def swap_copy(source, target, sems, number, partner):
    return pltpu.make_async_remote_copy(
        src_ref=source,
        dst_ref=target,
        send_sem=sems.at[0, number],
        recv_sem=sems.at[1, number],
        device_id=partner,
        device_id_type=MESH,
    )


def layer_norm_back(values, gain, grads):
    average = jnp.mean(values, axis=-1, keepdims=True)
    centred = values - average
    scale = lax.rsqrt(jnp.mean(centred * centred, axis=-1, keepdims=True) + epsilon)
    normed = centred * scale
    scaled = grads * gain
    first = jnp.mean(scaled, axis=-1, keepdims=True)
    second = jnp.mean(scaled * normed, axis=-1, keepdims=True)
    return (scaled - first - normed * second) * scale, grads * normed


def column_sum(values):
    return jnp.sum(values, axis=0, keepdims=True)


def transpose_rows(source, target):
    size = min(256, target.shape[0])

    def one(step):
        span = pl.ds(pl.multiple_of(step * size, size), size)
        target[span, :] = source[:, span].T

    repeat(target.shape[0] // size, one)


def nearest(layer, layers, step):
    tile = 0 * layer
    for here in range(layers):
        order = sorted(
            range(layers),
            key=lambda there: (there == here, abs(there - here), abs(2 * there - layers + 1)),
        )
        for number, there in enumerate(order):
            tile = jnp.where((layer == here) & (step == number), there, tile)
    return tile


def doubling_gather(
    weight, recv_sem, send_sem, layer_recv, layer_send, chip, chips, core, layer, layers, dp_index
):
    stages = chips.bit_length() - 1
    steps = weight.shape[0]
    slot_of = (lambda step: step) if layer_recv is None else (lambda step: nearest(layer, layers, step))

    def layer_copy(tile, way):
        block = weight.at[tile, chip]
        return pltpu.make_async_remote_copy(
            src_ref=block,
            dst_ref=block,
            send_sem=layer_send.at[tile, way],
            recv_sem=layer_recv.at[tile],
            device_id=(dp_index, layer + 2 * way - 1),
            device_id_type=MESH,
        )

    def ways(tile, body):
        for way in range(2):
            inside = (layer + 1 < layers) & (tile <= layer) if way else (layer > 0) & (tile >= layer)

            @pl.when(inside)
            def _():
                body(layer_copy(tile, way))

    def spread():
        ways(layer, lambda copy: copy.start())

    rows = weight.shape[2] // 2

    def half(order):
        return pl.ds(pl.multiple_of(order * rows, rows), rows)

    def place(order, stage, step):
        size = jnp.where(order == 0, 2**stage, chips // 2 ** (stage + 1))
        bit = chip // size % 2
        across = size * (1 - 2 * bit)
        held = jnp.where(
            order == 0,
            chip // 2**stage * 2**stage + step,
            chip % (chips // 2**stage) + step * (chips // 2**stage),
        )
        return held, held + across, chip + across

    def copy(step, stage, order, number):
        slot = slot_of(step)
        held, _, partner = place(order, stage, number)
        block = weight.at[slot, held, half(order), :]
        return pltpu.make_async_remote_copy(
            src_ref=block,
            dst_ref=block,
            send_sem=send_sem.at[slot, 2**stage - 1 + number, order],
            recv_sem=recv_sem.at[slot, held, order],
            device_id=(2 * partner + core, layer),
            device_id_type=MESH,
        )

    def wait_block(block, sem):
        pltpu.make_async_remote_copy(
            src_ref=block,
            dst_ref=block,
            send_sem=send_sem.at[0, 0, 0],
            recv_sem=sem,
            device_id=(2 * chip + 1 - core, layer),
            device_id_type=MESH,
        ).wait_recv()

    def each(stage, body):
        repeat(2 * 2**stage, lambda number: body(number % 2, number // 2))

    def arrived(step, stage):
        slot = slot_of(step)

        def one(order, number):
            _, got, _ = place(order, stage, number)
            wait_block(weight.at[slot, got, half(order), :], recv_sem.at[slot, got, order])

        each(stage, one)

    def advance(number):
        for stage in range(stages):
            step = number - stage

            @pl.when((step >= 0) & (step < steps))
            def _():
                if stage > 0:
                    arrived(step, stage - 1)
                else:

                    if layer_recv is not None:

                        tile = slot_of(step)

                        @pl.when(tile != layer)
                        def _():
                            wait_block(weight.at[tile, chip], layer_recv.at[tile])
                            ways(tile, lambda copy: copy.start())

                each(stage, lambda order, each_number: copy(step, stage, order, each_number).start())

    def ready(step):
        arrived(step, stages - 1)

    def sent():
        if layer_send is not None:
            repeat(steps, lambda tile: ways(tile, lambda copy: copy.wait_send()))

        def one(step):
            for stage in range(stages):
                each(
                    stage,
                    lambda order, number: copy(step, stage, order, number).wait_send(),
                )

        repeat(steps, one)

    return spread, advance, ready, sent


def picked(rows, lanes, owner_of, lane_of, keep):
    lane = lax.broadcasted_iota(jnp.int32, (128, lanes), 1)
    source = lax.broadcasted_iota(jnp.int32, (128, lanes), 0)
    spread = nn(rows.astype(bf16), jnp.where(source == lane_of(lane), 1.0, 0.0).astype(bf16))
    lane = lax.broadcasted_iota(jnp.int32, (rows.shape[0], lanes), 1)
    owner = lax.broadcasted_iota(jnp.int32, (rows.shape[0], lanes), 0)
    return column_sum(jnp.where((owner == owner_of(lane)) & keep(lane), spread, 0.0))


def project_kernel(
    dp_count,
    tensor_count,
    span,
    x_ref,
    small_ref,
    shard_ref,
    feed_ref,
    normed_ref,
    mixed_ref,
    weight_out_ref,
    vectors_ref,
    up_shift_ref,
    block_ref,
    normed,
    weight,
    smalls,
    outbox,
    swap_sem,
    small_send,
    small_recv,
    half_sem,
    gather_recv,
    gather_send,
    layer_recv,
    layer_send,
    out_sem,
    send_sem,
    recv_sem,
    local_sem,
    pass_send,
    pass_recv,
):
    dp_index, tensor_index = lax.axis_index("dp"), lax.axis_index("tensor")
    rows, width = x_ref.shape
    hidden = weight.shape[3]
    columns = hidden - 128
    piece = shard_ref.shape[1]
    core = dp_index % 2
    base = dp_index // span * span
    chip = dp_index % span // 2
    chips = span // 2
    layer_chip, layer_chips = dp_index // 2, dp_count // 2
    partner = (dp_index + 1 - 2 * core, tensor_index)
    total = dp_count * tensor_count
    me = dp_index * tensor_count + tensor_index

    def small_copy(step):
        other = (me + step) % total
        place = smalls.at[dp_index, tensor_index]
        return pltpu.make_async_remote_copy(
            src_ref=place,
            dst_ref=place,
            send_sem=small_send.at[other // tensor_count, other % tensor_count],
            recv_sem=small_recv.at[dp_index, tensor_index],
            device_id=(other // tensor_count, other % tensor_count),
            device_id_type=MESH,
        )

    def small_wait(step):
        other = (me + step) % total
        there = other // tensor_count, other % tensor_count
        place = smalls.at[there[0], there[1]]
        pltpu.make_async_remote_copy(
            src_ref=place,
            dst_ref=place,
            send_sem=small_send.at[there[0], there[1]],
            recv_sem=small_recv.at[there[0], there[1]],
            device_id=partner,
            device_id_type=MESH,
        ).wait_recv()

    own_rows = pl.ds(pl.multiple_of(core * piece, piece), piece)
    smalls[dp_index, tensor_index] = small_ref[...]
    weight[tensor_index, layer_chip, own_rows, :] = shard_ref[core]
    greet_all(dp_count, tensor_count, dp_index, tensor_index)
    half = pltpu.make_async_remote_copy(
        src_ref=shard_ref.at[1 - core],
        dst_ref=weight.at[tensor_index, layer_chip, own_rows, :],
        send_sem=half_sem.at[0],
        recv_sem=half_sem.at[1],
        device_id=partner,
        device_id_type=MESH,
    )
    half.start()
    block_ref[own_rows, :] = feed_ref[core]
    feed_half = pltpu.make_async_remote_copy(
        src_ref=feed_ref.at[1 - core],
        dst_ref=block_ref.at[own_rows, :],
        send_sem=half_sem.at[2],
        recv_sem=half_sem.at[3],
        device_id=partner,
        device_id_type=MESH,
    )
    feed_half.start()
    repeat(total - 1, lambda step: small_copy(step + 1).start())
    spread, advance, ready, gather_sent = doubling_gather(
        weight,
        gather_recv,
        gather_send,
        layer_recv,
        layer_send,
        layer_chip,
        layer_chips,
        core,
        tensor_index,
        tensor_count,
        dp_index,
    )
    half.wait_recv()
    spread()
    repeat(total - 1, lambda step: small_wait(step + 1))

    def vector(number):
        here = smalls[:, tensor_index].astype(f32)[:, number, :]
        return picked(
            here, width, lambda lane: lane // piece, lambda lane: lane % piece, lambda lane: lane >= 0
        )

    normed[core] = normalize(x_ref[...].astype(f32), vector(0), vector(1)).astype(bf16)
    swap = pltpu.make_async_remote_copy(
        src_ref=normed.at[core],
        dst_ref=normed.at[core],
        send_sem=swap_sem.at[0],
        recv_sem=swap_sem.at[1],
        device_id=partner,
        device_id_type=MESH,
    )
    swap.start()
    stages = layer_chips.bit_length() - 1
    for number in range(stages):
        advance(number)
    vectors_ref[...] = jnp.zeros_like(vectors_ref)
    for number in (0, 2, 3, 4, 5):
        vectors_ref[number : number + 1, :] = vector(number)

    bias_width = 2 * HD // dp_count

    def qkv_shift(owner):
        here = smalls[:, owner].astype(f32)[:, 6, :]

        def column(lane):
            return lane % HD + jnp.where(lane % (3 * HD) < HD, 0, HD)

        return picked(
            here,
            columns,
            lambda lane: column(lane) // bias_width,
            lambda lane: (2 * core + lane // (3 * HD)) * bias_width + column(lane) % bias_width,
            lambda lane: (lane % (3 * HD) < HD) | (lane % (3 * HD) >= 2 * HD),
        )

    def up_shift(owner):
        here = smalls[:, owner].astype(f32)[:, 7, :]
        return picked(
            here,
            hidden,
            lambda lane: lane % 128 // bias_width,
            lambda lane: (core * (hidden // 128) + lane // 128) * bias_width
            + lane % 128 % bias_width,
            lambda lane: lane >= 0,
        )

    swap.wait_recv()

    def out_copy(owner):
        return pltpu.make_async_copy(weight.at[owner], weight_out_ref.at[owner], out_sem.at[owner])

    def slot(place_dp, place_tensor):
        return mixed_ref.at[place_dp * tensor_count + place_tensor]

    def send(owner, part, pair):
        head_chip = 2 * core + pair
        target = (base + 2 * head_chip + (part + flipped(chip, chips)) % 2, owner)
        here = (target[0] == dp_index) & (owner == tensor_index)
        return here, pltpu.make_async_remote_copy(
            src_ref=outbox.at[owner, part, pair],
            dst_ref=slot(2 * chip + part, tensor_index),
            send_sem=send_sem.at[owner, part, pair],
            recv_sem=recv_sem.at[chip, tensor_index],
            device_id=target,
            device_id_type=MESH,
        ), pltpu.make_async_copy(
            outbox.at[owner, part, pair], slot(2 * chip + part, tensor_index), local_sem.at[0]
        )

    def one_tile(step):
        owner = nearest(tensor_index, tensor_count, step)
        advance(step + stages)
        ready(step)
        out_copy(owner).start()
        shift = qkv_shift(owner)
        up_shift_ref[owner] = jnp.broadcast_to(up_shift(owner), up_shift_ref.shape[1:])

        def one_part(part):
            matrix = weight[owner, :, :, 0:columns].reshape(width, columns)
            result = nn(normed[part], matrix) + shift
            first = [result[:, 0:128], result[:, 192:320]]
            last = [result[:, 128:192], result[:, 320:384]]
            for pair in range(2):
                outbox[owner, part, pair, 0:rows, :] = first[pair].astype(bf16)
                outbox[owner, part, pair, rows:, :] = jnp.concatenate(
                    [last[pair][: rows // 2], last[pair][rows // 2 :]], axis=1
                ).astype(bf16)
                here, far, near = send(owner, part, pair)

                @pl.when(here)
                def _():
                    near.start()

                @pl.when(jnp.logical_not(here))
                def _():
                    far.start()

        repeat(2, one_part)

    repeat(tensor_count, one_tile)
    normed_ref[...] = normed[...]

    def arrival(step):
        from_chip, from_tensor = step % chips, nearest(tensor_index, tensor_count, step // chips)
        mine = slot(2 * from_chip + (core + flipped(from_chip, chips)) % 2, from_tensor)
        theirs = slot(2 * from_chip + (core + flipped(from_chip, chips) + 1) % 2, from_tensor)
        here = (from_chip == chip) & (from_tensor == tensor_index) & (chip // 2 == core)

        def passing(place):
            return pltpu.make_async_remote_copy(
                src_ref=place,
                dst_ref=place,
                send_sem=pass_send.at[from_chip, from_tensor],
                recv_sem=pass_recv.at[from_chip, from_tensor],
                device_id=partner,
                device_id_type=MESH,
            )

        return mine, theirs, here, passing, from_chip, from_tensor

    def hand_on(step):
        mine, _theirs, here, passing, from_chip, from_tensor = arrival(step)

        @pl.when(here)
        def _():
            pltpu.make_async_copy(mine, mine, local_sem.at[0]).wait()

        @pl.when(jnp.logical_not(here))
        def _():
            pltpu.make_async_remote_copy(
                src_ref=mine,
                dst_ref=mine,
                send_sem=pass_send.at[from_chip, from_tensor],
                recv_sem=recv_sem.at[from_chip, from_tensor],
                device_id=partner,
                device_id_type=MESH,
            ).wait_recv()

        passing(mine).start()

    repeat(chips * tensor_count, hand_on)

    def finish(step):
        mine, theirs, _here, passing, _a, _b = arrival(step)
        passing(mine).wait_send()
        passing(theirs).wait_recv()

    repeat(chips * tensor_count, finish)

    def sent(step):
        here, far, _near = send(step // 4, step // 2 % 2, step % 2)

        @pl.when(jnp.logical_not(here))
        def _():
            far.wait_send()

    repeat(4 * tensor_count, sent)
    repeat(total - 1, lambda step: small_copy(step + 1).wait_send())
    repeat(tensor_count, lambda owner: out_copy(owner).wait())
    half.wait_send()
    feed_half.wait()
    swap.wait_send()
    gather_sent()


def project(inputs, small, shard, feed, dp_count, tensor_count, span):
    rows, width = inputs.shape
    _, piece, hidden = shard.shape
    messages = span * tensor_count
    chips, layer_chips = span // 2, dp_count // 2
    dma = pltpu.SemaphoreType.DMA
    vmem = pl.BlockSpec(memory_space=pltpu.VMEM)
    anywhere = pl.BlockSpec(memory_space=pl.ANY)
    weight = (tensor_count, layer_chips, 2 * piece, hidden)
    return pl.pallas_call(
        functools.partial(project_kernel, dp_count, tensor_count, span),
        in_specs=[vmem] * 4,
        out_specs=[vmem, anywhere, anywhere, vmem, vmem, vmem],
        out_shape=[
            jax.ShapeDtypeStruct((2, rows, width), bf16),
            jax.ShapeDtypeStruct((messages, rows * 3 // 2, 128), bf16),
            jax.ShapeDtypeStruct(weight, bf16),
            jax.ShapeDtypeStruct((8, width), f32),
            jax.ShapeDtypeStruct((tensor_count, 8, hidden), f32),
            jax.ShapeDtypeStruct((2 * piece, feed.shape[2]), bf16),
        ],
        scratch_shapes=[
            pltpu.VMEM((2, rows, width), bf16),
            pltpu.VMEM(weight, bf16),
            pltpu.VMEM((dp_count, tensor_count, 16, 128), bf16),
            pltpu.VMEM((tensor_count, 2, 2, rows * 3 // 2, 128), bf16),
            dma((2,)),
            dma((dp_count, tensor_count)),
            dma((dp_count, tensor_count)),
            dma((4,)),
            dma((tensor_count, layer_chips, 2)),
            dma((tensor_count, layer_chips - 1, 2)),
            dma((tensor_count,)),
            dma((tensor_count, 2)),
            dma((tensor_count,)),
            dma((tensor_count, 2, 2)),
            dma((chips, tensor_count)),
            dma((1,)),
            dma((chips, tensor_count)),
            dma((chips, tensor_count)),
        ],
        compiler_params=pltpu.CompilerParams(
            collective_id=0, has_side_effects=True, vmem_limit_bytes=40 * 2**20
        ),
        cost_estimate=pl.CostEstimate(
            flops=2 * 2 * rows * width * hidden * tensor_count,
            bytes_accessed=20_000_000,
            transcendentals=0,
        ),
        name="project",
    )(inputs, small, shard, feed)


def halving_scatter(parts, inbox, send_sem, recv_sem, chip, chips, core, layer):
    stages = chips.bit_length() - 1
    rows = parts.shape[2] // 2

    def places(order, stage, step):
        size = jnp.where(order == 0, 2**stage, chips // 2 ** (stage + 1))
        bit = chip // size % 2
        low, high = chip % size, chip // (2 * size) * (2 * size)
        rest = jnp.where(order == 0, low + step * 2 * size, high + step)
        theirs = rest + (1 - bit) * size
        return theirs, rest + bit * size, chip + (1 - 2 * bit) * size

    def half(order):
        return pl.ds(pl.multiple_of(order * rows, rows), rows)

    def copy(item, stage, order, step):
        theirs, _, partner = places(order, stage, step)
        where = chips - chips // 2**stage + step
        return pltpu.make_async_remote_copy(
            src_ref=parts.at[item, theirs, half(order), :],
            dst_ref=inbox.at[item, where, half(order), :],
            send_sem=send_sem.at[item, where, order],
            recv_sem=recv_sem.at[item, where, order],
            device_id=(2 * partner + core, layer),
            device_id_type=MESH,
        )

    def each(stage, body):
        count = chips // 2 ** (stage + 1)
        repeat(2 * count, lambda number: body(number % 2, number // 2))

    def start(item, stage):
        each(stage, lambda order, step: copy(item, stage, order, step).start())

    def finish(item, stage):
        def one(order, step):
            copy(item, stage, order, step).wait_recv()
            _, keep, _ = places(order, stage, step)
            where = chips - chips // 2**stage + step
            parts[item, keep, half(order), :] = (
                parts[item, keep, half(order), :].astype(f32)
                + inbox[item, where, half(order), :].astype(f32)
            ).astype(bf16)

        each(stage, one)

    def add(item, stage):
        def one(order, step):
            _, keep, _ = places(order, stage, step)
            where = chips - chips // 2**stage + step
            parts[item, keep, half(order), :] = (
                parts[item, keep, half(order), :].astype(f32)
                + inbox[item, where, half(order), :].astype(f32)
            ).astype(bf16)

        each(stage, one)

    def sent(item, stage):
        each(stage, lambda order, step: copy(item, stage, order, step).wait_send())

    return stages, start, finish, sent, add


def middle_kernel(
    dp_count,
    tensor_count,
    span,
    context_ref,
    x_ref,
    cot_ref,
    cot_across_ref,
    vectors_in_ref,
    up_shift_ref,
    feed_ref,
    weight_ref,
    block_ref,
    middle_grad_ref,
    feed_sum_ref,
    dense_send0_ref,
    dense_send1_ref,
    dense_keep_ref,
    vectors_ref,
    up_shift_grad_ref,
    grads_ref,
    context_in,
    context,
    dense,
    feed,
    middle,
    normed,
    cot,
    turned_normed,
    turned_cot,
    active,
    upper_grad,
    out_total,
    normed_total,
    swap_in,
    core_in,
    pair_in,
    low_grad,
    outbox,
    parts,
    inbox,
    dense_parts,
    weight_sem,
    swap_sem,
    share_send,
    share_recv,
    context_send,
    context_recv,
    outbox_send,
    outbox_recv,
    local_sem,
    gather_recv,
    gather_send,
    parts_send,
    parts_recv,
    dense_sem,
):
    dp_index, tensor_index = lax.axis_index("dp"), lax.axis_index("tensor")
    rows, width = x_ref.shape
    hidden = active.shape[2]
    steps = feed.shape[0]
    core = dp_index % 2
    base = dp_index // span * span
    chip = dp_index % span // 2
    chips = span // 2
    layer_chip, layer_chips = dp_index // 2, dp_count // 2
    pair_rows_count = parts.shape[2]
    piece = pair_rows_count // 2
    side = tensor_index % 2
    partner = (dp_index + 1 - 2 * core, tensor_index)
    across = (dp_index, tensor_index + 1 - 2 * side)
    own_part = 2 * side + core
    part_span = lambda part: pl.ds(pl.multiple_of(part * rows, 64), rows)
    mine, theirs = part_span(core), part_span(1 - core)

    def dense_copy(owner):
        return pltpu.make_async_copy(
            weight_ref.at[owner, :, pl.ds(weight_ref.shape[2] - 128, 128)],
            dense.at[:, pl.ds(pl.multiple_of(owner * 128, 128), 128)],
            weight_sem.at[owner],
        )

    repeat(tensor_count, lambda owner: dense_copy(owner).start())
    gain_ref, bias_ref, dense_shift_ref, down_shift_ref = (
        vectors_in_ref.at[number : number + 1] for number in range(2, 6)
    )
    across_part = own_part + 2 - 4 * side
    cot[part_span(own_part), :] = cot_ref[...]
    cot[part_span(across_part), :] = cot_across_ref[...]
    feed[:, layer_chip] = feed_ref[...]
    greet_all(dp_count, tensor_count, dp_index, tensor_index)
    _, gather, ready, gather_sent = doubling_gather(
        feed,
        gather_recv,
        gather_send,
        None,
        None,
        layer_chip,
        layer_chips,
        core,
        tensor_index,
        tensor_count,
        dp_index,
    )
    gather_steps = steps + layer_chips.bit_length() - 2

    def context_out(step):
        place, owner = step // tensor_count, step % tensor_count
        owner = (tensor_index + 1 + owner) % tensor_count
        part = (core + flipped(place, chips)) % 2
        target = (base + 2 * place + chip // 2, owner)
        here = (target[0] == dp_index) & (owner == tensor_index)
        source = context_ref.at[place, owner]
        destination = context_in.at[tensor_index, chip % 2, part]
        far = pltpu.make_async_remote_copy(
            src_ref=source,
            dst_ref=destination,
            send_sem=context_send.at[place, owner],
            recv_sem=context_recv.at[tensor_index, chip % 2, part],
            device_id=target,
            device_id_type=MESH,
        )
        near = pltpu.make_async_copy(source, destination, local_sem.at[0])
        return here, far, near

    def send_context(step):
        here, far, near = context_out(step)

        @pl.when(here)
        def _():
            near.start()

        @pl.when(jnp.logical_not(here))
        def _():
            far.start()

    repeat(chips * tensor_count, send_context)

    def share_copy(array, which, number):
        source = own_part if number < 2 else own_part + 2 - 4 * side
        block = array.at[part_span(source)]
        return pltpu.make_async_remote_copy(
            src_ref=block,
            dst_ref=block,
            send_sem=share_send.at[which, number],
            recv_sem=share_recv.at[which, number],
            device_id=across if number == 1 else partner,
            device_id_type=MESH,
        )

    def share_arrival(array, which, number):
        source = (
            own_part + 1 - 2 * core,
            own_part + 2 - 4 * side,
            own_part + 2 - 4 * side + 1 - 2 * core,
        )[number]
        block = array.at[part_span(source)]
        return pltpu.make_async_remote_copy(
            src_ref=block,
            dst_ref=block,
            send_sem=share_send.at[which, number],
            recv_sem=share_recv.at[which, number],
            device_id=partner,
            device_id_type=MESH,
        )

    gather(0)
    share_copy(cot, 0, 0).start()
    share_copy(cot, 0, 2).start()
    repeat(4, lambda part: out_total.__setitem__(part, jnp.zeros((rows, width), f32)))
    repeat(4, lambda part: normed_total.__setitem__(part, jnp.zeros((rows, width), f32)))

    def take_context(step):
        owner, part = (tensor_index + step // 2) % tensor_count, step % 2
        for pair in range(2):
            destination = context_in.at[owner, pair, part]
            here = (
                (owner == tensor_index)
                & (chip == 2 * core + pair)
                & ((part + flipped(chip, chips)) % 2 == core)
            )

            @pl.when(here)
            def _():
                pltpu.make_async_copy(destination, destination, local_sem.at[0]).wait()

            @pl.when(jnp.logical_not(here))
            def _():
                pltpu.make_async_remote_copy(
                    src_ref=destination,
                    dst_ref=destination,
                    send_sem=context_send.at[0, 0],
                    recv_sem=context_recv.at[owner, pair, part],
                    device_id=partner,
                    device_id_type=MESH,
                ).wait_recv()

        first, second = context_in[owner, 0, part], context_in[owner, 1, part]
        lanes = pl.ds(pl.multiple_of(owner * 128, 128), 128)
        half = rows // 2
        for number in range(2):
            cut = slice(number * HD, (number + 1) * HD)
            where = pl.ds(pl.multiple_of(part * rows + number * half, 32), half)
            context[where, lanes] = jnp.concatenate([first[:, cut], second[:, cut]], axis=1)

    for number in range(1, gather_steps):
        gather(number)
    repeat(2 * tensor_count, take_context)
    repeat(tensor_count, lambda owner: dense_copy(owner).wait())

    low_grad[theirs, :] = nt(context[theirs, :], dense[...]).astype(bf16)
    first_swap = swap_copy(low_grad.at[theirs], swap_in, swap_sem, 0, partner)
    first_swap.start()
    own = x_ref[...].astype(f32) + dense_shift_ref[...] + nt(context[mine, :], dense[...])
    first_swap.wait()
    middle[...] = own + swap_in[...].astype(f32)
    normed[part_span(own_part), :] = normalize(middle[...], gain_ref[...], bias_ref[...]).astype(bf16)
    share_copy(normed, 1, 1).start()
    share_copy(normed, 1, 0).start()
    share_arrival(cot, 0, 0).wait_recv()
    share_arrival(cot, 0, 2).wait_recv()
    transpose_rows(cot, turned_cot)
    share_arrival(normed, 1, 0).wait_recv()

    def one_part(index):
        step, turn = index % (2 * steps) // 2, index // (2 * steps) * 2 + index % 2
        owner = (tensor_index + step * (tensor_count // steps)) % tensor_count
        part = 2 * ((side + turn // 2) % 2) + (core + turn) % 2

        @pl.when(turn == 0)
        def _():
            ready(step)
            up_shift_grad_ref[step] = jnp.zeros((8, hidden), f32)

        @pl.when((step == 0) & (turn == 2))
        def _():
            share_arrival(normed, 1, 1).wait_recv()
            share_copy(normed, 1, 2).start()

        @pl.when((step == 0) & (turn == 3))
        def _():
            share_arrival(normed, 1, 2).wait_recv()

        here = part_span(part)
        up_matrix = feed[step, :, :, 0:hidden].reshape(width, hidden)
        down_matrix = feed[step, :, :, hidden:].reshape(width, hidden)
        upper = nn(normed[here, :], up_matrix) + up_shift_ref[owner, 0:1]
        active_grad = nn(cot[here, :], down_matrix)
        square = upper * upper
        bent = jnp.tanh(0.7978845608 * upper * (1.0 + 0.044715 * square))
        rising = 0.5 * (1.0 + bent)
        slope = rising + 0.5 * upper * (1.0 - bent * bent) * 0.7978845608 * (
            1.0 + 3.0 * 0.044715 * square
        )
        low = (active_grad * slope).astype(bf16)
        active_low = (upper * rising).astype(bf16)
        active[step, here, :] = active_low
        upper_grad[step, here, :] = low
        up_shift_grad_ref[step, 0:1] += column_sum(low.astype(f32))
        normed_total[part] += nt(low, up_matrix)
        out_total[part] += nt(active_low, down_matrix)

    repeat(4 * steps, one_part)

    def core_copy(which):
        return swap_copy(
            cot.at[pl.ds(2 * which * rows, 2 * rows)], core_in.at[which], swap_sem, 1 + which, partner
        )

    def pair_copy(which):
        source = normed.at[pl.ds(0, rows)] if which else swap_in
        return swap_copy(source, pair_in.at[which], swap_sem, 3 + which, across)

    totals = (normed_total, out_total)
    for number in (0, 2):
        share_copy(cot, 0, number).wait_send()
    for which in range(2):
        for number in range(2):
            cot[pl.ds((2 * which + number) * rows, rows), :] = totals[which][
                2 * number + 1 - core
            ].astype(bf16)
        core_copy(which).start()
    def add_cores(which):
        core_copy(which).wait_recv()
        value = (
            totals[which][2 * (1 - side) + core] + core_in[which, part_span(1 - side), :].astype(f32)
        ).astype(bf16)
        if which:
            normed[pl.ds(0, rows), :] = value
        else:
            swap_in[...] = value
        pair_copy(which).start()

    def whole(which):
        pair_copy(which).wait_recv()
        return (
            totals[which][own_part]
            + core_in[which, part_span(side), :].astype(f32)
            + pair_in[which].astype(f32)
        )

    add_cores(0)

    transpose_rows(normed, turned_normed)
    half_chips = layer_chips // 2

    def set_out(array, refs, item, place, sems):
        for order in range(2):
            bit = place % 2 if order == 0 else place // half_chips
            own_bit = layer_chip % 2 if order == 0 else layer_chip // half_chips
            slot = place // 2 if order == 0 else place % half_chips
            block = array.at[pl.ds(order * piece, piece), :]
            goes = pltpu.make_async_copy(block, refs[order].at[item, slot], sems.at[order])
            stays = pltpu.make_async_copy(block, refs[2].at[order, item, slot], sems.at[order])

            @pl.when(bit == own_bit)
            def _():
                stays.start()

            @pl.when(bit != own_bit)
            def _():
                goes.start()

    def set_out_wait(array, refs, sems):
        for order in range(2):
            block = array.at[pl.ds(order * piece, piece), :]
            pltpu.make_async_copy(block, refs[2].at[order, 0, 0], sems.at[order]).wait()

    stages, start, finish, sent, _ = halving_scatter(
        parts, inbox, parts_send, parts_recv, layer_chip, layer_chips, core, tensor_index
    )
    dense_refs = (dense_send0_ref, dense_send1_ref, dense_keep_ref)

    def one_chip(index):
        step, place = index // layer_chips, index % layer_chips
        here = pl.ds(pl.multiple_of(place * pair_rows_count, pair_rows_count), pair_rows_count)
        parts[step, place, :, 0:hidden] = nn(turned_normed[here, :], upper_grad[step]).astype(bf16)
        parts[step, place, :, hidden:] = nn(turned_cot[here, :], active[step]).astype(bf16)

        @pl.when(place == layer_chips - 1)
        def _():
            start(step, 0)

    repeat(steps * layer_chips, one_chip)
    grads = whole(0)
    for number in range(3):
        share_copy(normed, 1, number).wait_send()
    add_cores(1)
    vectors_ref[...] = jnp.zeros_like(vectors_ref)
    vectors_ref[2:3] = column_sum(grads)
    part_grad, gain_part = layer_norm_back(middle[...], gain_ref[...], grads)
    vectors_ref[1:2] = column_sum(gain_part)
    own_cot = cot_ref[...].astype(f32)
    vectors_ref[3:4] = column_sum(own_cot)
    middle_grad = own_cot + part_grad
    middle_grad_ref[...] = middle_grad
    vectors_ref[0:1] = column_sum(middle_grad)
    low_grad[mine, :] = middle_grad.astype(bf16)
    low_swap = swap_copy(low_grad.at[mine], low_grad.at[mine], swap_sem, 5, partner)
    low_swap.start()
    swap_copy(low_grad.at[theirs], low_grad.at[theirs], swap_sem, 5, partner).wait_recv()

    def grads_out(owner, part, pair):
        target = (base + 2 * (2 * core + pair) + (part + flipped(chip, chips)) % 2, owner)
        here = (target[0] == dp_index) & (owner == tensor_index)
        source = outbox.at[owner, part, pair]
        destination = grads_ref.at[chip, tensor_index]
        far = pltpu.make_async_remote_copy(
            src_ref=source,
            dst_ref=destination,
            send_sem=outbox_send.at[owner, part, pair],
            recv_sem=outbox_recv.at[chip, tensor_index],
            device_id=target,
            device_id_type=MESH,
        )
        return here, far, pltpu.make_async_copy(source, destination, local_sem.at[1])

    def send_grads(step):
        owner, part = (tensor_index + 1 + step // 2) % tensor_count, step % 2
        lanes = pl.ds(pl.multiple_of(owner * 128, 128), 128)
        result = nn(low_grad[part_span(part), :], dense[:, lanes]).astype(bf16)
        half = rows // 2
        for pair in range(2):
            cut = slice(pair * HD, (pair + 1) * HD)
            outbox[owner, part, pair] = jnp.concatenate(
                [result[:half, cut], result[half:, cut]], axis=1
            )
            here, far, near = grads_out(owner, part, pair)

            @pl.when(here)
            def _():
                near.start()

            @pl.when(jnp.logical_not(here))
            def _():
                far.start()

    repeat(2 * tensor_count, send_grads)

    def advance(stage):
        for step in range(steps):
            finish(step, stage)
            if stage + 1 < stages:
                start(step, stage + 1)

    advance(0)
    turned_low = turned_cot.at[:, 0 : 2 * rows]
    transpose_rows(low_grad, turned_low)

    def dense_chip(place):
        here = pl.ds(pl.multiple_of(place * pair_rows_count, pair_rows_count), pair_rows_count)
        dense_parts[place] = nn(turned_low[here, :], context[...]).astype(bf16)
        set_out(dense_parts.at[place], dense_refs, 0, place, dense_sem.at[place])

    repeat(layer_chips, dense_chip)
    block_ref[...] = (middle[...] + whole(1) + down_shift_ref[...]).astype(bf16)

    for stage in range(1, stages):
        advance(stage)
    for step in range(steps):
        feed_sum_ref[step] = parts[step, layer_chip]
    repeat(
        layer_chips,
        lambda place: set_out_wait(dense_parts.at[place], dense_refs, dense_sem.at[place]),
    )

    def arrived(step):
        place, owner = step // tensor_count, step % tensor_count
        destination = grads_ref.at[place, owner]
        here = (place == chip) & (owner == tensor_index) & (chip // 2 == core)

        @pl.when(here)
        def _():
            pltpu.make_async_copy(destination, destination, local_sem.at[1]).wait()

        @pl.when(jnp.logical_not(here))
        def _():
            pltpu.make_async_remote_copy(
                src_ref=destination,
                dst_ref=destination,
                send_sem=context_send.at[0, 0],
                recv_sem=outbox_recv.at[place, owner],
                device_id=partner,
                device_id_type=MESH,
            ).wait_recv()

    repeat(chips * tensor_count, arrived)

    def context_sent(step):
        here, far, _near = context_out(step)

        @pl.when(jnp.logical_not(here))
        def _():
            far.wait_send()

    repeat(chips * tensor_count, context_sent)

    def grads_sent(step):
        here, far, _near = grads_out(step // 4, step // 2 % 2, step % 2)

        @pl.when(jnp.logical_not(here))
        def _():
            far.wait_send()

    repeat(4 * tensor_count, grads_sent)

    for step in range(steps):
        for stage in range(stages):
            sent(step, stage)
    for which in range(2):
        core_copy(which).wait_send()
        pair_copy(which).wait_send()
    gather_sent()
    low_swap.wait_send()


def middle_part(
    context, inputs, cotangent, across, vectors, up_shift, feed, weight, dp_count, tensor_count, span
):
    rows, width = inputs.shape
    hidden = feed.shape[2] // 2
    piece = width // dp_count
    steps = tensor_count // 2
    chips, layer_chips = span // 2, dp_count // 2
    dma = pltpu.SemaphoreType.DMA
    vmem = pl.BlockSpec(memory_space=pltpu.VMEM)
    anywhere = pl.BlockSpec(memory_space=pl.ANY)
    dense_part = (piece, 128 * tensor_count)
    return pl.pallas_call(
        functools.partial(middle_kernel, dp_count, tensor_count, span),
        in_specs=[vmem] * 7 + [anywhere],
        out_specs=[vmem] * 3 + [anywhere] * 3 + [vmem] * 2 + [anywhere],
        out_shape=[
            jax.ShapeDtypeStruct((rows, width), bf16),
            jax.ShapeDtypeStruct((rows, width), f32),
            jax.ShapeDtypeStruct((steps, 2 * piece, 2 * hidden), bf16),
            jax.ShapeDtypeStruct((1, layer_chips // 2, *dense_part), bf16),
            jax.ShapeDtypeStruct((1, layer_chips // 2, *dense_part), bf16),
            jax.ShapeDtypeStruct((2, 1, layer_chips // 2, *dense_part), bf16),
            jax.ShapeDtypeStruct((8, width), f32),
            jax.ShapeDtypeStruct((steps, 8, hidden), f32),
            jax.ShapeDtypeStruct((chips, tensor_count, rows // 2, 128), bf16),
        ],
        scratch_shapes=[
            pltpu.VMEM((tensor_count, 2, 2, rows // 2, 128), bf16),
            pltpu.VMEM((2 * rows, 128 * tensor_count), bf16),
            pltpu.VMEM((width, 128 * tensor_count), bf16),
            pltpu.VMEM((steps, layer_chips, 2 * piece, 2 * hidden), bf16),
            pltpu.VMEM((rows, width), f32),
            pltpu.VMEM((4 * rows, width), bf16),
            pltpu.VMEM((4 * rows, width), bf16),
            pltpu.VMEM((width, 4 * rows), bf16),
            pltpu.VMEM((width, 4 * rows), bf16),
            pltpu.VMEM((steps, 4 * rows, hidden), bf16),
            pltpu.VMEM((steps, 4 * rows, hidden), bf16),
            pltpu.VMEM((4, rows, width), f32),
            pltpu.VMEM((4, rows, width), f32),
            pltpu.VMEM((rows, width), bf16),
            pltpu.VMEM((2, 2 * rows, width), bf16),
            pltpu.VMEM((2, rows, width), bf16),
            pltpu.VMEM((2 * rows, width), bf16),
            pltpu.VMEM((tensor_count, 2, 2, rows // 2, 128), bf16),
            pltpu.VMEM((steps, layer_chips, 2 * piece, 2 * hidden), bf16),
            pltpu.VMEM((steps, layer_chips - 1, 2 * piece, 2 * hidden), bf16),
            pltpu.VMEM((layer_chips, 2 * piece, 128 * tensor_count), bf16),
            dma((tensor_count,)),
            dma((2, 8)),
            dma((2, 3)),
            dma((2, 3)),
            dma((chips, tensor_count)),
            dma((tensor_count, 2, 2)),
            dma((tensor_count, 2, 2)),
            dma((chips, tensor_count)),
            dma((2,)),
            dma((steps, layer_chips, 2)),
            dma((steps, layer_chips - 1, 2)),
            dma((steps, layer_chips - 1, 2)),
            dma((steps, layer_chips - 1, 2)),
            dma((layer_chips, 2)),
        ],
        compiler_params=pltpu.CompilerParams(
            collective_id=1, has_side_effects=True, vmem_limit_bytes=62 * 2**20
        ),
        cost_estimate=pl.CostEstimate(
            flops=6 * 2 * 2 * rows * width * hidden * tensor_count,
            bytes_accessed=40_000_000,
            transcendentals=0,
        ),
        name="middle_part",
    )(context, inputs, cotangent, across, vectors, up_shift, feed, weight)


def finish_kernel(
    dp_count,
    tensor_count,
    span,
    dq_ref,
    dkv_ref,
    normed_ref,
    x_ref,
    vectors_in_ref,
    middle_grad_ref,
    vector_grads_ref,
    up_rows_ref,
    feed_sum_ref,
    feed_got_ref,
    dense_keep_ref,
    dense_got0_ref,
    dense_got1_ref,
    weight_ref,
    input_grad_ref,
    weight_grad_ref,
    up_grad_ref,
    down_grad_ref,
    dense_grad_ref,
    early_vectors_ref,
    late_vectors_ref,
    sums_ref,
    weight,
    turned_normed,
    dkv_in,
    outbox,
    mixed_in,
    gathered,
    normed_total,
    swap_out,
    swap_in,
    parts,
    inbox,
    layer_inbox,
    dense_parts,
    dense_inbox,
    dense_layer_inbox,
    last_out,
    last_in,
    last_feed_out,
    last_feed_in,
    last_dense_out,
    last_dense_in,
    late,
    column_sums,
    sums_out,
    sums_in,
    weight_sem,
    dense_load_sem,
    swap_sem,
    dkv_send,
    dkv_recv,
    outbox_send,
    mixed_recv,
    parts_send,
    parts_recv,
    layer_send,
    layer_recv,
    dense_send,
    dense_recv,
    dense_layer_send,
    dense_layer_recv,
    sums_send,
    sums_recv,
    local_sem,
):
    dp_index, tensor_index = lax.axis_index("dp"), lax.axis_index("tensor")
    rows, width = x_ref.shape
    columns = weight.shape[2]
    hidden = up_rows_ref.shape[1]
    core = dp_index % 2
    base = dp_index // span * span
    chip = dp_index % span // 2
    chips = span // 2
    layer_chip, layer_chips = dp_index // 2, dp_count // 2
    pair_rows_count = parts.shape[2]
    piece = pair_rows_count // 2
    partner = (dp_index + 1 - 2 * core, tensor_index)
    part_span = lambda part: pl.ds(pl.multiple_of(part * rows, 64), rows)
    dp_rows = rows * tensor_count
    devices = dp_count * tensor_count
    me = dp_index * tensor_count + tensor_index

    def weight_copy(owner):
        return pltpu.make_async_copy(
            weight_ref.at[owner, :, pl.ds(0, columns)], weight.at[owner], weight_sem.at[owner]
        )

    def loads(parts, inbox, keep_ref, got_refs, sems, item, slot):
        copies = []
        for order in range(2):
            rows_here = pl.ds(order * piece, piece)
            if order == 0:
                place = 2 * slot + layer_chip % 2
            else:
                place = slot + layer_chip // (layer_chips // 2) * (layer_chips // 2)
            copies += [
                pltpu.make_async_copy(
                    keep_ref.at[order, item, slot],
                    parts.at[item, place, rows_here, :],
                    sems.at[item, slot, order],
                ),
                pltpu.make_async_copy(
                    got_refs[order].at[item, slot],
                    inbox.at[item, slot, rows_here, :],
                    sems.at[item, slot, 2 + order],
                ),
            ]
        return copies

    def dense_loads(index):
        return loads(
            dense_parts,
            dense_inbox,
            dense_keep_ref,
            (dense_got0_ref, dense_got1_ref),
            dense_load_sem,
            0,
            index,
        )

    repeat(layer_chips // 2, lambda index: [copy.start() for copy in dense_loads(index)])
    repeat(tensor_count, lambda owner: weight_copy(owner).start())
    greet_all(dp_count, tensor_count, dp_index, tensor_index)

    def dkv_copy(place, whose):
        taken = 2 * place + (whose + flipped(place, chips)) % 2
        return pltpu.make_async_remote_copy(
            src_ref=dkv_ref.at[pl.ds(pl.multiple_of(taken * dp_rows, 128), dp_rows)],
            dst_ref=dkv_in.at[place],
            send_sem=dkv_send.at[place],
            recv_sem=dkv_recv.at[place],
            device_id=partner,
            device_id_type=MESH,
        )

    repeat(chips, lambda place: dkv_copy(place, 1 - core).start())
    place_here = (layer_chip, layer_chips, core, tensor_index)
    stages = layer_chips.bit_length() - 1
    _, dense_start, dense_finish, dense_sent, dense_add = halving_scatter(
        dense_parts, dense_inbox, dense_send, dense_recv, *place_here
    )
    repeat(2, lambda part: normed_total.__setitem__(part, jnp.zeros((rows, width), f32)))
    repeat(chips, lambda place: dkv_copy(place, 1 - core).wait_recv())

    def message(place, owner):
        part = (core + flipped(place, chips)) % 2
        target = (base + 2 * place + chip // 2, owner)
        here = (target[0] == dp_index) & (owner == tensor_index)
        source = outbox.at[place, owner]
        destination = mixed_in.at[tensor_index, chip % 2, part]
        far = pltpu.make_async_remote_copy(
            src_ref=source,
            dst_ref=destination,
            send_sem=outbox_send.at[place, owner],
            recv_sem=mixed_recv.at[tensor_index, chip % 2, part],
            device_id=target,
            device_id_type=MESH,
        )
        return here, far, pltpu.make_async_copy(source, destination, local_sem.at[0])

    def send_message(step):
        owner, place = nearest(tensor_index, tensor_count, step // chips), step % chips
        taken = 2 * place + (core + flipped(place, chips)) % 2
        own = pl.ds(pl.multiple_of(taken * dp_rows + owner * rows, 64), rows)
        total = dkv_ref[own, :].astype(f32) + dkv_in[
            place, pl.ds(pl.multiple_of(owner * rows, 64), rows), :
        ].astype(f32)
        queries = dq_ref[
            pl.ds(pl.multiple_of(place * dp_rows + owner * rows, 64), rows), :
        ].astype(f32)
        outbox[place, owner, 0:rows, :] = jnp.concatenate([queries, total[:, :HD]], axis=1).astype(
            bf16
        )
        half = rows // 2
        outbox[place, owner, rows:, :] = jnp.concatenate(
            [total[:half, HD:], total[half:, HD:]], axis=1
        ).astype(bf16)
        here, far, near = message(place, owner)

        @pl.when(here)
        def _():
            near.start()

        @pl.when(jnp.logical_not(here))
        def _():
            far.start()

    repeat(chips * tensor_count, send_message)

    def dense_layer_copy(step):
        owner = (tensor_index + step) % tensor_count
        return pltpu.make_async_remote_copy(
            src_ref=dense_parts.at[
                0, layer_chip, :, pl.ds(pl.multiple_of(owner * 128, 128), 128)
            ],
            dst_ref=dense_layer_inbox.at[step - 1],
            send_sem=dense_layer_send.at[step - 1],
            recv_sem=dense_layer_recv.at[step - 1],
            device_id=(dp_index, owner),
            device_id_type=MESH,
        )

    repeat(layer_chips // 2, lambda index: [copy.wait() for copy in dense_loads(index)])
    dense_add(0, 0)
    if stages > 1:
        dense_start(0, 1)
    transpose_rows(normed_ref, turned_normed)

    def sum_copy(which, step):
        other = (me + step) % devices
        there = (other // tensor_count, other % tensor_count)
        return pltpu.make_async_remote_copy(
            src_ref=sums_out.at[which, there[0], there[1]],
            dst_ref=sums_in.at[which, dp_index, tensor_index],
            send_sem=sums_send.at[which, there[0], there[1]],
            recv_sem=sums_recv.at[which, dp_index, tensor_index],
            device_id=there,
            device_id_type=MESH,
        )

    def sum_message(which, owner_dp, owner, vector_rows, row, count, vectors):
        block = pl.ds(pl.multiple_of(owner_dp * piece // 128 * 128, 128), 128)
        sums_out[which, owner_dp, owner] = jnp.zeros((8, 128), f32)
        sums_out[which, owner_dp, owner, 0:vector_rows, :] = vectors[0:vector_rows, block]
        for number in range(count):
            sums_out[which, owner_dp, owner, vector_rows + number : vector_rows + number + 1, :] = row[
                :, number * 128 : (number + 1) * 128
            ]

    def send_sums(which, vector_rows, row_of, count, vectors):
        def one(step):
            other = (me + step) % devices
            owner_dp, owner = other // tensor_count, other % tensor_count
            sum_message(which, owner_dp, owner, vector_rows, row_of(owner), count, vectors)

            @pl.when(step > 0)
            def _():
                sum_copy(which, step).start()

        repeat(devices, one)
        sums_in[which, dp_index, tensor_index] = sums_out[which, dp_index, tensor_index]

    send_sums(
        0, 4, lambda owner: up_rows_ref[pl.ds(2 * owner + core, 1), :], hidden // 128, vector_grads_ref
    )

    def layer_copy(step):
        owner = (tensor_index + step) % tensor_count
        return pltpu.make_async_remote_copy(
            src_ref=parts.at[owner, layer_chip],
            dst_ref=layer_inbox.at[step - 1],
            send_sem=layer_send.at[step - 1],
            recv_sem=layer_recv.at[step - 1],
            device_id=(dp_index, owner),
            device_id_type=MESH,
        )

    def tile_of(step):
        return jnp.where(step == 0, tensor_index, nearest(tensor_index, tensor_count, step - 1))

    def chip_copy(step, hop):
        target = (layer_chip + hop) % layer_chips
        return pltpu.make_async_remote_copy(
            src_ref=parts.at[step, target],
            dst_ref=inbox.at[step, hop - 1],
            send_sem=parts_send.at[step, hop - 1],
            recv_sem=parts_recv.at[step, hop - 1],
            device_id=(2 * target + core, tensor_index),
            device_id_type=MESH,
        )

    def hops(body):
        repeat(layer_chips - 1, lambda number: body(number + 1))

    def advance(step):
        tile = tile_of(step - 1)

        @pl.when(step > 0)
        def _():
            hops(lambda hop: chip_copy(tile, hop).wait_recv())
            value = parts[tile, layer_chip].astype(f32)
            for number in range(layer_chips - 1):
                value = value + inbox[tile, number].astype(f32)
            parts[tile, layer_chip] = value.astype(bf16)

            @pl.when(tile != tensor_index)
            def _():
                layer_copy((tile - tensor_index + tensor_count) % tensor_count).start()

    def dense_advance(stage):
        dense_finish(0, stage)
        if stage + 1 < stages:
            dense_start(0, stage + 1)
        else:
            for step in range(1, tensor_count):
                dense_layer_copy(step).start()

    def one_owner(step):
        owner = tile_of(step)
        weight_copy(owner).wait()
        column_sums[owner] = jnp.zeros(column_sums.shape[1:], f32)

        def one_part(part):
            for pair in range(2):
                destination = mixed_in.at[owner, pair, part]
                here = (
                    (owner == tensor_index)
                    & (chip == 2 * core + pair)
                    & ((part + flipped(chip, chips)) % 2 == core)
                )

                @pl.when(here)
                def _():
                    pltpu.make_async_copy(destination, destination, local_sem.at[0]).wait()

                @pl.when(jnp.logical_not(here))
                def _():
                    pltpu.make_async_remote_copy(
                        src_ref=destination,
                        dst_ref=destination,
                        send_sem=outbox_send.at[0, 0],
                        recv_sem=mixed_recv.at[owner, pair, part],
                        device_id=partner,
                        device_id_type=MESH,
                    ).wait_recv()

            pieces_here = []
            for pair in range(2):
                value = mixed_in[owner, pair, part]
                pieces_here += [value[:rows], pair_rows(value[rows:])]
            grads = jnp.concatenate(pieces_here, axis=1)
            gathered[part_span(part), :] = grads
            column_sums[owner, 0:1] += column_sum(grads.astype(f32))
            normed_total[part] += nt(grads, weight[owner])

        repeat(2, one_part)

        def one_chip(place):
            here = pl.ds(pl.multiple_of(place * pair_rows_count, pair_rows_count), pair_rows_count)
            parts[owner, place] = nn(turned_normed[here, :], gathered[...]).astype(bf16)

        repeat(layer_chips, one_chip)
        hops(lambda hop: chip_copy(owner, hop).start())
        advance(step)
        for stage in range(1, stages):

            @pl.when(step == min(stage, tensor_count - 1))
            def _():
                dense_advance(stage)

    repeat(tensor_count, one_owner)

    swap_out[...] = normed_total[1 - core].astype(bf16)
    swap = swap_copy(swap_out, swap_in, swap_sem, 0, partner)
    swap.start()
    advance(tensor_count)
    swap.wait_recv()
    grads = normed_total[core] + swap_in[...].astype(f32)
    part_grad, gain_part = layer_norm_back(x_ref[...].astype(f32), vectors_in_ref[0:1, :], grads)
    input_grad_ref[...] = middle_grad_ref[...] + part_grad
    late[...] = jnp.zeros_like(late)
    late[0:1] = column_sum(gain_part)
    late[1:2] = column_sum(grads)
    send_sums(1, 2, lambda owner: column_sums[owner, 0:1, :], columns // 128, late)

    kept = pl.ds(pl.multiple_of(core * piece, piece), piece)
    given = pl.ds(pl.multiple_of((1 - core) * piece, piece), piece)

    def total(array, arrived, where):
        value = array[tensor_index, layer_chip, where, :].astype(f32)
        for step in range(arrived.shape[0]):
            value = value + arrived[step, where, :].astype(f32)
        return value

    def dense_total(where):
        lanes = pl.ds(pl.multiple_of(tensor_index * 128, 128), 128)
        value = dense_parts[0, layer_chip, where, lanes].astype(f32)
        for step in range(1, tensor_count):
            value = value + dense_layer_inbox[step - 1, where, :].astype(f32)
        return value

    def feed_total(where):
        value = feed_sum_ref[0, where, :].astype(f32)
        for number in range(feed_got_ref.shape[0]):
            value = value + feed_got_ref[number, where, :].astype(f32)
        return value

    last_feed_out[...] = feed_total(given)
    last_feed = swap_copy(last_feed_out, last_feed_in, swap_sem, 2, partner)
    last_feed.start()
    own_total = feed_total(kept)
    my_half = pl.ds(pl.multiple_of(core * hidden, 128), hidden)
    their_half = pl.ds(pl.multiple_of((1 - core) * hidden, 128), hidden)
    up_grad_ref[:, my_half] = own_total[:, :hidden]
    down_grad_ref[my_half, :] = own_total[:, hidden:].T
    for step in range(1, tensor_count):
        dense_layer_copy(step).wait_recv()
    last_dense_out[...] = dense_total(given)
    last_dense = swap_copy(last_dense_out, last_dense_in, swap_sem, 3, partner)
    last_dense.start()
    dense_grad_ref[pl.ds(pl.multiple_of(core * 128, 128), 128), :] = dense_total(kept).T

    for step in range(1, tensor_count):
        layer_copy(step).wait_recv()
    last_out[...] = total(parts, layer_inbox, given)
    last = swap_copy(last_out, last_in, swap_sem, 1, partner)
    last.start()
    weight_grad_ref[:, pl.ds(pl.multiple_of(core * columns, 128), columns)] = total(
        parts, layer_inbox, kept
    )
    last_feed.wait()
    up_grad_ref[:, their_half] = last_feed_in[:, :hidden]
    down_grad_ref[their_half, :] = last_feed_in[:, hidden:].T
    last_dense.wait()
    dense_grad_ref[pl.ds(pl.multiple_of((1 - core) * 128, 128), 128), :] = last_dense_in[...].T
    last.wait()
    weight_grad_ref[:, pl.ds(pl.multiple_of((1 - core) * columns, 128), columns)] = last_in[...]

    for which in range(2):

        def sum_wait(step):
            other = (me + step + 1) % devices
            there = (other // tensor_count, other % tensor_count)
            place = sums_in.at[which, there[0], there[1]]
            pltpu.make_async_remote_copy(
                src_ref=place,
                dst_ref=place,
                send_sem=sums_send.at[which, there[0], there[1]],
                recv_sem=sums_recv.at[which, there[0], there[1]],
                device_id=partner,
                device_id_type=MESH,
            ).wait_recv()

        repeat(devices - 1, sum_wait)
        sums_ref[which] = jnp.zeros(sums_ref.shape[1:], f32)

        def add_one(step):
            owner_dp, owner = step // tensor_count, step % tensor_count
            sums_ref[which, owner_dp % 2] += sums_in[which, owner_dp, owner]

        repeat(devices, add_one)
        vectors = (early_vectors_ref, late_vectors_ref)[which]
        for number in range(vectors.shape[0]):
            vectors[number] = (
                sums_ref[which, 0, number : number + 1] + sums_ref[which, 1, number : number + 1]
            )

    repeat(chips, lambda place: dkv_copy(place, 1 - core).wait_send())

    def message_sent(step):
        here, far, _near = message(step // tensor_count, step % tensor_count)

        @pl.when(jnp.logical_not(here))
        def _():
            far.wait_send()

    repeat(chips * tensor_count, message_sent)
    for stage in range(stages):
        if stage > 0:
            dense_sent(0, stage)
    repeat(tensor_count, lambda step: hops(lambda hop: chip_copy(step, hop).wait_send()))
    for step in range(1, tensor_count):
        layer_copy(step).wait_send()
        dense_layer_copy(step).wait_send()
    for which in range(2):
        repeat(devices - 1, lambda step: sum_copy(which, step + 1).wait_send())
    swap.wait_send()


def finish_part(
    dq,
    dkv,
    normed,
    inputs,
    vectors,
    middle_grad,
    vector_grads,
    up_rows,
    feed_sum,
    feed_got,
    dense_keep,
    dense_got,
    weight,
    dp_count,
    tensor_count,
    span,
):
    rows, width = inputs.shape
    columns = weight.shape[2] - 128
    hidden = up_rows.shape[1]
    piece = width // dp_count
    chips, layer_chips = span // 2, dp_count // 2
    dma = pltpu.SemaphoreType.DMA
    vmem = pl.BlockSpec(memory_space=pltpu.VMEM)
    anywhere = pl.BlockSpec(memory_space=pl.ANY)
    message = (rows * 3 // 2, 128)
    part = (2 * piece, columns)
    dense_part = (2 * piece, dense_keep.shape[4])
    halving = (layer_chips - 1, 2)
    return pl.pallas_call(
        functools.partial(finish_kernel, dp_count, tensor_count, span),
        in_specs=[vmem] * 10 + [anywhere] * 4,
        out_specs=[vmem] * 8,
        out_shape=[
            jax.ShapeDtypeStruct((rows, width), f32),
            jax.ShapeDtypeStruct((piece, 2 * columns), f32),
            jax.ShapeDtypeStruct((piece, 2 * hidden), f32),
            jax.ShapeDtypeStruct((2 * hidden, piece), f32),
            jax.ShapeDtypeStruct((2 * 128, piece), f32),
            jax.ShapeDtypeStruct((4, 1, 128), f32),
            jax.ShapeDtypeStruct((2, 1, 128), f32),
            jax.ShapeDtypeStruct((2, 2, 8, 128), f32),
        ],
        scratch_shapes=[
            pltpu.VMEM((tensor_count, width, columns), bf16),
            pltpu.VMEM((width, 2 * rows), bf16),
            pltpu.VMEM((chips, rows * tensor_count, 128), bf16),
            pltpu.VMEM((chips, tensor_count, *message), bf16),
            pltpu.VMEM((tensor_count, 2, 2, *message), bf16),
            pltpu.VMEM((2 * rows, columns), bf16),
            pltpu.VMEM((2, rows, width), f32),
            pltpu.VMEM((rows, width), bf16),
            pltpu.VMEM((rows, width), bf16),
            pltpu.VMEM((tensor_count, layer_chips, *part), bf16),
            pltpu.VMEM((tensor_count, layer_chips - 1, *part), bf16),
            pltpu.VMEM((tensor_count - 1, *part), bf16),
            pltpu.VMEM((1, layer_chips, *dense_part), bf16),
            pltpu.VMEM((1, layer_chips - 1, *dense_part), bf16),
            pltpu.VMEM((tensor_count - 1, 2 * piece, 128), bf16),
            pltpu.VMEM((piece, columns), f32),
            pltpu.VMEM((piece, columns), f32),
            pltpu.VMEM((piece, 2 * hidden), f32),
            pltpu.VMEM((piece, 2 * hidden), f32),
            pltpu.VMEM((piece, 128), f32),
            pltpu.VMEM((piece, 128), f32),
            pltpu.VMEM((8, width), f32),
            pltpu.VMEM((tensor_count, 8, columns), f32),
            pltpu.VMEM((2, dp_count, tensor_count, 8, 128), f32),
            pltpu.VMEM((2, dp_count, tensor_count, 8, 128), f32),
            dma((tensor_count,)),
            dma((1, layer_chips // 2, 4)),
            dma((2, 4)),
            dma((chips,)),
            dma((chips,)),
            dma((chips, tensor_count)),
            dma((tensor_count, 2, 2)),
            dma((tensor_count, layer_chips - 1)),
            dma((tensor_count, layer_chips - 1)),
            dma((tensor_count - 1,)),
            dma((tensor_count - 1,)),
            dma((1, *halving)),
            dma((1, *halving)),
            dma((tensor_count - 1,)),
            dma((tensor_count - 1,)),
            dma((2, dp_count, tensor_count)),
            dma((2, dp_count, tensor_count)),
            dma((1,)),
        ],
        compiler_params=pltpu.CompilerParams(
            collective_id=2, has_side_effects=True, vmem_limit_bytes=60 * 2**20
        ),
        cost_estimate=pl.CostEstimate(
            flops=2 * 2 * 2 * rows * width * columns * tensor_count,
            bytes_accessed=30_000_000,
            transcendentals=0,
        ),
        name="finish_part",
    )(
        dq,
        dkv,
        normed,
        inputs,
        vectors,
        middle_grad,
        vector_grads,
        up_rows,
        feed_sum,
        feed_got,
        dense_keep,
        *dense_got,
        weight,
    )


def per_device(
    block_in,
    norm1_gain,
    norm1_bias,
    qkv_weight,
    qv_bias,
    dense_weight,
    dense_bias,
    norm2_gain,
    norm2_bias,
    up_weight,
    up_bias,
    down_weight,
    down_bias,
    cotangent,
    seg_parent,
    seg_length,
):
    dp_count, tensor_count = lax.axis_size("dp"), lax.axis_size("tensor")
    dp_index, tensor_index = lax.axis_index("dp"), lax.axis_index("tensor")
    rows, width = block_in.shape
    dp_rows = rows * tensor_count
    span = PAIR_TOKENS // dp_rows
    heads_here = HEADS // tensor_count
    local_index = lax.rem(dp_index, span)
    core = lax.rem(dp_index, 2)

    piece = norm1_gain.shape[0]

    def small_row(value):
        return jnp.pad(value.reshape(1, -1), ((0, 0), (0, 128 - value.size)))

    small = [norm1_gain, norm1_bias, norm2_gain, norm2_bias, dense_bias, down_bias, qv_bias, up_bias]
    small = jnp.pad(jnp.concatenate([small_row(value) for value in small]), ((0, 8), (0, 0)))

    def by_core(value):
        return value.reshape(value.shape[0], 2, -1).transpose(1, 0, 2)

    shard = jnp.concatenate([by_core(qkv_weight), by_core(dense_weight.T)], axis=2)
    feed_shard = jnp.concatenate([by_core(up_weight), by_core(down_weight.T)], axis=2)
    head = tensor_index * heads_here + local_index // 2
    slope = jnp.exp2(-8.0 * (head.astype(f32) + 1.0) / HEADS) / TRUNK
    half = span // 2
    taken = jnp.stack([2 * i + (core + flipped(i, half)) % 2 for i in range(half)])
    block_ids = (
        taken[:, None] * (dp_rows // QUERY_BLOCK)
        + jnp.arange(dp_rows // QUERY_BLOCK, dtype=jnp.int32)[None, :]
    ).reshape(-1)

    across = [(layer, layer + 1 - 2 * (layer % 2)) for layer in range(tensor_count)]
    normed_both, mixed, weight, vectors, up_shift, feed_block = project(
        block_in, small, shard, feed_shard, dp_count, tensor_count, span
    )
    weight = weight.reshape(tensor_count, width, -1)
    feed_block, cotangent = lax.optimization_barrier((feed_block, cotangent))
    cot_across = lax.ppermute(cotangent, "tensor", across)
    feed_far = [
        lax.ppermute(
            feed_block, "tensor", [(layer, (layer + hop) % tensor_count) for layer in range(tensor_count)]
        )
        for hop in range(tensor_count - 2, 0, -2)
    ]
    feed = jnp.stack([feed_block] + feed_far)
    bounds, by_segment, block_list, block_count = pair_tables(
        seg_parent, seg_length, dp_index // span, slope, block_ids
    )
    tables = (block_ids, block_count, block_list, bounds, by_segment)
    packed_context, out_float = attention_forward(*tables, mixed, tensor_count)
    (
        block_out,
        middle_grad,
        feed_sum,
        dense_send0,
        dense_send1,
        dense_keep,
        vector_grads,
        up_shift_part,
        packed_grads,
    ) = middle_part(
        packed_context,
        block_in,
        cotangent,
        cot_across,
        vectors,
        up_shift,
        feed,
        weight,
        dp_count,
        tensor_count,
        span,
    )
    low_bit = [(device, device + 2 - 4 * (device // 2 % 2)) for device in range(dp_count)]
    half_dp = dp_count // 2
    high_bit = [(device, (device + half_dp) % dp_count) for device in range(dp_count)]
    feed_got = jnp.stack(
        [
            lax.ppermute(
                feed_sum[step],
                "tensor",
                [(layer, (layer + 2 * step) % tensor_count) for layer in range(tensor_count)],
            )
            for step in range(1, feed_sum.shape[0])
        ]
    )
    dense_got = (lax.ppermute(dense_send0, "dp", low_bit), lax.ppermute(dense_send1, "dp", high_bit))
    dq, dkv = attention_backward(*tables, mixed, packed_grads, out_float)
    hidden = up_shift_part.shape[2]
    up_part = jnp.zeros((tensor_count, 2, hidden), f32)
    for step in range(up_shift_part.shape[0]):
        owner = lax.rem(tensor_index + step * (tensor_count // up_shift_part.shape[0]), tensor_count)
        up_part = lax.dynamic_update_slice(up_part, up_shift_part[step, :1][None], (owner, core, 0))
    up_rows = up_part.reshape(2 * tensor_count, hidden)
    (
        input_grad,
        qkv_weight_grad,
        up_grad,
        down_grad,
        dense_grad,
        early_vectors,
        late_vectors,
        sums,
    ) = finish_part(
        dq,
        dkv,
        normed_both.reshape(2 * rows, width),
        block_in,
        vectors,
        middle_grad,
        vector_grads,
        up_rows,
        feed_sum,
        feed_got,
        dense_keep,
        dense_got,
        weight,
        dp_count,
        tensor_count,
        span,
    )
    offset = lax.rem(dp_index * piece, 128)

    def own_vector(values, number):
        if piece % 128 == 0:
            return values[number, 0]
        return lax.dynamic_slice_in_dim(values[number, 0], offset, piece, 0)

    def own_matrix(whole, shape):
        return lax.dynamic_slice_in_dim(whole, dp_index * shape[1], shape[1], 1)

    qkv_totals = sums[1, :, 2:5].reshape(heads_here, 3, HD)
    qv_grad = jnp.concatenate([qkv_totals[:, 0], qkv_totals[:, 2]], axis=1)
    up_totals = sums[0, :, 4:].reshape(up_bias.shape[0], 128)
    return (
        block_out,
        input_grad,
        own_vector(late_vectors, 0),
        own_vector(late_vectors, 1),
        qkv_weight_grad,
        own_matrix(qv_grad, qv_bias.shape),
        dense_grad,
        own_vector(early_vectors, 0),
        own_vector(early_vectors, 1),
        own_vector(early_vectors, 2),
        up_grad,
        own_matrix(up_totals, up_bias.shape),
        down_grad,
        own_vector(early_vectors, 3),
    )


def solution(mesh):
    rows = P(("dp", "tensor"), None)
    in_specs = (
        rows,
        P("dp"),
        P("dp"),
        P("dp", "tensor"),
        P("tensor", "dp"),
        P("tensor", "dp"),
        P("dp"),
        P("dp"),
        P("dp"),
        P("dp", "tensor"),
        P("tensor", "dp"),
        P("tensor", "dp"),
        P("dp"),
        rows,
        P(),
        P(),
    )
    out_specs = (
        rows,
        rows,
        P("dp"),
        P("dp"),
        P("dp", "tensor"),
        P("tensor", "dp"),
        P("tensor", "dp"),
        P("dp"),
        P("dp"),
        P("dp"),
        P("dp", "tensor"),
        P("tensor", "dp"),
        P("tensor", "dp"),
        P("dp"),
    )
    return jax.shard_map(
        per_device, mesh=mesh, in_specs=in_specs, out_specs=out_specs, check_vma=False
    )
```

```python
import functools

import jax
import jax.numpy as jnp
from jax import lax
from jax.experimental import pallas as pl
from jax.experimental.pallas import tpu as pltpu
from jax.sharding import PartitionSpec as P

HEADS = 16
HD = 64
TRUNK = 2048
SEG = 256
PAIR_TOKENS = 2 * (TRUNK + 12 * SEG)
PAIR_SEGS = 26
QUERY_BLOCK = 256
KEY_BLOCK = 256
BIG = 2.0**100
VALUE_ROWS = 80

epsilon = 1e-05
f32 = jnp.float32
bf16 = jnp.bfloat16
MESH = pl.DeviceIdType.MESH


def normalize(values, gain_row, bias_row):
    average = jnp.mean(values, axis=-1, keepdims=True)
    centred = values - average
    spread = jnp.mean(centred * centred, axis=-1, keepdims=True)
    return centred * lax.rsqrt(spread + epsilon) * gain_row + bias_row


def nn(left, right):
    return lax.dot_general(left, right, (((1,), (0,)), ((), ())), preferred_element_type=f32)


def nt(left, right):
    return lax.dot_general(left, right, (((1,), (1,)), ((), ())), preferred_element_type=f32)


def tn(left, right):
    return lax.dot_general(left, right, (((0,), (0,)), ((), ())), preferred_element_type=f32)


def pieces(value, count):
    parts = []
    for _ in range(count):
        part = lax.reduce_precision(value, 8, 7)
        parts.append(part)
        value = value - part
    return parts


def pair_tables(seg_parent, seg_length, group, slope, block_ids):
    first = group * PAIR_SEGS
    parent = lax.dynamic_slice_in_dim(seg_parent, first, PAIR_SEGS, 0) - first
    length = lax.dynamic_slice_in_dim(seg_length, first, PAIR_SEGS, 0)
    ids = jnp.arange(PAIR_SEGS, dtype=jnp.int32)
    begin = jnp.sum(jnp.where(ids[None, :] < ids[:, None], length[None, :], 0), axis=1)
    end = begin + length
    is_parent = parent[:, None] == ids[None, :]
    grand = jnp.sum(jnp.where(is_parent, parent[None, :], 0), axis=1)
    is_grand = grand[:, None] == ids[None, :]
    parent_length = jnp.sum(jnp.where(is_parent, length[None, :], 0), axis=1)
    grand_length = jnp.sum(jnp.where(is_grand, length[None, :], 0), axis=1)
    path_start = jnp.where(
        parent == ids, 0, parent_length + jnp.where(grand == parent, 0, grand_length)
    )
    related = is_parent | is_grand | (ids[:, None] == ids[None, :])
    high, low = pieces(slope * (path_start - begin).astype(f32), 2)
    slope_high, slope_low = pieces(slope, 2)
    by_segment = jnp.concatenate(
        [
            jnp.where(related, high[None, :], -BIG),
            jnp.where(related, low[None, :], 0.0),
            jnp.broadcast_to(
                jnp.stack([256.0 * slope_high, 256.0 * slope_low, slope_high, slope_low])[None, :],
                (PAIR_SEGS, 4),
            ),
        ],
        axis=1,
    )
    by_segment = jnp.pad(
        by_segment, ((0, 128 - PAIR_SEGS), (0, 128 - by_segment.shape[1]))
    ).astype(bf16)
    bounds = jnp.pad(jnp.stack([jnp.tile(begin, 2), jnp.tile(end, 2)]), ((0, 6), (0, 128 - 2 * PAIR_SEGS)))
    key_blocks = PAIR_TOKENS // KEY_BLOCK
    q_begin = block_ids * QUERY_BLOCK
    k_begin = jnp.arange(key_blocks, dtype=jnp.int32) * KEY_BLOCK
    q_has = (begin[None, :] < q_begin[:, None] + QUERY_BLOCK) & (end[None, :] > q_begin[:, None])
    k_has = (begin[None, :] < k_begin[:, None] + KEY_BLOCK) & (end[None, :] > k_begin[:, None])
    q_sees = jnp.any(q_has[:, :, None] & related[None], axis=1)
    seen = jnp.any(q_sees[:, None, :] & k_has[None, :, :], axis=2)
    seen = seen & (k_begin[None, :] + KEY_BLOCK <= q_begin[:, None])
    rank = jnp.sum(
        jnp.where(k_begin[None, None, :] < k_begin[None, :, None], seen[:, None, :], False),
        axis=2,
        dtype=jnp.int32,
    )
    slots = jnp.arange(key_blocks + 8, dtype=jnp.int32)
    numbers = jnp.arange(key_blocks, dtype=jnp.int32)
    block_list = jnp.sum(
        jnp.where(
            seen[:, :, None] & (rank[:, :, None] == slots[None, None, :]), numbers[None, :, None], 0
        ),
        axis=1,
    )
    block_count = jnp.sum(seen, axis=1, dtype=jnp.int32)
    return bounds, by_segment, block_list, block_count


def causal_scores(scores, key_first, query_first):
    rows = key_first + lax.broadcasted_iota(jnp.int32, scores.shape, 0)
    columns = query_first + lax.broadcasted_iota(jnp.int32, scores.shape, 1)
    return jnp.where(rows <= columns, scores, -BIG)


def token_lanes(bounds_ref, first, count):
    token = first + lax.broadcasted_iota(jnp.int32, (count, 128), 0)
    lane = lax.broadcasted_iota(jnp.int32, (count, 128), 1)
    member = (token >= bounds_ref[0:1, :]) & (token < bounds_ref[1:2, :])
    base = 2 * PAIR_SEGS
    number = jnp.where(lane < base + 2, lax.shift_right_logical(token, 8), token & 255)
    fixed = jnp.where(lane < base + 7, 1, 0)
    number = jnp.where(lane < base + 4, number, fixed)
    return jnp.where(lane < base, jnp.where(member, 1, 0), number).astype(f32)


def pair_rows(packed):
    return jnp.concatenate([packed[:, :HD], packed[:, HD:]], axis=0)


def build_keys(bounds_ref, mixed_ref, keys, step):
    rows = mixed_ref.shape[1] * 2 // 3
    lane = lax.broadcasted_iota(jnp.int32, (rows, 128), 1)
    for part in range(2):
        first = (2 * step + part) * rows
        both = mixed_ref[2 * step + part, 0:rows, :].astype(f32)
        keys[pl.ds(pl.multiple_of(first, 64), rows), :] = jnp.where(
            lane < HD, token_lanes(bounds_ref, first, rows), both
        ).astype(bf16)


def query_lanes(bounds_ref, by_segment_ref, mixed_ref, number):
    rows = mixed_ref.shape[1] * 2 // 3
    meta = nn(token_lanes(bounds_ref, number * rows, rows).astype(bf16), by_segment_ref[...])
    queries = mixed_ref[number, 0:rows, 0:HD].astype(f32) * 0.125
    return jnp.concatenate([meta[:, :HD], queries], axis=1)


def forward_kernel(
    block_of,
    count_of,
    list_of,
    bounds_ref,
    by_segment_ref,
    mixed_ref,
    context_ref,
    out_ref,
    keys_ref,
    queries_ref,
    keys,
    values_t,
    queries_all,
    scores_a,
    scores_b,
    out_sem,
):
    messages, message_rows, _ = mixed_ref.shape
    rows = message_rows * 2 // 3
    tensor_count = context_ref.shape[1]
    steps = queries_all.shape[0] // QUERY_BLOCK

    def prepare(step, _):
        build_keys(bounds_ref, mixed_ref, keys, step)
        values = jnp.concatenate(
            [pair_rows(mixed_ref[2 * step + part, rows:, :]) for part in range(2)], axis=0
        )
        lane = lax.broadcasted_iota(jnp.int32, (2 * rows, HD), 1)
        ones = jnp.where(lane == 0, 1.0, 0.0).astype(bf16)
        wide = jnp.concatenate([values, ones], axis=1)
        values_t[:, pl.ds(pl.multiple_of(step * 2 * rows, 128), 2 * rows)] = wide.T[:VALUE_ROWS]
        return 0

    lax.fori_loop(0, messages // 2, prepare, 0)
    half = messages // (2 * tensor_count)

    def prepare_queries(step, _):
        number = block_of[(step // tensor_count) * (steps // half)] * QUERY_BLOCK // rows
        number = number + step % tensor_count
        queries_all[pl.ds(pl.multiple_of(step * rows, 64), rows), :] = query_lanes(
            bounds_ref, by_segment_ref, mixed_ref, number
        ).astype(bf16)
        return 0

    lax.fori_loop(0, messages // 2, prepare_queries, 0)
    keys_out = pltpu.make_async_copy(keys, keys_ref, out_sem.at[0])
    queries_out = pltpu.make_async_copy(queries_all, queries_ref, out_sem.at[1])
    keys_out.start()
    queries_out.start()

    def one_block(number, _):
        query_first = block_of[number] * QUERY_BLOCK
        here = pl.ds(pl.multiple_of(number * QUERY_BLOCK, QUERY_BLOCK), QUERY_BLOCK)
        queries = queries_all[here, :]

        count = count_of[number]

        def block_span(step):
            first = pl.multiple_of(list_of[number, step] * KEY_BLOCK, KEY_BLOCK)
            return pl.ds(first, KEY_BLOCK)

        def score_four(buffer, step):
            for part in range(4):
                buffer[part * KEY_BLOCK : (part + 1) * KEY_BLOCK, :] = nt(
                    keys[block_span(4 * step + part), :], queries
                )

        def absorb(scores, spans, carry):
            top, total = carry
            new_top = jnp.maximum(top, jnp.max(scores, axis=0, keepdims=True))
            weights = jnp.exp(scores - new_top).astype(bf16)
            total = total * jnp.exp(top - new_top)
            for part, span in enumerate(spans):
                total = total + nn(
                    values_t[:, span], weights[part * KEY_BLOCK : (part + 1) * KEY_BLOCK]
                )
            return new_top, total

        def absorb_four(buffer, step, carry):
            return absorb(buffer[...], [block_span(4 * step + part) for part in range(4)], carry)

        score_four(scores_a, 0)
        span = pl.ds(pl.multiple_of(query_first, KEY_BLOCK), KEY_BLOCK)
        scores = causal_scores(nt(keys[span, :], queries), query_first, query_first)
        carry = (jnp.full((1, QUERY_BLOCK), -BIG, f32), jnp.zeros((VALUE_ROWS, QUERY_BLOCK), f32))
        carry = absorb(scores, [span], carry)

        def eight_blocks(step, carry):
            score_four(scores_b, 2 * step + 1)
            carry = absorb_four(scores_a, 2 * step, carry)
            score_four(scores_a, 2 * step + 2)
            return absorb_four(scores_b, 2 * step + 1, carry)

        fours = count // 4
        carry = lax.fori_loop(0, fours // 2, eight_blocks, carry)
        carry = lax.fori_loop(
            0, fours % 2, lambda _, kept: absorb_four(scores_a, fours - 1, kept), carry
        )

        def last_blocks(blocks):
            def one(_, kept):
                spans = [block_span(count - count % (2 * blocks) + part) for part in range(blocks)]
                scores = [nt(keys[span, :], queries) for span in spans]
                return absorb(jnp.concatenate(scores, axis=0), spans, kept)

            return one

        carry = lax.fori_loop(0, count % 4 // 2, last_blocks(2), carry)
        top, total = lax.fori_loop(0, count % 2, last_blocks(1), carry)
        row_sum = total[HD : HD + 1]
        log_total = jnp.broadcast_to(top + jnp.log(row_sum), (HD, QUERY_BLOCK))
        out_ref[here, :] = jnp.concatenate([total[:HD] / row_sum, log_total], axis=0).T
        return 0

    lax.fori_loop(0, steps, one_block, 0)

    def pack(step, _):
        first = pl.multiple_of(step * rows, 64)
        half_rows = rows // 2
        context_ref[step // tensor_count, step % tensor_count] = jnp.concatenate(
            [
                out_ref[pl.ds(first, half_rows), 0:HD],
                out_ref[pl.ds(pl.multiple_of(first + half_rows, 32), half_rows), 0:HD],
            ],
            axis=1,
        ).astype(bf16)
        return 0

    lax.fori_loop(0, messages // 2, pack, 0)
    keys_out.wait()
    queries_out.wait()


def attention_forward(blocks, counts, lists, bounds, by_segment, mixed, tensor_count):
    messages, message_rows, _ = mixed.shape
    rows = message_rows * 2 // 3
    half = messages // 2 * rows
    smem = pl.BlockSpec(memory_space=pltpu.SMEM)
    vmem = pl.BlockSpec(memory_space=pltpu.VMEM)
    return pl.pallas_call(
        forward_kernel,
        in_specs=[smem] * 3 + [vmem] * 3,
        out_specs=[vmem, vmem] + [pl.BlockSpec(memory_space=pltpu.HBM)] * 2,
        out_shape=[
            jax.ShapeDtypeStruct(
                (messages // 2 // tensor_count, tensor_count, rows // 2, 2 * HD), bf16
            ),
            jax.ShapeDtypeStruct((half, 128), f32),
            jax.ShapeDtypeStruct((PAIR_TOKENS, 128), bf16),
            jax.ShapeDtypeStruct((half, 128), bf16),
        ],
        scratch_shapes=[
            pltpu.VMEM((PAIR_TOKENS, 128), bf16),
            pltpu.VMEM((VALUE_ROWS, PAIR_TOKENS), bf16),
            pltpu.VMEM((half, 128), bf16),
            pltpu.VMEM((4 * KEY_BLOCK, QUERY_BLOCK), f32),
            pltpu.VMEM((4 * KEY_BLOCK, QUERY_BLOCK), f32),
            pltpu.SemaphoreType.DMA((2,)),
        ],
        compiler_params=pltpu.CompilerParams(vmem_limit_bytes=40 * 2**20),
        cost_estimate=pl.CostEstimate(
            flops=2 * 256 * 2 * 12_000_000, bytes_accessed=10_000_000, transcendentals=12_000_000
        ),
        name="attention_forward",
    )(blocks, counts, lists, bounds, by_segment, mixed)


def backward_kernel(
    block_of,
    count_of,
    list_of,
    keys,
    forward_queries,
    mixed_ref,
    grads_ref,
    out_ref,
    dq_ref,
    dkv_ref,
    keys_t,
    values,
    queries_all,
    grads_all,
    queries_only,
    grads_only,
    dkv,
):
    messages, message_rows, _ = mixed_ref.shape
    rows = message_rows * 2 // 3
    tensor_count = grads_ref.shape[1]
    steps = queries_all.shape[0] // QUERY_BLOCK
    half = messages // (2 * tensor_count)

    def with_pieces(value, first_lane, wide):
        lane = lax.broadcasted_iota(jnp.int32, wide.shape, 1)
        for piece in range(3):
            part = value.astype(bf16).astype(f32)
            wide = jnp.where(lane == first_lane + piece, part, wide)
            value = value - part
        return wide

    def prepare(step, _):
        span = pl.ds(pl.multiple_of(step * 2 * rows, 128), 2 * rows)
        keys_t[:, span] = keys[span, :].T[HD:]
        packed = jnp.concatenate(
            [pair_rows(mixed_ref[2 * step + part, rows:, :]) for part in range(2)], axis=0
        )
        lane = lax.broadcasted_iota(jnp.int32, (2 * rows, HD), 1)
        ones = jnp.where(lane < 3, 1.0, 0.0).astype(bf16)
        values[span, :] = jnp.concatenate([ones, packed], axis=1)
        dkv[span, :] = jnp.zeros((2 * rows, 128), f32)
        return 0

    lax.fori_loop(0, messages // 2, prepare, 0)

    def prepare_queries(step, _):
        number = block_of[(step // tensor_count) * (steps // half)] * QUERY_BLOCK // rows
        number = number + step % tensor_count
        span = pl.ds(pl.multiple_of(step * rows, 64), rows)
        wide = forward_queries[span, :].astype(f32)
        out = out_ref[span, :]
        queries_all[span, :] = with_pieces(-out[:, HD : HD + 1], 2 * PAIR_SEGS + 4, wide).astype(bf16)
        lane = lax.broadcasted_iota(jnp.int32, (rows, 128), 1)
        queries = mixed_ref[number, 0:rows, :].astype(f32) * 0.125
        queries_only[span, :] = jnp.where(lane < HD, queries, 0.0).astype(bf16)
        grads = pair_rows(grads_ref[step // tensor_count, step % tensor_count].astype(f32))
        inner = jnp.sum(grads * out[:, :HD], axis=1, keepdims=True)
        wide = jnp.concatenate([jnp.zeros((rows, HD), f32), grads], axis=1)
        grads_only[span, :] = wide.astype(bf16)
        grads_all[span, :] = with_pieces(-inner, 0, wide).astype(bf16)
        return 0

    lax.fori_loop(0, messages // 2, prepare_queries, 0)

    def one_block(number, _):
        query_first = block_of[number] * QUERY_BLOCK
        here = pl.ds(pl.multiple_of(number * QUERY_BLOCK, QUERY_BLOCK), QUERY_BLOCK)
        queries = queries_all[here, :]
        grads = grads_all[here, :]
        both = jnp.concatenate([queries_only[here, :], grads_only[here, :]], axis=0)

        count = count_of[number]

        def attend(blocks, dq, masked):
            spans = [pl.ds(pl.multiple_of(block * KEY_BLOCK, KEY_BLOCK), KEY_BLOCK) for block in blocks]
            scores = [nt(keys[span, :], queries) for span in spans]
            if masked:
                scores = [causal_scores(scores[0], blocks[0] * KEY_BLOCK, query_first)]
            grads_of = [nt(values[span, :], grads) for span in spans]
            for span, score, grad in zip(spans, scores, grads_of):
                weights = jnp.exp(score)
                score_grad = (weights * grad).astype(bf16)
                dkv[span, :] += nn(
                    jnp.concatenate([score_grad, weights.astype(bf16)], axis=1), both
                )
                dq = dq + nn(keys_t[:, span], score_grad)
            return dq

        def listed(first, blocks):
            return lambda step, kept: attend(
                [list_of[number, first + blocks * step + part] for part in range(blocks)], kept, False
            )

        dq = attend([query_first // KEY_BLOCK], jnp.zeros((HD, QUERY_BLOCK), f32), True)
        eights, rest = count // 8, count % 8
        dq = lax.fori_loop(0, eights, listed(0, 8), dq)
        dq = lax.fori_loop(0, rest // 4, listed(8 * eights, 4), dq)
        dq = lax.fori_loop(0, rest % 4 // 2, listed(count - rest % 4, 2), dq)
        dq = lax.fori_loop(0, rest % 2, listed(count - 1, 1), dq)
        dq_ref[here, :] = (dq * 0.125).T.astype(bf16)
        return 0

    lax.fori_loop(0, steps, one_block, 0)

    def write(step, _):
        span = pl.ds(pl.multiple_of(step * KEY_BLOCK, KEY_BLOCK), KEY_BLOCK)
        dkv_ref[span, :] = dkv[span, :].astype(bf16)
        return 0

    lax.fori_loop(0, PAIR_TOKENS // KEY_BLOCK, write, 0)


def attention_backward(blocks, counts, lists, keys, queries, mixed, grads, out):
    smem = pl.BlockSpec(memory_space=pltpu.SMEM)
    vmem = pl.BlockSpec(memory_space=pltpu.VMEM)
    half = out.shape[0]
    return pl.pallas_call(
        backward_kernel,
        in_specs=[smem] * 3 + [vmem] * 5,
        out_specs=[vmem, vmem],
        out_shape=[
            jax.ShapeDtypeStruct((half, HD), bf16),
            jax.ShapeDtypeStruct((PAIR_TOKENS, 128), bf16),
        ],
        scratch_shapes=[
            pltpu.VMEM((HD, PAIR_TOKENS), bf16),
            pltpu.VMEM((PAIR_TOKENS, 128), bf16),
            pltpu.VMEM((half, 128), bf16),
            pltpu.VMEM((half, 128), bf16),
            pltpu.VMEM((half, 128), bf16),
            pltpu.VMEM((half, 128), bf16),
            pltpu.VMEM((PAIR_TOKENS, 128), f32),
        ],
        compiler_params=pltpu.CompilerParams(vmem_limit_bytes=56 * 2**20),
        cost_estimate=pl.CostEstimate(
            flops=5 * 256 * 2 * 12_000_000, bytes_accessed=16_000_000, transcendentals=12_000_000
        ),
        name="attention_backward",
    )(blocks, counts, lists, keys, queries, mixed, grads, out)


def flipped(chip, chips):
    return (chip + chips - 1) // chips


def greet_all(dp_count, tensor_count, dp_index, tensor_index):
    barrier = pltpu.get_barrier_semaphore()
    total = dp_count * tensor_count
    me = dp_index * tensor_count + tensor_index

    def greet(step, _):
        other = (me + step) % total
        pl.semaphore_signal(
            barrier,
            inc=1,
            device_id=(other // tensor_count, other % tensor_count),
            device_id_type=MESH,
        )
        return 0

    lax.fori_loop(1, total, greet, 0)
    pl.semaphore_wait(barrier, total - 1)


def repeat(count, body):
    def one(step, _):
        body(step)
        return 0

    lax.fori_loop(0, count, one, 0)


def swap_copy(source, target, sems, number, partner):
    return pltpu.make_async_remote_copy(
        src_ref=source,
        dst_ref=target,
        send_sem=sems.at[0, number],
        recv_sem=sems.at[1, number],
        device_id=partner,
        device_id_type=MESH,
    )


def layer_norm_back(values, gain, grads):
    average = jnp.mean(values, axis=-1, keepdims=True)
    centred = values - average
    scale = lax.rsqrt(jnp.mean(centred * centred, axis=-1, keepdims=True) + epsilon)
    normed = centred * scale
    scaled = grads * gain
    first = jnp.mean(scaled, axis=-1, keepdims=True)
    second = jnp.mean(scaled * normed, axis=-1, keepdims=True)
    return (scaled - first - normed * second) * scale, grads * normed


def column_sum(values):
    return jnp.sum(values, axis=0, keepdims=True)


def transpose_rows(source, target):
    size = min(256, target.shape[0])

    def one(step):
        span = pl.ds(pl.multiple_of(step * size, size), size)
        target[span, :] = source[:, span].T

    repeat(target.shape[0] // size, one)


def nearest(layer, layers, step):
    tile = 0 * layer
    for here in range(layers):
        order = sorted(
            range(layers),
            key=lambda there: (there == here, abs(there - here), abs(2 * there - layers + 1)),
        )
        for number, there in enumerate(order):
            tile = jnp.where((layer == here) & (step == number), there, tile)
    return tile


def doubling_gather(
    weight, recv_sem, send_sem, layer_recv, layer_send, chip, chips, core, layer, layers, dp_index
):
    stages = chips.bit_length() - 1
    steps = weight.shape[0]
    slot_of = (lambda step: step) if layer_recv is None else (lambda step: nearest(layer, layers, step))

    def layer_copy(tile, way):
        block = weight.at[tile, chip]
        return pltpu.make_async_remote_copy(
            src_ref=block,
            dst_ref=block,
            send_sem=layer_send.at[tile, way],
            recv_sem=layer_recv.at[tile],
            device_id=(dp_index, layer + 2 * way - 1),
            device_id_type=MESH,
        )

    def ways(tile, body):
        for way in range(2):
            inside = (layer + 1 < layers) & (tile <= layer) if way else (layer > 0) & (tile >= layer)

            @pl.when(inside)
            def _():
                body(layer_copy(tile, way))

    def spread():
        ways(layer, lambda copy: copy.start())

    rows = weight.shape[2] // 2

    def half(order):
        return pl.ds(pl.multiple_of(order * rows, rows), rows)

    def place(order, stage, step):
        size = jnp.where(order == 0, 2**stage, chips // 2 ** (stage + 1))
        bit = chip // size % 2
        across = size * (1 - 2 * bit)
        held = jnp.where(
            order == 0,
            chip // 2**stage * 2**stage + step,
            chip % (chips // 2**stage) + step * (chips // 2**stage),
        )
        return held, held + across, chip + across

    def copy(step, stage, order, number):
        slot = slot_of(step)
        held, _, partner = place(order, stage, number)
        block = weight.at[slot, held, half(order), :]
        return pltpu.make_async_remote_copy(
            src_ref=block,
            dst_ref=block,
            send_sem=send_sem.at[slot, 2**stage - 1 + number, order],
            recv_sem=recv_sem.at[slot, held, order],
            device_id=(2 * partner + core, layer),
            device_id_type=MESH,
        )

    def wait_block(block, sem):
        pltpu.make_async_remote_copy(
            src_ref=block,
            dst_ref=block,
            send_sem=send_sem.at[0, 0, 0],
            recv_sem=sem,
            device_id=(2 * chip + 1 - core, layer),
            device_id_type=MESH,
        ).wait_recv()

    def each(stage, body):
        repeat(2 * 2**stage, lambda number: body(number % 2, number // 2))

    def arrived(step, stage):
        slot = slot_of(step)

        def one(order, number):
            _, got, _ = place(order, stage, number)
            wait_block(weight.at[slot, got, half(order), :], recv_sem.at[slot, got, order])

        each(stage, one)

    def advance(number):
        for stage in range(stages):
            step = number - stage

            @pl.when((step >= 0) & (step < steps))
            def _():
                if stage > 0:
                    arrived(step, stage - 1)
                else:

                    if layer_recv is not None:

                        tile = slot_of(step)

                        @pl.when(tile != layer)
                        def _():
                            wait_block(weight.at[tile, chip], layer_recv.at[tile])
                            ways(tile, lambda copy: copy.start())

                each(stage, lambda order, each_number: copy(step, stage, order, each_number).start())

    def ready(step):
        arrived(step, stages - 1)

    def sent():
        if layer_send is not None:
            repeat(steps, lambda tile: ways(tile, lambda copy: copy.wait_send()))

        def one(step):
            for stage in range(stages):
                each(
                    stage,
                    lambda order, number: copy(step, stage, order, number).wait_send(),
                )

        repeat(steps, one)

    return spread, advance, ready, sent


def picked(rows, lanes, owner_of, lane_of, keep):
    lane = lax.broadcasted_iota(jnp.int32, (128, lanes), 1)
    source = lax.broadcasted_iota(jnp.int32, (128, lanes), 0)
    spread = nn(rows.astype(bf16), jnp.where(source == lane_of(lane), 1.0, 0.0).astype(bf16))
    lane = lax.broadcasted_iota(jnp.int32, (rows.shape[0], lanes), 1)
    owner = lax.broadcasted_iota(jnp.int32, (rows.shape[0], lanes), 0)
    return column_sum(jnp.where((owner == owner_of(lane)) & keep(lane), spread, 0.0))


def project_kernel(
    dp_count,
    tensor_count,
    span,
    x_ref,
    small_ref,
    shard_ref,
    feed_ref,
    normed_ref,
    mixed_ref,
    weight_out_ref,
    vectors_ref,
    up_shift_ref,
    block_ref,
    normed,
    weight,
    smalls,
    outbox,
    swap_sem,
    small_send,
    small_recv,
    half_sem,
    gather_recv,
    gather_send,
    layer_recv,
    layer_send,
    out_sem,
    send_sem,
    recv_sem,
    local_sem,
    pass_send,
    pass_recv,
):
    dp_index, tensor_index = lax.axis_index("dp"), lax.axis_index("tensor")
    rows, width = x_ref.shape
    hidden = weight.shape[3]
    columns = hidden - 128
    piece = shard_ref.shape[1]
    core = dp_index % 2
    base = dp_index // span * span
    chip = dp_index % span // 2
    chips = span // 2
    layer_chip, layer_chips = dp_index // 2, dp_count // 2
    partner = (dp_index + 1 - 2 * core, tensor_index)
    total = dp_count * tensor_count
    me = dp_index * tensor_count + tensor_index

    def small_copy(step):
        other = (me + step) % total
        place = smalls.at[dp_index, tensor_index]
        return pltpu.make_async_remote_copy(
            src_ref=place,
            dst_ref=place,
            send_sem=small_send.at[other // tensor_count, other % tensor_count],
            recv_sem=small_recv.at[dp_index, tensor_index],
            device_id=(other // tensor_count, other % tensor_count),
            device_id_type=MESH,
        )

    def small_wait(step):
        other = (me + step) % total
        there = other // tensor_count, other % tensor_count
        place = smalls.at[there[0], there[1]]
        pltpu.make_async_remote_copy(
            src_ref=place,
            dst_ref=place,
            send_sem=small_send.at[there[0], there[1]],
            recv_sem=small_recv.at[there[0], there[1]],
            device_id=partner,
            device_id_type=MESH,
        ).wait_recv()

    own_rows = pl.ds(pl.multiple_of(core * piece, piece), piece)
    smalls[dp_index, tensor_index] = small_ref[...]
    weight[tensor_index, layer_chip, own_rows, :] = shard_ref[core]
    greet_all(dp_count, tensor_count, dp_index, tensor_index)
    half = pltpu.make_async_remote_copy(
        src_ref=shard_ref.at[1 - core],
        dst_ref=weight.at[tensor_index, layer_chip, own_rows, :],
        send_sem=half_sem.at[0],
        recv_sem=half_sem.at[1],
        device_id=partner,
        device_id_type=MESH,
    )
    half.start()
    block_ref[own_rows, :] = feed_ref[core]
    feed_half = pltpu.make_async_remote_copy(
        src_ref=feed_ref.at[1 - core],
        dst_ref=block_ref.at[own_rows, :],
        send_sem=half_sem.at[2],
        recv_sem=half_sem.at[3],
        device_id=partner,
        device_id_type=MESH,
    )
    feed_half.start()
    repeat(total - 1, lambda step: small_copy(step + 1).start())
    spread, advance, ready, gather_sent = doubling_gather(
        weight,
        gather_recv,
        gather_send,
        layer_recv,
        layer_send,
        layer_chip,
        layer_chips,
        core,
        tensor_index,
        tensor_count,
        dp_index,
    )
    half.wait_recv()
    spread()
    repeat(total - 1, lambda step: small_wait(step + 1))

    def vector(number):
        here = smalls[:, tensor_index].astype(f32)[:, number, :]
        return picked(
            here, width, lambda lane: lane // piece, lambda lane: lane % piece, lambda lane: lane >= 0
        )

    normed[core] = normalize(x_ref[...].astype(f32), vector(0), vector(1)).astype(bf16)
    swap = pltpu.make_async_remote_copy(
        src_ref=normed.at[core],
        dst_ref=normed.at[core],
        send_sem=swap_sem.at[0],
        recv_sem=swap_sem.at[1],
        device_id=partner,
        device_id_type=MESH,
    )
    swap.start()
    stages = layer_chips.bit_length() - 1
    for number in range(stages):
        advance(number)
    vectors_ref[...] = jnp.zeros_like(vectors_ref)
    for number in (0, 2, 3, 4, 5):
        vectors_ref[number : number + 1, :] = vector(number)

    bias_width = 2 * HD // dp_count

    def qkv_shift(owner):
        here = smalls[:, owner].astype(f32)[:, 6, :]

        def column(lane):
            return lane % HD + jnp.where(lane % (3 * HD) < HD, 0, HD)

        return picked(
            here,
            columns,
            lambda lane: column(lane) // bias_width,
            lambda lane: (2 * core + lane // (3 * HD)) * bias_width + column(lane) % bias_width,
            lambda lane: (lane % (3 * HD) < HD) | (lane % (3 * HD) >= 2 * HD),
        )

    def up_shift(owner):
        here = smalls[:, owner].astype(f32)[:, 7, :]
        return picked(
            here,
            hidden,
            lambda lane: lane % 128 // bias_width,
            lambda lane: (core * (hidden // 128) + lane // 128) * bias_width
            + lane % 128 % bias_width,
            lambda lane: lane >= 0,
        )

    swap.wait_recv()

    def out_copy(owner):
        return pltpu.make_async_copy(weight.at[owner], weight_out_ref.at[owner], out_sem.at[owner])

    def slot(place_dp, place_tensor):
        return mixed_ref.at[place_dp * tensor_count + place_tensor]

    def send(owner, part, pair):
        head_chip = 2 * core + pair
        target = (base + 2 * head_chip + (part + flipped(chip, chips)) % 2, owner)
        here = (target[0] == dp_index) & (owner == tensor_index)
        return here, pltpu.make_async_remote_copy(
            src_ref=outbox.at[owner, part, pair],
            dst_ref=slot(2 * chip + part, tensor_index),
            send_sem=send_sem.at[owner, part, pair],
            recv_sem=recv_sem.at[chip, tensor_index],
            device_id=target,
            device_id_type=MESH,
        ), pltpu.make_async_copy(
            outbox.at[owner, part, pair], slot(2 * chip + part, tensor_index), local_sem.at[0]
        )

    def one_tile(step):
        owner = nearest(tensor_index, tensor_count, step)
        advance(step + stages)
        ready(step)
        out_copy(owner).start()
        shift = qkv_shift(owner)
        up_shift_ref[owner] = jnp.broadcast_to(up_shift(owner), up_shift_ref.shape[1:])

        def one_part(part):
            matrix = weight[owner, :, :, 0:columns].reshape(width, columns)
            result = nn(normed[part], matrix) + shift
            first = [result[:, 0:128], result[:, 192:320]]
            last = [result[:, 128:192], result[:, 320:384]]
            for pair in range(2):
                outbox[owner, part, pair, 0:rows, :] = first[pair].astype(bf16)
                outbox[owner, part, pair, rows:, :] = jnp.concatenate(
                    [last[pair][: rows // 2], last[pair][rows // 2 :]], axis=1
                ).astype(bf16)
                here, far, near = send(owner, part, pair)

                @pl.when(here)
                def _():
                    near.start()

                @pl.when(jnp.logical_not(here))
                def _():
                    far.start()

        repeat(2, one_part)

    repeat(tensor_count, one_tile)
    normed_ref[...] = normed[...]

    def arrival(step):
        from_chip, from_tensor = step % chips, nearest(tensor_index, tensor_count, step // chips)
        mine = slot(2 * from_chip + (core + flipped(from_chip, chips)) % 2, from_tensor)
        theirs = slot(2 * from_chip + (core + flipped(from_chip, chips) + 1) % 2, from_tensor)
        here = (from_chip == chip) & (from_tensor == tensor_index) & (chip // 2 == core)

        def passing(place):
            return pltpu.make_async_remote_copy(
                src_ref=place,
                dst_ref=place,
                send_sem=pass_send.at[from_chip, from_tensor],
                recv_sem=pass_recv.at[from_chip, from_tensor],
                device_id=partner,
                device_id_type=MESH,
            )

        return mine, theirs, here, passing, from_chip, from_tensor

    def hand_on(step):
        mine, _theirs, here, passing, from_chip, from_tensor = arrival(step)

        @pl.when(here)
        def _():
            pltpu.make_async_copy(mine, mine, local_sem.at[0]).wait()

        @pl.when(jnp.logical_not(here))
        def _():
            pltpu.make_async_remote_copy(
                src_ref=mine,
                dst_ref=mine,
                send_sem=pass_send.at[from_chip, from_tensor],
                recv_sem=recv_sem.at[from_chip, from_tensor],
                device_id=partner,
                device_id_type=MESH,
            ).wait_recv()

        passing(mine).start()

    repeat(chips * tensor_count, hand_on)

    def finish(step):
        mine, theirs, _here, passing, _a, _b = arrival(step)
        passing(mine).wait_send()
        passing(theirs).wait_recv()

    repeat(chips * tensor_count, finish)

    def sent(step):
        here, far, _near = send(step // 4, step // 2 % 2, step % 2)

        @pl.when(jnp.logical_not(here))
        def _():
            far.wait_send()

    repeat(4 * tensor_count, sent)
    repeat(total - 1, lambda step: small_copy(step + 1).wait_send())
    repeat(tensor_count, lambda owner: out_copy(owner).wait())
    half.wait_send()
    feed_half.wait()
    swap.wait_send()
    gather_sent()


def project(inputs, small, shard, feed, dp_count, tensor_count, span):
    rows, width = inputs.shape
    _, piece, hidden = shard.shape
    messages = span * tensor_count
    chips, layer_chips = span // 2, dp_count // 2
    dma = pltpu.SemaphoreType.DMA
    vmem = pl.BlockSpec(memory_space=pltpu.VMEM)
    anywhere = pl.BlockSpec(memory_space=pl.ANY)
    weight = (tensor_count, layer_chips, 2 * piece, hidden)
    return pl.pallas_call(
        functools.partial(project_kernel, dp_count, tensor_count, span),
        in_specs=[vmem] * 4,
        out_specs=[vmem, anywhere, pl.BlockSpec(memory_space=pltpu.HBM), vmem, vmem, vmem],
        out_shape=[
            jax.ShapeDtypeStruct((2, rows, width), bf16),
            jax.ShapeDtypeStruct((messages, rows * 3 // 2, 128), bf16),
            jax.ShapeDtypeStruct(weight, bf16),
            jax.ShapeDtypeStruct((8, width), f32),
            jax.ShapeDtypeStruct((tensor_count, 8, hidden), f32),
            jax.ShapeDtypeStruct((2 * piece, feed.shape[2]), bf16),
        ],
        scratch_shapes=[
            pltpu.VMEM((2, rows, width), bf16),
            pltpu.VMEM(weight, bf16),
            pltpu.VMEM((dp_count, tensor_count, 16, 128), bf16),
            pltpu.VMEM((tensor_count, 2, 2, rows * 3 // 2, 128), bf16),
            dma((2,)),
            dma((dp_count, tensor_count)),
            dma((dp_count, tensor_count)),
            dma((4,)),
            dma((tensor_count, layer_chips, 2)),
            dma((tensor_count, layer_chips - 1, 2)),
            dma((tensor_count,)),
            dma((tensor_count, 2)),
            dma((tensor_count,)),
            dma((tensor_count, 2, 2)),
            dma((chips, tensor_count)),
            dma((1,)),
            dma((chips, tensor_count)),
            dma((chips, tensor_count)),
        ],
        compiler_params=pltpu.CompilerParams(
            collective_id=0, has_side_effects=True, vmem_limit_bytes=40 * 2**20
        ),
        cost_estimate=pl.CostEstimate(
            flops=2 * 2 * rows * width * hidden * tensor_count,
            bytes_accessed=20_000_000,
            transcendentals=0,
        ),
        name="project",
    )(inputs, small, shard, feed)


def halving_scatter(parts, inbox, send_sem, recv_sem, chip, chips, core, layer):
    stages = chips.bit_length() - 1
    rows = parts.shape[2] // 2

    def places(order, stage, step):
        size = jnp.where(order == 0, 2**stage, chips // 2 ** (stage + 1))
        bit = chip // size % 2
        low, high = chip % size, chip // (2 * size) * (2 * size)
        rest = jnp.where(order == 0, low + step * 2 * size, high + step)
        theirs = rest + (1 - bit) * size
        return theirs, rest + bit * size, chip + (1 - 2 * bit) * size

    def half(order):
        return pl.ds(pl.multiple_of(order * rows, rows), rows)

    def copy(item, stage, order, step):
        theirs, _, partner = places(order, stage, step)
        where = chips - chips // 2**stage + step
        return pltpu.make_async_remote_copy(
            src_ref=parts.at[item, theirs, half(order), :],
            dst_ref=inbox.at[item, where, half(order), :],
            send_sem=send_sem.at[item, where, order],
            recv_sem=recv_sem.at[item, where, order],
            device_id=(2 * partner + core, layer),
            device_id_type=MESH,
        )

    def each(stage, body):
        count = chips // 2 ** (stage + 1)
        repeat(2 * count, lambda number: body(number % 2, number // 2))

    def start(item, stage):
        each(stage, lambda order, step: copy(item, stage, order, step).start())

    def finish(item, stage):
        def one(order, step):
            copy(item, stage, order, step).wait_recv()
            _, keep, _ = places(order, stage, step)
            where = chips - chips // 2**stage + step
            parts[item, keep, half(order), :] = (
                parts[item, keep, half(order), :].astype(f32)
                + inbox[item, where, half(order), :].astype(f32)
            ).astype(bf16)

        each(stage, one)

    def add(item, stage):
        def one(order, step):
            _, keep, _ = places(order, stage, step)
            where = chips - chips // 2**stage + step
            parts[item, keep, half(order), :] = (
                parts[item, keep, half(order), :].astype(f32)
                + inbox[item, where, half(order), :].astype(f32)
            ).astype(bf16)

        each(stage, one)

    def sent(item, stage):
        each(stage, lambda order, step: copy(item, stage, order, step).wait_send())

    return stages, start, finish, sent, add


def middle_kernel(
    dp_count,
    tensor_count,
    span,
    context_ref,
    x_ref,
    cot_ref,
    cot_across_ref,
    vectors_in_ref,
    up_shift_ref,
    feed_ref,
    weight_ref,
    block_ref,
    middle_grad_ref,
    feed_sum_ref,
    dense_send0_ref,
    dense_send1_ref,
    dense_keep_ref,
    vectors_ref,
    up_shift_grad_ref,
    grads_ref,
    context_in,
    context,
    dense,
    feed,
    middle,
    normed,
    cot,
    turned_normed,
    turned_cot,
    active,
    upper_grad,
    out_total,
    normed_total,
    swap_in,
    core_in,
    pair_in,
    low_grad,
    outbox,
    parts,
    inbox,
    dense_parts,
    weight_sem,
    swap_sem,
    share_send,
    share_recv,
    context_send,
    context_recv,
    outbox_send,
    outbox_recv,
    local_sem,
    gather_recv,
    gather_send,
    parts_send,
    parts_recv,
    dense_sem,
):
    dp_index, tensor_index = lax.axis_index("dp"), lax.axis_index("tensor")
    rows, width = x_ref.shape
    hidden = active.shape[2]
    steps = feed.shape[0]
    core = dp_index % 2
    base = dp_index // span * span
    chip = dp_index % span // 2
    chips = span // 2
    layer_chip, layer_chips = dp_index // 2, dp_count // 2
    pair_rows_count = parts.shape[2]
    piece = pair_rows_count // 2
    side = tensor_index % 2
    partner = (dp_index + 1 - 2 * core, tensor_index)
    across = (dp_index, tensor_index + 1 - 2 * side)
    own_part = 2 * side + core
    part_span = lambda part: pl.ds(pl.multiple_of(part * rows, 64), rows)
    mine, theirs = part_span(core), part_span(1 - core)

    def dense_copy(owner):
        return pltpu.make_async_copy(
            weight_ref.at[owner, :, pl.ds(weight_ref.shape[2] - 128, 128)],
            dense.at[:, pl.ds(pl.multiple_of(owner * 128, 128), 128)],
            weight_sem.at[owner],
        )

    repeat(tensor_count, lambda owner: dense_copy(owner).start())
    gain_ref, bias_ref, dense_shift_ref, down_shift_ref = (
        vectors_in_ref.at[number : number + 1] for number in range(2, 6)
    )
    across_part = own_part + 2 - 4 * side
    cot[part_span(own_part), :] = cot_ref[...]
    cot[part_span(across_part), :] = cot_across_ref[...]
    feed[:, layer_chip] = feed_ref[...]
    greet_all(dp_count, tensor_count, dp_index, tensor_index)
    _, gather, ready, gather_sent = doubling_gather(
        feed,
        gather_recv,
        gather_send,
        None,
        None,
        layer_chip,
        layer_chips,
        core,
        tensor_index,
        tensor_count,
        dp_index,
    )
    gather_steps = steps + layer_chips.bit_length() - 2

    def context_out(step):
        place = step % chips
        owner = nearest(tensor_index, tensor_count, (2 * tensor_count - 2 - step // chips) % tensor_count)
        part = (core + flipped(place, chips)) % 2
        target = (base + 2 * place + chip // 2, owner)
        here = (target[0] == dp_index) & (owner == tensor_index)
        source = context_ref.at[place, owner]
        destination = context_in.at[tensor_index, chip % 2, part]
        far = pltpu.make_async_remote_copy(
            src_ref=source,
            dst_ref=destination,
            send_sem=context_send.at[place, owner],
            recv_sem=context_recv.at[tensor_index, chip % 2, part],
            device_id=target,
            device_id_type=MESH,
        )
        near = pltpu.make_async_copy(source, destination, local_sem.at[0])
        return here, far, near

    def send_context(step):
        here, far, near = context_out(step)

        @pl.when(here)
        def _():
            near.start()

        @pl.when(jnp.logical_not(here))
        def _():
            far.start()

    repeat(chips * tensor_count, send_context)

    def share_copy(array, which, number):
        source = own_part if number < 2 else own_part + 2 - 4 * side
        block = array.at[part_span(source)]
        return pltpu.make_async_remote_copy(
            src_ref=block,
            dst_ref=block,
            send_sem=share_send.at[which, number],
            recv_sem=share_recv.at[which, number],
            device_id=across if number == 1 else partner,
            device_id_type=MESH,
        )

    def share_arrival(array, which, number):
        source = (
            own_part + 1 - 2 * core,
            own_part + 2 - 4 * side,
            own_part + 2 - 4 * side + 1 - 2 * core,
        )[number]
        block = array.at[part_span(source)]
        return pltpu.make_async_remote_copy(
            src_ref=block,
            dst_ref=block,
            send_sem=share_send.at[which, number],
            recv_sem=share_recv.at[which, number],
            device_id=partner,
            device_id_type=MESH,
        )

    gather(0)
    share_copy(cot, 0, 0).start()
    share_copy(cot, 0, 2).start()
    repeat(4, lambda part: out_total.__setitem__(part, jnp.zeros((rows, width), f32)))
    repeat(4, lambda part: normed_total.__setitem__(part, jnp.zeros((rows, width), f32)))

    def take_context(step):
        owner, part = (tensor_index + step // 2) % tensor_count, step % 2
        for pair in range(2):
            destination = context_in.at[owner, pair, part]
            here = (
                (owner == tensor_index)
                & (chip == 2 * core + pair)
                & ((part + flipped(chip, chips)) % 2 == core)
            )

            @pl.when(here)
            def _():
                pltpu.make_async_copy(destination, destination, local_sem.at[0]).wait()

            @pl.when(jnp.logical_not(here))
            def _():
                pltpu.make_async_remote_copy(
                    src_ref=destination,
                    dst_ref=destination,
                    send_sem=context_send.at[0, 0],
                    recv_sem=context_recv.at[owner, pair, part],
                    device_id=partner,
                    device_id_type=MESH,
                ).wait_recv()

        first, second = context_in[owner, 0, part], context_in[owner, 1, part]
        lanes = pl.ds(pl.multiple_of(owner * 128, 128), 128)
        half = rows // 2
        for number in range(2):
            cut = slice(number * HD, (number + 1) * HD)
            where = pl.ds(pl.multiple_of(part * rows + number * half, 32), half)
            context[where, lanes] = jnp.concatenate([first[:, cut], second[:, cut]], axis=1)

    for number in range(1, gather_steps):
        gather(number)
    repeat(2 * tensor_count, take_context)
    repeat(tensor_count, lambda owner: dense_copy(owner).wait())

    low_grad[theirs, :] = nt(context[theirs, :], dense[...]).astype(bf16)
    first_swap = swap_copy(low_grad.at[theirs], swap_in, swap_sem, 0, partner)
    first_swap.start()
    own = x_ref[...].astype(f32) + dense_shift_ref[...] + nt(context[mine, :], dense[...])
    first_swap.wait()
    middle[...] = own + swap_in[...].astype(f32)
    normed[part_span(own_part), :] = normalize(middle[...], gain_ref[...], bias_ref[...]).astype(bf16)
    share_copy(normed, 1, 1).start()
    share_copy(normed, 1, 0).start()
    share_arrival(cot, 0, 0).wait_recv()
    share_arrival(cot, 0, 2).wait_recv()
    transpose_rows(cot, turned_cot)
    share_arrival(normed, 1, 0).wait_recv()

    def one_part(index):
        step, turn = index % (2 * steps) // 2, index // (2 * steps) * 2 + index % 2
        owner = (tensor_index + step * (tensor_count // steps)) % tensor_count
        part = 2 * ((side + turn // 2) % 2) + (core + turn) % 2

        @pl.when(turn == 0)
        def _():
            ready(step)
            up_shift_grad_ref[step] = jnp.zeros((8, hidden), f32)

        @pl.when((step == 0) & (turn == 2))
        def _():
            share_arrival(normed, 1, 1).wait_recv()
            share_copy(normed, 1, 2).start()

        @pl.when((step == 0) & (turn == 3))
        def _():
            share_arrival(normed, 1, 2).wait_recv()

        here = part_span(part)
        up_matrix = feed[step, :, :, 0:hidden].reshape(width, hidden)
        down_matrix = feed[step, :, :, hidden:].reshape(width, hidden)
        upper = nn(normed[here, :], up_matrix) + up_shift_ref[owner, 0:1]
        active_grad = nn(cot[here, :], down_matrix)
        square = upper * upper
        bent = jnp.tanh(0.7978845608 * upper * (1.0 + 0.044715 * square))
        rising = 0.5 * (1.0 + bent)
        slope = rising + 0.5 * upper * (1.0 - bent * bent) * 0.7978845608 * (
            1.0 + 3.0 * 0.044715 * square
        )
        low = (active_grad * slope).astype(bf16)
        active_low = (upper * rising).astype(bf16)
        active[step, here, :] = active_low
        upper_grad[step, here, :] = low
        up_shift_grad_ref[step, 0:1] += column_sum(low.astype(f32))
        normed_total[part] += nt(low, up_matrix)
        out_total[part] += nt(active_low, down_matrix)

    repeat(4 * steps, one_part)

    def core_copy(which):
        return swap_copy(
            cot.at[pl.ds(2 * which * rows, 2 * rows)], core_in.at[which], swap_sem, 1 + which, partner
        )

    def pair_copy(which):
        source = normed.at[pl.ds(0, rows)] if which else swap_in
        return swap_copy(source, pair_in.at[which], swap_sem, 3 + which, across)

    totals = (normed_total, out_total)
    for number in (0, 2):
        share_copy(cot, 0, number).wait_send()
    for which in range(2):
        for number in range(2):
            cot[pl.ds((2 * which + number) * rows, rows), :] = totals[which][
                2 * number + 1 - core
            ].astype(bf16)
        core_copy(which).start()
    def add_cores(which):
        core_copy(which).wait_recv()
        value = (
            totals[which][2 * (1 - side) + core] + core_in[which, part_span(1 - side), :].astype(f32)
        ).astype(bf16)
        if which:
            normed[pl.ds(0, rows), :] = value
        else:
            swap_in[...] = value
        pair_copy(which).start()

    def whole(which):
        pair_copy(which).wait_recv()
        return (
            totals[which][own_part]
            + core_in[which, part_span(side), :].astype(f32)
            + pair_in[which].astype(f32)
        )

    add_cores(0)

    transpose_rows(normed, turned_normed)
    half_chips = layer_chips // 2

    def set_out(array, refs, item, place, sems):
        for order in range(2):
            bit = place % 2 if order == 0 else place // half_chips
            own_bit = layer_chip % 2 if order == 0 else layer_chip // half_chips
            slot = place // 2 if order == 0 else place % half_chips
            block = array.at[pl.ds(order * piece, piece), :]
            goes = pltpu.make_async_copy(block, refs[order].at[item, slot], sems.at[order])
            stays = pltpu.make_async_copy(block, refs[2].at[order, item, slot], sems.at[order])

            @pl.when(bit == own_bit)
            def _():
                stays.start()

            @pl.when(bit != own_bit)
            def _():
                goes.start()

    def set_out_wait(array, refs, sems):
        for order in range(2):
            block = array.at[pl.ds(order * piece, piece), :]
            pltpu.make_async_copy(block, refs[2].at[order, 0, 0], sems.at[order]).wait()

    stages, start, finish, sent, _ = halving_scatter(
        parts, inbox, parts_send, parts_recv, layer_chip, layer_chips, core, tensor_index
    )
    dense_refs = (dense_send0_ref, dense_send1_ref, dense_keep_ref)

    def one_chip(index):
        step, place = index // layer_chips, index % layer_chips
        here = pl.ds(pl.multiple_of(place * pair_rows_count, pair_rows_count), pair_rows_count)
        parts[step, place, :, 0:hidden] = nn(turned_normed[here, :], upper_grad[step]).astype(bf16)
        parts[step, place, :, hidden:] = nn(turned_cot[here, :], active[step]).astype(bf16)

        @pl.when(place == layer_chips - 1)
        def _():
            start(step, 0)

    repeat(steps * layer_chips, one_chip)
    grads = whole(0)
    for number in range(3):
        share_copy(normed, 1, number).wait_send()
    add_cores(1)
    vectors_ref[...] = jnp.zeros_like(vectors_ref)
    vectors_ref[2:3] = column_sum(grads)
    part_grad, gain_part = layer_norm_back(middle[...], gain_ref[...], grads)
    vectors_ref[1:2] = column_sum(gain_part)
    own_cot = cot_ref[...].astype(f32)
    vectors_ref[3:4] = column_sum(own_cot)
    middle_grad = own_cot + part_grad
    middle_grad_ref[...] = middle_grad
    vectors_ref[0:1] = column_sum(middle_grad)
    low_grad[mine, :] = middle_grad.astype(bf16)
    low_swap = swap_copy(low_grad.at[mine], low_grad.at[mine], swap_sem, 5, partner)
    low_swap.start()
    swap_copy(low_grad.at[theirs], low_grad.at[theirs], swap_sem, 5, partner).wait_recv()

    def grads_out(owner, part, pair):
        target = (base + 2 * (2 * core + pair) + (part + flipped(chip, chips)) % 2, owner)
        here = (target[0] == dp_index) & (owner == tensor_index)
        source = outbox.at[owner, part, pair]
        destination = grads_ref.at[chip, tensor_index]
        far = pltpu.make_async_remote_copy(
            src_ref=source,
            dst_ref=destination,
            send_sem=outbox_send.at[owner, part, pair],
            recv_sem=outbox_recv.at[chip, tensor_index],
            device_id=target,
            device_id_type=MESH,
        )
        return here, far, pltpu.make_async_copy(source, destination, local_sem.at[1])

    def send_grads(step):
        owner = nearest(tensor_index, tensor_count, (2 * tensor_count - 2 - step // 2) % tensor_count)
        part = step % 2
        lanes = pl.ds(pl.multiple_of(owner * 128, 128), 128)
        result = nn(low_grad[part_span(part), :], dense[:, lanes]).astype(bf16)
        half = rows // 2
        for pair in range(2):
            cut = slice(pair * HD, (pair + 1) * HD)
            outbox[owner, part, pair] = jnp.concatenate(
                [result[:half, cut], result[half:, cut]], axis=1
            )
            here, far, near = grads_out(owner, part, pair)

            @pl.when(here)
            def _():
                near.start()

            @pl.when(jnp.logical_not(here))
            def _():
                far.start()

    repeat(2 * tensor_count, send_grads)

    def advance(stage):
        for step in range(steps):
            finish(step, stage)
            if stage + 1 < stages:
                start(step, stage + 1)

    advance(0)
    turned_low = turned_cot.at[:, 0 : 2 * rows]
    transpose_rows(low_grad, turned_low)

    def dense_chip(place):
        here = pl.ds(pl.multiple_of(place * pair_rows_count, pair_rows_count), pair_rows_count)
        dense_parts[place] = nn(turned_low[here, :], context[...]).astype(bf16)
        set_out(dense_parts.at[place], dense_refs, 0, place, dense_sem.at[place])

    repeat(layer_chips, dense_chip)
    block_ref[...] = (middle[...] + whole(1) + down_shift_ref[...]).astype(bf16)

    for stage in range(1, stages):
        advance(stage)
    for step in range(steps):
        feed_sum_ref[step] = parts[step, layer_chip]
    repeat(
        layer_chips,
        lambda place: set_out_wait(dense_parts.at[place], dense_refs, dense_sem.at[place]),
    )

    def arrived(step):
        place, owner = step // tensor_count, step % tensor_count
        destination = grads_ref.at[place, owner]
        here = (place == chip) & (owner == tensor_index) & (chip // 2 == core)

        @pl.when(here)
        def _():
            pltpu.make_async_copy(destination, destination, local_sem.at[1]).wait()

        @pl.when(jnp.logical_not(here))
        def _():
            pltpu.make_async_remote_copy(
                src_ref=destination,
                dst_ref=destination,
                send_sem=context_send.at[0, 0],
                recv_sem=outbox_recv.at[place, owner],
                device_id=partner,
                device_id_type=MESH,
            ).wait_recv()

    repeat(chips * tensor_count, arrived)

    def context_sent(step):
        here, far, _near = context_out(step)

        @pl.when(jnp.logical_not(here))
        def _():
            far.wait_send()

    repeat(chips * tensor_count, context_sent)

    def grads_sent(step):
        here, far, _near = grads_out(step // 4, step // 2 % 2, step % 2)

        @pl.when(jnp.logical_not(here))
        def _():
            far.wait_send()

    repeat(4 * tensor_count, grads_sent)

    for step in range(steps):
        for stage in range(stages):
            sent(step, stage)
    for which in range(2):
        core_copy(which).wait_send()
        pair_copy(which).wait_send()
    gather_sent()
    low_swap.wait_send()


def middle_part(
    context, inputs, cotangent, across, vectors, up_shift, feed, weight, dp_count, tensor_count, span
):
    rows, width = inputs.shape
    hidden = feed.shape[2] // 2
    piece = width // dp_count
    steps = tensor_count // 2
    chips, layer_chips = span // 2, dp_count // 2
    dma = pltpu.SemaphoreType.DMA
    vmem = pl.BlockSpec(memory_space=pltpu.VMEM)
    anywhere = pl.BlockSpec(memory_space=pl.ANY)
    dense_part = (piece, 128 * tensor_count)
    return pl.pallas_call(
        functools.partial(middle_kernel, dp_count, tensor_count, span),
        in_specs=[vmem] * 7 + [anywhere],
        out_specs=[vmem] * 3 + [anywhere] * 3 + [vmem] * 2 + [anywhere],
        out_shape=[
            jax.ShapeDtypeStruct((rows, width), bf16),
            jax.ShapeDtypeStruct((rows, width), f32),
            jax.ShapeDtypeStruct((steps, 2 * piece, 2 * hidden), bf16),
            jax.ShapeDtypeStruct((1, layer_chips // 2, *dense_part), bf16),
            jax.ShapeDtypeStruct((1, layer_chips // 2, *dense_part), bf16),
            jax.ShapeDtypeStruct((2, 1, layer_chips // 2, *dense_part), bf16),
            jax.ShapeDtypeStruct((8, width), f32),
            jax.ShapeDtypeStruct((steps, 8, hidden), f32),
            jax.ShapeDtypeStruct((chips, tensor_count, rows // 2, 128), bf16),
        ],
        scratch_shapes=[
            pltpu.VMEM((tensor_count, 2, 2, rows // 2, 128), bf16),
            pltpu.VMEM((2 * rows, 128 * tensor_count), bf16),
            pltpu.VMEM((width, 128 * tensor_count), bf16),
            pltpu.VMEM((steps, layer_chips, 2 * piece, 2 * hidden), bf16),
            pltpu.VMEM((rows, width), f32),
            pltpu.VMEM((4 * rows, width), bf16),
            pltpu.VMEM((4 * rows, width), bf16),
            pltpu.VMEM((width, 4 * rows), bf16),
            pltpu.VMEM((width, 4 * rows), bf16),
            pltpu.VMEM((steps, 4 * rows, hidden), bf16),
            pltpu.VMEM((steps, 4 * rows, hidden), bf16),
            pltpu.VMEM((4, rows, width), f32),
            pltpu.VMEM((4, rows, width), f32),
            pltpu.VMEM((rows, width), bf16),
            pltpu.VMEM((2, 2 * rows, width), bf16),
            pltpu.VMEM((2, rows, width), bf16),
            pltpu.VMEM((2 * rows, width), bf16),
            pltpu.VMEM((tensor_count, 2, 2, rows // 2, 128), bf16),
            pltpu.VMEM((steps, layer_chips, 2 * piece, 2 * hidden), bf16),
            pltpu.VMEM((steps, layer_chips - 1, 2 * piece, 2 * hidden), bf16),
            pltpu.VMEM((layer_chips, 2 * piece, 128 * tensor_count), bf16),
            dma((tensor_count,)),
            dma((2, 8)),
            dma((2, 3)),
            dma((2, 3)),
            dma((chips, tensor_count)),
            dma((tensor_count, 2, 2)),
            dma((tensor_count, 2, 2)),
            dma((chips, tensor_count)),
            dma((2,)),
            dma((steps, layer_chips, 2)),
            dma((steps, layer_chips - 1, 2)),
            dma((steps, layer_chips - 1, 2)),
            dma((steps, layer_chips - 1, 2)),
            dma((layer_chips, 2)),
        ],
        compiler_params=pltpu.CompilerParams(
            collective_id=1, has_side_effects=True, vmem_limit_bytes=62 * 2**20
        ),
        cost_estimate=pl.CostEstimate(
            flops=6 * 2 * 2 * rows * width * hidden * tensor_count,
            bytes_accessed=40_000_000,
            transcendentals=0,
        ),
        name="middle_part",
    )(context, inputs, cotangent, across, vectors, up_shift, feed, weight)


def finish_kernel(
    dp_count,
    tensor_count,
    span,
    dq_ref,
    dkv_ref,
    normed_ref,
    x_ref,
    vectors_in_ref,
    middle_grad_ref,
    vector_grads_ref,
    up_rows_ref,
    feed_sum_ref,
    feed_got_ref,
    dense_keep_ref,
    dense_got0_ref,
    dense_got1_ref,
    weight_ref,
    input_grad_ref,
    weight_grad_ref,
    up_grad_ref,
    down_grad_ref,
    dense_grad_ref,
    dense_bias_ref,
    gain_two_ref,
    bias_two_ref,
    down_bias_ref,
    gain_one_ref,
    bias_one_ref,
    up_sums_ref,
    qkv_sums_ref,
    weight,
    turned_normed,
    dkv_in,
    outbox,
    mixed_in,
    gathered,
    normed_total,
    swap_out,
    swap_in,
    parts,
    inbox,
    layer_inbox,
    dense_parts,
    dense_inbox,
    dense_layer_inbox,
    last_out,
    last_in,
    last_feed_out,
    last_feed_in,
    last_dense_out,
    last_dense_in,
    late,
    column_sums,
    sums_out,
    sums_in,
    sums,
    weight_sem,
    dense_load_sem,
    swap_sem,
    dkv_send,
    dkv_recv,
    outbox_send,
    mixed_recv,
    parts_send,
    parts_recv,
    layer_send,
    layer_recv,
    dense_send,
    dense_recv,
    dense_layer_send,
    dense_layer_recv,
    sums_send,
    sums_recv,
    local_sem,
):
    dp_index, tensor_index = lax.axis_index("dp"), lax.axis_index("tensor")
    rows, width = x_ref.shape
    columns = weight.shape[2]
    hidden = up_rows_ref.shape[1]
    core = dp_index % 2
    base = dp_index // span * span
    chip = dp_index % span // 2
    chips = span // 2
    layer_chip, layer_chips = dp_index // 2, dp_count // 2
    pair_rows_count = parts.shape[2]
    piece = pair_rows_count // 2
    partner = (dp_index + 1 - 2 * core, tensor_index)
    part_span = lambda part: pl.ds(pl.multiple_of(part * rows, 64), rows)
    dp_rows = rows * tensor_count
    devices = dp_count * tensor_count
    me = dp_index * tensor_count + tensor_index

    def weight_copy(owner):
        return pltpu.make_async_copy(
            weight_ref.at[owner, :, pl.ds(0, columns)], weight.at[owner], weight_sem.at[owner]
        )

    def loads(parts, inbox, keep_ref, got_refs, sems, item, slot):
        copies = []
        for order in range(2):
            rows_here = pl.ds(order * piece, piece)
            if order == 0:
                place = 2 * slot + layer_chip % 2
            else:
                place = slot + layer_chip // (layer_chips // 2) * (layer_chips // 2)
            copies += [
                pltpu.make_async_copy(
                    keep_ref.at[order, item, slot],
                    parts.at[item, place, rows_here, :],
                    sems.at[item, slot, order],
                ),
                pltpu.make_async_copy(
                    got_refs[order].at[item, slot],
                    inbox.at[item, slot, rows_here, :],
                    sems.at[item, slot, 2 + order],
                ),
            ]
        return copies

    def dense_loads(index):
        return loads(
            dense_parts,
            dense_inbox,
            dense_keep_ref,
            (dense_got0_ref, dense_got1_ref),
            dense_load_sem,
            0,
            index,
        )

    repeat(layer_chips // 2, lambda index: [copy.start() for copy in dense_loads(index)])
    repeat(tensor_count, lambda owner: weight_copy(owner).start())
    greet_all(dp_count, tensor_count, dp_index, tensor_index)

    def dkv_copy(place, whose):
        taken = 2 * place + (whose + flipped(place, chips)) % 2
        return pltpu.make_async_remote_copy(
            src_ref=dkv_ref.at[pl.ds(pl.multiple_of(taken * dp_rows, 128), dp_rows)],
            dst_ref=dkv_in.at[place],
            send_sem=dkv_send.at[place],
            recv_sem=dkv_recv.at[place],
            device_id=partner,
            device_id_type=MESH,
        )

    repeat(chips, lambda place: dkv_copy(place, 1 - core).start())
    place_here = (layer_chip, layer_chips, core, tensor_index)
    stages = layer_chips.bit_length() - 1
    _, dense_start, dense_finish, dense_sent, dense_add = halving_scatter(
        dense_parts, dense_inbox, dense_send, dense_recv, *place_here
    )
    repeat(2, lambda part: normed_total.__setitem__(part, jnp.zeros((rows, width), f32)))
    repeat(chips, lambda place: dkv_copy(place, 1 - core).wait_recv())

    def message(place, owner):
        part = (core + flipped(place, chips)) % 2
        target = (base + 2 * place + chip // 2, owner)
        here = (target[0] == dp_index) & (owner == tensor_index)
        source = outbox.at[place, owner]
        destination = mixed_in.at[tensor_index, chip % 2, part]
        far = pltpu.make_async_remote_copy(
            src_ref=source,
            dst_ref=destination,
            send_sem=outbox_send.at[place, owner],
            recv_sem=mixed_recv.at[tensor_index, chip % 2, part],
            device_id=target,
            device_id_type=MESH,
        )
        return here, far, pltpu.make_async_copy(source, destination, local_sem.at[0])

    def send_message(step):
        owner, place = nearest(tensor_index, tensor_count, step // chips), step % chips
        taken = 2 * place + (core + flipped(place, chips)) % 2
        own = pl.ds(pl.multiple_of(taken * dp_rows + owner * rows, 64), rows)
        total = dkv_ref[own, :].astype(f32) + dkv_in[
            place, pl.ds(pl.multiple_of(owner * rows, 64), rows), :
        ].astype(f32)
        queries = dq_ref[
            pl.ds(pl.multiple_of(place * dp_rows + owner * rows, 64), rows), :
        ].astype(f32)
        outbox[place, owner, 0:rows, :] = jnp.concatenate([queries, total[:, :HD]], axis=1).astype(
            bf16
        )
        half = rows // 2
        outbox[place, owner, rows:, :] = jnp.concatenate(
            [total[:half, HD:], total[half:, HD:]], axis=1
        ).astype(bf16)
        here, far, near = message(place, owner)

        @pl.when(here)
        def _():
            near.start()

        @pl.when(jnp.logical_not(here))
        def _():
            far.start()

    repeat(chips * tensor_count, send_message)

    def dense_layer_copy(step):
        owner = (tensor_index + step) % tensor_count
        return pltpu.make_async_remote_copy(
            src_ref=dense_parts.at[
                0, layer_chip, :, pl.ds(pl.multiple_of(owner * 128, 128), 128)
            ],
            dst_ref=dense_layer_inbox.at[step - 1],
            send_sem=dense_layer_send.at[step - 1],
            recv_sem=dense_layer_recv.at[step - 1],
            device_id=(dp_index, owner),
            device_id_type=MESH,
        )

    repeat(layer_chips // 2, lambda index: [copy.wait() for copy in dense_loads(index)])
    dense_add(0, 0)
    if stages > 1:
        dense_start(0, 1)
    transpose_rows(normed_ref, turned_normed)

    def sum_copy(which, step):
        other = (me + step) % devices
        there = (other // tensor_count, other % tensor_count)
        return pltpu.make_async_remote_copy(
            src_ref=sums_out.at[which, there[0], there[1]],
            dst_ref=sums_in.at[which, dp_index, tensor_index],
            send_sem=sums_send.at[which, there[0], there[1]],
            recv_sem=sums_recv.at[which, dp_index, tensor_index],
            device_id=there,
            device_id_type=MESH,
        )

    def sum_message(which, owner_dp, owner, vector_rows, row, count, vectors):
        block = pl.ds(pl.multiple_of(owner_dp * piece // 128 * 128, 128), 128)
        sums_out[which, owner_dp, owner] = jnp.zeros((8, 128), f32)
        sums_out[which, owner_dp, owner, 0:vector_rows, :] = vectors[0:vector_rows, block]
        for number in range(count):
            sums_out[which, owner_dp, owner, vector_rows + number : vector_rows + number + 1, :] = row[
                :, number * 128 : (number + 1) * 128
            ]

    def send_sums(which, vector_rows, row_of, count, vectors):
        def one(step):
            other = (me + step) % devices
            owner_dp, owner = other // tensor_count, other % tensor_count
            sum_message(which, owner_dp, owner, vector_rows, row_of(owner), count, vectors)

            @pl.when(step > 0)
            def _():
                sum_copy(which, step).start()

        repeat(devices, one)
        sums_in[which, dp_index, tensor_index] = sums_out[which, dp_index, tensor_index]

    send_sums(
        0, 4, lambda owner: up_rows_ref[pl.ds(2 * owner + core, 1), :], hidden // 128, vector_grads_ref
    )

    def layer_copy(step):
        owner = (tensor_index + step) % tensor_count
        return pltpu.make_async_remote_copy(
            src_ref=parts.at[owner, layer_chip],
            dst_ref=layer_inbox.at[step - 1],
            send_sem=layer_send.at[step - 1],
            recv_sem=layer_recv.at[step - 1],
            device_id=(dp_index, owner),
            device_id_type=MESH,
        )

    def tile_of(step):
        return jnp.where(step == 0, tensor_index, nearest(tensor_index, tensor_count, step - 1))

    def chip_copy(step, hop):
        target = (layer_chip + hop) % layer_chips
        return pltpu.make_async_remote_copy(
            src_ref=parts.at[step, target],
            dst_ref=inbox.at[step, hop - 1],
            send_sem=parts_send.at[step, hop - 1],
            recv_sem=parts_recv.at[step, hop - 1],
            device_id=(2 * target + core, tensor_index),
            device_id_type=MESH,
        )

    def hops(body):
        repeat(layer_chips - 1, lambda number: body(number + 1))

    def advance(step):
        tile = tile_of(step - 1)

        @pl.when(step > 0)
        def _():
            hops(lambda hop: chip_copy(tile, hop).wait_recv())
            value = parts[tile, layer_chip].astype(f32)
            for number in range(layer_chips - 1):
                value = value + inbox[tile, number].astype(f32)
            parts[tile, layer_chip] = value.astype(bf16)

            @pl.when(tile != tensor_index)
            def _():
                layer_copy((tile - tensor_index + tensor_count) % tensor_count).start()

    def dense_advance(stage):
        dense_finish(0, stage)
        if stage + 1 < stages:
            dense_start(0, stage + 1)
        else:
            for step in range(1, tensor_count):
                dense_layer_copy(step).start()

    def one_owner(step):
        owner = tile_of(step)
        weight_copy(owner).wait()
        column_sums[owner] = jnp.zeros(column_sums.shape[1:], f32)

        def one_part(part):
            for pair in range(2):
                destination = mixed_in.at[owner, pair, part]
                here = (
                    (owner == tensor_index)
                    & (chip == 2 * core + pair)
                    & ((part + flipped(chip, chips)) % 2 == core)
                )

                @pl.when(here)
                def _():
                    pltpu.make_async_copy(destination, destination, local_sem.at[0]).wait()

                @pl.when(jnp.logical_not(here))
                def _():
                    pltpu.make_async_remote_copy(
                        src_ref=destination,
                        dst_ref=destination,
                        send_sem=outbox_send.at[0, 0],
                        recv_sem=mixed_recv.at[owner, pair, part],
                        device_id=partner,
                        device_id_type=MESH,
                    ).wait_recv()

            pieces_here = []
            for pair in range(2):
                value = mixed_in[owner, pair, part]
                pieces_here += [value[:rows], pair_rows(value[rows:])]
            grads = jnp.concatenate(pieces_here, axis=1)
            gathered[part_span(part), :] = grads
            column_sums[owner, 0:1] += column_sum(grads.astype(f32))
            normed_total[part] += nt(grads, weight[owner])

        repeat(2, one_part)

        def one_chip(place):
            here = pl.ds(pl.multiple_of(place * pair_rows_count, pair_rows_count), pair_rows_count)
            parts[owner, place] = nn(turned_normed[here, :], gathered[...]).astype(bf16)

        repeat(layer_chips, one_chip)
        hops(lambda hop: chip_copy(owner, hop).start())
        advance(step)
        for stage in range(1, stages):

            @pl.when(step == min(stage, tensor_count - 1))
            def _():
                dense_advance(stage)

    repeat(tensor_count, one_owner)

    swap_out[...] = normed_total[1 - core].astype(bf16)
    swap = swap_copy(swap_out, swap_in, swap_sem, 0, partner)
    swap.start()
    advance(tensor_count)
    swap.wait_recv()
    grads = normed_total[core] + swap_in[...].astype(f32)
    part_grad, gain_part = layer_norm_back(x_ref[...].astype(f32), vectors_in_ref[0:1, :], grads)
    input_grad_ref[...] = middle_grad_ref[...] + part_grad
    late[...] = jnp.zeros_like(late)
    late[0:1] = column_sum(gain_part)
    late[1:2] = column_sum(grads)
    send_sums(1, 2, lambda owner: column_sums[owner, 0:1, :], columns // 128, late)

    kept = pl.ds(pl.multiple_of(core * piece, piece), piece)
    given = pl.ds(pl.multiple_of((1 - core) * piece, piece), piece)

    def total(array, arrived, where):
        value = array[tensor_index, layer_chip, where, :].astype(f32)
        for step in range(arrived.shape[0]):
            value = value + arrived[step, where, :].astype(f32)
        return value

    def dense_total(where):
        lanes = pl.ds(pl.multiple_of(tensor_index * 128, 128), 128)
        value = dense_parts[0, layer_chip, where, lanes].astype(f32)
        for step in range(1, tensor_count):
            value = value + dense_layer_inbox[step - 1, where, :].astype(f32)
        return value

    def feed_total(where):
        value = feed_sum_ref[0, where, :].astype(f32)
        for number in range(feed_got_ref.shape[0]):
            value = value + feed_got_ref[number, where, :].astype(f32)
        return value

    last_feed_out[...] = feed_total(given)
    last_feed = swap_copy(last_feed_out, last_feed_in, swap_sem, 2, partner)
    last_feed.start()
    own_total = feed_total(kept)
    my_half = pl.ds(pl.multiple_of(core * hidden, 128), hidden)
    their_half = pl.ds(pl.multiple_of((1 - core) * hidden, 128), hidden)
    up_grad_ref[:, my_half] = own_total[:, :hidden]
    down_grad_ref[my_half, :] = own_total[:, hidden:].T
    for step in range(1, tensor_count):
        dense_layer_copy(step).wait_recv()
    last_dense_out[...] = dense_total(given)
    last_dense = swap_copy(last_dense_out, last_dense_in, swap_sem, 3, partner)
    last_dense.start()
    dense_grad_ref[pl.ds(pl.multiple_of(core * 128, 128), 128), :] = dense_total(kept).T

    for step in range(1, tensor_count):
        layer_copy(step).wait_recv()
    last_out[...] = total(parts, layer_inbox, given)
    last = swap_copy(last_out, last_in, swap_sem, 1, partner)
    last.start()
    weight_grad_ref[:, pl.ds(pl.multiple_of(core * columns, 128), columns)] = total(
        parts, layer_inbox, kept
    )
    last_feed.wait()
    up_grad_ref[:, their_half] = last_feed_in[:, :hidden]
    down_grad_ref[their_half, :] = last_feed_in[:, hidden:].T
    last_dense.wait()
    dense_grad_ref[pl.ds(pl.multiple_of((1 - core) * 128, 128), 128), :] = last_dense_in[...].T
    last.wait()
    weight_grad_ref[:, pl.ds(pl.multiple_of((1 - core) * columns, 128), columns)] = last_in[...]

    for which in range(2):

        def sum_wait(step):
            other = (me + step + 1) % devices
            there = (other // tensor_count, other % tensor_count)
            place = sums_in.at[which, there[0], there[1]]
            pltpu.make_async_remote_copy(
                src_ref=place,
                dst_ref=place,
                send_sem=sums_send.at[which, there[0], there[1]],
                recv_sem=sums_recv.at[which, there[0], there[1]],
                device_id=partner,
                device_id_type=MESH,
            ).wait_recv()

        repeat(devices - 1, sum_wait)
        sums[which] = jnp.zeros(sums.shape[1:], f32)

        def add_one(step):
            owner_dp, owner = step // tensor_count, step % tensor_count
            sums[which, owner_dp % 2] += sums_in[which, owner_dp, owner]

        repeat(devices, add_one)
        vectors = (
            (dense_bias_ref, gain_two_ref, bias_two_ref, down_bias_ref),
            (gain_one_ref, bias_one_ref),
        )[which]
        for number, vector in enumerate(vectors):
            vector[...] = sums[which, 0, number : number + 1] + sums[which, 1, number : number + 1]
    up_sums_ref[...] = sums[0, :, 4:]
    qkv_sums_ref[...] = sums[1, :, 2:5]

    repeat(chips, lambda place: dkv_copy(place, 1 - core).wait_send())

    def message_sent(step):
        here, far, _near = message(step // tensor_count, step % tensor_count)

        @pl.when(jnp.logical_not(here))
        def _():
            far.wait_send()

    repeat(chips * tensor_count, message_sent)
    for stage in range(stages):
        if stage > 0:
            dense_sent(0, stage)
    repeat(tensor_count, lambda step: hops(lambda hop: chip_copy(step, hop).wait_send()))
    for step in range(1, tensor_count):
        layer_copy(step).wait_send()
        dense_layer_copy(step).wait_send()
    for which in range(2):
        repeat(devices - 1, lambda step: sum_copy(which, step + 1).wait_send())
    swap.wait_send()


def finish_part(
    dq,
    dkv,
    normed,
    inputs,
    vectors,
    middle_grad,
    vector_grads,
    up_rows,
    feed_sum,
    feed_got,
    dense_keep,
    dense_got,
    weight,
    dp_count,
    tensor_count,
    span,
):
    rows, width = inputs.shape
    columns = weight.shape[2] - 128
    hidden = up_rows.shape[1]
    piece = width // dp_count
    chips, layer_chips = span // 2, dp_count // 2
    dma = pltpu.SemaphoreType.DMA
    vmem = pl.BlockSpec(memory_space=pltpu.VMEM)
    anywhere = pl.BlockSpec(memory_space=pl.ANY)
    message = (rows * 3 // 2, 128)
    part = (2 * piece, columns)
    dense_part = (2 * piece, dense_keep.shape[4])
    halving = (layer_chips - 1, 2)
    return pl.pallas_call(
        functools.partial(finish_kernel, dp_count, tensor_count, span),
        in_specs=[vmem] * 10 + [anywhere] * 4,
        out_specs=[vmem] * 13,
        out_shape=[
            jax.ShapeDtypeStruct((rows, width), f32),
            jax.ShapeDtypeStruct((piece, 2 * columns), f32),
            jax.ShapeDtypeStruct((piece, 2 * hidden), f32),
            jax.ShapeDtypeStruct((2 * hidden, piece), f32),
            jax.ShapeDtypeStruct((2 * 128, piece), f32),
            *[jax.ShapeDtypeStruct((1, 128), f32)] * 6,
            jax.ShapeDtypeStruct((2, 4, 128), f32),
            jax.ShapeDtypeStruct((2, 3, 128), f32),
        ],
        scratch_shapes=[
            pltpu.VMEM((tensor_count, width, columns), bf16),
            pltpu.VMEM((width, 2 * rows), bf16),
            pltpu.VMEM((chips, rows * tensor_count, 128), bf16),
            pltpu.VMEM((chips, tensor_count, *message), bf16),
            pltpu.VMEM((tensor_count, 2, 2, *message), bf16),
            pltpu.VMEM((2 * rows, columns), bf16),
            pltpu.VMEM((2, rows, width), f32),
            pltpu.VMEM((rows, width), bf16),
            pltpu.VMEM((rows, width), bf16),
            pltpu.VMEM((tensor_count, layer_chips, *part), bf16),
            pltpu.VMEM((tensor_count, layer_chips - 1, *part), bf16),
            pltpu.VMEM((tensor_count - 1, *part), bf16),
            pltpu.VMEM((1, layer_chips, *dense_part), bf16),
            pltpu.VMEM((1, layer_chips - 1, *dense_part), bf16),
            pltpu.VMEM((tensor_count - 1, 2 * piece, 128), bf16),
            pltpu.VMEM((piece, columns), f32),
            pltpu.VMEM((piece, columns), f32),
            pltpu.VMEM((piece, 2 * hidden), f32),
            pltpu.VMEM((piece, 2 * hidden), f32),
            pltpu.VMEM((piece, 128), f32),
            pltpu.VMEM((piece, 128), f32),
            pltpu.VMEM((8, width), f32),
            pltpu.VMEM((tensor_count, 8, columns), f32),
            pltpu.VMEM((2, dp_count, tensor_count, 8, 128), f32),
            pltpu.VMEM((2, dp_count, tensor_count, 8, 128), f32),
            pltpu.VMEM((2, 2, 8, 128), f32),
            dma((tensor_count,)),
            dma((1, layer_chips // 2, 4)),
            dma((2, 4)),
            dma((chips,)),
            dma((chips,)),
            dma((chips, tensor_count)),
            dma((tensor_count, 2, 2)),
            dma((tensor_count, layer_chips - 1)),
            dma((tensor_count, layer_chips - 1)),
            dma((tensor_count - 1,)),
            dma((tensor_count - 1,)),
            dma((1, *halving)),
            dma((1, *halving)),
            dma((tensor_count - 1,)),
            dma((tensor_count - 1,)),
            dma((2, dp_count, tensor_count)),
            dma((2, dp_count, tensor_count)),
            dma((1,)),
        ],
        compiler_params=pltpu.CompilerParams(
            collective_id=2, has_side_effects=True, vmem_limit_bytes=60 * 2**20
        ),
        cost_estimate=pl.CostEstimate(
            flops=2 * 2 * 2 * rows * width * columns * tensor_count,
            bytes_accessed=30_000_000,
            transcendentals=0,
        ),
        name="finish_part",
    )(
        dq,
        dkv,
        normed,
        inputs,
        vectors,
        middle_grad,
        vector_grads,
        up_rows,
        feed_sum,
        feed_got,
        dense_keep,
        *dense_got,
        weight,
    )


def per_device(
    block_in,
    norm1_gain,
    norm1_bias,
    qkv_weight,
    qv_bias,
    dense_weight,
    dense_bias,
    norm2_gain,
    norm2_bias,
    up_weight,
    up_bias,
    down_weight,
    down_bias,
    cotangent,
    seg_parent,
    seg_length,
):
    dp_count, tensor_count = lax.axis_size("dp"), lax.axis_size("tensor")
    dp_index, tensor_index = lax.axis_index("dp"), lax.axis_index("tensor")
    rows, width = block_in.shape
    dp_rows = rows * tensor_count
    span = PAIR_TOKENS // dp_rows
    heads_here = HEADS // tensor_count
    local_index = lax.rem(dp_index, span)
    core = lax.rem(dp_index, 2)

    piece = norm1_gain.shape[0]

    def small_row(value):
        return jnp.pad(value.reshape(1, -1), ((0, 0), (0, 128 - value.size)))

    small = [norm1_gain, norm1_bias, norm2_gain, norm2_bias, dense_bias, down_bias, qv_bias, up_bias]
    small = jnp.pad(jnp.concatenate([small_row(value) for value in small]), ((0, 8), (0, 0)))

    def by_core(value):
        return value.reshape(value.shape[0], 2, -1).transpose(1, 0, 2)

    shard = jnp.concatenate([by_core(qkv_weight), by_core(dense_weight.T)], axis=2)
    feed_shard = jnp.concatenate([by_core(up_weight), by_core(down_weight.T)], axis=2)
    head = tensor_index * heads_here + local_index // 2
    slope = jnp.exp2(-8.0 * (head.astype(f32) + 1.0) / HEADS) / TRUNK
    half = span // 2
    taken = jnp.stack([2 * i + (core + flipped(i, half)) % 2 for i in range(half)])
    block_ids = (
        taken[:, None] * (dp_rows // QUERY_BLOCK)
        + jnp.arange(dp_rows // QUERY_BLOCK, dtype=jnp.int32)[None, :]
    ).reshape(-1)

    across = [(layer, layer + 1 - 2 * (layer % 2)) for layer in range(tensor_count)]
    normed_both, mixed, weight, vectors, up_shift, feed_block = project(
        block_in, small, shard, feed_shard, dp_count, tensor_count, span
    )
    weight = weight.reshape(tensor_count, width, -1)
    feed_block, cotangent = lax.optimization_barrier((feed_block, cotangent))
    cot_across = lax.ppermute(cotangent, "tensor", across)
    feed_far = [
        lax.ppermute(
            feed_block, "tensor", [(layer, (layer + hop) % tensor_count) for layer in range(tensor_count)]
        )
        for hop in range(tensor_count - 2, 0, -2)
    ]
    feed = jnp.stack([feed_block] + feed_far)
    bounds, by_segment, block_list, block_count = pair_tables(
        seg_parent, seg_length, dp_index // span, slope, block_ids
    )
    tables = (block_ids, block_count, block_list, bounds, by_segment)
    packed_context, out_float, keys, queries = attention_forward(*tables, mixed, tensor_count)
    (
        block_out,
        middle_grad,
        feed_sum,
        dense_send0,
        dense_send1,
        dense_keep,
        vector_grads,
        up_shift_part,
        packed_grads,
    ) = middle_part(
        packed_context,
        block_in,
        cotangent,
        cot_across,
        vectors,
        up_shift,
        feed,
        weight,
        dp_count,
        tensor_count,
        span,
    )
    low_bit = [(device, device + 2 - 4 * (device // 2 % 2)) for device in range(dp_count)]
    half_dp = dp_count // 2
    high_bit = [(device, (device + half_dp) % dp_count) for device in range(dp_count)]
    feed_got = jnp.stack(
        [
            lax.ppermute(
                feed_sum[step],
                "tensor",
                [(layer, (layer + 2 * step) % tensor_count) for layer in range(tensor_count)],
            )
            for step in range(1, feed_sum.shape[0])
        ]
    )
    dense_got = (lax.ppermute(dense_send0, "dp", low_bit), lax.ppermute(dense_send1, "dp", high_bit))
    dq, dkv = attention_backward(*tables[:3], keys, queries, mixed, packed_grads, out_float)
    hidden = up_shift_part.shape[2]
    up_part = jnp.zeros((tensor_count, 2, hidden), f32)
    for step in range(up_shift_part.shape[0]):
        owner = lax.rem(tensor_index + step * (tensor_count // up_shift_part.shape[0]), tensor_count)
        up_part = lax.dynamic_update_slice(up_part, up_shift_part[step, :1][None], (owner, core, 0))
    up_rows = up_part.reshape(2 * tensor_count, hidden)
    (
        input_grad,
        qkv_weight_grad,
        up_grad,
        down_grad,
        dense_grad,
        *vectors_out,
        up_sums,
        qkv_sums,
    ) = finish_part(
        dq,
        dkv,
        normed_both.reshape(2 * rows, width),
        block_in,
        vectors,
        middle_grad,
        vector_grads,
        up_rows,
        feed_sum,
        feed_got,
        dense_keep,
        dense_got,
        weight,
        dp_count,
        tensor_count,
        span,
    )
    offset = lax.rem(dp_index * piece, 128)

    def own_vector(number):
        value = vectors_out[number].reshape(128)
        if piece % 128 == 0:
            return value
        return lax.dynamic_slice_in_dim(value, offset, piece, 0)

    def own_matrix(whole, shape):
        return lax.dynamic_slice_in_dim(whole, dp_index * shape[1], shape[1], 1)

    qkv_totals = qkv_sums.reshape(heads_here, 3, HD)
    qv_grad = jnp.concatenate([qkv_totals[:, 0], qkv_totals[:, 2]], axis=1)
    up_totals = up_sums.reshape(up_bias.shape[0], 128)
    return (
        block_out,
        input_grad,
        own_vector(4),
        own_vector(5),
        qkv_weight_grad,
        own_matrix(qv_grad, qv_bias.shape),
        dense_grad,
        own_vector(0),
        own_vector(1),
        own_vector(2),
        up_grad,
        own_matrix(up_totals, up_bias.shape),
        down_grad,
        own_vector(3),
    )


def solution(mesh):
    rows = P(("dp", "tensor"), None)
    in_specs = (
        rows,
        P("dp"),
        P("dp"),
        P("dp", "tensor"),
        P("tensor", "dp"),
        P("tensor", "dp"),
        P("dp"),
        P("dp"),
        P("dp"),
        P("dp", "tensor"),
        P("tensor", "dp"),
        P("tensor", "dp"),
        P("dp"),
        rows,
        P(),
        P(),
    )
    out_specs = (
        rows,
        rows,
        P("dp"),
        P("dp"),
        P("dp", "tensor"),
        P("tensor", "dp"),
        P("tensor", "dp"),
        P("dp"),
        P("dp"),
        P("dp"),
        P("dp", "tensor"),
        P("tensor", "dp"),
        P("tensor", "dp"),
        P("dp"),
    )
    return jax.shard_map(
        per_device, mesh=mesh, in_specs=in_specs, out_specs=out_specs, check_vma=False
    )
```

```python
import functools

import jax
import jax.numpy as jnp
from jax import lax
from jax.experimental import pallas as pl
from jax.experimental.pallas import tpu as pltpu
from jax.sharding import PartitionSpec as P

HEADS = 16
HD = 64
TRUNK = 2048
SEG = 256
PAIR_TOKENS = 2 * (TRUNK + 12 * SEG)
PAIR_SEGS = 26
QUERY_BLOCK = 256
KEY_BLOCK = 256
BIG = 2.0**100
VALUE_ROWS = 80

epsilon = 1e-05
f32 = jnp.float32
bf16 = jnp.bfloat16
MESH = pl.DeviceIdType.MESH


def normalize(values, gain_row, bias_row):
    average = jnp.mean(values, axis=-1, keepdims=True)
    centred = values - average
    spread = jnp.mean(centred * centred, axis=-1, keepdims=True)
    return centred * lax.rsqrt(spread + epsilon) * gain_row + bias_row


def nn(left, right):
    return lax.dot_general(left, right, (((1,), (0,)), ((), ())), preferred_element_type=f32)


def nt(left, right):
    return lax.dot_general(left, right, (((1,), (1,)), ((), ())), preferred_element_type=f32)


def tn(left, right):
    return lax.dot_general(left, right, (((0,), (0,)), ((), ())), preferred_element_type=f32)


def pieces(value, count):
    parts = []
    for _ in range(count):
        part = lax.reduce_precision(value, 8, 7)
        parts.append(part)
        value = value - part
    return parts


def pair_tables(seg_parent, seg_length, group, slope, block_ids):
    first = group * PAIR_SEGS
    parent = lax.dynamic_slice_in_dim(seg_parent, first, PAIR_SEGS, 0) - first
    length = lax.dynamic_slice_in_dim(seg_length, first, PAIR_SEGS, 0)
    ids = jnp.arange(PAIR_SEGS, dtype=jnp.int32)
    begin = jnp.sum(jnp.where(ids[None, :] < ids[:, None], length[None, :], 0), axis=1)
    end = begin + length
    is_parent = parent[:, None] == ids[None, :]
    grand = jnp.sum(jnp.where(is_parent, parent[None, :], 0), axis=1)
    is_grand = grand[:, None] == ids[None, :]
    parent_length = jnp.sum(jnp.where(is_parent, length[None, :], 0), axis=1)
    grand_length = jnp.sum(jnp.where(is_grand, length[None, :], 0), axis=1)
    path_start = jnp.where(
        parent == ids, 0, parent_length + jnp.where(grand == parent, 0, grand_length)
    )
    related = is_parent | is_grand | (ids[:, None] == ids[None, :])
    high, low = pieces(slope * (path_start - begin).astype(f32), 2)
    slope_high, slope_low = pieces(slope, 2)
    by_segment = jnp.concatenate(
        [
            jnp.where(related, high[None, :], -BIG),
            jnp.where(related, low[None, :], 0.0),
            jnp.broadcast_to(
                jnp.stack([256.0 * slope_high, 256.0 * slope_low, slope_high, slope_low])[None, :],
                (PAIR_SEGS, 4),
            ),
        ],
        axis=1,
    )
    by_segment = jnp.pad(
        by_segment, ((0, 128 - PAIR_SEGS), (0, 128 - by_segment.shape[1]))
    ).astype(bf16)
    bounds = jnp.pad(jnp.stack([jnp.tile(begin, 2), jnp.tile(end, 2)]), ((0, 6), (0, 128 - 2 * PAIR_SEGS)))
    key_blocks = PAIR_TOKENS // KEY_BLOCK
    q_begin = block_ids * QUERY_BLOCK
    k_begin = jnp.arange(key_blocks, dtype=jnp.int32) * KEY_BLOCK
    q_has = (begin[None, :] < q_begin[:, None] + QUERY_BLOCK) & (end[None, :] > q_begin[:, None])
    k_has = (begin[None, :] < k_begin[:, None] + KEY_BLOCK) & (end[None, :] > k_begin[:, None])
    q_sees = jnp.any(q_has[:, :, None] & related[None], axis=1)
    seen = jnp.any(q_sees[:, None, :] & k_has[None, :, :], axis=2)
    seen = seen & (k_begin[None, :] + KEY_BLOCK <= q_begin[:, None])
    rank = jnp.sum(
        jnp.where(k_begin[None, None, :] < k_begin[None, :, None], seen[:, None, :], False),
        axis=2,
        dtype=jnp.int32,
    )
    slots = jnp.arange(key_blocks + 8, dtype=jnp.int32)
    numbers = jnp.arange(key_blocks, dtype=jnp.int32)
    block_list = jnp.sum(
        jnp.where(
            seen[:, :, None] & (rank[:, :, None] == slots[None, None, :]), numbers[None, :, None], 0
        ),
        axis=1,
    )
    block_count = jnp.sum(seen, axis=1, dtype=jnp.int32)
    return bounds, by_segment, block_list, block_count


def causal_scores(scores, key_first, query_first):
    rows = key_first + lax.broadcasted_iota(jnp.int32, scores.shape, 0)
    columns = query_first + lax.broadcasted_iota(jnp.int32, scores.shape, 1)
    return jnp.where(rows <= columns, scores, -BIG)


def token_lanes(bounds_ref, first, count):
    token = first + lax.broadcasted_iota(jnp.int32, (count, 128), 0)
    lane = lax.broadcasted_iota(jnp.int32, (count, 128), 1)
    member = (token >= bounds_ref[0:1, :]) & (token < bounds_ref[1:2, :])
    base = 2 * PAIR_SEGS
    number = jnp.where(lane < base + 2, lax.shift_right_logical(token, 8), token & 255)
    fixed = jnp.where(lane < base + 7, 1, 0)
    number = jnp.where(lane < base + 4, number, fixed)
    return jnp.where(lane < base, jnp.where(member, 1, 0), number).astype(f32)


def pair_rows(packed):
    return jnp.concatenate([packed[:, :HD], packed[:, HD:]], axis=0)


def build_keys(bounds_ref, mixed_ref, keys, step):
    rows = mixed_ref.shape[1] * 2 // 3
    lane = lax.broadcasted_iota(jnp.int32, (rows, 128), 1)
    for part in range(2):
        first = (2 * step + part) * rows
        both = mixed_ref[2 * step + part, 0:rows, :].astype(f32)
        keys[pl.ds(pl.multiple_of(first, 64), rows), :] = jnp.where(
            lane < HD, token_lanes(bounds_ref, first, rows), both
        ).astype(bf16)


def query_lanes(bounds_ref, by_segment_ref, mixed_ref, number):
    rows = mixed_ref.shape[1] * 2 // 3
    meta = nn(token_lanes(bounds_ref, number * rows, rows).astype(bf16), by_segment_ref[...])
    queries = mixed_ref[number, 0:rows, 0:HD].astype(f32) * 0.125
    return jnp.concatenate([meta[:, :HD], queries], axis=1)


def forward_kernel(
    block_of,
    count_of,
    list_of,
    bounds_ref,
    by_segment_ref,
    mixed_ref,
    context_ref,
    out_ref,
    keys_ref,
    queries_ref,
    keys,
    values_t,
    queries_all,
    scores_a,
    scores_b,
    out_sem,
):
    messages, message_rows, _ = mixed_ref.shape
    rows = message_rows * 2 // 3
    tensor_count = context_ref.shape[1]
    steps = queries_all.shape[0] // QUERY_BLOCK

    def prepare(step, _):
        build_keys(bounds_ref, mixed_ref, keys, step)
        values = jnp.concatenate(
            [pair_rows(mixed_ref[2 * step + part, rows:, :]) for part in range(2)], axis=0
        )
        lane = lax.broadcasted_iota(jnp.int32, (2 * rows, HD), 1)
        ones = jnp.where(lane == 0, 1.0, 0.0).astype(bf16)
        wide = jnp.concatenate([values, ones], axis=1)
        values_t[:, pl.ds(pl.multiple_of(step * 2 * rows, 128), 2 * rows)] = wide.T[:VALUE_ROWS]
        return 0

    lax.fori_loop(0, messages // 2, prepare, 0)
    half = messages // (2 * tensor_count)

    def prepare_queries(step, _):
        number = block_of[(step // tensor_count) * (steps // half)] * QUERY_BLOCK // rows
        number = number + step % tensor_count
        queries_all[pl.ds(pl.multiple_of(step * rows, 64), rows), :] = query_lanes(
            bounds_ref, by_segment_ref, mixed_ref, number
        ).astype(bf16)
        return 0

    lax.fori_loop(0, messages // 2, prepare_queries, 0)
    keys_out = pltpu.make_async_copy(keys, keys_ref, out_sem.at[0])
    queries_out = pltpu.make_async_copy(queries_all, queries_ref, out_sem.at[1])
    keys_out.start()
    queries_out.start()

    def one_block(number, _):
        query_first = block_of[number] * QUERY_BLOCK
        here = pl.ds(pl.multiple_of(number * QUERY_BLOCK, QUERY_BLOCK), QUERY_BLOCK)
        queries = queries_all[here, :]

        count = count_of[number]

        def block_span(step):
            first = pl.multiple_of(list_of[number, step] * KEY_BLOCK, KEY_BLOCK)
            return pl.ds(first, KEY_BLOCK)

        def score_four(buffer, step):
            for part in range(4):
                buffer[part * KEY_BLOCK : (part + 1) * KEY_BLOCK, :] = nt(
                    keys[block_span(4 * step + part), :], queries
                )

        def absorb(scores, spans, carry):
            top, total = carry
            new_top = jnp.maximum(top, jnp.max(scores, axis=0, keepdims=True))
            weights = jnp.exp(scores - new_top).astype(bf16)
            total = total * jnp.exp(top - new_top)
            for part, span in enumerate(spans):
                total = total + nn(
                    values_t[:, span], weights[part * KEY_BLOCK : (part + 1) * KEY_BLOCK]
                )
            return new_top, total

        def absorb_four(buffer, step, carry):
            return absorb(buffer[...], [block_span(4 * step + part) for part in range(4)], carry)

        score_four(scores_a, 0)
        span = pl.ds(pl.multiple_of(query_first, KEY_BLOCK), KEY_BLOCK)
        scores = causal_scores(nt(keys[span, :], queries), query_first, query_first)
        carry = (jnp.full((1, QUERY_BLOCK), -BIG, f32), jnp.zeros((VALUE_ROWS, QUERY_BLOCK), f32))
        carry = absorb(scores, [span], carry)

        def eight_blocks(step, carry):
            score_four(scores_b, 2 * step + 1)
            carry = absorb_four(scores_a, 2 * step, carry)
            score_four(scores_a, 2 * step + 2)
            return absorb_four(scores_b, 2 * step + 1, carry)

        fours = count // 4
        carry = lax.fori_loop(0, fours // 2, eight_blocks, carry)
        carry = lax.fori_loop(
            0, fours % 2, lambda _, kept: absorb_four(scores_a, fours - 1, kept), carry
        )

        def last_blocks(blocks):
            def one(_, kept):
                spans = [block_span(count - count % (2 * blocks) + part) for part in range(blocks)]
                scores = [nt(keys[span, :], queries) for span in spans]
                return absorb(jnp.concatenate(scores, axis=0), spans, kept)

            return one

        carry = lax.fori_loop(0, count % 4 // 2, last_blocks(2), carry)
        top, total = lax.fori_loop(0, count % 2, last_blocks(1), carry)
        row_sum = total[HD : HD + 1]
        log_total = jnp.broadcast_to(top + jnp.log(row_sum), (HD, QUERY_BLOCK))
        out_ref[here, :] = jnp.concatenate([total[:HD] / row_sum, log_total], axis=0).T
        return 0

    lax.fori_loop(0, steps, one_block, 0)

    def pack(step, _):
        first = pl.multiple_of(step * rows, 64)
        half_rows = rows // 2
        context_ref[step // tensor_count, step % tensor_count] = jnp.concatenate(
            [
                out_ref[pl.ds(first, half_rows), 0:HD],
                out_ref[pl.ds(pl.multiple_of(first + half_rows, 32), half_rows), 0:HD],
            ],
            axis=1,
        ).astype(bf16)
        return 0

    lax.fori_loop(0, messages // 2, pack, 0)
    keys_out.wait()
    queries_out.wait()


def attention_forward(blocks, counts, lists, bounds, by_segment, mixed, tensor_count):
    messages, message_rows, _ = mixed.shape
    rows = message_rows * 2 // 3
    half = messages // 2 * rows
    smem = pl.BlockSpec(memory_space=pltpu.SMEM)
    vmem = pl.BlockSpec(memory_space=pltpu.VMEM)
    return pl.pallas_call(
        forward_kernel,
        in_specs=[smem] * 3 + [vmem] * 3,
        out_specs=[vmem, vmem] + [pl.BlockSpec(memory_space=pltpu.HBM)] * 2,
        out_shape=[
            jax.ShapeDtypeStruct(
                (messages // 2 // tensor_count, tensor_count, rows // 2, 2 * HD), bf16
            ),
            jax.ShapeDtypeStruct((half, 128), f32),
            jax.ShapeDtypeStruct((PAIR_TOKENS, 128), bf16),
            jax.ShapeDtypeStruct((half, 128), bf16),
        ],
        scratch_shapes=[
            pltpu.VMEM((PAIR_TOKENS, 128), bf16),
            pltpu.VMEM((VALUE_ROWS, PAIR_TOKENS), bf16),
            pltpu.VMEM((half, 128), bf16),
            pltpu.VMEM((4 * KEY_BLOCK, QUERY_BLOCK), f32),
            pltpu.VMEM((4 * KEY_BLOCK, QUERY_BLOCK), f32),
            pltpu.SemaphoreType.DMA((2,)),
        ],
        compiler_params=pltpu.CompilerParams(vmem_limit_bytes=40 * 2**20),
        cost_estimate=pl.CostEstimate(
            flops=2 * 256 * 2 * 12_000_000, bytes_accessed=10_000_000, transcendentals=12_000_000
        ),
        name="attention_forward",
    )(blocks, counts, lists, bounds, by_segment, mixed)


def backward_kernel(
    block_of,
    count_of,
    list_of,
    keys,
    forward_queries,
    mixed_ref,
    grads_ref,
    out_ref,
    dq_ref,
    dkv_ref,
    keys_t,
    values,
    queries_all,
    grads_all,
    queries_only,
    grads_only,
    dkv,
):
    messages, message_rows, _ = mixed_ref.shape
    rows = message_rows * 2 // 3
    tensor_count = grads_ref.shape[1]
    steps = queries_all.shape[0] // QUERY_BLOCK
    half = messages // (2 * tensor_count)

    def with_pieces(value, first_lane, wide):
        lane = lax.broadcasted_iota(jnp.int32, wide.shape, 1)
        for piece in range(3):
            part = value.astype(bf16).astype(f32)
            wide = jnp.where(lane == first_lane + piece, part, wide)
            value = value - part
        return wide

    def prepare(step, _):
        span = pl.ds(pl.multiple_of(step * 2 * rows, 128), 2 * rows)
        keys_t[:, span] = keys[span, :].T[HD:]
        packed = jnp.concatenate(
            [pair_rows(mixed_ref[2 * step + part, rows:, :]) for part in range(2)], axis=0
        )
        lane = lax.broadcasted_iota(jnp.int32, (2 * rows, HD), 1)
        ones = jnp.where(lane < 3, 1.0, 0.0).astype(bf16)
        values[span, :] = jnp.concatenate([ones, packed], axis=1)
        dkv[span, :] = jnp.zeros((2 * rows, 128), f32)
        return 0

    lax.fori_loop(0, messages // 2, prepare, 0)

    def prepare_queries(step, _):
        number = block_of[(step // tensor_count) * (steps // half)] * QUERY_BLOCK // rows
        number = number + step % tensor_count
        span = pl.ds(pl.multiple_of(step * rows, 64), rows)
        wide = forward_queries[span, :].astype(f32)
        out = out_ref[span, :]
        queries_all[span, :] = with_pieces(-out[:, HD : HD + 1], 2 * PAIR_SEGS + 4, wide).astype(bf16)
        lane = lax.broadcasted_iota(jnp.int32, (rows, 128), 1)
        queries = mixed_ref[number, 0:rows, :].astype(f32) * 0.125
        queries_only[span, :] = jnp.where(lane < HD, queries, 0.0).astype(bf16)
        grads = pair_rows(grads_ref[step // tensor_count, step % tensor_count].astype(f32))
        inner = jnp.sum(grads * out[:, :HD], axis=1, keepdims=True)
        wide = jnp.concatenate([jnp.zeros((rows, HD), f32), grads], axis=1)
        grads_only[span, :] = wide.astype(bf16)
        grads_all[span, :] = with_pieces(-inner, 0, wide).astype(bf16)
        return 0

    lax.fori_loop(0, messages // 2, prepare_queries, 0)

    def one_block(number, _):
        query_first = block_of[number] * QUERY_BLOCK
        here = pl.ds(pl.multiple_of(number * QUERY_BLOCK, QUERY_BLOCK), QUERY_BLOCK)
        queries = queries_all[here, :]
        grads = grads_all[here, :]
        both = jnp.concatenate([queries_only[here, :], grads_only[here, :]], axis=0)

        count = count_of[number]

        def attend(blocks, dq, masked):
            spans = [pl.ds(pl.multiple_of(block * KEY_BLOCK, KEY_BLOCK), KEY_BLOCK) for block in blocks]
            scores = [nt(keys[span, :], queries) for span in spans]
            if masked:
                scores = [causal_scores(scores[0], blocks[0] * KEY_BLOCK, query_first)]
            grads_of = [nt(values[span, :], grads) for span in spans]
            for span, score, grad in zip(spans, scores, grads_of):
                weights = jnp.exp(score)
                score_grad = (weights * grad).astype(bf16)
                dkv[span, :] += nn(
                    jnp.concatenate([score_grad, weights.astype(bf16)], axis=1), both
                )
                dq = dq + nn(keys_t[:, span], score_grad)
            return dq

        def listed(first, blocks):
            return lambda step, kept: attend(
                [list_of[number, first + blocks * step + part] for part in range(blocks)], kept, False
            )

        dq = attend([query_first // KEY_BLOCK], jnp.zeros((HD, QUERY_BLOCK), f32), True)
        eights, rest = count // 8, count % 8
        dq = lax.fori_loop(0, eights, listed(0, 8), dq)
        dq = lax.fori_loop(0, rest // 4, listed(8 * eights, 4), dq)
        dq = lax.fori_loop(0, rest % 4 // 2, listed(count - rest % 4, 2), dq)
        dq = lax.fori_loop(0, rest % 2, listed(count - 1, 1), dq)
        dq_ref[here, :] = (dq * 0.125).T.astype(bf16)
        return 0

    lax.fori_loop(0, steps, one_block, 0)

    def write(step, _):
        span = pl.ds(pl.multiple_of(step * KEY_BLOCK, KEY_BLOCK), KEY_BLOCK)
        dkv_ref[span, :] = dkv[span, :].astype(bf16)
        return 0

    lax.fori_loop(0, PAIR_TOKENS // KEY_BLOCK, write, 0)


def attention_backward(blocks, counts, lists, keys, queries, mixed, grads, out):
    smem = pl.BlockSpec(memory_space=pltpu.SMEM)
    vmem = pl.BlockSpec(memory_space=pltpu.VMEM)
    half = out.shape[0]
    return pl.pallas_call(
        backward_kernel,
        in_specs=[smem] * 3 + [vmem] * 5,
        out_specs=[vmem, vmem],
        out_shape=[
            jax.ShapeDtypeStruct((half, HD), bf16),
            jax.ShapeDtypeStruct((PAIR_TOKENS, 128), bf16),
        ],
        scratch_shapes=[
            pltpu.VMEM((HD, PAIR_TOKENS), bf16),
            pltpu.VMEM((PAIR_TOKENS, 128), bf16),
            pltpu.VMEM((half, 128), bf16),
            pltpu.VMEM((half, 128), bf16),
            pltpu.VMEM((half, 128), bf16),
            pltpu.VMEM((half, 128), bf16),
            pltpu.VMEM((PAIR_TOKENS, 128), f32),
        ],
        compiler_params=pltpu.CompilerParams(vmem_limit_bytes=56 * 2**20),
        cost_estimate=pl.CostEstimate(
            flops=5 * 256 * 2 * 12_000_000, bytes_accessed=16_000_000, transcendentals=12_000_000
        ),
        name="attention_backward",
    )(blocks, counts, lists, keys, queries, mixed, grads, out)


def flipped(chip, chips):
    return (chip + chips - 1) // chips


def greet_all(dp_count, tensor_count, dp_index, tensor_index):
    barrier = pltpu.get_barrier_semaphore()
    total = dp_count * tensor_count
    me = dp_index * tensor_count + tensor_index

    def greet(step, _):
        other = (me + step) % total
        pl.semaphore_signal(
            barrier,
            inc=1,
            device_id=(other // tensor_count, other % tensor_count),
            device_id_type=MESH,
        )
        return 0

    lax.fori_loop(1, total, greet, 0)
    pl.semaphore_wait(barrier, total - 1)


def repeat(count, body):
    def one(step, _):
        body(step)
        return 0

    lax.fori_loop(0, count, one, 0)


def swap_copy(source, target, sems, number, partner):
    return pltpu.make_async_remote_copy(
        src_ref=source,
        dst_ref=target,
        send_sem=sems.at[0, number],
        recv_sem=sems.at[1, number],
        device_id=partner,
        device_id_type=MESH,
    )


def layer_norm_back(values, gain, grads):
    average = jnp.mean(values, axis=-1, keepdims=True)
    centred = values - average
    scale = lax.rsqrt(jnp.mean(centred * centred, axis=-1, keepdims=True) + epsilon)
    normed = centred * scale
    scaled = grads * gain
    first = jnp.mean(scaled, axis=-1, keepdims=True)
    second = jnp.mean(scaled * normed, axis=-1, keepdims=True)
    return (scaled - first - normed * second) * scale, grads * normed


def column_sum(values):
    return jnp.sum(values, axis=0, keepdims=True)


def transpose_rows(source, target):
    size = min(256, target.shape[0])

    def one(step):
        span = pl.ds(pl.multiple_of(step * size, size), size)
        target[span, :] = source[:, span].T

    repeat(target.shape[0] // size, one)


def nearest(layer, layers, step):
    tile = 0 * layer
    for here in range(layers):
        order = sorted(
            range(layers),
            key=lambda there: (there == here, abs(there - here), abs(2 * there - layers + 1)),
        )
        for number, there in enumerate(order):
            tile = jnp.where((layer == here) & (step == number), there, tile)
    return tile


def doubling_gather(
    weight, recv_sem, send_sem, layer_recv, layer_send, chip, chips, core, layer, layers, dp_index
):
    stages = chips.bit_length() - 1
    steps = weight.shape[0]
    slot_of = (lambda step: step) if layer_recv is None else (lambda step: nearest(layer, layers, step))

    def layer_copy(tile, way):
        block = weight.at[tile, chip]
        return pltpu.make_async_remote_copy(
            src_ref=block,
            dst_ref=block,
            send_sem=layer_send.at[tile, way],
            recv_sem=layer_recv.at[tile],
            device_id=(dp_index, layer + 2 * way - 1),
            device_id_type=MESH,
        )

    def ways(tile, body):
        for way in range(2):
            inside = (layer + 1 < layers) & (tile <= layer) if way else (layer > 0) & (tile >= layer)

            @pl.when(inside)
            def _():
                body(layer_copy(tile, way))

    def spread():
        ways(layer, lambda copy: copy.start())

    rows = weight.shape[2] // 2

    def half(order):
        return pl.ds(pl.multiple_of(order * rows, rows), rows)

    def place(order, stage, step):
        size = jnp.where(order == 0, 2**stage, chips // 2 ** (stage + 1))
        bit = chip // size % 2
        across = size * (1 - 2 * bit)
        held = jnp.where(
            order == 0,
            chip // 2**stage * 2**stage + step,
            chip % (chips // 2**stage) + step * (chips // 2**stage),
        )
        return held, held + across, chip + across

    def copy(step, stage, order, number):
        slot = slot_of(step)
        held, _, partner = place(order, stage, number)
        block = weight.at[slot, held, half(order), :]
        return pltpu.make_async_remote_copy(
            src_ref=block,
            dst_ref=block,
            send_sem=send_sem.at[slot, 2**stage - 1 + number, order],
            recv_sem=recv_sem.at[slot, held, order],
            device_id=(2 * partner + core, layer),
            device_id_type=MESH,
        )

    def wait_block(block, sem):
        pltpu.make_async_remote_copy(
            src_ref=block,
            dst_ref=block,
            send_sem=send_sem.at[0, 0, 0],
            recv_sem=sem,
            device_id=(2 * chip + 1 - core, layer),
            device_id_type=MESH,
        ).wait_recv()

    def each(stage, body):
        repeat(2 * 2**stage, lambda number: body(number % 2, number // 2))

    def arrived(step, stage):
        slot = slot_of(step)

        def one(order, number):
            _, got, _ = place(order, stage, number)
            wait_block(weight.at[slot, got, half(order), :], recv_sem.at[slot, got, order])

        each(stage, one)

    def advance(number):
        for stage in range(stages):
            step = number - stage

            @pl.when((step >= 0) & (step < steps))
            def _():
                if stage > 0:
                    arrived(step, stage - 1)
                else:

                    if layer_recv is not None:

                        tile = slot_of(step)

                        @pl.when(tile != layer)
                        def _():
                            wait_block(weight.at[tile, chip], layer_recv.at[tile])
                            ways(tile, lambda copy: copy.start())

                each(stage, lambda order, each_number: copy(step, stage, order, each_number).start())

    def ready(step):
        arrived(step, stages - 1)

    def sent():
        if layer_send is not None:
            repeat(steps, lambda tile: ways(tile, lambda copy: copy.wait_send()))

        def one(step):
            for stage in range(stages):
                each(
                    stage,
                    lambda order, number: copy(step, stage, order, number).wait_send(),
                )

        repeat(steps, one)

    return spread, advance, ready, sent


def picked(rows, lanes, owner_of, lane_of, keep):
    lane = lax.broadcasted_iota(jnp.int32, (128, lanes), 1)
    source = lax.broadcasted_iota(jnp.int32, (128, lanes), 0)
    spread = nn(rows.astype(bf16), jnp.where(source == lane_of(lane), 1.0, 0.0).astype(bf16))
    lane = lax.broadcasted_iota(jnp.int32, (rows.shape[0], lanes), 1)
    owner = lax.broadcasted_iota(jnp.int32, (rows.shape[0], lanes), 0)
    return column_sum(jnp.where((owner == owner_of(lane)) & keep(lane), spread, 0.0))


def project_kernel(
    dp_count,
    tensor_count,
    span,
    x_ref,
    small_ref,
    shard_ref,
    feed_ref,
    normed_ref,
    mixed_ref,
    weight_out_ref,
    vectors_ref,
    up_shift_ref,
    block_ref,
    normed,
    weight,
    smalls,
    outbox,
    swap_sem,
    small_send,
    small_recv,
    half_sem,
    gather_recv,
    gather_send,
    layer_recv,
    layer_send,
    out_sem,
    send_sem,
    recv_sem,
    local_sem,
    pass_send,
    pass_recv,
):
    dp_index, tensor_index = lax.axis_index("dp"), lax.axis_index("tensor")
    rows, width = x_ref.shape
    hidden = weight.shape[3]
    columns = hidden - 128
    piece = shard_ref.shape[1]
    core = dp_index % 2
    base = dp_index // span * span
    chip = dp_index % span // 2
    chips = span // 2
    layer_chip, layer_chips = dp_index // 2, dp_count // 2
    partner = (dp_index + 1 - 2 * core, tensor_index)
    total = dp_count * tensor_count
    me = dp_index * tensor_count + tensor_index

    def small_copy(step):
        other = (me + step) % total
        place = smalls.at[dp_index, tensor_index]
        return pltpu.make_async_remote_copy(
            src_ref=place,
            dst_ref=place,
            send_sem=small_send.at[other // tensor_count, other % tensor_count],
            recv_sem=small_recv.at[dp_index, tensor_index],
            device_id=(other // tensor_count, other % tensor_count),
            device_id_type=MESH,
        )

    def small_wait(step):
        other = (me + step) % total
        there = other // tensor_count, other % tensor_count
        place = smalls.at[there[0], there[1]]
        pltpu.make_async_remote_copy(
            src_ref=place,
            dst_ref=place,
            send_sem=small_send.at[there[0], there[1]],
            recv_sem=small_recv.at[there[0], there[1]],
            device_id=partner,
            device_id_type=MESH,
        ).wait_recv()

    own_rows = pl.ds(pl.multiple_of(core * piece, piece), piece)
    smalls[dp_index, tensor_index] = small_ref[...]
    weight[tensor_index, layer_chip, own_rows, :] = shard_ref[core]
    greet_all(dp_count, tensor_count, dp_index, tensor_index)
    half = pltpu.make_async_remote_copy(
        src_ref=shard_ref.at[1 - core],
        dst_ref=weight.at[tensor_index, layer_chip, own_rows, :],
        send_sem=half_sem.at[0],
        recv_sem=half_sem.at[1],
        device_id=partner,
        device_id_type=MESH,
    )
    half.start()
    block_ref[own_rows, :] = feed_ref[core]
    feed_half = pltpu.make_async_remote_copy(
        src_ref=feed_ref.at[1 - core],
        dst_ref=block_ref.at[own_rows, :],
        send_sem=half_sem.at[2],
        recv_sem=half_sem.at[3],
        device_id=partner,
        device_id_type=MESH,
    )
    feed_half.start()
    repeat(total - 1, lambda step: small_copy(step + 1).start())
    spread, advance, ready, gather_sent = doubling_gather(
        weight,
        gather_recv,
        gather_send,
        layer_recv,
        layer_send,
        layer_chip,
        layer_chips,
        core,
        tensor_index,
        tensor_count,
        dp_index,
    )
    half.wait_recv()
    spread()
    repeat(total - 1, lambda step: small_wait(step + 1))

    def vector(number):
        here = smalls[:, tensor_index].astype(f32)[:, number, :]
        return picked(
            here, width, lambda lane: lane // piece, lambda lane: lane % piece, lambda lane: lane >= 0
        )

    normed[core] = normalize(x_ref[...].astype(f32), vector(0), vector(1)).astype(bf16)
    swap = pltpu.make_async_remote_copy(
        src_ref=normed.at[core],
        dst_ref=normed.at[core],
        send_sem=swap_sem.at[0],
        recv_sem=swap_sem.at[1],
        device_id=partner,
        device_id_type=MESH,
    )
    swap.start()
    stages = layer_chips.bit_length() - 1
    for number in range(stages):
        advance(number)

    bias_width = 2 * HD // dp_count

    def qkv_shift(owner):
        here = smalls[:, owner].astype(f32)[:, 6, :]

        def column(lane):
            return lane % HD + jnp.where(lane % (3 * HD) < HD, 0, HD)

        return picked(
            here,
            columns,
            lambda lane: column(lane) // bias_width,
            lambda lane: (2 * core + lane // (3 * HD)) * bias_width + column(lane) % bias_width,
            lambda lane: (lane % (3 * HD) < HD) | (lane % (3 * HD) >= 2 * HD),
        )

    def up_shift(owner):
        here = smalls[:, owner].astype(f32)[:, 7, :]
        return picked(
            here,
            hidden,
            lambda lane: lane % 128 // bias_width,
            lambda lane: (core * (hidden // 128) + lane // 128) * bias_width
            + lane % 128 % bias_width,
            lambda lane: lane >= 0,
        )

    swap.wait_recv()

    def out_copy(owner):
        return pltpu.make_async_copy(weight.at[owner], weight_out_ref.at[owner], out_sem.at[owner])

    def slot(place_dp, place_tensor):
        return mixed_ref.at[place_dp * tensor_count + place_tensor]

    def send(owner, part, pair):
        head_chip = 2 * core + pair
        target = (base + 2 * head_chip + (part + flipped(chip, chips)) % 2, owner)
        here = (target[0] == dp_index) & (owner == tensor_index)
        return here, pltpu.make_async_remote_copy(
            src_ref=outbox.at[owner, part, pair],
            dst_ref=slot(2 * chip + part, tensor_index),
            send_sem=send_sem.at[owner, part, pair],
            recv_sem=recv_sem.at[chip, tensor_index],
            device_id=target,
            device_id_type=MESH,
        ), pltpu.make_async_copy(
            outbox.at[owner, part, pair], slot(2 * chip + part, tensor_index), local_sem.at[0]
        )

    def one_tile(step):
        owner = nearest(tensor_index, tensor_count, step)
        advance(step + stages)
        ready(step)
        out_copy(owner).start()
        shift = qkv_shift(owner)

        def one_part(part):
            matrix = weight[owner, :, :, 0:columns].reshape(width, columns)
            result = nn(normed[part], matrix) + shift
            first = [result[:, 0:128], result[:, 192:320]]
            last = [result[:, 128:192], result[:, 320:384]]
            for pair in range(2):
                outbox[owner, part, pair, 0:rows, :] = first[pair].astype(bf16)
                outbox[owner, part, pair, rows:, :] = jnp.concatenate(
                    [last[pair][: rows // 2], last[pair][rows // 2 :]], axis=1
                ).astype(bf16)
                here, far, near = send(owner, part, pair)

                @pl.when(here)
                def _():
                    near.start()

                @pl.when(jnp.logical_not(here))
                def _():
                    far.start()

        repeat(2, one_part)

    repeat(tensor_count, one_tile)
    normed_ref[...] = normed[...]

    vectors_ref[...] = jnp.zeros_like(vectors_ref)
    for number in (0, 2, 3, 4, 5):
        vectors_ref[number : number + 1, :] = vector(number)

    def put_up_shift(owner):
        up_shift_ref[owner] = jnp.broadcast_to(up_shift(owner), up_shift_ref.shape[1:])

    repeat(tensor_count, put_up_shift)

    def arrival(step):
        from_chip, from_tensor = step % chips, nearest(tensor_index, tensor_count, step // chips)
        mine = slot(2 * from_chip + (core + flipped(from_chip, chips)) % 2, from_tensor)
        theirs = slot(2 * from_chip + (core + flipped(from_chip, chips) + 1) % 2, from_tensor)
        here = (from_chip == chip) & (from_tensor == tensor_index) & (chip // 2 == core)

        def passing(place):
            return pltpu.make_async_remote_copy(
                src_ref=place,
                dst_ref=place,
                send_sem=pass_send.at[from_chip, from_tensor],
                recv_sem=pass_recv.at[from_chip, from_tensor],
                device_id=partner,
                device_id_type=MESH,
            )

        return mine, theirs, here, passing, from_chip, from_tensor

    def hand_on(step):
        mine, _theirs, here, passing, from_chip, from_tensor = arrival(step)

        @pl.when(here)
        def _():
            pltpu.make_async_copy(mine, mine, local_sem.at[0]).wait()

        @pl.when(jnp.logical_not(here))
        def _():
            pltpu.make_async_remote_copy(
                src_ref=mine,
                dst_ref=mine,
                send_sem=pass_send.at[from_chip, from_tensor],
                recv_sem=recv_sem.at[from_chip, from_tensor],
                device_id=partner,
                device_id_type=MESH,
            ).wait_recv()

        passing(mine).start()

    repeat(chips * tensor_count, hand_on)

    def finish(step):
        mine, theirs, _here, passing, _a, _b = arrival(step)
        passing(mine).wait_send()
        passing(theirs).wait_recv()

    repeat(chips * tensor_count, finish)

    def sent(step):
        here, far, _near = send(step // 4, step // 2 % 2, step % 2)

        @pl.when(jnp.logical_not(here))
        def _():
            far.wait_send()

    repeat(4 * tensor_count, sent)
    repeat(total - 1, lambda step: small_copy(step + 1).wait_send())
    repeat(tensor_count, lambda owner: out_copy(owner).wait())
    half.wait_send()
    feed_half.wait()
    swap.wait_send()
    gather_sent()


def project(inputs, small, shard, feed, dp_count, tensor_count, span):
    rows, width = inputs.shape
    _, piece, hidden = shard.shape
    messages = span * tensor_count
    chips, layer_chips = span // 2, dp_count // 2
    dma = pltpu.SemaphoreType.DMA
    vmem = pl.BlockSpec(memory_space=pltpu.VMEM)
    anywhere = pl.BlockSpec(memory_space=pl.ANY)
    weight = (tensor_count, layer_chips, 2 * piece, hidden)
    return pl.pallas_call(
        functools.partial(project_kernel, dp_count, tensor_count, span),
        in_specs=[vmem] * 4,
        out_specs=[vmem, anywhere, pl.BlockSpec(memory_space=pltpu.HBM), vmem, vmem, vmem],
        out_shape=[
            jax.ShapeDtypeStruct((2, rows, width), bf16),
            jax.ShapeDtypeStruct((messages, rows * 3 // 2, 128), bf16),
            jax.ShapeDtypeStruct(weight, bf16),
            jax.ShapeDtypeStruct((8, width), f32),
            jax.ShapeDtypeStruct((tensor_count, 8, hidden), f32),
            jax.ShapeDtypeStruct((2 * piece, feed.shape[2]), bf16),
        ],
        scratch_shapes=[
            pltpu.VMEM((2, rows, width), bf16),
            pltpu.VMEM(weight, bf16),
            pltpu.VMEM((dp_count, tensor_count, 16, 128), bf16),
            pltpu.VMEM((tensor_count, 2, 2, rows * 3 // 2, 128), bf16),
            dma((2,)),
            dma((dp_count, tensor_count)),
            dma((dp_count, tensor_count)),
            dma((4,)),
            dma((tensor_count, layer_chips, 2)),
            dma((tensor_count, layer_chips - 1, 2)),
            dma((tensor_count,)),
            dma((tensor_count, 2)),
            dma((tensor_count,)),
            dma((tensor_count, 2, 2)),
            dma((chips, tensor_count)),
            dma((1,)),
            dma((chips, tensor_count)),
            dma((chips, tensor_count)),
        ],
        compiler_params=pltpu.CompilerParams(
            collective_id=0, has_side_effects=True, vmem_limit_bytes=40 * 2**20
        ),
        cost_estimate=pl.CostEstimate(
            flops=2 * 2 * rows * width * hidden * tensor_count,
            bytes_accessed=20_000_000,
            transcendentals=0,
        ),
        name="project",
    )(inputs, small, shard, feed)


def halving_scatter(parts, inbox, send_sem, recv_sem, chip, chips, core, layer):
    stages = chips.bit_length() - 1
    rows = parts.shape[2] // 2

    def places(order, stage, step):
        size = jnp.where(order == 0, 2**stage, chips // 2 ** (stage + 1))
        bit = chip // size % 2
        low, high = chip % size, chip // (2 * size) * (2 * size)
        rest = jnp.where(order == 0, low + step * 2 * size, high + step)
        theirs = rest + (1 - bit) * size
        return theirs, rest + bit * size, chip + (1 - 2 * bit) * size

    def half(order):
        return pl.ds(pl.multiple_of(order * rows, rows), rows)

    def copy(item, stage, order, step):
        theirs, _, partner = places(order, stage, step)
        where = chips - chips // 2**stage + step
        return pltpu.make_async_remote_copy(
            src_ref=parts.at[item, theirs, half(order), :],
            dst_ref=inbox.at[item, where, half(order), :],
            send_sem=send_sem.at[item, where, order],
            recv_sem=recv_sem.at[item, where, order],
            device_id=(2 * partner + core, layer),
            device_id_type=MESH,
        )

    def each(stage, body):
        count = chips // 2 ** (stage + 1)
        repeat(2 * count, lambda number: body(number % 2, number // 2))

    def start(item, stage):
        each(stage, lambda order, step: copy(item, stage, order, step).start())

    def finish(item, stage):
        def one(order, step):
            copy(item, stage, order, step).wait_recv()
            _, keep, _ = places(order, stage, step)
            where = chips - chips // 2**stage + step
            parts[item, keep, half(order), :] = (
                parts[item, keep, half(order), :].astype(f32)
                + inbox[item, where, half(order), :].astype(f32)
            ).astype(bf16)

        each(stage, one)

    def add(item, stage):
        def one(order, step):
            _, keep, _ = places(order, stage, step)
            where = chips - chips // 2**stage + step
            parts[item, keep, half(order), :] = (
                parts[item, keep, half(order), :].astype(f32)
                + inbox[item, where, half(order), :].astype(f32)
            ).astype(bf16)

        each(stage, one)

    def sent(item, stage):
        each(stage, lambda order, step: copy(item, stage, order, step).wait_send())

    return stages, start, finish, sent, add


def middle_kernel(
    dp_count,
    tensor_count,
    span,
    context_ref,
    x_ref,
    cot_ref,
    cot_across_ref,
    vectors_in_ref,
    up_shift_ref,
    feed_ref,
    weight_ref,
    block_ref,
    middle_grad_ref,
    feed_sum_ref,
    dense_send0_ref,
    dense_send1_ref,
    dense_keep_ref,
    vectors_ref,
    up_shift_grad_ref,
    grads_ref,
    context_in,
    context,
    dense,
    feed,
    middle,
    normed,
    cot,
    turned_normed,
    turned_cot,
    active,
    upper_grad,
    out_total,
    normed_total,
    swap_in,
    core_in,
    pair_in,
    low_grad,
    outbox,
    parts,
    inbox,
    dense_parts,
    weight_sem,
    swap_sem,
    share_send,
    share_recv,
    context_send,
    context_recv,
    outbox_send,
    outbox_recv,
    local_sem,
    gather_recv,
    gather_send,
    parts_send,
    parts_recv,
    dense_sem,
):
    dp_index, tensor_index = lax.axis_index("dp"), lax.axis_index("tensor")
    rows, width = x_ref.shape
    hidden = active.shape[2]
    steps = feed.shape[0]
    core = dp_index % 2
    base = dp_index // span * span
    chip = dp_index % span // 2
    chips = span // 2
    layer_chip, layer_chips = dp_index // 2, dp_count // 2
    pair_rows_count = parts.shape[2]
    piece = pair_rows_count // 2
    side = tensor_index % 2
    partner = (dp_index + 1 - 2 * core, tensor_index)
    across = (dp_index, tensor_index + 1 - 2 * side)
    own_part = 2 * side + core
    part_span = lambda part: pl.ds(pl.multiple_of(part * rows, 64), rows)
    mine, theirs = part_span(core), part_span(1 - core)

    def dense_copy(owner):
        return pltpu.make_async_copy(
            weight_ref.at[owner, :, pl.ds(weight_ref.shape[2] - 128, 128)],
            dense.at[:, pl.ds(pl.multiple_of(owner * 128, 128), 128)],
            weight_sem.at[owner],
        )

    repeat(tensor_count, lambda owner: dense_copy(owner).start())
    gain_ref, bias_ref, dense_shift_ref, down_shift_ref = (
        vectors_in_ref.at[number : number + 1] for number in range(2, 6)
    )
    across_part = own_part + 2 - 4 * side
    cot[part_span(own_part), :] = cot_ref[...]
    cot[part_span(across_part), :] = cot_across_ref[...]
    feed[:, layer_chip] = feed_ref[...]
    greet_all(dp_count, tensor_count, dp_index, tensor_index)
    _, gather, ready, gather_sent = doubling_gather(
        feed,
        gather_recv,
        gather_send,
        None,
        None,
        layer_chip,
        layer_chips,
        core,
        tensor_index,
        tensor_count,
        dp_index,
    )
    gather_steps = steps + layer_chips.bit_length() - 2

    def context_out(step):
        place = step % chips
        owner = nearest(tensor_index, tensor_count, (2 * tensor_count - 2 - step // chips) % tensor_count)
        part = (core + flipped(place, chips)) % 2
        target = (base + 2 * place + chip // 2, owner)
        here = (target[0] == dp_index) & (owner == tensor_index)
        source = context_ref.at[place, owner]
        destination = context_in.at[tensor_index, chip % 2, part]
        far = pltpu.make_async_remote_copy(
            src_ref=source,
            dst_ref=destination,
            send_sem=context_send.at[place, owner],
            recv_sem=context_recv.at[tensor_index, chip % 2, part],
            device_id=target,
            device_id_type=MESH,
        )
        near = pltpu.make_async_copy(source, destination, local_sem.at[0])
        return here, far, near

    def send_context(step):
        here, far, near = context_out(step)

        @pl.when(here)
        def _():
            near.start()

        @pl.when(jnp.logical_not(here))
        def _():
            far.start()

    repeat(chips * tensor_count, send_context)

    def share_copy(array, which, number):
        source = own_part if number < 2 else own_part + 2 - 4 * side
        block = array.at[part_span(source)]
        return pltpu.make_async_remote_copy(
            src_ref=block,
            dst_ref=block,
            send_sem=share_send.at[which, number],
            recv_sem=share_recv.at[which, number],
            device_id=across if number == 1 else partner,
            device_id_type=MESH,
        )

    def share_arrival(array, which, number):
        source = (
            own_part + 1 - 2 * core,
            own_part + 2 - 4 * side,
            own_part + 2 - 4 * side + 1 - 2 * core,
        )[number]
        block = array.at[part_span(source)]
        return pltpu.make_async_remote_copy(
            src_ref=block,
            dst_ref=block,
            send_sem=share_send.at[which, number],
            recv_sem=share_recv.at[which, number],
            device_id=partner,
            device_id_type=MESH,
        )

    gather(0)
    share_copy(cot, 0, 0).start()
    share_copy(cot, 0, 2).start()
    repeat(4, lambda part: out_total.__setitem__(part, jnp.zeros((rows, width), f32)))
    repeat(4, lambda part: normed_total.__setitem__(part, jnp.zeros((rows, width), f32)))

    def take_context(step):
        owner, part = (tensor_index + step // 2) % tensor_count, step % 2
        for pair in range(2):
            destination = context_in.at[owner, pair, part]
            here = (
                (owner == tensor_index)
                & (chip == 2 * core + pair)
                & ((part + flipped(chip, chips)) % 2 == core)
            )

            @pl.when(here)
            def _():
                pltpu.make_async_copy(destination, destination, local_sem.at[0]).wait()

            @pl.when(jnp.logical_not(here))
            def _():
                pltpu.make_async_remote_copy(
                    src_ref=destination,
                    dst_ref=destination,
                    send_sem=context_send.at[0, 0],
                    recv_sem=context_recv.at[owner, pair, part],
                    device_id=partner,
                    device_id_type=MESH,
                ).wait_recv()

        first, second = context_in[owner, 0, part], context_in[owner, 1, part]
        lanes = pl.ds(pl.multiple_of(owner * 128, 128), 128)
        half = rows // 2
        for number in range(2):
            cut = slice(number * HD, (number + 1) * HD)
            where = pl.ds(pl.multiple_of(part * rows + number * half, 32), half)
            context[where, lanes] = jnp.concatenate([first[:, cut], second[:, cut]], axis=1)

    for number in range(1, gather_steps):
        gather(number)
    repeat(2 * tensor_count, take_context)
    repeat(tensor_count, lambda owner: dense_copy(owner).wait())

    low_grad[theirs, :] = nt(context[theirs, :], dense[...]).astype(bf16)
    first_swap = swap_copy(low_grad.at[theirs], swap_in, swap_sem, 0, partner)
    first_swap.start()
    own = x_ref[...].astype(f32) + dense_shift_ref[...] + nt(context[mine, :], dense[...])
    first_swap.wait()
    middle[...] = own + swap_in[...].astype(f32)
    normed[part_span(own_part), :] = normalize(middle[...], gain_ref[...], bias_ref[...]).astype(bf16)
    share_copy(normed, 1, 1).start()
    share_copy(normed, 1, 0).start()
    share_arrival(cot, 0, 0).wait_recv()
    share_arrival(cot, 0, 2).wait_recv()
    transpose_rows(cot, turned_cot)
    share_arrival(normed, 1, 0).wait_recv()

    def one_part(index):
        step, turn = index % (2 * steps) // 2, index // (2 * steps) * 2 + index % 2
        owner = (tensor_index + step * (tensor_count // steps)) % tensor_count
        part = 2 * ((side + turn // 2) % 2) + (core + turn) % 2

        @pl.when(turn == 0)
        def _():
            ready(step)
            up_shift_grad_ref[step] = jnp.zeros((8, hidden), f32)

        @pl.when((step == 0) & (turn == 2))
        def _():
            share_arrival(normed, 1, 1).wait_recv()
            share_copy(normed, 1, 2).start()

        @pl.when((step == 0) & (turn == 3))
        def _():
            share_arrival(normed, 1, 2).wait_recv()

        here = part_span(part)
        up_matrix = feed[step, :, :, 0:hidden].reshape(width, hidden)
        down_matrix = feed[step, :, :, hidden:].reshape(width, hidden)
        upper = nn(normed[here, :], up_matrix) + up_shift_ref[owner, 0:1]
        active_grad = nn(cot[here, :], down_matrix)
        square = upper * upper
        bent = jnp.tanh(0.7978845608 * upper * (1.0 + 0.044715 * square))
        rising = 0.5 * (1.0 + bent)
        slope = rising + 0.5 * upper * (1.0 - bent * bent) * 0.7978845608 * (
            1.0 + 3.0 * 0.044715 * square
        )
        low = (active_grad * slope).astype(bf16)
        active_low = (upper * rising).astype(bf16)
        active[step, here, :] = active_low
        upper_grad[step, here, :] = low
        up_shift_grad_ref[step, 0:1] += column_sum(low.astype(f32))
        normed_total[part] += nt(low, up_matrix)
        out_total[part] += nt(active_low, down_matrix)

    repeat(4 * steps, one_part)

    def core_copy(which):
        return swap_copy(
            cot.at[pl.ds(2 * which * rows, 2 * rows)], core_in.at[which], swap_sem, 1 + which, partner
        )

    def pair_copy(which):
        source = normed.at[pl.ds(0, rows)] if which else swap_in
        return swap_copy(source, pair_in.at[which], swap_sem, 3 + which, across)

    totals = (normed_total, out_total)
    for number in (0, 2):
        share_copy(cot, 0, number).wait_send()
    for which in range(2):
        for number in range(2):
            cot[pl.ds((2 * which + number) * rows, rows), :] = totals[which][
                2 * number + 1 - core
            ].astype(bf16)
        core_copy(which).start()
    def add_cores(which):
        core_copy(which).wait_recv()
        value = (
            totals[which][2 * (1 - side) + core] + core_in[which, part_span(1 - side), :].astype(f32)
        ).astype(bf16)
        if which:
            normed[pl.ds(0, rows), :] = value
        else:
            swap_in[...] = value
        pair_copy(which).start()

    def whole(which):
        pair_copy(which).wait_recv()
        return (
            totals[which][own_part]
            + core_in[which, part_span(side), :].astype(f32)
            + pair_in[which].astype(f32)
        )

    add_cores(0)

    transpose_rows(normed, turned_normed)
    half_chips = layer_chips // 2

    def set_out(array, refs, item, place, sems):
        for order in range(2):
            bit = place % 2 if order == 0 else place // half_chips
            own_bit = layer_chip % 2 if order == 0 else layer_chip // half_chips
            slot = place // 2 if order == 0 else place % half_chips
            block = array.at[pl.ds(order * piece, piece), :]
            goes = pltpu.make_async_copy(block, refs[order].at[item, slot], sems.at[order])
            stays = pltpu.make_async_copy(block, refs[2].at[order, item, slot], sems.at[order])

            @pl.when(bit == own_bit)
            def _():
                stays.start()

            @pl.when(bit != own_bit)
            def _():
                goes.start()

    def set_out_wait(array, refs, sems):
        for order in range(2):
            block = array.at[pl.ds(order * piece, piece), :]
            pltpu.make_async_copy(block, refs[2].at[order, 0, 0], sems.at[order]).wait()

    stages, start, finish, sent, _ = halving_scatter(
        parts, inbox, parts_send, parts_recv, layer_chip, layer_chips, core, tensor_index
    )
    dense_refs = (dense_send0_ref, dense_send1_ref, dense_keep_ref)

    def one_chip(index):
        step, place = index // layer_chips, index % layer_chips
        here = pl.ds(pl.multiple_of(place * pair_rows_count, pair_rows_count), pair_rows_count)
        parts[step, place, :, 0:hidden] = nn(turned_normed[here, :], upper_grad[step]).astype(bf16)
        parts[step, place, :, hidden:] = nn(turned_cot[here, :], active[step]).astype(bf16)

        @pl.when(place == layer_chips - 1)
        def _():
            start(step, 0)

    repeat(steps * layer_chips, one_chip)
    grads = whole(0)
    for number in range(3):
        share_copy(normed, 1, number).wait_send()
    add_cores(1)
    vectors_ref[...] = jnp.zeros_like(vectors_ref)
    vectors_ref[2:3] = column_sum(grads)
    part_grad, gain_part = layer_norm_back(middle[...], gain_ref[...], grads)
    vectors_ref[1:2] = column_sum(gain_part)
    own_cot = cot_ref[...].astype(f32)
    vectors_ref[3:4] = column_sum(own_cot)
    middle_grad = own_cot + part_grad
    middle_grad_ref[...] = middle_grad
    vectors_ref[0:1] = column_sum(middle_grad)
    low_grad[mine, :] = middle_grad.astype(bf16)
    low_swap = swap_copy(low_grad.at[mine], low_grad.at[mine], swap_sem, 5, partner)
    low_swap.start()
    swap_copy(low_grad.at[theirs], low_grad.at[theirs], swap_sem, 5, partner).wait_recv()

    def grads_out(owner, part, pair):
        target = (base + 2 * (2 * core + pair) + (part + flipped(chip, chips)) % 2, owner)
        here = (target[0] == dp_index) & (owner == tensor_index)
        source = outbox.at[owner, part, pair]
        destination = grads_ref.at[chip, tensor_index]
        far = pltpu.make_async_remote_copy(
            src_ref=source,
            dst_ref=destination,
            send_sem=outbox_send.at[owner, part, pair],
            recv_sem=outbox_recv.at[chip, tensor_index],
            device_id=target,
            device_id_type=MESH,
        )
        return here, far, pltpu.make_async_copy(source, destination, local_sem.at[1])

    def send_grads(step):
        owner = nearest(tensor_index, tensor_count, (2 * tensor_count - 2 - step // 2) % tensor_count)
        part = step % 2
        lanes = pl.ds(pl.multiple_of(owner * 128, 128), 128)
        result = nn(low_grad[part_span(part), :], dense[:, lanes]).astype(bf16)
        half = rows // 2
        for pair in range(2):
            cut = slice(pair * HD, (pair + 1) * HD)
            outbox[owner, part, pair] = jnp.concatenate(
                [result[:half, cut], result[half:, cut]], axis=1
            )
            here, far, near = grads_out(owner, part, pair)

            @pl.when(here)
            def _():
                near.start()

            @pl.when(jnp.logical_not(here))
            def _():
                far.start()

    repeat(2 * tensor_count, send_grads)

    def advance(stage):
        for step in range(steps):
            finish(step, stage)
            if stage + 1 < stages:
                start(step, stage + 1)

    advance(0)
    turned_low = turned_cot.at[:, 0 : 2 * rows]
    transpose_rows(low_grad, turned_low)

    def dense_chip(place):
        here = pl.ds(pl.multiple_of(place * pair_rows_count, pair_rows_count), pair_rows_count)
        dense_parts[place] = nn(turned_low[here, :], context[...]).astype(bf16)
        set_out(dense_parts.at[place], dense_refs, 0, place, dense_sem.at[place])

    repeat(layer_chips, dense_chip)
    block_ref[...] = (middle[...] + whole(1) + down_shift_ref[...]).astype(bf16)

    for stage in range(1, stages):
        advance(stage)
    for step in range(steps):
        feed_sum_ref[step] = parts[step, layer_chip]
    repeat(
        layer_chips,
        lambda place: set_out_wait(dense_parts.at[place], dense_refs, dense_sem.at[place]),
    )

    def arrived(step):
        place, owner = step // tensor_count, step % tensor_count
        destination = grads_ref.at[place, owner]
        here = (place == chip) & (owner == tensor_index) & (chip // 2 == core)

        @pl.when(here)
        def _():
            pltpu.make_async_copy(destination, destination, local_sem.at[1]).wait()

        @pl.when(jnp.logical_not(here))
        def _():
            pltpu.make_async_remote_copy(
                src_ref=destination,
                dst_ref=destination,
                send_sem=context_send.at[0, 0],
                recv_sem=outbox_recv.at[place, owner],
                device_id=partner,
                device_id_type=MESH,
            ).wait_recv()

    repeat(chips * tensor_count, arrived)

    def context_sent(step):
        here, far, _near = context_out(step)

        @pl.when(jnp.logical_not(here))
        def _():
            far.wait_send()

    repeat(chips * tensor_count, context_sent)

    def grads_sent(step):
        here, far, _near = grads_out(step // 4, step // 2 % 2, step % 2)

        @pl.when(jnp.logical_not(here))
        def _():
            far.wait_send()

    repeat(4 * tensor_count, grads_sent)

    for step in range(steps):
        for stage in range(stages):
            sent(step, stage)
    for which in range(2):
        core_copy(which).wait_send()
        pair_copy(which).wait_send()
    gather_sent()
    low_swap.wait_send()


def middle_part(
    context, inputs, cotangent, across, vectors, up_shift, feed, weight, dp_count, tensor_count, span
):
    rows, width = inputs.shape
    hidden = feed.shape[2] // 2
    piece = width // dp_count
    steps = tensor_count // 2
    chips, layer_chips = span // 2, dp_count // 2
    dma = pltpu.SemaphoreType.DMA
    vmem = pl.BlockSpec(memory_space=pltpu.VMEM)
    anywhere = pl.BlockSpec(memory_space=pl.ANY)
    dense_part = (piece, 128 * tensor_count)
    return pl.pallas_call(
        functools.partial(middle_kernel, dp_count, tensor_count, span),
        in_specs=[vmem] * 7 + [anywhere],
        out_specs=[vmem] * 3 + [anywhere] * 3 + [vmem] * 2 + [anywhere],
        out_shape=[
            jax.ShapeDtypeStruct((rows, width), bf16),
            jax.ShapeDtypeStruct((rows, width), f32),
            jax.ShapeDtypeStruct((steps, 2 * piece, 2 * hidden), bf16),
            jax.ShapeDtypeStruct((1, layer_chips // 2, *dense_part), bf16),
            jax.ShapeDtypeStruct((1, layer_chips // 2, *dense_part), bf16),
            jax.ShapeDtypeStruct((2, 1, layer_chips // 2, *dense_part), bf16),
            jax.ShapeDtypeStruct((8, width), f32),
            jax.ShapeDtypeStruct((steps, 8, hidden), f32),
            jax.ShapeDtypeStruct((chips, tensor_count, rows // 2, 128), bf16),
        ],
        scratch_shapes=[
            pltpu.VMEM((tensor_count, 2, 2, rows // 2, 128), bf16),
            pltpu.VMEM((2 * rows, 128 * tensor_count), bf16),
            pltpu.VMEM((width, 128 * tensor_count), bf16),
            pltpu.VMEM((steps, layer_chips, 2 * piece, 2 * hidden), bf16),
            pltpu.VMEM((rows, width), f32),
            pltpu.VMEM((4 * rows, width), bf16),
            pltpu.VMEM((4 * rows, width), bf16),
            pltpu.VMEM((width, 4 * rows), bf16),
            pltpu.VMEM((width, 4 * rows), bf16),
            pltpu.VMEM((steps, 4 * rows, hidden), bf16),
            pltpu.VMEM((steps, 4 * rows, hidden), bf16),
            pltpu.VMEM((4, rows, width), f32),
            pltpu.VMEM((4, rows, width), f32),
            pltpu.VMEM((rows, width), bf16),
            pltpu.VMEM((2, 2 * rows, width), bf16),
            pltpu.VMEM((2, rows, width), bf16),
            pltpu.VMEM((2 * rows, width), bf16),
            pltpu.VMEM((tensor_count, 2, 2, rows // 2, 128), bf16),
            pltpu.VMEM((steps, layer_chips, 2 * piece, 2 * hidden), bf16),
            pltpu.VMEM((steps, layer_chips - 1, 2 * piece, 2 * hidden), bf16),
            pltpu.VMEM((layer_chips, 2 * piece, 128 * tensor_count), bf16),
            dma((tensor_count,)),
            dma((2, 8)),
            dma((2, 3)),
            dma((2, 3)),
            dma((chips, tensor_count)),
            dma((tensor_count, 2, 2)),
            dma((tensor_count, 2, 2)),
            dma((chips, tensor_count)),
            dma((2,)),
            dma((steps, layer_chips, 2)),
            dma((steps, layer_chips - 1, 2)),
            dma((steps, layer_chips - 1, 2)),
            dma((steps, layer_chips - 1, 2)),
            dma((layer_chips, 2)),
        ],
        compiler_params=pltpu.CompilerParams(
            collective_id=1, has_side_effects=True, vmem_limit_bytes=62 * 2**20
        ),
        cost_estimate=pl.CostEstimate(
            flops=6 * 2 * 2 * rows * width * hidden * tensor_count,
            bytes_accessed=40_000_000,
            transcendentals=0,
        ),
        name="middle_part",
    )(context, inputs, cotangent, across, vectors, up_shift, feed, weight)


def finish_kernel(
    dp_count,
    tensor_count,
    span,
    dq_ref,
    dkv_ref,
    normed_ref,
    x_ref,
    vectors_in_ref,
    middle_grad_ref,
    vector_grads_ref,
    up_rows_ref,
    feed_sum_ref,
    feed_got_ref,
    dense_keep_ref,
    dense_got0_ref,
    dense_got1_ref,
    weight_ref,
    input_grad_ref,
    weight_grad_ref,
    up_grad_ref,
    down_grad_ref,
    dense_grad_ref,
    dense_bias_ref,
    gain_two_ref,
    bias_two_ref,
    down_bias_ref,
    gain_one_ref,
    bias_one_ref,
    up_sums_ref,
    qkv_sums_ref,
    weight,
    turned_normed,
    dkv_in,
    outbox,
    mixed_in,
    gathered,
    normed_total,
    swap_out,
    swap_in,
    parts,
    inbox,
    layer_inbox,
    dense_parts,
    dense_inbox,
    dense_layer_inbox,
    last_out,
    last_in,
    last_feed_out,
    last_feed_in,
    last_dense_out,
    last_dense_in,
    late,
    column_sums,
    sums_out,
    sums_in,
    sums,
    weight_sem,
    dense_load_sem,
    swap_sem,
    dkv_send,
    dkv_recv,
    outbox_send,
    mixed_recv,
    parts_send,
    parts_recv,
    layer_send,
    layer_recv,
    dense_send,
    dense_recv,
    dense_layer_send,
    dense_layer_recv,
    sums_send,
    sums_recv,
    local_sem,
):
    dp_index, tensor_index = lax.axis_index("dp"), lax.axis_index("tensor")
    rows, width = x_ref.shape
    columns = weight.shape[2]
    hidden = up_rows_ref.shape[1]
    core = dp_index % 2
    base = dp_index // span * span
    chip = dp_index % span // 2
    chips = span // 2
    layer_chip, layer_chips = dp_index // 2, dp_count // 2
    pair_rows_count = parts.shape[2]
    piece = pair_rows_count // 2
    partner = (dp_index + 1 - 2 * core, tensor_index)
    part_span = lambda part: pl.ds(pl.multiple_of(part * rows, 64), rows)
    dp_rows = rows * tensor_count
    devices = dp_count * tensor_count
    me = dp_index * tensor_count + tensor_index

    def weight_copy(owner):
        return pltpu.make_async_copy(
            weight_ref.at[owner, :, pl.ds(0, columns)], weight.at[owner], weight_sem.at[owner]
        )

    def loads(parts, inbox, keep_ref, got_refs, sems, item, slot):
        copies = []
        for order in range(2):
            rows_here = pl.ds(order * piece, piece)
            if order == 0:
                place = 2 * slot + layer_chip % 2
            else:
                place = slot + layer_chip // (layer_chips // 2) * (layer_chips // 2)
            copies += [
                pltpu.make_async_copy(
                    keep_ref.at[order, item, slot],
                    parts.at[item, place, rows_here, :],
                    sems.at[item, slot, order],
                ),
                pltpu.make_async_copy(
                    got_refs[order].at[item, slot],
                    inbox.at[item, slot, rows_here, :],
                    sems.at[item, slot, 2 + order],
                ),
            ]
        return copies

    def dense_loads(index):
        return loads(
            dense_parts,
            dense_inbox,
            dense_keep_ref,
            (dense_got0_ref, dense_got1_ref),
            dense_load_sem,
            0,
            index,
        )

    repeat(layer_chips // 2, lambda index: [copy.start() for copy in dense_loads(index)])
    repeat(tensor_count, lambda owner: weight_copy(owner).start())
    greet_all(dp_count, tensor_count, dp_index, tensor_index)

    def dkv_copy(place, whose):
        taken = 2 * place + (whose + flipped(place, chips)) % 2
        return pltpu.make_async_remote_copy(
            src_ref=dkv_ref.at[pl.ds(pl.multiple_of(taken * dp_rows, 128), dp_rows)],
            dst_ref=dkv_in.at[place],
            send_sem=dkv_send.at[place],
            recv_sem=dkv_recv.at[place],
            device_id=partner,
            device_id_type=MESH,
        )

    repeat(chips, lambda place: dkv_copy(place, 1 - core).start())
    place_here = (layer_chip, layer_chips, core, tensor_index)
    stages = layer_chips.bit_length() - 1
    _, dense_start, dense_finish, dense_sent, dense_add = halving_scatter(
        dense_parts, dense_inbox, dense_send, dense_recv, *place_here
    )
    repeat(2, lambda part: normed_total.__setitem__(part, jnp.zeros((rows, width), f32)))
    repeat(chips, lambda place: dkv_copy(place, 1 - core).wait_recv())

    def message(place, owner):
        part = (core + flipped(place, chips)) % 2
        target = (base + 2 * place + chip // 2, owner)
        here = (target[0] == dp_index) & (owner == tensor_index)
        source = outbox.at[place, owner]
        destination = mixed_in.at[tensor_index, chip % 2, part]
        far = pltpu.make_async_remote_copy(
            src_ref=source,
            dst_ref=destination,
            send_sem=outbox_send.at[place, owner],
            recv_sem=mixed_recv.at[tensor_index, chip % 2, part],
            device_id=target,
            device_id_type=MESH,
        )
        return here, far, pltpu.make_async_copy(source, destination, local_sem.at[0])

    def send_message(step):
        owner, place = nearest(tensor_index, tensor_count, step // chips), step % chips
        taken = 2 * place + (core + flipped(place, chips)) % 2
        own = pl.ds(pl.multiple_of(taken * dp_rows + owner * rows, 64), rows)
        total = dkv_ref[own, :].astype(f32) + dkv_in[
            place, pl.ds(pl.multiple_of(owner * rows, 64), rows), :
        ].astype(f32)
        queries = dq_ref[
            pl.ds(pl.multiple_of(place * dp_rows + owner * rows, 64), rows), :
        ].astype(f32)
        outbox[place, owner, 0:rows, :] = jnp.concatenate([queries, total[:, :HD]], axis=1).astype(
            bf16
        )
        half = rows // 2
        outbox[place, owner, rows:, :] = jnp.concatenate(
            [total[:half, HD:], total[half:, HD:]], axis=1
        ).astype(bf16)
        here, far, near = message(place, owner)

        @pl.when(here)
        def _():
            near.start()

        @pl.when(jnp.logical_not(here))
        def _():
            far.start()

    repeat(chips * tensor_count, send_message)

    def dense_layer_copy(step):
        owner = (tensor_index + step) % tensor_count
        return pltpu.make_async_remote_copy(
            src_ref=dense_parts.at[
                0, layer_chip, :, pl.ds(pl.multiple_of(owner * 128, 128), 128)
            ],
            dst_ref=dense_layer_inbox.at[step - 1],
            send_sem=dense_layer_send.at[step - 1],
            recv_sem=dense_layer_recv.at[step - 1],
            device_id=(dp_index, owner),
            device_id_type=MESH,
        )

    repeat(layer_chips // 2, lambda index: [copy.wait() for copy in dense_loads(index)])
    dense_add(0, 0)
    if stages > 1:
        dense_start(0, 1)
    transpose_rows(normed_ref, turned_normed)

    def sum_copy(which, step):
        other = (me + step) % devices
        there = (other // tensor_count, other % tensor_count)
        return pltpu.make_async_remote_copy(
            src_ref=sums_out.at[which, there[0], there[1]],
            dst_ref=sums_in.at[which, dp_index, tensor_index],
            send_sem=sums_send.at[which, there[0], there[1]],
            recv_sem=sums_recv.at[which, dp_index, tensor_index],
            device_id=there,
            device_id_type=MESH,
        )

    def sum_message(which, owner_dp, owner, vector_rows, row, count, vectors):
        block = pl.ds(pl.multiple_of(owner_dp * piece // 128 * 128, 128), 128)
        sums_out[which, owner_dp, owner] = jnp.zeros((8, 128), f32)
        sums_out[which, owner_dp, owner, 0:vector_rows, :] = vectors[0:vector_rows, block]
        for number in range(count):
            sums_out[which, owner_dp, owner, vector_rows + number : vector_rows + number + 1, :] = row[
                :, number * 128 : (number + 1) * 128
            ]

    def send_sums(which, vector_rows, row_of, count, vectors):
        def one(step):
            other = (me + step) % devices
            owner_dp, owner = other // tensor_count, other % tensor_count
            sum_message(which, owner_dp, owner, vector_rows, row_of(owner), count, vectors)

            @pl.when(step > 0)
            def _():
                sum_copy(which, step).start()

        repeat(devices, one)
        sums_in[which, dp_index, tensor_index] = sums_out[which, dp_index, tensor_index]

    send_sums(
        0, 4, lambda owner: up_rows_ref[pl.ds(2 * owner + core, 1), :], hidden // 128, vector_grads_ref
    )

    def layer_copy(step):
        owner = (tensor_index + step) % tensor_count
        return pltpu.make_async_remote_copy(
            src_ref=parts.at[owner, layer_chip],
            dst_ref=layer_inbox.at[step - 1],
            send_sem=layer_send.at[step - 1],
            recv_sem=layer_recv.at[step - 1],
            device_id=(dp_index, owner),
            device_id_type=MESH,
        )

    def tile_of(step):
        return jnp.where(step == 0, tensor_index, nearest(tensor_index, tensor_count, step - 1))

    def chip_copy(step, hop):
        target = (layer_chip + hop) % layer_chips
        return pltpu.make_async_remote_copy(
            src_ref=parts.at[step, target],
            dst_ref=inbox.at[step, hop - 1],
            send_sem=parts_send.at[step, hop - 1],
            recv_sem=parts_recv.at[step, hop - 1],
            device_id=(2 * target + core, tensor_index),
            device_id_type=MESH,
        )

    def hops(body):
        repeat(layer_chips - 1, lambda number: body(number + 1))

    def advance(step):
        tile = tile_of(step - 1)

        @pl.when(step > 0)
        def _():
            hops(lambda hop: chip_copy(tile, hop).wait_recv())
            value = parts[tile, layer_chip].astype(f32)
            for number in range(layer_chips - 1):
                value = value + inbox[tile, number].astype(f32)
            parts[tile, layer_chip] = value.astype(bf16)

            @pl.when(tile != tensor_index)
            def _():
                layer_copy((tile - tensor_index + tensor_count) % tensor_count).start()

    def dense_advance(stage):
        dense_finish(0, stage)
        if stage + 1 < stages:
            dense_start(0, stage + 1)
        else:
            for step in range(1, tensor_count):
                dense_layer_copy(step).start()

    def one_owner(step):
        owner = tile_of(step)
        weight_copy(owner).wait()
        column_sums[owner] = jnp.zeros(column_sums.shape[1:], f32)

        def one_part(part):
            for pair in range(2):
                destination = mixed_in.at[owner, pair, part]
                here = (
                    (owner == tensor_index)
                    & (chip == 2 * core + pair)
                    & ((part + flipped(chip, chips)) % 2 == core)
                )

                @pl.when(here)
                def _():
                    pltpu.make_async_copy(destination, destination, local_sem.at[0]).wait()

                @pl.when(jnp.logical_not(here))
                def _():
                    pltpu.make_async_remote_copy(
                        src_ref=destination,
                        dst_ref=destination,
                        send_sem=outbox_send.at[0, 0],
                        recv_sem=mixed_recv.at[owner, pair, part],
                        device_id=partner,
                        device_id_type=MESH,
                    ).wait_recv()

            pieces_here = []
            for pair in range(2):
                value = mixed_in[owner, pair, part]
                pieces_here += [value[:rows], pair_rows(value[rows:])]
            grads = jnp.concatenate(pieces_here, axis=1)
            gathered[part_span(part), :] = grads
            column_sums[owner, 0:1] += column_sum(grads.astype(f32))
            normed_total[part] += nt(grads, weight[owner])

        repeat(2, one_part)

        def one_chip(place):
            here = pl.ds(pl.multiple_of(place * pair_rows_count, pair_rows_count), pair_rows_count)
            parts[owner, place] = nn(turned_normed[here, :], gathered[...]).astype(bf16)

        repeat(layer_chips, one_chip)
        hops(lambda hop: chip_copy(owner, hop).start())
        advance(step)
        for stage in range(1, stages):

            @pl.when(step == min(stage, tensor_count - 1))
            def _():
                dense_advance(stage)

    repeat(tensor_count, one_owner)

    swap_out[...] = normed_total[1 - core].astype(bf16)
    swap = swap_copy(swap_out, swap_in, swap_sem, 0, partner)
    swap.start()
    advance(tensor_count)
    swap.wait_recv()
    grads = normed_total[core] + swap_in[...].astype(f32)
    part_grad, gain_part = layer_norm_back(x_ref[...].astype(f32), vectors_in_ref[0:1, :], grads)
    input_grad_ref[...] = middle_grad_ref[...] + part_grad
    late[...] = jnp.zeros_like(late)
    late[0:1] = column_sum(gain_part)
    late[1:2] = column_sum(grads)
    send_sums(1, 2, lambda owner: column_sums[owner, 0:1, :], columns // 128, late)

    kept = pl.ds(pl.multiple_of(core * piece, piece), piece)
    given = pl.ds(pl.multiple_of((1 - core) * piece, piece), piece)

    def total(array, arrived, where):
        value = array[tensor_index, layer_chip, where, :].astype(f32)
        for step in range(arrived.shape[0]):
            value = value + arrived[step, where, :].astype(f32)
        return value

    def dense_total(where):
        lanes = pl.ds(pl.multiple_of(tensor_index * 128, 128), 128)
        value = dense_parts[0, layer_chip, where, lanes].astype(f32)
        for step in range(1, tensor_count):
            value = value + dense_layer_inbox[step - 1, where, :].astype(f32)
        return value

    def feed_total(where):
        value = feed_sum_ref[0, where, :].astype(f32)
        for number in range(feed_got_ref.shape[0]):
            value = value + feed_got_ref[number, where, :].astype(f32)
        return value

    last_feed_out[...] = feed_total(given)
    last_feed = swap_copy(last_feed_out, last_feed_in, swap_sem, 2, partner)
    last_feed.start()
    own_total = feed_total(kept)
    my_half = pl.ds(pl.multiple_of(core * hidden, 128), hidden)
    their_half = pl.ds(pl.multiple_of((1 - core) * hidden, 128), hidden)
    up_grad_ref[:, my_half] = own_total[:, :hidden]
    down_grad_ref[my_half, :] = own_total[:, hidden:].T
    for step in range(1, tensor_count):
        dense_layer_copy(step).wait_recv()
    last_dense_out[...] = dense_total(given)
    last_dense = swap_copy(last_dense_out, last_dense_in, swap_sem, 3, partner)
    last_dense.start()
    dense_grad_ref[pl.ds(pl.multiple_of(core * 128, 128), 128), :] = dense_total(kept).T

    for step in range(1, tensor_count):
        layer_copy(step).wait_recv()
    last_out[...] = total(parts, layer_inbox, given)
    last = swap_copy(last_out, last_in, swap_sem, 1, partner)
    last.start()
    weight_grad_ref[:, pl.ds(pl.multiple_of(core * columns, 128), columns)] = total(
        parts, layer_inbox, kept
    )
    last_feed.wait()
    up_grad_ref[:, their_half] = last_feed_in[:, :hidden]
    down_grad_ref[their_half, :] = last_feed_in[:, hidden:].T
    last_dense.wait()
    dense_grad_ref[pl.ds(pl.multiple_of((1 - core) * 128, 128), 128), :] = last_dense_in[...].T
    last.wait()
    weight_grad_ref[:, pl.ds(pl.multiple_of((1 - core) * columns, 128), columns)] = last_in[...]

    for which in range(2):

        def sum_wait(step):
            other = (me + step + 1) % devices
            there = (other // tensor_count, other % tensor_count)
            place = sums_in.at[which, there[0], there[1]]
            pltpu.make_async_remote_copy(
                src_ref=place,
                dst_ref=place,
                send_sem=sums_send.at[which, there[0], there[1]],
                recv_sem=sums_recv.at[which, there[0], there[1]],
                device_id=partner,
                device_id_type=MESH,
            ).wait_recv()

        repeat(devices - 1, sum_wait)
        sums[which] = jnp.zeros(sums.shape[1:], f32)

        def add_one(step):
            owner_dp, owner = step // tensor_count, step % tensor_count
            sums[which, owner_dp % 2] += sums_in[which, owner_dp, owner]

        repeat(devices, add_one)
        vectors = (
            (dense_bias_ref, gain_two_ref, bias_two_ref, down_bias_ref),
            (gain_one_ref, bias_one_ref),
        )[which]
        for number, vector in enumerate(vectors):
            vector[...] = sums[which, 0, number : number + 1] + sums[which, 1, number : number + 1]
    up_sums_ref[...] = sums[0, :, 4:]
    qkv_sums_ref[...] = sums[1, :, 2:5]

    repeat(chips, lambda place: dkv_copy(place, 1 - core).wait_send())

    def message_sent(step):
        here, far, _near = message(step // tensor_count, step % tensor_count)

        @pl.when(jnp.logical_not(here))
        def _():
            far.wait_send()

    repeat(chips * tensor_count, message_sent)
    for stage in range(stages):
        if stage > 0:
            dense_sent(0, stage)
    repeat(tensor_count, lambda step: hops(lambda hop: chip_copy(step, hop).wait_send()))
    for step in range(1, tensor_count):
        layer_copy(step).wait_send()
        dense_layer_copy(step).wait_send()
    for which in range(2):
        repeat(devices - 1, lambda step: sum_copy(which, step + 1).wait_send())
    swap.wait_send()


def finish_part(
    dq,
    dkv,
    normed,
    inputs,
    vectors,
    middle_grad,
    vector_grads,
    up_rows,
    feed_sum,
    feed_got,
    dense_keep,
    dense_got,
    weight,
    dp_count,
    tensor_count,
    span,
):
    rows, width = inputs.shape
    columns = weight.shape[2] - 128
    hidden = up_rows.shape[1]
    piece = width // dp_count
    chips, layer_chips = span // 2, dp_count // 2
    dma = pltpu.SemaphoreType.DMA
    vmem = pl.BlockSpec(memory_space=pltpu.VMEM)
    anywhere = pl.BlockSpec(memory_space=pl.ANY)
    message = (rows * 3 // 2, 128)
    part = (2 * piece, columns)
    dense_part = (2 * piece, dense_keep.shape[4])
    halving = (layer_chips - 1, 2)
    return pl.pallas_call(
        functools.partial(finish_kernel, dp_count, tensor_count, span),
        in_specs=[vmem] * 10 + [anywhere] * 4,
        out_specs=[vmem] * 13,
        out_shape=[
            jax.ShapeDtypeStruct((rows, width), f32),
            jax.ShapeDtypeStruct((piece, 2 * columns), f32),
            jax.ShapeDtypeStruct((piece, 2 * hidden), f32),
            jax.ShapeDtypeStruct((2 * hidden, piece), f32),
            jax.ShapeDtypeStruct((2 * 128, piece), f32),
            *[jax.ShapeDtypeStruct((1, 128), f32)] * 6,
            jax.ShapeDtypeStruct((2, 4, 128), f32),
            jax.ShapeDtypeStruct((2, 3, 128), f32),
        ],
        scratch_shapes=[
            pltpu.VMEM((tensor_count, width, columns), bf16),
            pltpu.VMEM((width, 2 * rows), bf16),
            pltpu.VMEM((chips, rows * tensor_count, 128), bf16),
            pltpu.VMEM((chips, tensor_count, *message), bf16),
            pltpu.VMEM((tensor_count, 2, 2, *message), bf16),
            pltpu.VMEM((2 * rows, columns), bf16),
            pltpu.VMEM((2, rows, width), f32),
            pltpu.VMEM((rows, width), bf16),
            pltpu.VMEM((rows, width), bf16),
            pltpu.VMEM((tensor_count, layer_chips, *part), bf16),
            pltpu.VMEM((tensor_count, layer_chips - 1, *part), bf16),
            pltpu.VMEM((tensor_count - 1, *part), bf16),
            pltpu.VMEM((1, layer_chips, *dense_part), bf16),
            pltpu.VMEM((1, layer_chips - 1, *dense_part), bf16),
            pltpu.VMEM((tensor_count - 1, 2 * piece, 128), bf16),
            pltpu.VMEM((piece, columns), f32),
            pltpu.VMEM((piece, columns), f32),
            pltpu.VMEM((piece, 2 * hidden), f32),
            pltpu.VMEM((piece, 2 * hidden), f32),
            pltpu.VMEM((piece, 128), f32),
            pltpu.VMEM((piece, 128), f32),
            pltpu.VMEM((8, width), f32),
            pltpu.VMEM((tensor_count, 8, columns), f32),
            pltpu.VMEM((2, dp_count, tensor_count, 8, 128), f32),
            pltpu.VMEM((2, dp_count, tensor_count, 8, 128), f32),
            pltpu.VMEM((2, 2, 8, 128), f32),
            dma((tensor_count,)),
            dma((1, layer_chips // 2, 4)),
            dma((2, 4)),
            dma((chips,)),
            dma((chips,)),
            dma((chips, tensor_count)),
            dma((tensor_count, 2, 2)),
            dma((tensor_count, layer_chips - 1)),
            dma((tensor_count, layer_chips - 1)),
            dma((tensor_count - 1,)),
            dma((tensor_count - 1,)),
            dma((1, *halving)),
            dma((1, *halving)),
            dma((tensor_count - 1,)),
            dma((tensor_count - 1,)),
            dma((2, dp_count, tensor_count)),
            dma((2, dp_count, tensor_count)),
            dma((1,)),
        ],
        compiler_params=pltpu.CompilerParams(
            collective_id=2, has_side_effects=True, vmem_limit_bytes=60 * 2**20
        ),
        cost_estimate=pl.CostEstimate(
            flops=2 * 2 * 2 * rows * width * columns * tensor_count,
            bytes_accessed=30_000_000,
            transcendentals=0,
        ),
        name="finish_part",
    )(
        dq,
        dkv,
        normed,
        inputs,
        vectors,
        middle_grad,
        vector_grads,
        up_rows,
        feed_sum,
        feed_got,
        dense_keep,
        *dense_got,
        weight,
    )


def per_device(
    block_in,
    norm1_gain,
    norm1_bias,
    qkv_weight,
    qv_bias,
    dense_weight,
    dense_bias,
    norm2_gain,
    norm2_bias,
    up_weight,
    up_bias,
    down_weight,
    down_bias,
    cotangent,
    seg_parent,
    seg_length,
):
    dp_count, tensor_count = lax.axis_size("dp"), lax.axis_size("tensor")
    dp_index, tensor_index = lax.axis_index("dp"), lax.axis_index("tensor")
    rows, width = block_in.shape
    dp_rows = rows * tensor_count
    span = PAIR_TOKENS // dp_rows
    heads_here = HEADS // tensor_count
    local_index = lax.rem(dp_index, span)
    core = lax.rem(dp_index, 2)

    piece = norm1_gain.shape[0]

    def small_row(value):
        return jnp.pad(value.reshape(1, -1), ((0, 0), (0, 128 - value.size)))

    small = [norm1_gain, norm1_bias, norm2_gain, norm2_bias, dense_bias, down_bias, qv_bias, up_bias]
    small = jnp.pad(jnp.concatenate([small_row(value) for value in small]), ((0, 8), (0, 0)))

    def by_core(value):
        return value.reshape(value.shape[0], 2, -1).transpose(1, 0, 2)

    shard = jnp.concatenate([by_core(qkv_weight), by_core(dense_weight.T)], axis=2)
    feed_shard = jnp.concatenate([by_core(up_weight), by_core(down_weight.T)], axis=2)
    head = tensor_index * heads_here + local_index // 2
    slope = jnp.exp2(-8.0 * (head.astype(f32) + 1.0) / HEADS) / TRUNK
    half = span // 2
    taken = jnp.stack([2 * i + (core + flipped(i, half)) % 2 for i in range(half)])
    block_ids = (
        taken[:, None] * (dp_rows // QUERY_BLOCK)
        + jnp.arange(dp_rows // QUERY_BLOCK, dtype=jnp.int32)[None, :]
    ).reshape(-1)

    across = [(layer, layer + 1 - 2 * (layer % 2)) for layer in range(tensor_count)]
    normed_both, mixed, weight, vectors, up_shift, feed_block = project(
        block_in, small, shard, feed_shard, dp_count, tensor_count, span
    )
    weight = weight.reshape(tensor_count, width, -1)
    feed_block, cotangent = lax.optimization_barrier((feed_block, cotangent))
    cot_across = lax.ppermute(cotangent, "tensor", across)
    feed_far = [
        lax.ppermute(
            feed_block, "tensor", [(layer, (layer + hop) % tensor_count) for layer in range(tensor_count)]
        )
        for hop in range(tensor_count - 2, 0, -2)
    ]
    feed = jnp.stack([feed_block] + feed_far)
    bounds, by_segment, block_list, block_count = pair_tables(
        seg_parent, seg_length, dp_index // span, slope, block_ids
    )
    tables = (block_ids, block_count, block_list, bounds, by_segment)
    packed_context, out_float, keys, queries = attention_forward(*tables, mixed, tensor_count)
    (
        block_out,
        middle_grad,
        feed_sum,
        dense_send0,
        dense_send1,
        dense_keep,
        vector_grads,
        up_shift_part,
        packed_grads,
    ) = middle_part(
        packed_context,
        block_in,
        cotangent,
        cot_across,
        vectors,
        up_shift,
        feed,
        weight,
        dp_count,
        tensor_count,
        span,
    )
    low_bit = [(device, device + 2 - 4 * (device // 2 % 2)) for device in range(dp_count)]
    half_dp = dp_count // 2
    high_bit = [(device, (device + half_dp) % dp_count) for device in range(dp_count)]
    feed_got = jnp.stack(
        [
            lax.ppermute(
                feed_sum[step],
                "tensor",
                [(layer, (layer + 2 * step) % tensor_count) for layer in range(tensor_count)],
            )
            for step in range(1, feed_sum.shape[0])
        ]
    )
    dense_got = (lax.ppermute(dense_send0, "dp", low_bit), lax.ppermute(dense_send1, "dp", high_bit))
    dq, dkv = attention_backward(*tables[:3], keys, queries, mixed, packed_grads, out_float)
    hidden = up_shift_part.shape[2]
    up_part = jnp.zeros((tensor_count, 2, hidden), f32)
    for step in range(up_shift_part.shape[0]):
        owner = lax.rem(tensor_index + step * (tensor_count // up_shift_part.shape[0]), tensor_count)
        up_part = lax.dynamic_update_slice(up_part, up_shift_part[step, :1][None], (owner, core, 0))
    up_rows = up_part.reshape(2 * tensor_count, hidden)
    (
        input_grad,
        qkv_weight_grad,
        up_grad,
        down_grad,
        dense_grad,
        *vectors_out,
        up_sums,
        qkv_sums,
    ) = finish_part(
        dq,
        dkv,
        normed_both.reshape(2 * rows, width),
        block_in,
        vectors,
        middle_grad,
        vector_grads,
        up_rows,
        feed_sum,
        feed_got,
        dense_keep,
        dense_got,
        weight,
        dp_count,
        tensor_count,
        span,
    )
    offset = lax.rem(dp_index * piece, 128)

    def own_vector(number):
        value = vectors_out[number].reshape(128)
        if piece % 128 == 0:
            return value
        return lax.dynamic_slice_in_dim(value, offset, piece, 0)

    def own_matrix(whole, shape):
        return lax.dynamic_slice_in_dim(whole, dp_index * shape[1], shape[1], 1)

    qkv_totals = qkv_sums.reshape(heads_here, 3, HD)
    qv_grad = jnp.concatenate([qkv_totals[:, 0], qkv_totals[:, 2]], axis=1)
    up_totals = up_sums.reshape(up_bias.shape[0], 128)
    return (
        block_out,
        input_grad,
        own_vector(4),
        own_vector(5),
        qkv_weight_grad,
        own_matrix(qv_grad, qv_bias.shape),
        dense_grad,
        own_vector(0),
        own_vector(1),
        own_vector(2),
        up_grad,
        own_matrix(up_totals, up_bias.shape),
        down_grad,
        own_vector(3),
    )


def solution(mesh):
    rows = P(("dp", "tensor"), None)
    in_specs = (
        rows,
        P("dp"),
        P("dp"),
        P("dp", "tensor"),
        P("tensor", "dp"),
        P("tensor", "dp"),
        P("dp"),
        P("dp"),
        P("dp"),
        P("dp", "tensor"),
        P("tensor", "dp"),
        P("tensor", "dp"),
        P("dp"),
        rows,
        P(),
        P(),
    )
    out_specs = (
        rows,
        rows,
        P("dp"),
        P("dp"),
        P("dp", "tensor"),
        P("tensor", "dp"),
        P("tensor", "dp"),
        P("dp"),
        P("dp"),
        P("dp"),
        P("dp", "tensor"),
        P("tensor", "dp"),
        P("tensor", "dp"),
        P("dp"),
    )
    return jax.shard_map(
        per_device, mesh=mesh, in_specs=in_specs, out_specs=out_specs, check_vma=False
    )
```
